32 devices in a mesh: dp: 4 (over y, x), mp: 8 (over z, core).
Axes of the slice: x: 2, y: 2, z: 4, core: 2. Of those that a mesh axis runs over, the one named last changes fastest.
Arguments:
- text_states: bfloat16 [8, 2048, 2048], P('dp', 'mp'), may hold values from -6 to 6
- image_states: bfloat16 [8, 384, 2048], P('dp'), may hold values from -6 to 6
- image_offsets: int32 [8, 6], P('dp'), may hold values from 0 to 1984, as said below
- image_counts: int32 [8], P('dp'), may hold values from 0 to 6, as said below
- output_grad: bfloat16 [8, 2048, 2048], P('dp', 'mp'), may hold values from -6 to 6
- head_master: float32 [3, 2048, 2048], P(None, 'dp', 'mp'), may hold values from -0.1502602 to 0.1502602
- head_moment: float32 [3, 2048, 2048], P(None, 'dp', 'mp'), may hold values from -80 to 80
- head_square: float32 [3, 2048, 2048], P(None, 'dp', 'mp'), may hold values from 16.384 to 262.144
- outward_master: float32 [2048, 2048], P('dp'), may hold values from -0.1502602 to 0.1502602
- outward_moment: float32 [2048, 2048], P('dp'), may hold values from -80 to 80
- outward_square: float32 [2048, 2048], P('dp'), may hold values from 8.192 to 131.072
- upward_master: float32 [2048, 8192], P('dp', 'mp'), may hold values from -0.1502602 to 0.1502602
- upward_moment: float32 [2048, 8192], P('dp', 'mp'), may hold values from -80 to 80
- upward_square: float32 [2048, 8192], P('dp', 'mp'), may hold values from 8.192 to 131.072
- downward_master: float32 [8192, 2048], P('mp', 'dp'), may hold values from -0.0751301 to 0.0751301
- downward_moment: float32 [8192, 2048], P('mp', 'dp'), may hold values from -80 to 80
- downward_square: float32 [8192, 2048], P('mp', 'dp'), may hold values from 8.192 to 131.072
- gains_master: float32 [14336], replicated, may hold values from 0.525 to 1.925
- gains_moment: float32 [14336], replicated, may hold values from -80 to 80
- gains_square: float32 [14336], replicated, may hold values from 8.192 to 131.072
Outputs:
- layer_output: bfloat16 [8, 2048, 2048], P('dp', 'mp')
- input_grad: float32 [8, 2048, 2048], P('dp', 'mp')
- moment_head: float32 [3, 2048, 2048], P(None, 'dp', 'mp')
- square_head: float32 [3, 2048, 2048], P(None, 'dp', 'mp')
- updated_head: float32 [3, 2048, 2048], P(None, 'dp', 'mp')
- copied_head: bfloat16 [3, 2048, 2048], P(None, 'dp', 'mp')
- moment_outward: float32 [2048, 2048], P('dp')
- square_outward: float32 [2048, 2048], P('dp')
- updated_outward: float32 [2048, 2048], P('dp')
- copied_outward: bfloat16 [2048, 2048], P('dp')
- moment_upward: float32 [2048, 8192], P('dp', 'mp')
- square_upward: float32 [2048, 8192], P('dp', 'mp')
- updated_upward: float32 [2048, 8192], P('dp', 'mp')
- copied_upward: bfloat16 [2048, 8192], P('dp', 'mp')
- moment_downward: float32 [8192, 2048], P('mp', 'dp')
- square_downward: float32 [8192, 2048], P('mp', 'dp')
- updated_downward: float32 [8192, 2048], P('mp', 'dp')
- copied_downward: bfloat16 [8192, 2048], P('mp', 'dp')
- moment_gains: float32 [14336], replicated
- square_gains: float32 [14336], replicated
- updated_gains: float32 [14336], replicated
- update_norms: float32 [10, 2], replicated
The draws below stay inside these ranges and needn't reach their ends.
Inputs may be any that keep to these rules, and one draw needn't show every extreme that they name: `image_counts`: images in a sequence; in every draw some sequence holds 6 images and some holds none. `image_offsets`: start position of each image in its sequence; images lie inside the sequence in increasing order, each 64 positions long, none intersecting; entries at or after a sequence's count are ignored.
All inputs are finite; a program needn't handle non-finite values.
Results may differ from the reference program's by a relative error of at most 0.02.
Values may be sent and summed in bfloat16 or wider, within the bound.
A program may use at most 384 MiB of HBM per device.

```python
import jax
import jax.numpy as jnp
from jax import lax

D = 2048
HEAD_DIM = 64
FF = 8192
LENGTH = 2048
PICS = 6
PATCH = 64
STEP = 10
SEQS = 8
TOKENS = 16384
GAINS = 14336


def rising_factor(rows, cols, ratio, col_sign):
    row_frac = jnp.arange(rows, dtype=jnp.float32) / rows
    col_frac = jnp.arange(cols, dtype=jnp.float32) / cols
    return ratio ** (row_frac[:, None] - 0.5) * ratio ** (col_sign * (col_frac[None, :] - 0.5))


def square_law(key, shape, level):
    rows = shape[-2]
    cols = shape[-1]
    row_frac = jnp.arange(rows, dtype=jnp.float32) / rows
    col_frac = jnp.arange(cols, dtype=jnp.float32) / cols
    ramp = 1.0 + 1.5 * (row_frac[:, None] + col_frac[None, :])
    spread = jax.random.uniform(key, shape, jnp.float32, 0.5, 2.0)
    return level * 0.001 * TOKENS * spread * ramp


def gain_fraction():
    model_part = jnp.arange(D, dtype=jnp.float32) / D
    hidden_part = jnp.arange(FF, dtype=jnp.float32) / FF
    return jnp.concatenate([model_part, model_part, model_part, hidden_part])


def draw_head_master(key, part):
    key = jax.random.fold_in(key, 1)
    noise = jnp.clip(jax.random.normal(key, (3, D, D), jnp.float32), -4.0, 4.0)
    ratio = 1.7
    factor = jnp.stack([rising_factor(D, D, ratio, 1.0), rising_factor(D, D, ratio, -1.0), rising_factor(D, D, ratio, -1.0)])
    return noise * factor * D ** (-0.5)


def draw_outward_master(key, part):
    key = jax.random.fold_in(key, 2)
    noise = jnp.clip(jax.random.normal(key, (D, D), jnp.float32), -4.0, 4.0)
    ratio = 1.7
    return noise * rising_factor(D, D, ratio, 1.0) * D ** (-0.5)


def draw_upward_master(key, part):
    key = jax.random.fold_in(key, 3)
    noise = jnp.clip(jax.random.normal(key, (D, FF), jnp.float32), -4.0, 4.0)
    ratio = 1.7
    return noise * rising_factor(D, FF, ratio, 1.0) * D ** (-0.5)


def draw_downward_master(key, part):
    key = jax.random.fold_in(key, 4)
    noise = jnp.clip(jax.random.normal(key, (FF, D), jnp.float32), -4.0, 4.0)
    ratio = 1.7
    return noise * rising_factor(FF, D, ratio, 1.0) * FF ** (-0.5)


def draw_gains_master(key, part):
    key = jax.random.fold_in(key, 5)
    fraction = gain_fraction()
    return 0.8 * 1.7 ** fraction * jax.random.uniform(key, (GAINS,), jnp.float32, 0.85, 1.15)


def draw_head_square(key, part):
    key = jax.random.fold_in(key, 6)
    return square_law(key, (3, D, D), 2.0)


def draw_outward_square(key, part):
    key = jax.random.fold_in(key, 7)
    return square_law(key, (D, D), 1.0)


def draw_upward_square(key, part):
    key = jax.random.fold_in(key, 8)
    return square_law(key, (D, FF), 1.0)


def draw_downward_square(key, part):
    key = jax.random.fold_in(key, 9)
    return square_law(key, (FF, D), 1.0)


def draw_gains_square(key, part):
    key = jax.random.fold_in(key, 10)
    spread = jax.random.uniform(key, (GAINS,), jnp.float32, 0.5, 2.0)
    return 0.001 * TOKENS * spread * (1.0 + 3.0 * gain_fraction())


def draw_image_counts(key, part):
    key = jax.random.fold_in(key, 11)
    key_counts, key_order = jax.random.split(key)
    counts = jax.random.randint(key_counts, (SEQS,), 0, PICS + 1, dtype=jnp.int32)
    chosen = jax.random.permutation(key_order, SEQS)
    counts = counts.at[chosen[0]].set(PICS)
    return counts.at[chosen[1]].set(0)


def draw_image_offsets(key, part):
    key = jax.random.fold_in(key, 12)
    key_starts, key_row = jax.random.split(key)
    leftover = LENGTH - PICS * PATCH
    starts = jax.random.randint(key_starts, (SEQS, PICS), 0, leftover + 1, dtype=jnp.int32)
    row_pick = jax.random.randint(key_row, (), 0, SEQS, dtype=jnp.int32)
    row_hit = (jnp.arange(SEQS, dtype=jnp.int32) == row_pick)[:, None]
    column = jnp.arange(PICS, dtype=jnp.int32)[None, :]
    starts = jnp.where(row_hit & (column == 0), 0, starts)
    starts = jnp.where(row_hit & (column == PICS - 1), leftover, starts)
    starts = jnp.sort(starts, axis=-1)
    return starts + column * PATCH


def steps_of(own_key, shape, pieces, least, high):
    def one(dim, parts):
        heights = jax.random.uniform(jax.random.fold_in(jax.random.fold_in(own_key, 6), dim), (parts,), jnp.float32, least / len(pieces), high / len(pieces))
        return jnp.repeat(jnp.exp(heights), shape[dim] // parts).reshape((-1,) + (1,) * (len(shape) - dim - 1))

    gain = one(*pieces[0])
    for cut in pieces[1:]:
        gain = gain * one(*cut)
    return gain


def normal_values(key, extent, deviation, most, cuts=(), held_as=jnp.bfloat16):
    values = jax.random.normal(key, extent, jnp.float32) * deviation
    if len(cuts) > 0:
        values = steps_of(key, extent, cuts, -0.22, 0.18) * values
    return jnp.clip(values, min=-most, max=most).astype(held_as)


def setup_inputs(seed: int = 0) -> dict:
    keys = jax.random.split(jax.random.key(seed), 21)
    text_states = normal_values(keys[0], (SEQS, LENGTH, D), 1.0, 6.0, ((0, 4), (1, 8)))
    image_states = normal_values(keys[1], (SEQS, PICS * PATCH, D), 1.0, 6.0, ((0, 4),))
    image_offsets = draw_image_offsets(jax.random.fold_in(keys[20], 71), 0)
    image_counts = draw_image_counts(jax.random.fold_in(keys[20], 71), 0)
    output_grad = normal_values(keys[4], (SEQS, LENGTH, D), 1.0, 6.0, ((0, 4), (1, 8)))
    head_master = draw_head_master(jax.random.fold_in(keys[20], 71), 0)
    head_moment = normal_values(keys[6], (3, D, D), (0.11 * TOKENS ** 0.5), 80.0, ((1, 4), (2, 8)), jnp.float32)
    head_square = draw_head_square(jax.random.fold_in(keys[20], 71), 0)
    outward_master = draw_outward_master(jax.random.fold_in(keys[20], 71), 0)
    outward_moment = normal_values(keys[9], (D, D), (0.11 * TOKENS ** 0.5), 80.0, ((0, 4),), jnp.float32)
    outward_square = draw_outward_square(jax.random.fold_in(keys[20], 71), 0)
    upward_master = draw_upward_master(jax.random.fold_in(keys[20], 71), 0)
    upward_moment = normal_values(keys[12], (D, FF), (0.11 * TOKENS ** 0.5), 80.0, ((0, 4), (1, 8)), jnp.float32)
    upward_square = draw_upward_square(jax.random.fold_in(keys[20], 71), 0)
    downward_master = draw_downward_master(jax.random.fold_in(keys[20], 71), 0)
    downward_moment = normal_values(keys[15], (FF, D), (0.11 * TOKENS ** 0.5), 80.0, ((0, 8), (1, 4)), jnp.float32)
    downward_square = draw_downward_square(jax.random.fold_in(keys[20], 71), 0)
    gains_master = draw_gains_master(jax.random.fold_in(keys[20], 71), 0)
    gains_moment = normal_values(keys[18], (GAINS,), (0.11 * TOKENS ** 0.5), 80.0, (), jnp.float32)
    gains_square = draw_gains_square(jax.random.fold_in(keys[20], 71), 0)
    return dict(text_states=text_states, image_states=image_states, image_offsets=image_offsets, image_counts=image_counts, output_grad=output_grad, head_master=head_master, head_moment=head_moment, head_square=head_square, outward_master=outward_master, outward_moment=outward_moment, outward_square=outward_square, upward_master=upward_master, upward_moment=upward_moment, upward_square=upward_square, downward_master=downward_master, downward_moment=downward_moment, downward_square=downward_square, gains_master=gains_master, gains_moment=gains_moment, gains_square=gains_square)


EPS_NORM = 1e-05
BETA_ONE = 0.9
BETA_TWO = 0.999
EPS_ADAM = 1e-06
DECAY_RATE = 0.01
STEP_RATE = 0.5
HIGHEST = lax.Precision.HIGHEST

@jax.custom_vjp
def low(v):
    return lax.optimization_barrier(v.astype(jnp.bfloat16)).astype(jnp.float32)

@jax.custom_vjp
def low_back(v):
    return v

def low_keep(v):
    return (low(v), None)

def low_pass(kept, grad):
    return (grad,)

def back_keep(v):
    return (v, None)

def back_low(kept, grad):
    return (low(grad),)
low.defvjp(low_keep, low_pass)
low_back.defvjp(back_keep, back_low)

def layer_norm(inputs, gain_vector):
    centre = lax.optimization_barrier(jnp.mean(inputs, axis=-1, keepdims=True))
    shifted = inputs - centre
    spread = lax.optimization_barrier(jnp.mean(shifted * shifted, axis=-1, keepdims=True))
    return shifted * lax.rsqrt(spread + EPS_NORM) * gain_vector

def xpos_tables(length, head_size):
    halfway = head_size // 2
    pair_index = jnp.arange(halfway, dtype=jnp.float32)
    angular = jnp.exp(-(2.0 * pair_index / head_size) * jnp.log(10000.0))
    zeta_base = (2.0 * pair_index + 0.4 * head_size) / (1.4 * head_size)
    position = jnp.arange(length, dtype=jnp.float32)[:, None, None]
    return (jnp.cos(position * angular), jnp.sin(position * angular), position / 512.0 * jnp.log(zeta_base))

def rotate(inputs, tables, polarity):
    cosine, sine_part, exponent = tables
    halfway = inputs.shape[-1] // 2
    factor = jnp.exp(polarity * exponent)
    leading = inputs[..., :halfway]
    behind = inputs[..., halfway:]
    return jnp.concatenate([(leading * cosine - behind * sine_part) * factor, (behind * cosine + leading * sine_part) * factor], axis=-1)

def merge_images(text_rows, image_rows, offsets, image_count, position):
    slot_index = jnp.arange(offsets.shape[0], dtype=jnp.int32)
    inside = (position[:, None] >= offsets[None, :]) & (position[:, None] < offsets[None, :] + PATCH) & (slot_index[None, :] < image_count)
    picked = lax.optimization_barrier(jnp.sum(jnp.where(inside, slot_index[None, :] * PATCH + position[:, None] - offsets[None, :], 0), axis=-1)).astype(jnp.int32)
    chosen = jnp.take(image_rows, picked, axis=0)
    covered = jnp.any(inside, axis=-1)
    return jnp.where(covered[:, None], chosen, text_rows)

def attend(queries, key_rows, values):
    length = queries.shape[0]
    block_len = min(512, length)
    key_place = jnp.arange(length, dtype=jnp.int32)

    def one_block(start):
        query_block = lax.dynamic_slice_in_dim(queries, start, block_len, 0)
        scores = low_back(jnp.einsum('qhd,khd->hqk', query_block, key_rows, precision=HIGHEST) * 0.125)
        allowed = key_place[None, :] <= (start + jnp.arange(block_len, dtype=jnp.int32))[:, None]
        scores = jnp.where(allowed[None], scores, -1e+30)
        highest = lax.optimization_barrier(jnp.max(scores, axis=-1, keepdims=True))
        exponent = jnp.exp(scores - highest)
        attention = exponent / lax.optimization_barrier(jnp.sum(exponent, axis=-1, keepdims=True))
        return jnp.einsum('hqk,khd->qhd', low(attention), values, precision=HIGHEST)
    starts = jnp.arange(length // block_len, dtype=jnp.int32) * block_len
    blocks_out = lax.map(jax.checkpoint(one_block), starts)
    return blocks_out.reshape(length, queries.shape[1], queries.shape[2])

def forward(states, head_weight, outward_weight, upward_weight, downward_weight, gains_weight, tables):
    length, model_width = states.shape
    gain_in = gains_weight[:model_width]
    gain_ctx = gains_weight[model_width:2 * model_width]
    gain_mid = gains_weight[2 * model_width:3 * model_width]
    gain_hidden = gains_weight[3 * model_width:]
    normed = low(layer_norm(states, gain_in))
    projected = low_back(jnp.einsum('td,kde->kte', normed, low(head_weight), precision=HIGHEST))
    per_head = projected.reshape(3, length, model_width // HEAD_DIM, HEAD_DIM)
    queries = low(rotate(per_head[0], tables, 1.0))
    key_rows = low(rotate(per_head[1], tables, -1.0))
    values = low(per_head[2])
    context = low(low_back(attend(queries, key_rows, values).reshape(length, model_width)))
    mixed = low(layer_norm(context, gain_ctx))
    middle = states + low_back(jnp.dot(mixed, low(outward_weight), precision=HIGHEST))
    lifted = low(layer_norm(middle, gain_mid))
    hidden_rows = low_back(jnp.dot(lifted, low(upward_weight), precision=HIGHEST))
    squashed = low(layer_norm(jax.nn.gelu(hidden_rows, approximate=False), gain_hidden))
    return middle + low_back(jnp.dot(squashed, low(downward_weight), precision=HIGHEST))

def adapt_step(gradient, master, moment, square, decay_rate):
    moment_new = BETA_ONE * moment + (1.0 - BETA_ONE) * gradient
    square_new = BETA_TWO * square + (1.0 - BETA_TWO) * gradient * gradient
    direction = moment_new / (1.0 - BETA_ONE ** STEP) / (jnp.sqrt(square_new / (1.0 - BETA_TWO ** STEP)) + EPS_ADAM) + decay_rate * master
    return (moment_new, square_new, direction)

def trust_move(master, direction, weight_sum, update_sum):
    return master - STEP_RATE * jnp.sqrt(weight_sum) / (jnp.sqrt(update_sum) + EPS_ADAM) * direction

def gain_segments(entries, model_width):
    return jnp.stack([jnp.sum(entries[:model_width]), jnp.sum(entries[model_width:2 * model_width]), jnp.sum(entries[2 * model_width:3 * model_width]), jnp.sum(entries[3 * model_width:])])

def gain_spread(sums, model_width, hidden_width):
    return jnp.concatenate([jnp.broadcast_to(sums[0], (model_width,)), jnp.broadcast_to(sums[1], (model_width,)), jnp.broadcast_to(sums[2], (model_width,)), jnp.broadcast_to(sums[3], (hidden_width,))])

def pair_sums(master, direction):
    return jnp.stack([jnp.sum(master * master), jnp.sum(direction * direction)])[None]

def reference(text_states, image_states, image_offsets, image_counts, output_grad, head_master, head_moment, head_square, outward_master, outward_moment, outward_square, upward_master, upward_moment, upward_square, downward_master, downward_moment, downward_square, gains_master, gains_moment, gains_square):
    tables = xpos_tables(LENGTH, HEAD_DIM)
    position = jnp.arange(LENGTH, dtype=jnp.int32)
    merged = jax.vmap(lambda text_rows, image_rows, offsets, image_count: merge_images(text_rows, image_rows, offsets, image_count, position))(text_states, image_states, image_offsets, image_counts).astype(jnp.float32)
    masters = (head_master, outward_master, upward_master, downward_master, gains_master)

    def per_sequence(totals, inputs):
        states, cotangent = inputs
        result, pullback = jax.vjp(lambda seq_states, head_weight, outward_weight, upward_weight, downward_weight, gains_weight: forward(seq_states, head_weight, outward_weight, upward_weight, downward_weight, gains_weight, tables), states, *masters)
        gradients = pullback(cotangent.astype(jnp.float32))
        new_totals = tuple((total + gradient for total, gradient in zip(totals, gradients[1:])))
        return (new_totals, (result.astype(jnp.bfloat16), gradients[0]))
    zero_totals = tuple((jnp.zeros(master.shape, jnp.float32) for master in masters))
    totals, (layer_output, input_grad) = lax.scan(per_sequence, zero_totals, (merged, output_grad))
    moment_head, square_head, head_dir = adapt_step(totals[0], head_master, head_moment, head_square, DECAY_RATE)
    moment_outward, square_outward, outward_dir = adapt_step(totals[1], outward_master, outward_moment, outward_square, DECAY_RATE)
    moment_upward, square_upward, upward_dir = adapt_step(totals[2], upward_master, upward_moment, upward_square, DECAY_RATE)
    moment_downward, square_downward, downward_dir = adapt_step(totals[3], downward_master, downward_moment, downward_square, DECAY_RATE)
    moment_gains, square_gains, gains_dir = adapt_step(totals[4], gains_master, gains_moment, gains_square, 0.0)
    head_sums = jnp.stack([lax.optimization_barrier(jnp.sum(head_master * head_master, axis=(1, 2))), lax.optimization_barrier(jnp.sum(head_dir * head_dir, axis=(1, 2)))], axis=-1)
    outward_sums = pair_sums(outward_master, outward_dir)
    upward_sums = pair_sums(upward_master, upward_dir)
    downward_sums = pair_sums(downward_master, downward_dir)
    gains_sums = jnp.stack([gain_segments(gains_master * gains_master, D), gain_segments(gains_dir * gains_dir, D)], axis=-1)
    all_sums = jnp.concatenate([head_sums, outward_sums, upward_sums, downward_sums, gains_sums], axis=0)
    updated_head = trust_move(head_master, head_dir, head_sums[:, 0][:, None, None], head_sums[:, 1][:, None, None])
    updated_outward = trust_move(outward_master, outward_dir, outward_sums[0, 0], outward_sums[0, 1])
    updated_upward = trust_move(upward_master, upward_dir, upward_sums[0, 0], upward_sums[0, 1])
    updated_downward = trust_move(downward_master, downward_dir, downward_sums[0, 0], downward_sums[0, 1])
    updated_gains = trust_move(gains_master, gains_dir, gain_spread(gains_sums[:, 0], D, FF), gain_spread(gains_sums[:, 1], D, FF))
    update_norms = jnp.sqrt(all_sums)
    return (layer_output, input_grad, moment_head, square_head, updated_head, updated_head.astype(jnp.bfloat16), moment_outward, square_outward, updated_outward, updated_outward.astype(jnp.bfloat16), moment_upward, square_upward, updated_upward, updated_upward.astype(jnp.bfloat16), moment_downward, square_downward, updated_downward, updated_downward.astype(jnp.bfloat16), moment_gains, square_gains, updated_gains, update_norms)
```

```python
from functools import partial

import jax
import jax.numpy as jnp
from jax import lax
from jax.experimental import pallas as pl
from jax.experimental.pallas import tpu as pltpu
from jax.sharding import PartitionSpec as P

HEAD_DIM = 64
FF = 8192
PATCH = 64
STEP = 10


EPS_NORM = 1e-05
BETA_ONE = 0.9
BETA_TWO = 0.999
EPS_ADAM = 1e-06
DECAY_RATE = 0.01
STEP_RATE = 0.5


def layer_norm(inputs, gain_vector):
    centre = jnp.mean(inputs, axis=-1, keepdims=True)
    shifted = inputs - centre
    spread = jnp.mean(shifted * shifted, axis=-1, keepdims=True)
    return shifted * lax.rsqrt(spread + EPS_NORM) * gain_vector


def xpos_tables(length, head_size):
    halfway = head_size // 2
    pair_index = jnp.arange(halfway, dtype=jnp.float32)
    angular = jnp.exp(-(2.0 * pair_index / head_size) * jnp.log(10000.0))
    zeta_base = (2.0 * pair_index + 0.4 * head_size) / (1.4 * head_size)
    position = jnp.arange(length, dtype=jnp.float32)[:, None, None]
    return (
        jnp.cos(position * angular),
        jnp.sin(position * angular),
        position / 512.0 * jnp.log(zeta_base),
    )


def rotate(inputs, tables, polarity):
    cosine, sine_part, exponent = tables
    halfway = inputs.shape[-1] // 2
    factor = jnp.exp(polarity * exponent)
    leading = inputs[..., :halfway]
    behind = inputs[..., halfway:]
    return jnp.concatenate(
        [
            (leading * cosine - behind * sine_part) * factor,
            (behind * cosine + leading * sine_part) * factor,
        ],
        axis=-1,
    )


def merge_images(text_rows, image_rows, offsets, image_count, position):
    slot_index = jnp.arange(offsets.shape[0], dtype=jnp.int32)
    inside = (
        (position[:, None] >= offsets[None, :])
        & (position[:, None] < offsets[None, :] + PATCH)
        & (slot_index[None, :] < image_count)
    )
    picked = jnp.sum(
        jnp.where(inside, slot_index[None, :] * PATCH + position[:, None] - offsets[None, :], 0),
        axis=-1,
    )
    chosen = jnp.take(image_rows, picked, axis=0)
    covered = jnp.any(inside, axis=-1)
    return jnp.where(covered[:, None], chosen, text_rows)


def adapt_step(gradient, master, moment, square, decay_rate):
    moment_new = BETA_ONE * moment + (1.0 - BETA_ONE) * gradient
    square_new = BETA_TWO * square + (1.0 - BETA_TWO) * gradient * gradient
    direction = (
        moment_new
        / (1.0 - BETA_ONE**STEP)
        / (jnp.sqrt(square_new / (1.0 - BETA_TWO**STEP)) + EPS_ADAM)
        + decay_rate * master
    )
    return (moment_new, square_new, direction)


def trust_move(master, direction, weight_sum, update_sum):
    return master - STEP_RATE * jnp.sqrt(weight_sum) / (jnp.sqrt(update_sum) + EPS_ADAM) * direction


def gain_segments(entries, model_width):
    return jnp.stack(
        [
            jnp.sum(entries[:model_width]),
            jnp.sum(entries[model_width : 2 * model_width]),
            jnp.sum(entries[2 * model_width : 3 * model_width]),
            jnp.sum(entries[3 * model_width :]),
        ]
    )


def gain_spread(sums, model_width, hidden_width):
    return jnp.concatenate(
        [
            jnp.broadcast_to(sums[0], (model_width,)),
            jnp.broadcast_to(sums[1], (model_width,)),
            jnp.broadcast_to(sums[2], (model_width,)),
            jnp.broadcast_to(sums[3], (hidden_width,)),
        ]
    )


def pair_sums(master, direction):
    return jnp.stack([jnp.sum(master * master), jnp.sum(direction * direction)])[None]


def on_device_general(
    text_states,
    image_states,
    image_offsets,
    image_counts,
    output_grad,
    head_master,
    head_moment,
    head_square,
    outward_master,
    outward_moment,
    outward_square,
    upward_master,
    upward_moment,
    upward_square,
    downward_master,
    downward_moment,
    downward_square,
    gains_master,
    gains_moment,
    gains_square,
):
    groups = lax.axis_size("mp")
    model_rank = lax.axis_index("mp")
    seq_count, local_len, model_width = text_states.shape
    length = local_len * groups
    hidden_local = upward_master.shape[1]
    heads_local = head_master.shape[2] // HEAD_DIM
    tables = xpos_tables(length, HEAD_DIM)
    position = model_rank * local_len + jnp.arange(local_len, dtype=jnp.int32)
    merged = jax.vmap(
        lambda text_rows, image_rows, offsets, image_count: merge_images(
            text_rows, image_rows, offsets, image_count, position
        )
    )(text_states, image_states, image_offsets, image_counts).astype(jnp.float32)
    gain_in = gains_master[:model_width]
    gain_ctx = gains_master[model_width : 2 * model_width]
    gain_mid = gains_master[2 * model_width : 3 * model_width]
    hidden_start = 3 * model_width + model_rank * hidden_local
    gain_hidden = lax.dynamic_slice_in_dim(gains_master, hidden_start, hidden_local)
    head_weight_whole, outward_weight_whole, upward_weight_whole, down_weight_whole = (
        lax.all_gather(head_master.astype(jnp.bfloat16), "dp", axis=1, tiled=True),
        lax.all_gather(outward_master.astype(jnp.bfloat16), "dp", axis=0, tiled=True),
        lax.all_gather(upward_master.astype(jnp.bfloat16), "dp", axis=0, tiled=True),
        lax.all_gather(downward_master.astype(jnp.bfloat16), "dp", axis=1, tiled=True),
    )
    normed_low = layer_norm(merged, gain_in).astype(jnp.bfloat16)
    normed_rows_full, cotangent_rows_full = (
        lax.all_gather(normed_low, "mp", axis=1, tiled=True),
        lax.all_gather(output_grad, "mp", axis=1, tiled=True),
    )
    projected = jnp.einsum(
        "hvg,bga->bhva", normed_rows_full, head_weight_whole, preferred_element_type=jnp.float32
    )
    shaped = projected.reshape(3, seq_count, length, heads_local, HEAD_DIM)
    queries = rotate(shaped[0], tables, 1.0).astype(jnp.bfloat16)
    key_rows = rotate(shaped[1], tables, -1.0).astype(jnp.bfloat16)
    values = shaped[2].astype(jnp.bfloat16)
    block_len = min(512, length)
    block_count = length // block_len
    starts = jnp.arange(block_count, dtype=jnp.int32) * block_len
    key_place = jnp.arange(length, dtype=jnp.int32)

    def block_scores(query_block, start):
        scores = (
            jnp.einsum("sqhd,skhd->shqk", query_block, key_rows, preferred_element_type=jnp.float32)
            * 0.125
        )
        allowed = key_place[None, :] <= (start + jnp.arange(block_len, dtype=jnp.int32))[:, None]
        return jnp.where(allowed, scores, -1e30)

    def forward_block(start):
        query_block = lax.dynamic_slice_in_dim(queries, start, block_len, 1)
        scores = block_scores(query_block, start)
        highest = jnp.max(scores, axis=-1, keepdims=True)
        exponent = jnp.exp(scores - highest)
        total = jnp.sum(exponent, axis=-1, keepdims=True)
        attention = exponent / total
        context_block = jnp.einsum(
            "shqk,skhd->sqhd",
            attention.astype(jnp.bfloat16),
            values,
            preferred_element_type=jnp.float32,
        )
        return (context_block, highest[..., 0] + jnp.log(total[..., 0]))

    context_blocks, log_sums = lax.map(forward_block, starts)
    context = jnp.transpose(context_blocks, (1, 0, 2, 3, 4)).reshape(
        seq_count, length, heads_local * HEAD_DIM
    )
    context_rows = lax.all_to_all(
        context.astype(jnp.bfloat16), "mp", split_axis=1, concat_axis=2, tiled=True
    )
    context_in = context_rows.astype(jnp.float32)
    mixed_half_precision = layer_norm(context_in, gain_ctx).astype(jnp.bfloat16)
    middle = merged + jnp.einsum(
        "ymq,qc->ymc",
        mixed_half_precision,
        outward_weight_whole,
        preferred_element_type=jnp.float32,
    )
    lifted_low = layer_norm(middle, gain_mid).astype(jnp.bfloat16)
    lifted_rows_full = lax.all_gather(lifted_low, "mp", axis=1, tiled=True)
    hidden_rows = jnp.einsum(
        "orb,bg->org", lifted_rows_full, upward_weight_whole, preferred_element_type=jnp.float32
    )
    activated = jax.nn.gelu(hidden_rows, approximate=False)
    first_sum, second_sum = lax.psum(
        (jnp.sum(activated, axis=-1), jnp.sum(activated * activated, axis=-1)), "mp"
    )
    centre = first_sum / FF
    scale_inv = lax.rsqrt(second_sum / FF - centre * centre + EPS_NORM)[..., None]
    standard = (activated - centre[..., None]) * scale_inv
    squashed_half_precision = (standard * gain_hidden).astype(jnp.bfloat16)
    ffn_part = jnp.einsum(
        "wxp,pk->wxk",
        squashed_half_precision,
        down_weight_whole,
        preferred_element_type=jnp.float32,
    )
    ffn_rows = lax.psum_scatter(
        ffn_part.astype(jnp.bfloat16), "mp", scatter_dimension=1, tiled=True
    ).astype(jnp.float32)
    layer_output = (middle + ffn_rows).astype(jnp.bfloat16)
    down_grad = jnp.einsum(
        "uxy,uxo->yo",
        squashed_half_precision,
        cotangent_rows_full,
        preferred_element_type=jnp.float32,
    )
    squashed_grad = jnp.einsum(
        "yxr,ur->yxu", cotangent_rows_full, down_weight_whole, preferred_element_type=jnp.float32
    )
    hidden_gain_grad = jnp.sum(squashed_grad * standard, axis=(0, 1))
    scaled_grad = squashed_grad * gain_hidden
    mean_one, mean_two = (
        lax.psum(jnp.sum(scaled_grad, axis=-1).astype(jnp.bfloat16), "mp").astype(jnp.float32),
        lax.psum(jnp.sum(scaled_grad * standard, axis=-1).astype(jnp.bfloat16), "mp").astype(
            jnp.float32
        ),
    )
    activated_grad = (
        scaled_grad - mean_one[..., None] / FF - standard * (mean_two[..., None] / FF)
    ) * scale_inv
    gelu_out, gelu_back = jax.vjp(partial(jax.nn.gelu, approximate=False), hidden_rows)
    hidden_rows_grad = gelu_back(activated_grad)[0].astype(jnp.bfloat16)
    upward_gradient = jnp.einsum(
        "gki,gkt->it", lifted_rows_full, hidden_rows_grad, preferred_element_type=jnp.float32
    )
    lifted_part = jnp.einsum(
        "eiw,mw->eim", hidden_rows_grad, upward_weight_whole, preferred_element_type=jnp.float32
    )
    lifted_grad = lax.psum_scatter(lifted_part, "mp", scatter_dimension=1, tiled=True)
    norm_out, middle_back = jax.vjp(layer_norm, middle, gain_mid)
    middle_part, mid_gain_grad = middle_back(lifted_grad)
    middle_grad = output_grad.astype(jnp.float32) + middle_part
    middle_half_precision = middle_grad.astype(jnp.bfloat16)
    outward_part = jnp.einsum(
        "hyk,hyo->ko",
        mixed_half_precision,
        middle_half_precision,
        preferred_element_type=jnp.float32,
    )
    mixed_grad = jnp.einsum(
        "hox,kx->hok",
        middle_half_precision,
        outward_weight_whole,
        preferred_element_type=jnp.float32,
    )
    context_out, context_back = jax.vjp(layer_norm, context_in, gain_ctx)
    context_grad, ctx_gain_grad = context_back(mixed_grad)
    context_heads = lax.all_to_all(
        context_grad.astype(jnp.bfloat16), "mp", split_axis=2, concat_axis=1, tiled=True
    )
    grad_heads = context_heads.reshape(seq_count, length, heads_local, HEAD_DIM)

    def backward_block(totals, inputs):
        key_total, value_total = totals
        start, log_block = inputs
        query_block = lax.dynamic_slice_in_dim(queries, start, block_len, 1)
        grad_block = lax.dynamic_slice_in_dim(grad_heads, start, block_len, 1)
        scores = block_scores(query_block, start)
        attention = jnp.exp(scores - log_block[..., None])
        prob_grad = jnp.einsum(
            "sqhd,skhd->shqk", grad_block, values, preferred_element_type=jnp.float32
        )
        row_dot = jnp.sum(attention * prob_grad, axis=-1, keepdims=True)
        score_low = (attention * (prob_grad - row_dot)).astype(jnp.bfloat16)
        query_turned = (
            jnp.einsum("shqk,skhd->sqhd", score_low, key_rows, preferred_element_type=jnp.float32)
            * 0.125
        )
        key_total = (
            key_total
            + jnp.einsum(
                "shqk,sqhd->skhd", score_low, query_block, preferred_element_type=jnp.float32
            )
            * 0.125
        )
        value_total = value_total + jnp.einsum(
            "shqk,sqhd->skhd",
            attention.astype(jnp.bfloat16),
            grad_block,
            preferred_element_type=jnp.float32,
        )
        return ((key_total, value_total), query_turned)

    zero_heads = jnp.zeros((seq_count, length, heads_local, HEAD_DIM), jnp.float32)
    (key_turned, value_grad), query_blocks = lax.scan(
        backward_block, (zero_heads, zero_heads), (starts, log_sums)
    )
    query_turned = jnp.transpose(query_blocks, (1, 0, 2, 3, 4)).reshape(
        seq_count, length, heads_local, HEAD_DIM
    )
    query_out, query_back = jax.vjp(lambda inputs: rotate(inputs, tables, 1.0), shaped[0])
    key_out, key_back = jax.vjp(lambda inputs: rotate(inputs, tables, -1.0), shaped[1])
    projection_gradient = (
        jnp.stack([query_back(query_turned)[0], key_back(key_turned)[0], value_grad])
        .astype(jnp.bfloat16)
        .reshape(3, seq_count, length, heads_local * HEAD_DIM)
    )
    head_grad = jnp.einsum(
        "fbn,ufbj->unj", normed_rows_full, projection_gradient, preferred_element_type=jnp.float32
    )
    normed_part = jnp.einsum(
        "acqr,aur->cqu", projection_gradient, head_weight_whole, preferred_element_type=jnp.float32
    )
    normed_grad = lax.psum_scatter(
        normed_part.astype(jnp.bfloat16), "mp", scatter_dimension=1, tiled=True
    ).astype(jnp.float32)
    input_out, input_back = jax.vjp(layer_norm, merged, gain_in)
    merged_part, in_gain_grad = input_back(normed_grad)
    input_grad = middle_grad + merged_part
    head_sum, outward_sum, upward_sum, downward_sum = (
        lax.psum_scatter(
            head_grad.astype(jnp.bfloat16), "dp", scatter_dimension=1, tiled=True
        ).astype(jnp.float32),
        lax.psum_scatter(
            outward_part.astype(jnp.bfloat16), "dp", scatter_dimension=0, tiled=True
        ).astype(jnp.float32),
        lax.psum_scatter(
            upward_gradient.astype(jnp.bfloat16), "dp", scatter_dimension=0, tiled=True
        ).astype(jnp.float32),
        lax.psum_scatter(
            down_grad.astype(jnp.bfloat16), "dp", scatter_dimension=1, tiled=True
        ).astype(jnp.float32),
    )
    outward_sum = lax.psum(outward_sum.astype(jnp.bfloat16), "mp").astype(jnp.float32)
    moment_head, square_head, head_dir = adapt_step(
        head_sum, head_master, head_moment, head_square, DECAY_RATE
    )
    moment_outward, square_outward, outward_dir = adapt_step(
        outward_sum, outward_master, outward_moment, outward_square, DECAY_RATE
    )
    moment_upward, square_upward, upward_dir = adapt_step(
        upward_sum, upward_master, upward_moment, upward_square, DECAY_RATE
    )
    moment_downward, square_downward, downward_dir = adapt_step(
        downward_sum, downward_master, downward_moment, downward_square, DECAY_RATE
    )
    owner = (model_rank == 0).astype(jnp.float32)
    head_part = jnp.stack(
        [
            jnp.sum(head_master * head_master, axis=(1, 2)),
            jnp.sum(head_dir * head_dir, axis=(1, 2)),
        ],
        axis=-1,
    )
    norm_part = jnp.concatenate(
        [
            head_part,
            pair_sums(outward_master, outward_dir) * owner,
            pair_sums(upward_master, upward_dir),
            pair_sums(downward_master, downward_dir),
        ],
        axis=0,
    )
    gains_part = jnp.concatenate(
        [in_gain_grad, ctx_gain_grad, mid_gain_grad, jnp.zeros((FF,), jnp.float32)]
    )
    gains_part = lax.dynamic_update_slice(gains_part, hidden_gain_grad, (hidden_start,))
    gains_sum, norm_sums = lax.psum((gains_part, norm_part), ("dp", "mp"))
    moment_gains, square_gains, gains_dir = adapt_step(
        gains_sum, gains_master, gains_moment, gains_square, 0.0
    )
    gains_sums = jnp.stack(
        [
            gain_segments(gains_master * gains_master, model_width),
            gain_segments(gains_dir * gains_dir, model_width),
        ],
        axis=-1,
    )
    updated_head = trust_move(
        head_master, head_dir, norm_sums[0:3, 0][:, None, None], norm_sums[0:3, 1][:, None, None]
    )
    updated_outward = trust_move(outward_master, outward_dir, norm_sums[3, 0], norm_sums[3, 1])
    updated_upward = trust_move(upward_master, upward_dir, norm_sums[4, 0], norm_sums[4, 1])
    updated_downward = trust_move(downward_master, downward_dir, norm_sums[5, 0], norm_sums[5, 1])
    updated_gains = trust_move(
        gains_master,
        gains_dir,
        gain_spread(gains_sums[:, 0], model_width, FF),
        gain_spread(gains_sums[:, 1], model_width, FF),
    )
    update_norms = jnp.sqrt(jnp.concatenate([norm_sums, gains_sums], axis=0))
    return (
        layer_output,
        input_grad,
        moment_head,
        square_head,
        updated_head,
        updated_head.astype(jnp.bfloat16),
        moment_outward,
        square_outward,
        updated_outward,
        updated_outward.astype(jnp.bfloat16),
        moment_upward,
        square_upward,
        updated_upward,
        updated_upward.astype(jnp.bfloat16),
        moment_downward,
        square_downward,
        updated_downward,
        updated_downward.astype(jnp.bfloat16),
        moment_gains,
        square_gains,
        updated_gains,
        update_norms,
    )


LOG2E = 1.4426950408889634
LANES = 128
NT = (((1,), (1,)), ((), ()))
NN = (((1,), (0,)), ((), ()))
LOW = jnp.bfloat16
WIDE = jnp.float32
ONCE = pl.Buffered(1)


def dot(left, right, dims):
    return lax.dot_general(left, right, dims, preferred_element_type=WIDE)


def kernel_call(body, grid, in_specs, out_specs, out_shape, scratch, flops, moved, operands):
    return pl.pallas_call(
        body,
        grid_spec=pltpu.PrefetchScalarGridSpec(
            num_scalar_prefetch=1, grid=grid, in_specs=in_specs, out_specs=out_specs, scratch_shapes=scratch
        ),
        out_shape=out_shape,
        compiler_params=pltpu.CompilerParams(vmem_limit_bytes=56 << 20),
        cost_estimate=pl.CostEstimate(flops=int(flops), bytes_accessed=int(moved), transcendentals=0),
    )(*operands)


def own_rows(sub, rank, j, b):
    return pl.ds(pl.multiple_of(b * 4 * sub + (rank ^ j) * sub, sub), sub)


def own_block(place, k, width):
    return pl.ds(pl.multiple_of((place ^ k) * width, width), width)


def swap_halves(block):
    low = lax.broadcasted_iota(jnp.int32, (1, LANES), 1) % HEAD_DIM < HEAD_DIM // 2
    return jnp.where(low, pltpu.roll(block, LANES - HEAD_DIM // 2, 1), pltpu.roll(block, HEAD_DIM // 2, 1))


def project_kernel(ids, x, w0, w1, w2, w3, cq, sq, ck, sk, q, k, v):
    depth = w0.shape[1]
    width = w0.shape[2]
    for f, (out, c, s) in enumerate(((q, cq, sq), (k, ck, sk), (v, None, None))):
        total = None
        for n, w in enumerate((w0, w1, w2, w3)):
            part = dot(x[:, own_block(ids[1], n, depth)], w[f], NN)
            total = part if total is None else total + part
        for p in range(width // LANES):
            here = slice(p * LANES, (p + 1) * LANES)
            block = total[:, here]
            if c is not None:
                block = block * c[...] + swap_halves(block) * s[...]
            out[:, here] = block.astype(LOW)


def project(ids, x, weights, tables, j):
    rows, model = x.shape
    sub = rows // 2
    width = weights[0].shape[2]
    table = pl.BlockSpec((sub, LANES), lambda b, ids: (b * 4 + (ids[0] ^ j), 0))
    out = pl.BlockSpec((sub, width), lambda b, ids: (b, 0))
    return kernel_call(
        project_kernel,
        (2,),
        [pl.BlockSpec((sub, model), lambda b, ids: (b, 0))]
        + [pl.BlockSpec(weights[0].shape, lambda b, ids: (0, 0, 0), pipeline_mode=ONCE)] * 4
        + [table] * 4,
        [out] * 3,
        [jax.ShapeDtypeStruct((rows, width), LOW)] * 3,
        [],
        6 * rows * model * width,
        6 * model * width + 8 * rows * model,
        (ids, x, *weights, *tables),
    )


def attend_kernel(ids, *refs, bq, bk):
    q_, k_, v_, o_, lse_ref = refs[0:4], refs[4:8], refs[8:12], refs[12:16], refs[16]
    qs, ks, vt, os = refs[17:]
    rank = ids[0]
    length = qs.shape[0]
    sub = q_[0].shape[0] // 2
    for j in range(4):
        for b in range(2):
            rows = own_rows(sub, rank, j, b)
            here = slice(b * sub, (b + 1) * sub)
            qs[rows, :] = q_[j][here, :]
            ks[rows, :] = k_[j][here, :]
            vt[:, rows] = v_[j][here, :].T
    first = lax.broadcasted_iota(jnp.int32, (1, LANES), 1) < HEAD_DIM
    ratio = bq // bk

    def q_block(i, _):
        here = pl.ds(pl.multiple_of(i * bq, bq), bq)
        q = qs[here, :]
        zero = jnp.zeros_like(q)
        parted = (jnp.where(first, q, zero), jnp.where(first, zero, q))

        def step(j, carry, diagonal):
            at = pl.multiple_of(j * bk, bk)
            k = ks[pl.ds(at, bk), :]
            out = []
            for h in range(2):
                highest, total, sums = carry[h]
                scores = dot(k, parted[h], NT) * (0.125 * LOG2E)
                if diagonal is not None:
                    key = diagonal * bk + lax.broadcasted_iota(jnp.int32, (bk, bq), 0)
                    scores = jnp.where(key <= lax.broadcasted_iota(jnp.int32, (bk, bq), 1), scores, -1e30)
                new = jnp.maximum(highest, jnp.max(scores, axis=0, keepdims=True))
                probs = jnp.exp2(scores - new)
                scale = jnp.exp2(highest - new)
                total = total * scale + jnp.sum(probs, axis=0, keepdims=True)
                rows = vt[h * HEAD_DIM : (h + 1) * HEAD_DIM, pl.ds(at, bk)]
                out.append((new, total, sums * scale + dot(rows, probs.astype(LOW), NN)))
            return tuple(out)

        start = tuple(
            (jnp.full((1, bq), -1e30, WIDE), jnp.zeros((1, bq), WIDE), jnp.zeros((HEAD_DIM, bq), WIDE))
            for _ in range(2)
        )
        carry = lax.fori_loop(0, i * ratio, lambda j, c: step(j, c, None), start)
        for d in range(ratio):
            carry = step(i * ratio + d, carry, d)
        turned = jnp.concatenate([carry[h][2] / carry[h][1] for h in range(2)], axis=0)
        os[here, :] = turned.T.astype(LOW)
        for h in range(2):
            lse_ref[0, h : h + 1, here] = carry[h][0] + jnp.log2(carry[h][1])
        return 0

    lax.fori_loop(0, length // bq, q_block, 0)
    for j in range(4):
        for b in range(2):
            o_[j][b * sub : (b + 1) * sub, :] = os[own_rows(sub, rank, j, b), :]


def attend(ids, queries, keys, values):
    rows, width = queries[0].shape
    length, pairs = rows * 4, width // LANES
    chunk = pl.BlockSpec((rows, LANES), lambda p, ids: (0, p))
    low = pltpu.VMEM((length, LANES), LOW)
    result = kernel_call(
        partial(attend_kernel, bq=min(1024, length), bk=min(512, length)),
        (pairs,),
        [chunk] * 12,
        [chunk] * 4 + [pl.BlockSpec((1, 2, length), lambda p, ids: (p, 0, 0))],
        [jax.ShapeDtypeStruct((rows, width), LOW)] * 4 + [jax.ShapeDtypeStruct((pairs, 2, length), WIDE)],
        [low, low, pltpu.VMEM((LANES, length), LOW), low],
        40e9,
        10e6,
        (ids, *queries, *keys, *values),
    )
    return result[:4], result[4]


def attend_back_kernel(ids, *refs, bq, bk):
    q_, k_, v_, d_, o_ = refs[0:4], refs[4:8], refs[8:12], refs[12:16], refs[16:20]
    lse_ref, cq, sq, ck, sk = refs[20:25]
    dq_, dk_, dv_ = refs[25:29], refs[29:33], refs[33:37]
    qs, ks, vs, ds, kt, dqt, dks, dvs, delta = refs[37:]
    rank = ids[0]
    length = qs.shape[0]
    sub = q_[0].shape[0] // 2
    for j in range(4):
        for b in range(2):
            rows = own_rows(sub, rank, j, b)
            here = slice(b * sub, (b + 1) * sub)
            qs[rows, :] = q_[j][here, :]
            ks[rows, :] = k_[j][here, :]
            kt[:, rows] = k_[j][here, :].T
            vs[rows, :] = v_[j][here, :]
            ds[rows, :] = d_[j][here, :]
            product = (d_[j][here, :].astype(WIDE) * o_[j][here, :].astype(WIDE)).T
            delta[0:1, rows] = jnp.sum(product[:HEAD_DIM], axis=0, keepdims=True)
            delta[1:2, rows] = jnp.sum(product[HEAD_DIM:], axis=0, keepdims=True)
    first = lax.broadcasted_iota(jnp.int32, (1, LANES), 1) < HEAD_DIM
    dqt[...] = jnp.zeros_like(dqt)

    def k_block(j, _):
        at = pl.ds(pl.multiple_of(j * bk, bk), bk)
        k = ks[at, :]
        v = vs[at, :]

        def step(i, carry, diagonal):
            dk, dv = carry
            here = pl.ds(pl.multiple_of(i * bq, bq), bq)
            q, do = qs[here, :], ds[here, :]
            zero = jnp.zeros_like(q)
            for h in range(2):
                lanes = slice(h * HEAD_DIM, (h + 1) * HEAD_DIM)
                q_own = jnp.where(first, q, zero) if h == 0 else jnp.where(first, zero, q)
                do_own = jnp.where(first, do, zero) if h == 0 else jnp.where(first, zero, do)
                scores = dot(k, q_own, NT) * (0.125 * LOG2E) - lse_ref[0, h : h + 1, here]
                if diagonal:
                    key = lax.broadcasted_iota(jnp.int32, (bk, bq), 0)
                    scores = jnp.where(key <= lax.broadcasted_iota(jnp.int32, (bk, bq), 1), scores, -1e30)
                probs = jnp.exp2(scores)
                prob_grad = dot(v, do_own, NT)
                grad = (probs * (prob_grad - delta[h : h + 1, here])).astype(LOW)
                dv = dv + dot(probs.astype(LOW), do_own, NN)
                dk = dk + dot(grad, q_own, NN)
                dqt[lanes, here] += dot(kt[lanes, at], grad, NN)
            return dk, dv

        zeros = jnp.zeros((bk, LANES), WIDE)
        carry = step(j, (zeros, zeros), True)
        dk, dv = lax.fori_loop(j + 1, length // bq, lambda i, c: step(i, c, False), carry)
        dks[at, :] = dk * 0.125
        dvs[at, :] = dv.astype(LOW)
        return 0

    lax.fori_loop(0, length // bk, k_block, 0)
    for j in range(4):
        for b in range(2):
            rows = own_rows(sub, rank, j, b)
            here = slice(b * sub, (b + 1) * sub)
            query_grad = dqt[:, rows].T * 0.125
            dq_[j][here, :] = (query_grad * cq[rows, :] - swap_halves(query_grad) * sq[rows, :]).astype(LOW)
            key_grad = dks[rows, :]
            dk_[j][here, :] = (key_grad * ck[rows, :] - swap_halves(key_grad) * sk[rows, :]).astype(LOW)
            dv_[j][here, :] = dvs[rows, :]


def attend_back(ids, queries, keys, values, cotangents, contexts, lse, tables):
    rows, width = queries[0].shape
    length, pairs = rows * 4, width // LANES
    chunk = pl.BlockSpec((rows, LANES), lambda p, ids: (0, p))
    whole = pl.BlockSpec((length, LANES), lambda p, ids: (0, 0), pipeline_mode=ONCE)
    low = pltpu.VMEM((length, LANES), LOW)
    block = min(512, length)
    result = kernel_call(
        partial(attend_back_kernel, bq=block, bk=block),
        (pairs,),
        [chunk] * 20 + [pl.BlockSpec((1, 2, length), lambda p, ids: (p, 0, 0))] + [whole] * 4,
        [chunk] * 12,
        [jax.ShapeDtypeStruct((rows, width), LOW)] * 12,
        [
            low,
            low,
            low,
            low,
            pltpu.VMEM((LANES, length), LOW),
            pltpu.VMEM((LANES, length), WIDE),
            pltpu.VMEM((length, LANES), WIDE),
            low,
            pltpu.VMEM((2, length), WIDE),
        ],
        60e9,
        20e6,
        (ids, *queries, *keys, *values, *cotangents, *contexts, lse, *tables),
    )
    return result[0:4], result[4:8], result[8:12]


def centred(block):
    shifted = block - jnp.mean(block, axis=-1, keepdims=True)
    spread = jnp.mean(shifted * shifted, axis=-1, keepdims=True)
    scale = lax.rsqrt(spread + EPS_NORM)
    return shifted * scale, scale


def norm_back(standard, scale, gain, grad):
    scaled = grad * gain
    first = jnp.mean(scaled, axis=-1, keepdims=True)
    second = jnp.mean(scaled * standard, axis=-1, keepdims=True)
    return scale * (scaled - first - standard * second)


def context_lanes(ids, j, side, width):
    half = ids[2] ^ side
    return pl.ds(pl.multiple_of(half * 4 * width + (ids[0] ^ j) * width, width), width)


def mid_kernel(ids, c0, c1, c2, c3, merged, w0, w1, w2, w3, g_ctx, g_mid, ctx, mixed, middle, lifted):
    width = c0.shape[1] // 2
    for j, c in enumerate((c0, c1, c2, c3)):
        for side in range(2):
            ctx[:, context_lanes(ids, j, side, width)] = c[:, side * width : (side + 1) * width]
    standard, _ = centred(ctx[...].astype(WIDE))
    mixed[...] = (standard * g_ctx[...]).astype(LOW)
    total = merged[...].astype(WIDE)
    depth = w0.shape[0]
    for k, w in enumerate((w0, w1, w2, w3)):
        total = total + dot(mixed[:, own_block(ids[1], k, depth)], w[...], NN)
    middle[...] = total
    standard, _ = centred(total)
    lifted[...] = (standard * g_mid[...]).astype(LOW)


def mid_forward(ids, contexts, merged, weights, g_ctx, g_mid):
    rows, model = merged.shape
    block = min(256, rows)
    line = lambda width: pl.BlockSpec((block, width), lambda b, ids: (b, 0))
    gain = pl.BlockSpec((1, model), lambda b, ids: (0, 0))
    weight = pl.BlockSpec(weights[0].shape, lambda b, ids: (0, 0), pipeline_mode=ONCE)
    shape = lambda kind: jax.ShapeDtypeStruct((rows, model), kind)
    return kernel_call(
        mid_kernel,
        (rows // block,),
        [line(contexts[0].shape[1])] * 4 + [line(model)] + [weight] * 4 + [gain] * 2,
        [line(model)] * 4,
        [shape(LOW), shape(LOW), shape(WIDE), shape(LOW)],
        [],
        2 * rows * model * model,
        2 * model * model + 14 * rows * model,
        (ids, *contexts, merged, *weights, g_ctx, g_mid),
    )


def mid_back_kernel(
    ids, a, r, middle, og, ctx, w0, w1, w2, w3, g_mid, g_ctx, middle_grad, middle_low, d0, d1, d2, d3, gains, mixed_grad
):
    grad = a[...].astype(WIDE) + r[...].astype(WIDE)
    standard, scale = centred(middle[...])

    @pl.when(pl.program_id(0) == 0)
    def _():
        gains[...] = jnp.zeros_like(gains)

    gains[0:1, :] += jnp.sum(grad * standard, axis=0, keepdims=True)
    total = og[...].astype(WIDE) + norm_back(standard, scale, g_mid[...], grad)
    middle_grad[...] = total
    low = total.astype(LOW)
    middle_low[...] = low
    depth = w0.shape[0]
    for k, w in enumerate((w0, w1, w2, w3)):
        mixed_grad[:, own_block(ids[1], k, depth)] = dot(low, w[...], NT)
    grad = mixed_grad[...]
    standard, scale = centred(ctx[...].astype(WIDE))
    gains[1:2, :] += jnp.sum(grad * standard, axis=0, keepdims=True)
    mixed_grad[...] = norm_back(standard, scale, g_ctx[...], grad)
    width = d0.shape[1] // 2
    for j, d in enumerate((d0, d1, d2, d3)):
        for side in range(2):
            d[:, side * width : (side + 1) * width] = mixed_grad[:, context_lanes(ids, j, side, width)].astype(LOW)


def mid_backward(ids, parts, middle, og, ctx, weights, g_mid, g_ctx):
    rows, model = middle.shape
    block = min(256, rows)
    line = lambda width: pl.BlockSpec((block, width), lambda b, ids: (b, 0))
    gain = pl.BlockSpec((1, model), lambda b, ids: (0, 0))
    weight = pl.BlockSpec(weights[0].shape, lambda b, ids: (0, 0), pipeline_mode=ONCE)
    shape = lambda width, kind: jax.ShapeDtypeStruct((rows, width), kind)
    result = kernel_call(
        mid_back_kernel,
        (rows // block,),
        [line(model)] * 5 + [weight] * 4 + [gain] * 2,
        [line(model)] * 2 + [line(model // 4)] * 4 + [pl.BlockSpec((8, model), lambda b, ids: (0, 0))],
        [shape(model, WIDE), shape(model, LOW)]
        + [shape(model // 4, LOW)] * 4
        + [jax.ShapeDtypeStruct((8, model), WIDE)],
        [pltpu.VMEM((block, model), WIDE)],
        2 * rows * model * model,
        2 * model * model + 18 * rows * model,
        (ids, *parts, middle, og, ctx, *weights, g_mid, g_ctx),
    )
    return result[0], result[1], result[2:6], result[6]


def gelu_parts(hidden):
    share = 0.5 + 0.5 * lax.erf(hidden * 0.7071067811865476)
    return hidden * share, share


def gelu_slope(hidden, share):
    return share + hidden * (0.3989422804014327 * jnp.exp(-0.5 * hidden * hidden))


def fold(block):
    out = block[:, :LANES]
    for p in range(1, block.shape[1] // LANES):
        out = out + block[:, p * LANES : (p + 1) * LANES]
    return out


def ffn_first_kernel(ids, x, og, u0, u1, u2, u3, d0, d1, d2, d3, gain, hidden, squashed_grad, sums, acc):
    step = pl.program_id(0)
    depth = u0.shape[0]
    rows = x.shape[0]
    part = rows // 2

    @pl.when(step == 0)
    def _():
        acc[...] = jnp.zeros_like(acc)

    for b in range(2):
        here = slice(b * part, (b + 1) * part)
        h = None
        s = None
        for k, (u, d) in enumerate(((u0, d0), (u1, d1), (u2, d2), (u3, d3))):
            lanes = own_block(ids[1], k, depth)
            one = dot(x[here, lanes], u[...], NN)
            two = dot(og[here, lanes], d[...], NT)
            h = one if h is None else h + one
            s = two if s is None else s + two
        h = h.astype(LOW)
        s = s.astype(LOW)
        hidden[here, :] = h
        squashed_grad[here, :] = s
        activated, _ = gelu_parts(h.astype(WIDE))
        scaled = s.astype(WIDE) * gain[...]
        acc[0, here, :] += fold(activated)
        acc[1, here, :] += fold(activated * activated)
        acc[2, here, :] += fold(scaled)
        acc[3, here, :] += fold(scaled * activated)

    @pl.when(step == pl.num_programs(0) - 1)
    def _():
        for n in range(4):
            sums[n : n + 1, :] = jnp.sum(acc[n].T, axis=0, keepdims=True)
        sums[4:8, :] = jnp.zeros_like(sums[4:8, :])


def ffn_first(ids, x, og, upward, downward, gain):
    rows, model = x.shape
    units = upward[0].shape[1]
    block = min(512, units)
    line = pl.BlockSpec((rows, model), lambda u, ids: (0, 0), pipeline_mode=ONCE)
    out = pl.BlockSpec((rows, block), lambda u, ids: (0, u))
    return kernel_call(
        ffn_first_kernel,
        (units // block,),
        [line] * 2
        + [pl.BlockSpec((model // 4, block), lambda u, ids: (0, u))] * 4
        + [pl.BlockSpec((block, model // 4), lambda u, ids: (u, 0))] * 4
        + [pl.BlockSpec((1, block), lambda u, ids: (0, u))],
        [out] * 2 + [pl.BlockSpec((8, rows), lambda u, ids: (0, 0))],
        [jax.ShapeDtypeStruct((rows, units), LOW)] * 2 + [jax.ShapeDtypeStruct((8, rows), WIDE)],
        [pltpu.VMEM((4, rows, LANES), WIDE)],
        4 * rows * model * units,
        4 * model * units + 4 * rows * (model + units),
        (ids, x, og, *upward, *downward, gain),
    )


def ffn_second_kernel(ids, hidden, squashed_grad, sums, gain, u0, u1, u2, u3, squashed, hidden_grad, out, gains, acc, *, hidden_width):
    step = pl.program_id(0)
    depth = u0.shape[0]
    rows = hidden.shape[0]
    part = rows // 2

    @pl.when(step == 0)
    def _():
        acc[...] = jnp.zeros_like(acc)

    columns = sums[...].T
    gain_sum = None
    for b in range(2):
        here = slice(b * part, (b + 1) * part)
        centre = columns[here, 0:1] / hidden_width
        scale = lax.rsqrt(columns[here, 1:2] / hidden_width - centre * centre + EPS_NORM)
        mean_one = columns[here, 2:3] / hidden_width
        mean_two = scale * (columns[here, 3:4] - centre * columns[here, 2:3]) / hidden_width
        h = hidden[here, :].astype(WIDE)
        activated, share = gelu_parts(h)
        standard = (activated - centre) * scale
        squashed[here, :] = (standard * gain[...]).astype(LOW)
        s = squashed_grad[here, :].astype(WIDE)
        piece = jnp.sum(s * standard, axis=0, keepdims=True)
        gain_sum = piece if gain_sum is None else gain_sum + piece
        activated_grad = (s * gain[...] - mean_one - standard * mean_two) * scale
        grad = (activated_grad * gelu_slope(h, share)).astype(LOW)
        hidden_grad[here, :] = grad
        for k, u in enumerate((u0, u1, u2, u3)):
            acc[here, own_block(ids[1], k, depth)] += dot(grad, u[...], NT)
    gains[...] = jnp.broadcast_to(gain_sum, gains.shape)

    @pl.when(step == pl.num_programs(0) - 1)
    def _():
        out[...] = acc[...].astype(LOW)


def ffn_second(ids, hidden, squashed_grad, sums, gain, upward, hidden_width):
    rows, units = hidden.shape
    model = upward[0].shape[0] * 4
    block = min(512, units)
    line = pl.BlockSpec((rows, block), lambda u, ids: (0, u))
    return kernel_call(
        partial(ffn_second_kernel, hidden_width=hidden_width),
        (units // block,),
        [line] * 2
        + [pl.BlockSpec((8, rows), lambda u, ids: (0, 0)), pl.BlockSpec((1, block), lambda u, ids: (0, u))]
        + [pl.BlockSpec((model // 4, block), lambda u, ids: (0, u))] * 4,
        [line] * 2
        + [pl.BlockSpec((rows, model), lambda u, ids: (0, 0)), pl.BlockSpec((8, block), lambda u, ids: (0, u))],
        [jax.ShapeDtypeStruct((rows, units), LOW)] * 2
        + [jax.ShapeDtypeStruct((rows, model), LOW), jax.ShapeDtypeStruct((8, units), WIDE)],
        [pltpu.VMEM((rows, model), WIDE)],
        2 * rows * model * units,
        2 * model * units + 8 * rows * units + 2 * rows * model,
        (ids, hidden, squashed_grad, sums, gain, *upward),
    )


def spread_kernel(ids, x, w0, w1, w2, w3, out, acc):
    step = pl.program_id(0)
    depth = w0.shape[1]
    for k, w in enumerate((w0, w1, w2, w3)):
        lanes = own_block(ids[1], k, depth)
        part = dot(x[...], w[...], NN)

        @pl.when(step == 0)
        def _():
            acc[:, lanes] = part

        @pl.when(step > 0)
        def _():
            acc[:, lanes] += part

    @pl.when(step == pl.num_programs(0) - 1)
    def _():
        out[...] = acc[...].astype(LOW)


def ffn_out(ids, x, downward):
    rows, units = x.shape
    model = downward[0].shape[1] * 4
    block = min(512, units)
    return kernel_call(
        spread_kernel,
        (units // block,),
        [pl.BlockSpec((rows, block), lambda u, ids: (0, u))]
        + [pl.BlockSpec((block, model // 4), lambda u, ids: (u, 0))] * 4,
        [pl.BlockSpec((rows, model), lambda u, ids: (0, 0))],
        [jax.ShapeDtypeStruct((rows, model), LOW)],
        [pltpu.VMEM((rows, model), WIDE)],
        2 * rows * model * units,
        2 * model * units + 2 * rows * (units + model),
        (ids, x, *downward),
    )[0]


def unproject_kernel(ids, q, k, v, w0, w1, w2, w3, out):
    depth = w0.shape[1]
    for n, w in enumerate((w0, w1, w2, w3)):
        total = None
        for f, g in enumerate((q, k, v)):
            part = dot(g[...], w[f], NT)
            total = part if total is None else total + part
        out[:, own_block(ids[1], n, depth)] = total.astype(LOW)


def unproject(ids, q, k, v, weights):
    rows, width = q.shape
    model = weights[0].shape[1] * 4
    block = min(256, rows)
    line = pl.BlockSpec((block, width), lambda b, ids: (b, 0))
    return kernel_call(
        unproject_kernel,
        (rows // block,),
        [line] * 3 + [pl.BlockSpec(weights[0].shape, lambda b, ids: (0, 0, 0), pipeline_mode=ONCE)] * 4,
        [pl.BlockSpec((block, model), lambda b, ids: (b, 0))],
        [jax.ShapeDtypeStruct((rows, model), LOW)],
        [],
        6 * rows * model * width,
        6 * model * width + 2 * rows * (3 * width + model),
        (ids, q, k, v, *weights),
    )[0]


def flip(value, axis, mask):
    return lax.ppermute(value, axis, [(i, i ^ mask) for i in range(lax.axis_size(axis))])


def flip_both(value, mask_dp, mask_mp):
    count_mp = lax.axis_size("mp")
    pairs = [
        (d * count_mp + m, (d ^ mask_dp) * count_mp + (m ^ mask_mp))
        for d in range(lax.axis_size("dp"))
        for m in range(count_mp)
    ]
    return lax.ppermute(value, ("dp", "mp"), pairs)


def gather_tokens(chunk):
    across = flip(chunk, "mp", 2)
    return [chunk, flip(chunk, "mp", 1), across, flip(across, "mp", 1)]


def gather_weight(shard, x_first):
    if x_first:
        one = flip(shard, "dp", 1)
        return [shard, one, flip(shard, "dp", 2), flip(one, "dp", 2)]
    two = flip(shard, "dp", 2)
    return [shard, flip(shard, "dp", 1), two, flip(two, "dp", 1)]


def add_low(one, two):
    return (one.astype(WIDE) + two.astype(WIDE)).astype(LOW)


def scatter_grad(blocks, x_first):
    if x_first:
        kept = add_low(blocks[0], flip(blocks[1], "dp", 1))
        passed = add_low(blocks[2], flip(blocks[3], "dp", 1))
        return add_low(kept, flip(passed, "dp", 2))
    kept = add_low(blocks[0], flip(blocks[2], "dp", 2))
    passed = add_low(blocks[1], flip(blocks[3], "dp", 2))
    return add_low(kept, flip(passed, "dp", 1))


def scatter_tokens(parts):
    passed = add_low(parts[2], flip(parts[3], "mp", 1))
    kept = add_low(parts[0], flip(parts[1], "mp", 1))
    return kept, flip(passed, "mp", 2)


def sum_everywhere(value):
    value = (value + flip(value, "mp", 1)) + (flip(value, "mp", 2) + flip(value, "mp", 3))
    far = [flip_both(value, n // 2, 4 * (n % 2)) for n in range(1, 8)]
    return ((value + far[0]) + (far[1] + far[2])) + ((far[3] + far[4]) + (far[5] + far[6]))


def rotary_tables(length):
    cosine, sine_part, exponent = xpos_tables(length, HEAD_DIM)
    out = []
    for polarity in (1.0, -1.0):
        factor = jnp.exp(polarity * exponent)
        near = (cosine * factor)[:, 0]
        far = (sine_part * factor)[:, 0]
        out.append(jnp.concatenate([near] * 4, axis=-1))
        out.append(jnp.concatenate([-far, far, -far, far], axis=-1))
    return out


def on_device_paired(
    text_states,
    image_states,
    image_offsets,
    image_counts,
    output_grad,
    head_master,
    head_moment,
    head_square,
    outward_master,
    outward_moment,
    outward_square,
    upward_master,
    upward_moment,
    upward_square,
    downward_master,
    downward_moment,
    downward_square,
    gains_master,
    gains_moment,
    gains_square,
):
    model_rank = lax.axis_index("mp")
    side = model_rank // 4
    rank = model_rank % 4
    place = lax.axis_index("dp")
    ids = jnp.stack([rank, place, side]).astype(jnp.int32)
    _, local_len, model_width = text_states.shape
    length = local_len * 8
    rows = 2 * local_len
    hidden_local = upward_master.shape[1]
    hidden_width = hidden_local * 8

    def pick(value, index):
        return lax.dynamic_index_in_dim(value, index, 0, keepdims=False)

    def exchange(pair):
        kept, got = pick(pair, side), flip(pick(pair, 1 - side), "mp", 4)
        return jnp.where(side == 0, jnp.stack([kept, got]), jnp.stack([got, kept]))

    tables = rotary_tables(length)
    text = exchange(text_states)
    head_low = head_master.astype(LOW)
    head_shard = jnp.concatenate([head_low, flip(head_low, "mp", 4)], axis=2)
    head_weight = gather_weight(head_shard, True)
    cotangent = exchange(output_grad).reshape(rows, model_width)

    outward_low = outward_master.astype(LOW)
    core = rank % 2
    half_width = model_width // 2
    outward_half = lax.dynamic_slice_in_dim(outward_low, core * half_width, half_width, 1)
    outward_own = gather_weight(outward_half, False)
    outward_other = [flip(piece, "mp", 1) for piece in outward_own[1:]]
    outward_weight = [outward_low] + [
        jnp.where(
            core == 0,
            jnp.concatenate([own, other], axis=1),
            jnp.concatenate([other, own], axis=1),
        )
        for own, other in zip(outward_own[1:], outward_other)
    ]
    upward_low = upward_master.astype(LOW)
    upward_weight = gather_weight(jnp.concatenate([upward_low, flip(upward_low, "mp", 4)], axis=1), True)
    downward_low = downward_master.astype(LOW)
    downward_weight = gather_weight(jnp.concatenate([downward_low, flip(downward_low, "mp", 4)], axis=0), False)

    gain_in = gains_master[None, :model_width]
    gain_ctx = gains_master[None, model_width : 2 * model_width]
    gain_mid = gains_master[None, 2 * model_width : 3 * model_width]
    hidden_start = 3 * model_width + model_rank * hidden_local
    other_start = 3 * model_width + (model_rank ^ 4) * hidden_local
    gain_hidden = jnp.concatenate(
        [
            lax.dynamic_slice_in_dim(gains_master, hidden_start, hidden_local),
            lax.dynamic_slice_in_dim(gains_master, other_start, hidden_local),
        ]
    )[None]

    offsets = pick(image_offsets, side)
    image_count = pick(image_counts, side)
    position = (
        jnp.arange(2, dtype=jnp.int32)[:, None] * (4 * local_len)
        + rank * local_len
        + jnp.arange(local_len, dtype=jnp.int32)[None, :]
    ).reshape(rows)
    slot_index = jnp.arange(offsets.shape[0], dtype=jnp.int32)
    inside = (
        (position[:, None] >= offsets[None, :])
        & (position[:, None] < offsets[None, :] + PATCH)
        & (slot_index[None, :] < image_count)
    )
    picked = jnp.sum(
        jnp.where(inside, slot_index[None, :] * PATCH + position[:, None] - offsets[None, :], 0), axis=-1
    )
    covered = jnp.any(inside, axis=-1)
    place_index = jnp.arange(image_states.shape[1], dtype=jnp.int32)
    chosen = (covered[:, None] & (picked[:, None] == place_index[None, :])).astype(LOW)
    images = jnp.dot(chosen, pick(image_states, side), preferred_element_type=WIDE).astype(LOW)
    merged = jnp.where(covered[:, None], images, text.reshape(rows, model_width))

    normed = gather_tokens(layer_norm(merged.astype(WIDE), gain_in).astype(LOW))
    cotangents = gather_tokens(cotangent)
    projected = [project(ids, chunk, head_weight, tables, j) for j, chunk in enumerate(normed)]
    queries, keys, values = ([p[n] for p in projected] for n in range(3))
    contexts, lse = attend(ids, queries, keys, values)
    arrived = [contexts[0]] + [flip(contexts[j], "mp", j) for j in range(1, 4)]
    context, mixed, middle, lifted_own = mid_forward(ids, arrived, merged, outward_weight, gain_ctx, gain_mid)
    lifted = gather_tokens(lifted_own)
    first = [ffn_first(ids, x, g, upward_weight, downward_weight, gain_hidden) for x, g in zip(lifted, cotangents)]
    sums = jnp.stack([f[2] for f in first])
    others = [flip(sums, "mp", k) for k in range(1, 4)]
    whole_sums = [
        (sums[j] + others[0][j ^ 1]) + (others[1][j ^ 2] + others[2][j ^ 3]) for j in range(4)
    ]
    second = [
        ffn_second(ids, first[j][0], first[j][1], whole_sums[j], gain_hidden, upward_weight, hidden_width)
        for j in range(4)
    ]
    lifted_parts = scatter_tokens([s[2] for s in second])
    middle_grad, middle_low, context_grads, mid_gains = mid_backward(
        ids, lifted_parts, middle, cotangent, context, outward_weight, gain_mid, gain_ctx
    )
    context_heads = [context_grads[0]] + [flip(context_grads[j], "mp", j) for j in range(1, 4)]
    query_grads, key_grads, value_grads = attend_back(
        ids, queries, keys, values, context_heads, contexts, lse, tables
    )
    normed_parts = [unproject(ids, *g, head_weight) for g in zip(query_grads, key_grads, value_grads)]
    normed_kept, normed_got = scatter_tokens(normed_parts)
    normed_grad = normed_kept.astype(WIDE) + normed_got.astype(WIDE)
    _, input_back = jax.vjp(layer_norm, merged.astype(WIDE), gain_in)
    merged_part, in_gain_grad = input_back(normed_grad)
    input_rows = (middle_grad + merged_part).reshape(2, local_len, model_width)

    ffn_kept, ffn_got = scatter_tokens([ffn_out(ids, s[0], downward_weight) for s in second])
    output_rows = (
        (middle + (ffn_kept.astype(WIDE) + ffn_got.astype(WIDE))).astype(LOW).reshape(2, local_len, model_width)
    )

    def give_back(pair):
        kept = pick(pair, side)
        got = flip(pick(pair, 1 - side).astype(LOW), "mp", 4).astype(pair.dtype)
        return jnp.where(side == 0, jnp.stack([kept, got]), jnp.stack([got, kept]))

    layer_output = give_back(output_rows)
    input_grad = give_back(input_rows)

    tokens = (((0,), (0,)), ((), ()))
    squashed_rows = jnp.concatenate([s[0] for s in second])
    hidden_grad_rows = jnp.concatenate([s[1] for s in second])
    cotangent_rows = jnp.concatenate(cotangents)
    lifted_rows = jnp.concatenate(lifted)
    normed_rows = jnp.concatenate(normed)
    quarter = model_width // 4

    def lanes(value, k):
        return lax.dynamic_slice_in_dim(value, (place ^ k) * quarter, quarter, 1)

    down_grad = scatter_grad(
        [dot(squashed_rows, lanes(cotangent_rows, k), tokens).astype(LOW) for k in range(4)], False
    )
    down_sum = down_grad[:hidden_local].astype(WIDE) + flip(down_grad[hidden_local:], "mp", 4).astype(WIDE)
    up_grad = scatter_grad(
        [dot(lanes(lifted_rows, k), hidden_grad_rows, tokens).astype(LOW) for k in range(4)], True
    )
    up_sum = up_grad[:, :hidden_local].astype(WIDE) + flip(up_grad[:, hidden_local:], "mp", 4).astype(WIDE)

    outward_parts = [dot(lanes(mixed, k), middle_low, tokens).astype(LOW) for k in range(4)]
    outward_parts = [
        add_low(
            lax.dynamic_slice_in_dim(part, core * half_width, half_width, 1),
            flip(lax.dynamic_slice_in_dim(part, (1 - core) * half_width, half_width, 1), "mp", 1),
        )
        for part in outward_parts
    ]
    outward_grad = scatter_grad(outward_parts, False)
    bits = ((2, (rank // 2) % 2), (4, side))
    for mask, bit in bits:
        size = outward_grad.shape[0] // 2
        outward_grad = add_low(
            lax.dynamic_slice_in_dim(outward_grad, bit * size, size, 0),
            flip(lax.dynamic_slice_in_dim(outward_grad, (1 - bit) * size, size, 0), "mp", mask),
        )
    for mask, bit, axis in ((4, side, 0), (2, (rank // 2) % 2, 0), (1, core, 1)):
        got = flip(outward_grad, "mp", mask)
        outward_grad = jnp.where(
            bit == 0,
            jnp.concatenate([outward_grad, got], axis=axis),
            jnp.concatenate([got, outward_grad], axis=axis),
        )
    outward_sum = outward_grad.astype(WIDE)

    head_parts = [jnp.concatenate(g) for g in (query_grads, key_grads, value_grads)]
    head_grad = scatter_grad(
        [jnp.stack([dot(lanes(normed_rows, k), g, tokens).astype(LOW) for g in head_parts]) for k in range(4)], True
    )
    head_local = head_master.shape[2]
    head_sum = head_grad[:, :, :head_local].astype(WIDE) + flip(head_grad[:, :, head_local:], "mp", 4).astype(WIDE)

    moment_head, square_head, head_dir = adapt_step(head_sum, head_master, head_moment, head_square, DECAY_RATE)
    moment_outward, square_outward, outward_dir = adapt_step(
        outward_sum, outward_master, outward_moment, outward_square, DECAY_RATE
    )
    moment_upward, square_upward, upward_dir = adapt_step(
        up_sum, upward_master, upward_moment, upward_square, DECAY_RATE
    )
    moment_downward, square_downward, downward_dir = adapt_step(
        down_sum, downward_master, downward_moment, downward_square, DECAY_RATE
    )
    owner = (model_rank == 0).astype(WIDE)
    norm_early = sum_everywhere(
        jnp.concatenate(
            [
                pair_sums(outward_master, outward_dir) * owner,
                pair_sums(upward_master, upward_dir),
                pair_sums(downward_master, downward_dir),
            ],
            axis=0,
        )
    )
    head_part = jnp.stack(
        [jnp.sum(head_master * head_master, axis=(1, 2)), jnp.sum(head_dir * head_dir, axis=(1, 2))], axis=-1
    )
    hidden_gain = jnp.concatenate([s[3][0:1] for s in second], axis=0).sum(axis=0)
    gains_part = jnp.concatenate([in_gain_grad[0], mid_gains[1], mid_gains[0], jnp.zeros((hidden_width,), WIDE)])
    gains_part = lax.dynamic_update_slice(gains_part, hidden_gain[:hidden_local], (hidden_start,))
    gains_part = lax.dynamic_update_slice(gains_part, hidden_gain[hidden_local:], (other_start,))
    gains_sum = sum_everywhere(gains_part)
    head_norms = sum_everywhere(head_part)
    norm_sums = jnp.concatenate([head_norms, norm_early], axis=0)
    moment_gains, square_gains, gains_dir = adapt_step(gains_sum, gains_master, gains_moment, gains_square, 0.0)
    gains_sums = jnp.stack(
        [
            gain_segments(gains_master * gains_master, model_width),
            gain_segments(gains_dir * gains_dir, model_width),
        ],
        axis=-1,
    )
    updated_head = trust_move(
        head_master, head_dir, head_norms[:, 0][:, None, None], head_norms[:, 1][:, None, None]
    )
    updated_outward = trust_move(outward_master, outward_dir, norm_early[0, 0], norm_early[0, 1])
    updated_upward = trust_move(upward_master, upward_dir, norm_early[1, 0], norm_early[1, 1])
    updated_downward = trust_move(downward_master, downward_dir, norm_early[2, 0], norm_early[2, 1])
    updated_gains = trust_move(
        gains_master,
        gains_dir,
        gain_spread(gains_sums[:, 0], model_width, hidden_width),
        gain_spread(gains_sums[:, 1], model_width, hidden_width),
    )
    update_norms = jnp.sqrt(jnp.concatenate([norm_sums, gains_sums], axis=0))
    return (
        layer_output,
        input_grad,
        moment_head,
        square_head,
        updated_head,
        updated_head.astype(LOW),
        moment_outward,
        square_outward,
        updated_outward,
        updated_outward.astype(LOW),
        moment_upward,
        square_upward,
        updated_upward,
        updated_upward.astype(LOW),
        moment_downward,
        square_downward,
        updated_downward,
        updated_downward.astype(LOW),
        moment_gains,
        square_gains,
        updated_gains,
        update_norms,
    )


def solution(mesh):
    paired = mesh.shape["dp"] == 4 and mesh.shape["mp"] == 8
    return jax.shard_map(
        on_device_paired if paired else on_device_general,
        mesh=mesh,
        in_specs=(
            P("dp", "mp", None),
            P("dp", None, None),
            P("dp", None),
            P("dp"),
            P("dp", "mp", None),
            P(None, "dp", "mp"),
            P(None, "dp", "mp"),
            P(None, "dp", "mp"),
            P("dp", None),
            P("dp", None),
            P("dp", None),
            P("dp", "mp"),
            P("dp", "mp"),
            P("dp", "mp"),
            P("mp", "dp"),
            P("mp", "dp"),
            P("mp", "dp"),
            P(),
            P(),
            P(),
        ),
        out_specs=(
            P("dp", "mp", None),
            P("dp", "mp", None),
            P(None, "dp", "mp"),
            P(None, "dp", "mp"),
            P(None, "dp", "mp"),
            P(None, "dp", "mp"),
            P("dp", None),
            P("dp", None),
            P("dp", None),
            P("dp", None),
            P("dp", "mp"),
            P("dp", "mp"),
            P("dp", "mp"),
            P("dp", "mp"),
            P("mp", "dp"),
            P("mp", "dp"),
            P("mp", "dp"),
            P("mp", "dp"),
            P(),
            P(),
            P(),
            P(),
        ),
        check_vma=False,
    )
```

```python
from functools import partial

import jax
import jax.numpy as jnp
from jax import lax
from jax.experimental import pallas as pl
from jax.experimental.pallas import tpu as pltpu
from jax.sharding import PartitionSpec as P

HEAD_DIM = 64
FF = 8192
PATCH = 64
STEP = 10


EPS_NORM = 1e-05
BETA_ONE = 0.9
BETA_TWO = 0.999
EPS_ADAM = 1e-06
DECAY_RATE = 0.01
STEP_RATE = 0.5


def layer_norm(inputs, gain_vector):
    centre = jnp.mean(inputs, axis=-1, keepdims=True)
    shifted = inputs - centre
    spread = jnp.mean(shifted * shifted, axis=-1, keepdims=True)
    return shifted * lax.rsqrt(spread + EPS_NORM) * gain_vector


def xpos_tables(length, head_size):
    halfway = head_size // 2
    pair_index = jnp.arange(halfway, dtype=jnp.float32)
    angular = jnp.exp(-(2.0 * pair_index / head_size) * jnp.log(10000.0))
    zeta_base = (2.0 * pair_index + 0.4 * head_size) / (1.4 * head_size)
    position = jnp.arange(length, dtype=jnp.float32)[:, None, None]
    return (
        jnp.cos(position * angular),
        jnp.sin(position * angular),
        position / 512.0 * jnp.log(zeta_base),
    )


def rotate(inputs, tables, polarity):
    cosine, sine_part, exponent = tables
    halfway = inputs.shape[-1] // 2
    factor = jnp.exp(polarity * exponent)
    leading = inputs[..., :halfway]
    behind = inputs[..., halfway:]
    return jnp.concatenate(
        [
            (leading * cosine - behind * sine_part) * factor,
            (behind * cosine + leading * sine_part) * factor,
        ],
        axis=-1,
    )


def merge_images(text_rows, image_rows, offsets, image_count, position):
    slot_index = jnp.arange(offsets.shape[0], dtype=jnp.int32)
    inside = (
        (position[:, None] >= offsets[None, :])
        & (position[:, None] < offsets[None, :] + PATCH)
        & (slot_index[None, :] < image_count)
    )
    picked = jnp.sum(
        jnp.where(inside, slot_index[None, :] * PATCH + position[:, None] - offsets[None, :], 0),
        axis=-1,
    )
    chosen = jnp.take(image_rows, picked, axis=0)
    covered = jnp.any(inside, axis=-1)
    return jnp.where(covered[:, None], chosen, text_rows)


def adapt_step(gradient, master, moment, square, decay_rate):
    moment_new = BETA_ONE * moment + (1.0 - BETA_ONE) * gradient
    square_new = BETA_TWO * square + (1.0 - BETA_TWO) * gradient * gradient
    direction = (
        moment_new
        / (1.0 - BETA_ONE**STEP)
        / (jnp.sqrt(square_new / (1.0 - BETA_TWO**STEP)) + EPS_ADAM)
        + decay_rate * master
    )
    return (moment_new, square_new, direction)


def trust_move(master, direction, weight_sum, update_sum):
    return master - STEP_RATE * jnp.sqrt(weight_sum) / (jnp.sqrt(update_sum) + EPS_ADAM) * direction


def gain_segments(entries, model_width):
    return jnp.stack(
        [
            jnp.sum(entries[:model_width]),
            jnp.sum(entries[model_width : 2 * model_width]),
            jnp.sum(entries[2 * model_width : 3 * model_width]),
            jnp.sum(entries[3 * model_width :]),
        ]
    )


def gain_spread(sums, model_width, hidden_width):
    return jnp.concatenate(
        [
            jnp.broadcast_to(sums[0], (model_width,)),
            jnp.broadcast_to(sums[1], (model_width,)),
            jnp.broadcast_to(sums[2], (model_width,)),
            jnp.broadcast_to(sums[3], (hidden_width,)),
        ]
    )


def pair_sums(master, direction):
    return jnp.stack([jnp.sum(master * master), jnp.sum(direction * direction)])[None]


def on_device_general(
    text_states,
    image_states,
    image_offsets,
    image_counts,
    output_grad,
    head_master,
    head_moment,
    head_square,
    outward_master,
    outward_moment,
    outward_square,
    upward_master,
    upward_moment,
    upward_square,
    downward_master,
    downward_moment,
    downward_square,
    gains_master,
    gains_moment,
    gains_square,
):
    groups = lax.axis_size("mp")
    model_rank = lax.axis_index("mp")
    seq_count, local_len, model_width = text_states.shape
    length = local_len * groups
    hidden_local = upward_master.shape[1]
    heads_local = head_master.shape[2] // HEAD_DIM
    tables = xpos_tables(length, HEAD_DIM)
    position = model_rank * local_len + jnp.arange(local_len, dtype=jnp.int32)
    merged = jax.vmap(
        lambda text_rows, image_rows, offsets, image_count: merge_images(
            text_rows, image_rows, offsets, image_count, position
        )
    )(text_states, image_states, image_offsets, image_counts).astype(jnp.float32)
    gain_in = gains_master[:model_width]
    gain_ctx = gains_master[model_width : 2 * model_width]
    gain_mid = gains_master[2 * model_width : 3 * model_width]
    hidden_start = 3 * model_width + model_rank * hidden_local
    gain_hidden = lax.dynamic_slice_in_dim(gains_master, hidden_start, hidden_local)
    head_weight_whole, outward_weight_whole, upward_weight_whole, down_weight_whole = (
        lax.all_gather(head_master.astype(jnp.bfloat16), "dp", axis=1, tiled=True),
        lax.all_gather(outward_master.astype(jnp.bfloat16), "dp", axis=0, tiled=True),
        lax.all_gather(upward_master.astype(jnp.bfloat16), "dp", axis=0, tiled=True),
        lax.all_gather(downward_master.astype(jnp.bfloat16), "dp", axis=1, tiled=True),
    )
    normed_low = layer_norm(merged, gain_in).astype(jnp.bfloat16)
    normed_rows_full, cotangent_rows_full = (
        lax.all_gather(normed_low, "mp", axis=1, tiled=True),
        lax.all_gather(output_grad, "mp", axis=1, tiled=True),
    )
    projected = jnp.einsum(
        "hvg,bga->bhva", normed_rows_full, head_weight_whole, preferred_element_type=jnp.float32
    )
    shaped = projected.reshape(3, seq_count, length, heads_local, HEAD_DIM)
    queries = rotate(shaped[0], tables, 1.0).astype(jnp.bfloat16)
    key_rows = rotate(shaped[1], tables, -1.0).astype(jnp.bfloat16)
    values = shaped[2].astype(jnp.bfloat16)
    block_len = min(512, length)
    block_count = length // block_len
    starts = jnp.arange(block_count, dtype=jnp.int32) * block_len
    key_place = jnp.arange(length, dtype=jnp.int32)

    def block_scores(query_block, start):
        scores = (
            jnp.einsum("sqhd,skhd->shqk", query_block, key_rows, preferred_element_type=jnp.float32)
            * 0.125
        )
        allowed = key_place[None, :] <= (start + jnp.arange(block_len, dtype=jnp.int32))[:, None]
        return jnp.where(allowed, scores, -1e30)

    def forward_block(start):
        query_block = lax.dynamic_slice_in_dim(queries, start, block_len, 1)
        scores = block_scores(query_block, start)
        highest = jnp.max(scores, axis=-1, keepdims=True)
        exponent = jnp.exp(scores - highest)
        total = jnp.sum(exponent, axis=-1, keepdims=True)
        attention = exponent / total
        context_block = jnp.einsum(
            "shqk,skhd->sqhd",
            attention.astype(jnp.bfloat16),
            values,
            preferred_element_type=jnp.float32,
        )
        return (context_block, highest[..., 0] + jnp.log(total[..., 0]))

    context_blocks, log_sums = lax.map(forward_block, starts)
    context = jnp.transpose(context_blocks, (1, 0, 2, 3, 4)).reshape(
        seq_count, length, heads_local * HEAD_DIM
    )
    context_rows = lax.all_to_all(
        context.astype(jnp.bfloat16), "mp", split_axis=1, concat_axis=2, tiled=True
    )
    context_in = context_rows.astype(jnp.float32)
    mixed_half_precision = layer_norm(context_in, gain_ctx).astype(jnp.bfloat16)
    middle = merged + jnp.einsum(
        "ymq,qc->ymc",
        mixed_half_precision,
        outward_weight_whole,
        preferred_element_type=jnp.float32,
    )
    lifted_low = layer_norm(middle, gain_mid).astype(jnp.bfloat16)
    lifted_rows_full = lax.all_gather(lifted_low, "mp", axis=1, tiled=True)
    hidden_rows = jnp.einsum(
        "orb,bg->org", lifted_rows_full, upward_weight_whole, preferred_element_type=jnp.float32
    )
    activated = jax.nn.gelu(hidden_rows, approximate=False)
    first_sum, second_sum = lax.psum(
        (jnp.sum(activated, axis=-1), jnp.sum(activated * activated, axis=-1)), "mp"
    )
    centre = first_sum / FF
    scale_inv = lax.rsqrt(second_sum / FF - centre * centre + EPS_NORM)[..., None]
    standard = (activated - centre[..., None]) * scale_inv
    squashed_half_precision = (standard * gain_hidden).astype(jnp.bfloat16)
    ffn_part = jnp.einsum(
        "wxp,pk->wxk",
        squashed_half_precision,
        down_weight_whole,
        preferred_element_type=jnp.float32,
    )
    ffn_rows = lax.psum_scatter(
        ffn_part.astype(jnp.bfloat16), "mp", scatter_dimension=1, tiled=True
    ).astype(jnp.float32)
    layer_output = (middle + ffn_rows).astype(jnp.bfloat16)
    down_grad = jnp.einsum(
        "uxy,uxo->yo",
        squashed_half_precision,
        cotangent_rows_full,
        preferred_element_type=jnp.float32,
    )
    squashed_grad = jnp.einsum(
        "yxr,ur->yxu", cotangent_rows_full, down_weight_whole, preferred_element_type=jnp.float32
    )
    hidden_gain_grad = jnp.sum(squashed_grad * standard, axis=(0, 1))
    scaled_grad = squashed_grad * gain_hidden
    mean_one, mean_two = (
        lax.psum(jnp.sum(scaled_grad, axis=-1).astype(jnp.bfloat16), "mp").astype(jnp.float32),
        lax.psum(jnp.sum(scaled_grad * standard, axis=-1).astype(jnp.bfloat16), "mp").astype(
            jnp.float32
        ),
    )
    activated_grad = (
        scaled_grad - mean_one[..., None] / FF - standard * (mean_two[..., None] / FF)
    ) * scale_inv
    gelu_out, gelu_back = jax.vjp(partial(jax.nn.gelu, approximate=False), hidden_rows)
    hidden_rows_grad = gelu_back(activated_grad)[0].astype(jnp.bfloat16)
    upward_gradient = jnp.einsum(
        "gki,gkt->it", lifted_rows_full, hidden_rows_grad, preferred_element_type=jnp.float32
    )
    lifted_part = jnp.einsum(
        "eiw,mw->eim", hidden_rows_grad, upward_weight_whole, preferred_element_type=jnp.float32
    )
    lifted_grad = lax.psum_scatter(lifted_part, "mp", scatter_dimension=1, tiled=True)
    norm_out, middle_back = jax.vjp(layer_norm, middle, gain_mid)
    middle_part, mid_gain_grad = middle_back(lifted_grad)
    middle_grad = output_grad.astype(jnp.float32) + middle_part
    middle_half_precision = middle_grad.astype(jnp.bfloat16)
    outward_part = jnp.einsum(
        "hyk,hyo->ko",
        mixed_half_precision,
        middle_half_precision,
        preferred_element_type=jnp.float32,
    )
    mixed_grad = jnp.einsum(
        "hox,kx->hok",
        middle_half_precision,
        outward_weight_whole,
        preferred_element_type=jnp.float32,
    )
    context_out, context_back = jax.vjp(layer_norm, context_in, gain_ctx)
    context_grad, ctx_gain_grad = context_back(mixed_grad)
    context_heads = lax.all_to_all(
        context_grad.astype(jnp.bfloat16), "mp", split_axis=2, concat_axis=1, tiled=True
    )
    grad_heads = context_heads.reshape(seq_count, length, heads_local, HEAD_DIM)

    def backward_block(totals, inputs):
        key_total, value_total = totals
        start, log_block = inputs
        query_block = lax.dynamic_slice_in_dim(queries, start, block_len, 1)
        grad_block = lax.dynamic_slice_in_dim(grad_heads, start, block_len, 1)
        scores = block_scores(query_block, start)
        attention = jnp.exp(scores - log_block[..., None])
        prob_grad = jnp.einsum(
            "sqhd,skhd->shqk", grad_block, values, preferred_element_type=jnp.float32
        )
        row_dot = jnp.sum(attention * prob_grad, axis=-1, keepdims=True)
        score_low = (attention * (prob_grad - row_dot)).astype(jnp.bfloat16)
        query_turned = (
            jnp.einsum("shqk,skhd->sqhd", score_low, key_rows, preferred_element_type=jnp.float32)
            * 0.125
        )
        key_total = (
            key_total
            + jnp.einsum(
                "shqk,sqhd->skhd", score_low, query_block, preferred_element_type=jnp.float32
            )
            * 0.125
        )
        value_total = value_total + jnp.einsum(
            "shqk,sqhd->skhd",
            attention.astype(jnp.bfloat16),
            grad_block,
            preferred_element_type=jnp.float32,
        )
        return ((key_total, value_total), query_turned)

    zero_heads = jnp.zeros((seq_count, length, heads_local, HEAD_DIM), jnp.float32)
    (key_turned, value_grad), query_blocks = lax.scan(
        backward_block, (zero_heads, zero_heads), (starts, log_sums)
    )
    query_turned = jnp.transpose(query_blocks, (1, 0, 2, 3, 4)).reshape(
        seq_count, length, heads_local, HEAD_DIM
    )
    query_out, query_back = jax.vjp(lambda inputs: rotate(inputs, tables, 1.0), shaped[0])
    key_out, key_back = jax.vjp(lambda inputs: rotate(inputs, tables, -1.0), shaped[1])
    projection_gradient = (
        jnp.stack([query_back(query_turned)[0], key_back(key_turned)[0], value_grad])
        .astype(jnp.bfloat16)
        .reshape(3, seq_count, length, heads_local * HEAD_DIM)
    )
    head_grad = jnp.einsum(
        "fbn,ufbj->unj", normed_rows_full, projection_gradient, preferred_element_type=jnp.float32
    )
    normed_part = jnp.einsum(
        "acqr,aur->cqu", projection_gradient, head_weight_whole, preferred_element_type=jnp.float32
    )
    normed_grad = lax.psum_scatter(
        normed_part.astype(jnp.bfloat16), "mp", scatter_dimension=1, tiled=True
    ).astype(jnp.float32)
    input_out, input_back = jax.vjp(layer_norm, merged, gain_in)
    merged_part, in_gain_grad = input_back(normed_grad)
    input_grad = middle_grad + merged_part
    head_sum, outward_sum, upward_sum, downward_sum = (
        lax.psum_scatter(
            head_grad.astype(jnp.bfloat16), "dp", scatter_dimension=1, tiled=True
        ).astype(jnp.float32),
        lax.psum_scatter(
            outward_part.astype(jnp.bfloat16), "dp", scatter_dimension=0, tiled=True
        ).astype(jnp.float32),
        lax.psum_scatter(
            upward_gradient.astype(jnp.bfloat16), "dp", scatter_dimension=0, tiled=True
        ).astype(jnp.float32),
        lax.psum_scatter(
            down_grad.astype(jnp.bfloat16), "dp", scatter_dimension=1, tiled=True
        ).astype(jnp.float32),
    )
    outward_sum = lax.psum(outward_sum.astype(jnp.bfloat16), "mp").astype(jnp.float32)
    moment_head, square_head, head_dir = adapt_step(
        head_sum, head_master, head_moment, head_square, DECAY_RATE
    )
    moment_outward, square_outward, outward_dir = adapt_step(
        outward_sum, outward_master, outward_moment, outward_square, DECAY_RATE
    )
    moment_upward, square_upward, upward_dir = adapt_step(
        upward_sum, upward_master, upward_moment, upward_square, DECAY_RATE
    )
    moment_downward, square_downward, downward_dir = adapt_step(
        downward_sum, downward_master, downward_moment, downward_square, DECAY_RATE
    )
    owner = (model_rank == 0).astype(jnp.float32)
    head_part = jnp.stack(
        [
            jnp.sum(head_master * head_master, axis=(1, 2)),
            jnp.sum(head_dir * head_dir, axis=(1, 2)),
        ],
        axis=-1,
    )
    norm_part = jnp.concatenate(
        [
            head_part,
            pair_sums(outward_master, outward_dir) * owner,
            pair_sums(upward_master, upward_dir),
            pair_sums(downward_master, downward_dir),
        ],
        axis=0,
    )
    gains_part = jnp.concatenate(
        [in_gain_grad, ctx_gain_grad, mid_gain_grad, jnp.zeros((FF,), jnp.float32)]
    )
    gains_part = lax.dynamic_update_slice(gains_part, hidden_gain_grad, (hidden_start,))
    gains_sum, norm_sums = lax.psum((gains_part, norm_part), ("dp", "mp"))
    moment_gains, square_gains, gains_dir = adapt_step(
        gains_sum, gains_master, gains_moment, gains_square, 0.0
    )
    gains_sums = jnp.stack(
        [
            gain_segments(gains_master * gains_master, model_width),
            gain_segments(gains_dir * gains_dir, model_width),
        ],
        axis=-1,
    )
    updated_head = trust_move(
        head_master, head_dir, norm_sums[0:3, 0][:, None, None], norm_sums[0:3, 1][:, None, None]
    )
    updated_outward = trust_move(outward_master, outward_dir, norm_sums[3, 0], norm_sums[3, 1])
    updated_upward = trust_move(upward_master, upward_dir, norm_sums[4, 0], norm_sums[4, 1])
    updated_downward = trust_move(downward_master, downward_dir, norm_sums[5, 0], norm_sums[5, 1])
    updated_gains = trust_move(
        gains_master,
        gains_dir,
        gain_spread(gains_sums[:, 0], model_width, FF),
        gain_spread(gains_sums[:, 1], model_width, FF),
    )
    update_norms = jnp.sqrt(jnp.concatenate([norm_sums, gains_sums], axis=0))
    return (
        layer_output,
        input_grad,
        moment_head,
        square_head,
        updated_head,
        updated_head.astype(jnp.bfloat16),
        moment_outward,
        square_outward,
        updated_outward,
        updated_outward.astype(jnp.bfloat16),
        moment_upward,
        square_upward,
        updated_upward,
        updated_upward.astype(jnp.bfloat16),
        moment_downward,
        square_downward,
        updated_downward,
        updated_downward.astype(jnp.bfloat16),
        moment_gains,
        square_gains,
        updated_gains,
        update_norms,
    )


SHARE = 0.3
LOG2E = 1.4426950408889634
LANES = 128
NT = (((1,), (1,)), ((), ()))
NN = (((1,), (0,)), ((), ()))
LOW = jnp.bfloat16
WIDE = jnp.float32
ONCE = pl.Buffered(1)


def dot(left, right, dims):
    return lax.dot_general(left, right, dims, preferred_element_type=WIDE)


def kernel_call(body, grid, in_specs, out_specs, out_shape, scratch, flops, moved, operands):
    return pl.pallas_call(
        body,
        grid_spec=pltpu.PrefetchScalarGridSpec(
            num_scalar_prefetch=1, grid=grid, in_specs=in_specs, out_specs=out_specs, scratch_shapes=scratch
        ),
        out_shape=out_shape,
        compiler_params=pltpu.CompilerParams(vmem_limit_bytes=56 << 20),
        cost_estimate=pl.CostEstimate(flops=int(flops * SHARE), bytes_accessed=int(moved * SHARE), transcendentals=0),
    )(*operands)


def own_rows(sub, rank, j, b):
    return pl.ds(pl.multiple_of(b * 4 * sub + (rank ^ j) * sub, sub), sub)


def own_block(place, k, width):
    return pl.ds(pl.multiple_of((place ^ k) * width, width), width)


def swap_halves(block):
    low = lax.broadcasted_iota(jnp.int32, (1, LANES), 1) % HEAD_DIM < HEAD_DIM // 2
    return jnp.where(low, pltpu.roll(block, LANES - HEAD_DIM // 2, 1), pltpu.roll(block, HEAD_DIM // 2, 1))


def project_kernel(ids, x, w0, w1, w2, w3, cq, sq, ck, sk, q, k, v):
    depth = w0.shape[1]
    width = w0.shape[2]
    for f, (out, c, s) in enumerate(((q, cq, sq), (k, ck, sk), (v, None, None))):
        total = None
        for n, w in enumerate((w0, w1, w2, w3)):
            part = dot(x[:, own_block(ids[1], n, depth)], w[f], NN)
            total = part if total is None else total + part
        for p in range(width // LANES):
            here = slice(p * LANES, (p + 1) * LANES)
            block = total[:, here]
            if c is not None:
                block = block * c[...] + swap_halves(block) * s[...]
            out[:, here] = block.astype(LOW)


def quarters(weight):
    if isinstance(weight, list):
        spec = pl.BlockSpec(weight[0].shape, lambda b, ids: (0, 0, 0), pipeline_mode=ONCE)
        return weight, [spec] * 4
    kinds, model, width = weight.shape
    return [weight] * 4, [
        pl.BlockSpec((kinds, model // 4, width), partial(lambda n, b, ids: (0, ids[1] ^ n, 0), n), pipeline_mode=ONCE)
        for n in range(4)
    ]


def project(ids, x, weight, tables, j):
    rows, model = x.shape
    sub = rows // 2
    weights, specs = quarters(weight)
    width = weights[0].shape[2]
    table = pl.BlockSpec((sub, LANES), lambda b, ids: (b * 4 + (ids[0] ^ j), 0))
    out = pl.BlockSpec((sub, width), lambda b, ids: (b, 0))
    return kernel_call(
        project_kernel,
        (2,),
        [pl.BlockSpec((sub, model), lambda b, ids: (b, 0))] + specs + [table] * 4,
        [out] * 3,
        [jax.ShapeDtypeStruct((rows, width), LOW)] * 3,
        [],
        6 * rows * model * width,
        6 * model * width + 8 * rows * model,
        (ids, x, *weights, *tables),
    )


def attend_kernel(ids, *refs, bq, bk):
    q_, k_, v_, o_, lse_ref = refs[0:4], refs[4:8], refs[8:12], refs[12:16], refs[16]
    qs, ks, vt, os = refs[17:]
    rank = ids[0]
    length = qs.shape[0]
    sub = q_[0].shape[0] // 2
    for j in range(4):
        for b in range(2):
            rows = own_rows(sub, rank, j, b)
            here = slice(b * sub, (b + 1) * sub)
            qs[rows, :] = q_[j][here, :]
            ks[rows, :] = k_[j][here, :]
            vt[:, rows] = v_[j][here, :].T
    first = lax.broadcasted_iota(jnp.int32, (1, LANES), 1) < HEAD_DIM
    ratio = bq // bk

    def q_block(i, _):
        here = pl.ds(pl.multiple_of(i * bq, bq), bq)
        q = qs[here, :]
        zero = jnp.zeros_like(q)
        parted = (jnp.where(first, q, zero), jnp.where(first, zero, q))

        def step(j, carry, diagonal):
            at = pl.multiple_of(j * bk, bk)
            k = ks[pl.ds(at, bk), :]
            out = []
            for h in range(2):
                highest, total, sums = carry[h]
                scores = dot(k, parted[h], NT) * (0.125 * LOG2E)
                if diagonal is not None:
                    key = diagonal * bk + lax.broadcasted_iota(jnp.int32, (bk, bq), 0)
                    scores = jnp.where(key <= lax.broadcasted_iota(jnp.int32, (bk, bq), 1), scores, -1e30)
                new = jnp.maximum(highest, jnp.max(scores, axis=0, keepdims=True))
                probs = jnp.exp2(scores - new)
                scale = jnp.exp2(highest - new)
                total = total * scale + jnp.sum(probs, axis=0, keepdims=True)
                rows = vt[h * HEAD_DIM : (h + 1) * HEAD_DIM, pl.ds(at, bk)]
                out.append((new, total, sums * scale + dot(rows, probs.astype(LOW), NN)))
            return tuple(out)

        start = tuple(
            (jnp.full((1, bq), -1e30, WIDE), jnp.zeros((1, bq), WIDE), jnp.zeros((HEAD_DIM, bq), WIDE))
            for _ in range(2)
        )
        carry = lax.fori_loop(0, i * ratio, lambda j, c: step(j, c, None), start)
        for d in range(ratio):
            carry = step(i * ratio + d, carry, d)
        turned = jnp.concatenate([carry[h][2] / carry[h][1] for h in range(2)], axis=0)
        os[here, :] = turned.T.astype(LOW)
        for h in range(2):
            lse_ref[0, h : h + 1, here] = carry[h][0] + jnp.log2(carry[h][1])
        return 0

    lax.fori_loop(0, length // bq, q_block, 0)
    for j in range(4):
        for b in range(2):
            o_[j][b * sub : (b + 1) * sub, :] = os[own_rows(sub, rank, j, b), :]


def attend(ids, queries, keys, values):
    rows, width = queries[0].shape
    length, pairs = rows * 4, width // LANES
    chunk = pl.BlockSpec((rows, LANES), lambda p, ids: (0, p))
    low = pltpu.VMEM((length, LANES), LOW)
    result = kernel_call(
        partial(attend_kernel, bq=min(1024, length), bk=min(512, length)),
        (pairs,),
        [chunk] * 12,
        [chunk] * 4 + [pl.BlockSpec((1, 2, length), lambda p, ids: (p, 0, 0))],
        [jax.ShapeDtypeStruct((rows, width), LOW)] * 4 + [jax.ShapeDtypeStruct((pairs, 2, length), WIDE)],
        [low, low, pltpu.VMEM((LANES, length), LOW), low],
        40e9,
        10e6,
        (ids, *queries, *keys, *values),
    )
    return result[:4], result[4]


def attend_back_kernel(ids, *refs, bq, bk):
    q_, k_, v_, d_, o_ = refs[0:4], refs[4:8], refs[8:12], refs[12:16], refs[16:20]
    lse_ref, cq, sq, ck, sk = refs[20:25]
    dq_, dk_, dv_ = refs[25:29], refs[29:33], refs[33:37]
    qs, ks, vs, ds, kt, dqt, dks, dvs, delta = refs[37:]
    rank = ids[0]
    length = qs.shape[0]
    sub = q_[0].shape[0] // 2
    for j in range(4):
        for b in range(2):
            rows = own_rows(sub, rank, j, b)
            here = slice(b * sub, (b + 1) * sub)
            qs[rows, :] = q_[j][here, :]
            ks[rows, :] = k_[j][here, :]
            kt[:, rows] = k_[j][here, :].T
            vs[rows, :] = v_[j][here, :]
            ds[rows, :] = d_[j][here, :]
            product = (d_[j][here, :].astype(WIDE) * o_[j][here, :].astype(WIDE)).T
            delta[0:1, rows] = jnp.sum(product[:HEAD_DIM], axis=0, keepdims=True)
            delta[1:2, rows] = jnp.sum(product[HEAD_DIM:], axis=0, keepdims=True)
    first = lax.broadcasted_iota(jnp.int32, (1, LANES), 1) < HEAD_DIM
    dqt[...] = jnp.zeros_like(dqt)

    def k_block(j, _):
        at = pl.ds(pl.multiple_of(j * bk, bk), bk)
        k = ks[at, :]
        v = vs[at, :]

        def step(i, carry, diagonal):
            dk, dv = carry
            here = pl.ds(pl.multiple_of(i * bq, bq), bq)
            q, do = qs[here, :], ds[here, :]
            zero = jnp.zeros_like(q)
            for h in range(2):
                lanes = slice(h * HEAD_DIM, (h + 1) * HEAD_DIM)
                q_own = jnp.where(first, q, zero) if h == 0 else jnp.where(first, zero, q)
                do_own = jnp.where(first, do, zero) if h == 0 else jnp.where(first, zero, do)
                scores = dot(k, q_own, NT) * (0.125 * LOG2E) - lse_ref[0, h : h + 1, here]
                if diagonal:
                    key = lax.broadcasted_iota(jnp.int32, (bk, bq), 0)
                    scores = jnp.where(key <= lax.broadcasted_iota(jnp.int32, (bk, bq), 1), scores, -1e30)
                probs = jnp.exp2(scores)
                prob_grad = dot(v, do_own, NT)
                grad = (probs * (prob_grad - delta[h : h + 1, here])).astype(LOW)
                dv = dv + dot(probs.astype(LOW), do_own, NN)
                dk = dk + dot(grad, q_own, NN)
                dqt[lanes, here] += dot(kt[lanes, at], grad, NN)
            return dk, dv

        zeros = jnp.zeros((bk, LANES), WIDE)
        carry = step(j, (zeros, zeros), True)
        dk, dv = lax.fori_loop(j + 1, length // bq, lambda i, c: step(i, c, False), carry)
        dks[at, :] = dk * 0.125
        dvs[at, :] = dv.astype(LOW)
        return 0

    lax.fori_loop(0, length // bk, k_block, 0)
    for j in range(4):
        for b in range(2):
            rows = own_rows(sub, rank, j, b)
            here = slice(b * sub, (b + 1) * sub)
            query_grad = dqt[:, rows].T * 0.125
            dq_[j][here, :] = (query_grad * cq[rows, :] - swap_halves(query_grad) * sq[rows, :]).astype(LOW)
            key_grad = dks[rows, :]
            dk_[j][here, :] = (key_grad * ck[rows, :] - swap_halves(key_grad) * sk[rows, :]).astype(LOW)
            dv_[j][here, :] = dvs[rows, :]


def attend_back(ids, queries, keys, values, cotangents, contexts, lse, tables):
    rows, width = queries[0].shape
    length, pairs = rows * 4, width // LANES
    chunk = pl.BlockSpec((rows, LANES), lambda p, ids: (0, p))
    whole = pl.BlockSpec((length, LANES), lambda p, ids: (0, 0), pipeline_mode=ONCE)
    low = pltpu.VMEM((length, LANES), LOW)
    block = min(512, length)
    result = kernel_call(
        partial(attend_back_kernel, bq=block, bk=block),
        (pairs,),
        [chunk] * 20 + [pl.BlockSpec((1, 2, length), lambda p, ids: (p, 0, 0))] + [whole] * 4,
        [chunk] * 12,
        [jax.ShapeDtypeStruct((rows, width), LOW)] * 12,
        [
            low,
            low,
            low,
            low,
            pltpu.VMEM((LANES, length), LOW),
            pltpu.VMEM((LANES, length), WIDE),
            pltpu.VMEM((length, LANES), WIDE),
            low,
            pltpu.VMEM((2, length), WIDE),
        ],
        60e9,
        20e6,
        (ids, *queries, *keys, *values, *cotangents, *contexts, lse, *tables),
    )
    return result[0:4], result[4:8], result[8:12]


def centred(block):
    shifted = block - jnp.mean(block, axis=-1, keepdims=True)
    spread = jnp.mean(shifted * shifted, axis=-1, keepdims=True)
    scale = lax.rsqrt(spread + EPS_NORM)
    return shifted * scale, scale


def norm_back(standard, scale, gain, grad):
    scaled = grad * gain
    first = jnp.mean(scaled, axis=-1, keepdims=True)
    second = jnp.mean(scaled * standard, axis=-1, keepdims=True)
    return scale * (scaled - first - standard * second)


def context_lanes(ids, j, side, width):
    half = ids[2] ^ side
    return pl.ds(pl.multiple_of(half * 4 * width + (ids[0] ^ j) * width, width), width)


def mid_kernel(ids, *refs):
    pieces = refs[:8]
    merged, weights, (g_ctx, g_mid, ctx, mixed, middle, lifted) = refs[8], sheets(refs[9:13]), refs[13:]
    width = pieces[0].shape[1]
    for n, c in enumerate(pieces):
        ctx[:, context_lanes(ids, n % 4, n // 4, width)] = c[...]
    standard, _ = centred(ctx[...].astype(WIDE))
    mixed[...] = (standard * g_ctx[...]).astype(LOW)
    depth, half = weights[0].shape
    for n in range(2):
        lanes = core_lanes(ids, n, half)
        total = merged[:, lanes].astype(WIDE)
        for k in range(4):
            total = total + dot(mixed[:, own_block(ids[1], k, depth)], weights[4 * n + k][...], NN)
        middle[:, lanes] = total
    standard, _ = centred(middle[...])
    lifted[...] = (standard * g_mid[...]).astype(LOW)


def sheets(refs):
    own, pieces, other, others = refs
    return [own] + [pieces.at[n] for n in range(3)] + [other] + [others.at[n] for n in range(3)]


def core_lanes(ids, n, half):
    return pl.ds(pl.multiple_of((ids[0] % 2 ^ n) * half, half), half)


def mid_forward(ids, contexts, merged, weights, g_ctx, g_mid):
    rows, model = merged.shape
    specs = [pl.BlockSpec(w.shape, partial(lambda n, b, ids: (0,) * n, w.ndim), pipeline_mode=ONCE) for w in weights]
    block = min(256, rows)
    line = lambda width: pl.BlockSpec((block, width), lambda b, ids: (b, 0))
    gain = pl.BlockSpec((1, model), lambda b, ids: (0, 0))
    shape = lambda kind: jax.ShapeDtypeStruct((rows, model), kind)
    return kernel_call(
        mid_kernel,
        (rows // block,),
        [line(contexts[0].shape[1])] * 8 + [line(model)] + specs + [gain] * 2,
        [line(model)] * 4,
        [shape(LOW), shape(LOW), shape(WIDE), shape(LOW)],
        [],
        2 * rows * model * model,
        2 * model * model + 14 * rows * model,
        (ids, *contexts, merged, *weights, g_ctx, g_mid),
    )


def mid_back_kernel(ids, *refs):
    a, r, middle, og, ctx = refs[:5]
    weights, (g_mid, g_ctx, middle_grad, middle_low) = sheets(refs[5:9]), refs[9:13]
    pieces, gains, mixed_grad = refs[13:21], refs[21], refs[22]
    grad = a[...].astype(WIDE) + r[...].astype(WIDE)
    standard, scale = centred(middle[...])

    @pl.when(pl.program_id(0) == 0)
    def _():
        gains[...] = jnp.zeros_like(gains)

    gains[0:1, :] += jnp.sum(grad * standard, axis=0, keepdims=True)
    total = og[...].astype(WIDE) + norm_back(standard, scale, g_mid[...], grad)
    middle_grad[...] = total
    middle_low[...] = total.astype(LOW)
    depth, half = weights[0].shape
    own, other = middle_low[:, core_lanes(ids, 0, half)], middle_low[:, core_lanes(ids, 1, half)]
    for k in range(4):
        mixed_grad[:, own_block(ids[1], k, depth)] = dot(own, weights[k][...], NT) + dot(other, weights[4 + k][...], NT)
    grad = mixed_grad[...]
    standard, scale = centred(ctx[...].astype(WIDE))
    gains[1:2, :] += jnp.sum(grad * standard, axis=0, keepdims=True)
    mixed_grad[...] = norm_back(standard, scale, g_ctx[...], grad)
    width = pieces[0].shape[1]
    for n, d in enumerate(pieces):
        d[...] = mixed_grad[:, context_lanes(ids, n % 4, n // 4, width)].astype(LOW)


def mid_backward(ids, parts, middle, og, ctx, weights, g_mid, g_ctx):
    rows, model = middle.shape
    specs = [pl.BlockSpec(w.shape, partial(lambda n, b, ids: (0,) * n, w.ndim), pipeline_mode=ONCE) for w in weights]
    block = min(256, rows)
    line = lambda width: pl.BlockSpec((block, width), lambda b, ids: (b, 0))
    gain = pl.BlockSpec((1, model), lambda b, ids: (0, 0))
    shape = lambda width, kind: jax.ShapeDtypeStruct((rows, width), kind)
    result = kernel_call(
        mid_back_kernel,
        (rows // block,),
        [line(model)] * 5 + specs + [gain] * 2,
        [line(model)] * 2 + [line(model // 8)] * 8 + [pl.BlockSpec((8, model), lambda b, ids: (0, 0))],
        [shape(model, WIDE), shape(model, LOW)]
        + [shape(model // 8, LOW)] * 8
        + [jax.ShapeDtypeStruct((8, model), WIDE)],
        [pltpu.VMEM((block, model), WIDE)],
        2 * rows * model * model,
        2 * model * model + 18 * rows * model,
        (ids, *parts, middle, og, ctx, *weights, g_mid, g_ctx),
    )
    return result[0], result[1], result[2:6], result[6:10], result[10]


def gelu_parts(hidden):
    share = 0.5 + 0.5 * lax.erf(hidden * 0.7071067811865476)
    return hidden * share, share


def gelu_slope(hidden, share):
    return share + hidden * (0.3989422804014327 * jnp.exp(-0.5 * hidden * hidden))


def fold(block):
    out = block[:, :LANES]
    for p in range(1, block.shape[1] // LANES):
        out = out + block[:, p * LANES : (p + 1) * LANES]
    return out


def halves(count, rows_first):
    if rows_first:
        return (
            lambda u, ids: (jnp.minimum(u, count - 1), 0),
            lambda u, ids: (jnp.maximum(u - count, 0), 0),
        )
    return (
        lambda u, ids: (0, jnp.minimum(u, count - 1)),
        lambda u, ids: (0, jnp.maximum(u - count, 0)),
    )


def each_half(work, own, got):
    near = pl.program_id(0) < pl.num_programs(0) // 2

    @pl.when(near)
    def _():
        work(own)

    @pl.when(jnp.logical_not(near))
    def _():
        work(got)


def remote(source, target, sent, got, device):
    return pltpu.make_async_remote_copy(
        src_ref=source, dst_ref=target, send_sem=sent, recv_sem=got, device_id=device, device_id_type=MESH
    )


def ffn_up_kernel(
    lifted, own_cotangent, up_own, up_got, act, slope, sums, lifted_all, cotangent_all, x, acc, sent, got, local
):
    j, u = pl.program_id(0), pl.program_id(1)
    rows = x.shape[0]
    half = rows // 2
    _, _, over_core, over_low, _ = partners()
    parts = [pl.ds(b * half, half) for b in range(2)]

    def moves(source, whole, base):
        near = remote(source, whole.at[0], sent.at[base], got.at[base], over_core)
        far = [
            remote(source.at[part], whole.at[1, part], sent.at[base + 1 + b], got.at[base + 1 + b], over_low)
            for b, part in enumerate(parts)
        ]
        last = [
            remote(whole.at[1, part], whole.at[2, part], sent.at[base + 3 + b], got.at[base + 3 + b], over_core)
            for b, part in enumerate(parts)
        ]
        return near, far, last

    near, far, last = moves(lifted, lifted_all, 0)
    near_c, far_c, last_c = moves(own_cotangent, cotangent_all, 5)

    def load(source):
        copy = pltpu.make_async_copy(source, x, local)
        copy.start()
        copy.wait()

    @pl.when(u == 0)
    def _():
        acc[...] = jnp.zeros_like(acc)

    @pl.when((j == 0) & (u == 0))
    def _():
        greet((over_core, over_low))
        for copy in (*far, near, near_c):
            copy.start()
        load(lifted)

    @pl.when((j == 1) & (u == 0))
    def _():
        near.wait()
        load(lifted_all.at[0])

    @pl.when((j == 2) & (u == 0))
    def _():
        for copy, onward in zip(far, last):
            copy.wait()
            onward.start()
        for copy in far_c:
            copy.start()
        load(lifted_all.at[1])

    @pl.when((j == 3) & (u == 0))
    def _():
        for copy in last:
            copy.wait()
        load(lifted_all.at[2])

    def work(up):
        for b in range(2):
            here = slice(b * half, (b + 1) * half)
            h = dot(x[here, :], up[...], NN)
            activated, share = gelu_parts(h)
            low = activated.astype(LOW)
            act[0, here, :] = low
            slope[0, here, :] = gelu_slope(h, share).astype(LOW)
            activated = low.astype(WIDE)
            acc[0, here, :] += fold(activated)
            acc[1, here, :] += fold(activated * activated)

    steps = pl.num_programs(1)
    pl.when(u < steps // 2)(lambda: work(up_own))
    pl.when(u >= steps // 2)(lambda: work(up_got))

    @pl.when(u == steps - 1)
    def _():
        for n in range(2):
            sums[0, n : n + 1, :] = jnp.sum(acc[n].T, axis=0, keepdims=True)
        sums[0, 2:8, :] = jnp.zeros_like(sums[0, 2:8, :])

    @pl.when((j == 3) & (u == steps - 1))
    def _():
        for copy, onward in zip(far_c, last_c):
            copy.wait()
            onward.start()
        near_c.wait()
        for copy in last_c:
            copy.wait()


def in_halves(count, rows_first):
    near, far = (lambda u: jnp.minimum(u, count - 1)), (lambda u: jnp.maximum(u - count, 0))
    if rows_first:
        return [lambda j, u: (near(u), 0), lambda j, u: (far(u), 0)]
    return [lambda j, u: (0, near(u)), lambda j, u: (0, far(u))]


def ffn_up(lifted, cotangent, upward):
    rows, model = lifted.shape
    units = 2 * upward[0].shape[1]
    block = min(512, units // 2)
    count = units // 2 // block
    out = pl.BlockSpec((1, rows, block), lambda j, u: (j, 0, u))
    kept = jax.ShapeDtypeStruct((4, rows, units), LOW)
    others = jax.ShapeDtypeStruct((3, rows, model), LOW)
    return pl.pallas_call(
        ffn_up_kernel,
        grid=(4, 2 * count),
        in_specs=[ANYWHERE] * 2 + [pl.BlockSpec((model, block), at) for at in in_halves(count, False)],
        out_specs=[out] * 2 + [pl.BlockSpec((1, 8, rows), lambda j, u: (j, 0, 0))] + [ANYWHERE] * 2,
        out_shape=[kept] * 2 + [jax.ShapeDtypeStruct((4, 8, rows), WIDE)] + [others] * 2,
        scratch_shapes=[
            pltpu.VMEM((rows, model), LOW),
            pltpu.VMEM((2, rows, LANES), WIDE),
            pltpu.SemaphoreType.DMA((10,)),
            pltpu.SemaphoreType.DMA((10,)),
            pltpu.SemaphoreType.DMA,
        ],
        compiler_params=pltpu.CompilerParams(collective_id=2, has_side_effects=True, vmem_limit_bytes=56 << 20),
        cost_estimate=pl.CostEstimate(flops=80 * 10**9, bytes_accessed=100 << 20, transcendentals=0),
    )(lifted, cotangent, *upward)


def ffn_back_kernel(og, others, down_own, down_got, act, gain, squashed_grad, sums, x, acc, local):
    j, u = pl.program_id(0), pl.program_id(1)
    rows = x.shape[0]
    half = rows // 2

    @pl.when(u == 0)
    def _():
        acc[...] = jnp.zeros_like(acc)

    def load(source):
        copy = pltpu.make_async_copy(source, x, local)
        copy.start()
        copy.wait()

    pl.when((u == 0) & (j == 0))(lambda: load(og))
    pl.when((u == 0) & (j > 0))(lambda: load(others.at[jnp.maximum(j - 1, 0)]))

    def work(down):
        for b in range(2):
            here = slice(b * half, (b + 1) * half)
            s = dot(x[here, :], down[...], NT).astype(LOW)
            squashed_grad[0, here, :] = s
            scaled = s.astype(WIDE) * gain[...]
            acc[0, here, :] += fold(scaled)
            acc[1, here, :] += fold(scaled * act[0, here, :].astype(WIDE))

    steps = pl.num_programs(1)
    pl.when(u < steps // 2)(lambda: work(down_own))
    pl.when(u >= steps // 2)(lambda: work(down_got))

    @pl.when(u == steps - 1)
    def _():
        sums[0, 0:2, :] = jnp.zeros_like(sums[0, 0:2, :])
        for n in range(2):
            sums[0, n + 2 : n + 3, :] = jnp.sum(acc[n].T, axis=0, keepdims=True)
        sums[0, 4:8, :] = jnp.zeros_like(sums[0, 4:8, :])


def ffn_back(og, others, downward, act, gain):
    rows, model = og.shape
    units = act.shape[2]
    block = min(512, units // 2)
    count = units // 2 // block
    line = pl.BlockSpec((1, rows, block), lambda j, u: (j, 0, u))
    return pl.pallas_call(
        ffn_back_kernel,
        grid=(4, 2 * count),
        in_specs=[ANYWHERE] * 2
        + [pl.BlockSpec((block, model), at) for at in in_halves(count, True)]
        + [line, pl.BlockSpec((1, block), lambda j, u: (0, u))],
        out_specs=[line, pl.BlockSpec((1, 8, rows), lambda j, u: (j, 0, 0))],
        out_shape=[like(act), jax.ShapeDtypeStruct((4, 8, rows), WIDE)],
        scratch_shapes=[
            pltpu.VMEM((rows, model), LOW),
            pltpu.VMEM((2, rows, LANES), WIDE),
            pltpu.SemaphoreType.DMA,
        ],
        compiler_params=pltpu.CompilerParams(vmem_limit_bytes=56 << 20),
        cost_estimate=pl.CostEstimate(flops=60 * 10**9, bytes_accessed=100 << 20, transcendentals=0),
    )(og, others, *downward, act, gain)


def ffn_second_kernel(
    act,
    slope,
    squashed_grad,
    sums,
    gain,
    up_own,
    up_got,
    squashed,
    hidden_grad,
    kept,
    arrived,
    gains,
    acc,
    send_core,
    got_core,
    send_low,
    sent,
    got,
    *,
    hidden_width,
):
    n, u = pl.program_id(0), pl.program_id(1)
    steps = pl.num_programs(1)
    rows, block = act.shape[1:]
    half = rows // 2
    _, _, over_core, over_low, _ = partners()
    to_core = [remote(send_core.at[b], got_core.at[b], sent.at[b], got.at[b], over_core) for b in range(2)]
    to_low = remote(send_low, arrived, sent.at[2], got.at[2], over_low)

    @pl.when((n == 0) & (u == 0))
    def _():
        greet((over_core, over_low))
        gains[...] = jnp.zeros_like(gains)

    @pl.when(u == 0)
    def _():
        acc[...] = jnp.zeros_like(acc)

    columns = sums[0].T
    lanes = pl.ds(pl.multiple_of(u * block, block), block)

    def work(up):
        for b in range(2):
            here = slice(b * half, (b + 1) * half)
            centre = columns[here, 0:1] / hidden_width
            scale = lax.rsqrt(columns[here, 1:2] / hidden_width - centre * centre + EPS_NORM)
            mean_one = columns[here, 2:3] / hidden_width
            mean_two = scale * (columns[here, 3:4] - centre * columns[here, 2:3]) / hidden_width
            standard = (act[0, here, :].astype(WIDE) - centre) * scale
            squashed[0, here, :] = (standard * gain[...]).astype(LOW)
            s = squashed_grad[0, here, :].astype(WIDE)
            gains[0:1, lanes] += jnp.sum(s * standard, axis=0, keepdims=True)
            activated_grad = (s * gain[...] - mean_one - standard * mean_two) * scale
            grad = (activated_grad * slope[0, here, :].astype(WIDE)).astype(LOW)
            hidden_grad[0, here, :] = grad
            acc[here, :] += dot(grad, up[...], NT)

    pl.when(u < steps // 2)(lambda: work(up_own))
    pl.when(u >= steps // 2)(lambda: work(up_got))
    ends = u == steps - 1

    @pl.when(ends & (n == 0))
    def _():
        send_core[0] = acc[...].astype(LOW)
        to_core[0].start()

    @pl.when(ends & (n == 1))
    def _():
        to_core[0].wait()
        send_low[...] = (acc[...] + got_core[0].astype(WIDE)).astype(LOW)
        to_low.start()

    @pl.when(ends & (n == 2))
    def _():
        send_core[1] = acc[...].astype(LOW)
        to_core[1].start()

    @pl.when(ends & (n == 3))
    def _():
        to_core[1].wait()
        kept[...] = (acc[...] + got_core[1].astype(WIDE)).astype(LOW)
        to_low.wait()


def ffn_second(act, slope, squashed_grad, sums, gain, upward, hidden_width):
    _, rows, units = act.shape
    model = upward[0].shape[0]
    block = min(512, units // 2)
    count = units // 2 // block
    line = pl.BlockSpec((1, rows, block), lambda n, u: (3 - n, 0, u))
    piece = jax.ShapeDtypeStruct((rows, model), LOW)
    return pl.pallas_call(
        partial(ffn_second_kernel, hidden_width=hidden_width),
        grid=(4, 2 * count),
        in_specs=[line] * 3
        + [pl.BlockSpec((1, 8, rows), lambda n, u: (3 - n, 0, 0)), pl.BlockSpec((1, block), lambda n, u: (0, u))]
        + [pl.BlockSpec((model, block), at) for at in in_halves(count, False)],
        out_specs=[line] * 2
        + [pl.BlockSpec((rows, model), lambda n, u: (0, 0)), ANYWHERE, pl.BlockSpec((8, units), lambda n, u: (0, 0))],
        out_shape=[like(act)] * 2 + [piece] * 2 + [jax.ShapeDtypeStruct((8, units), WIDE)],
        scratch_shapes=[
            pltpu.VMEM((rows, model), WIDE),
            pltpu.VMEM((2, rows, model), LOW),
            pltpu.VMEM((2, rows, model), LOW),
            pltpu.VMEM((rows, model), LOW),
            pltpu.SemaphoreType.DMA((3,)),
            pltpu.SemaphoreType.DMA((3,)),
        ],
        compiler_params=pltpu.CompilerParams(collective_id=3, has_side_effects=True, vmem_limit_bytes=60 << 20),
        cost_estimate=pl.CostEstimate(flops=80 * 10**9, bytes_accessed=100 << 20, transcendentals=0),
    )(act, slope, squashed_grad, sums, gain, *upward)


def spread_kernel(ids, x, own, got, out, acc):
    step = pl.program_id(0)

    @pl.when(step == 0)
    def _():
        acc[...] = jnp.zeros_like(acc)

    def work(weight):
        acc[...] += dot(x[...], weight[...], NN)

    each_half(work, own, got)

    @pl.when(step == pl.num_programs(0) - 1)
    def _():
        out[...] = acc[...].astype(LOW)


def ffn_out(ids, x, j, downward):
    _, rows, units = x.shape
    model = downward[0].shape[1]
    block = min(512, units // 2)
    count = units // 2 // block
    return kernel_call(
        spread_kernel,
        (2 * count,),
        [pl.BlockSpec((pl.Squeezed(), rows, block), lambda u, ids: (j, 0, u))]
        + [pl.BlockSpec((block, model), at) for at in halves(count, True)],
        [pl.BlockSpec((rows, model), lambda u, ids: (0, 0))],
        [jax.ShapeDtypeStruct((rows, model), LOW)],
        [pltpu.VMEM((rows, model), WIDE)],
        2 * rows * model * units,
        2 * model * units + 2 * rows * (units + model),
        (ids, x, *downward),
    )[0]


def unproject_kernel(ids, *refs):
    grads, weights, out = refs[0:6], refs[6:14], refs[14]
    depth = weights[0].shape[1]
    for n in range(4):
        total = None
        for f in range(3):
            for half in range(2):
                part = dot(grads[3 * half + f][...], weights[4 * half + n][f], NT)
                total = part if total is None else total + part
        out[:, own_block(ids[1], n, depth)] = total.astype(LOW)


def unproject(ids, grads, heads):
    rows, width = grads[0].shape
    own, got = quarters(heads[0]), quarters(heads[1])
    model = heads[1].shape[1]
    block = min(256, rows)
    line = pl.BlockSpec((block, width), lambda b, ids: (b, 0))
    return kernel_call(
        unproject_kernel,
        (rows // block,),
        [line] * 6 + own[1] + got[1],
        [pl.BlockSpec((block, model), lambda b, ids: (b, 0))],
        [jax.ShapeDtypeStruct((rows, model), LOW)],
        [],
        12 * rows * model * width,
        12 * model * width + 2 * rows * (6 * width + model),
        (ids, *grads, *own[0], *got[0]),
    )[0]


def grad_kernel(ids, *refs, chunks, kinds, fixed):
    xs, ys = refs[:chunks], refs[chunks : chunks * (1 + kinds)]
    outs, turned = refs[chunks * (1 + kinds) : -1], refs[-1]
    step = pl.program_id(0)
    rows = xs[0].shape[0]

    def turn():
        for j in range(chunks):
            turned[:, j * rows : (j + 1) * rows] = xs[j][...].T

    if fixed:
        pl.when(step == 0)(turn)
    else:
        turn()
    for f in range(kinds):
        total = None
        for j in range(chunks):
            part = dot(turned[:, j * rows : (j + 1) * rows], ys[f * chunks + j][...], NN)
            total = part if total is None else total + part
        total = total.astype(LOW)
        if len(outs) == 1:
            outs[0][f] = total
        else:
            for k, out in enumerate(outs):

                @pl.when(step == k)
                def _():
                    out[f] = total


def weight_grad(ids, xs, ys, x_blocks, side=None, apart=False):
    chunks, kinds = len(xs), len(ys)
    rows, x_width = xs[0][0].shape[-2:]
    y_width = ys[0][0][0].shape[-1]

    def spec(piece, width, at, once):
        mode = {"pipeline_mode": ONCE} if once else {}
        if piece[1] is None:
            return pl.BlockSpec((rows, width), at, **mode)
        place = lambda b, ids, n=piece[1]: (n, *at(b, ids))
        return pl.BlockSpec((pl.Squeezed(), rows, width), place, **mode)

    shift = lambda b, ids: (0, ids[1] ^ b if apart else b)
    still = lambda b, ids: (0, side or 0)
    share = 1 if side is None else 2
    if x_blocks:
        x_width, y_width = x_width // 4, y_width // share
        x_at, y_at = (x_width, shift, False), (y_width, still, True)
        whole, out_at = (kinds, 4 * x_width, y_width), lambda b, ids: (0, b, 0)
    else:
        x_width, y_width = x_width // share, y_width // 4
        x_at, y_at = (x_width, still, True), (y_width, shift, False)
        whole, out_at = (kinds, x_width, 4 * y_width), lambda b, ids: (0, 0, b)
    out = (kinds, x_width, y_width)
    if apart:
        out_specs = [pl.BlockSpec(out, lambda b, ids: (0, 0, 0))] * 4
        out_shape = [jax.ShapeDtypeStruct(out, LOW)] * 4
    else:
        out_specs, out_shape = [pl.BlockSpec(out, out_at)], [jax.ShapeDtypeStruct(whole, LOW)]
    result = kernel_call(
        partial(grad_kernel, chunks=chunks, kinds=kinds, fixed=not x_blocks),
        (4,),
        [spec(x, *x_at) for x in xs] + [spec(y, *y_at) for group in ys for y in group],
        out_specs,
        out_shape,
        [pltpu.VMEM((x_width, rows * chunks), LOW)],
        8 * rows * chunks * x_width * y_width * kinds,
        2 * rows * chunks * (4 * x_width + 4 * y_width * kinds),
        (ids, *[x[0] for x in xs], *[y[0] for group in ys for y in group]),
    )
    return result if apart else result[0]


def flip(value, axis, mask):
    return lax.ppermute(value, axis, [(i, i ^ mask) for i in range(lax.axis_size(axis))])


def add_low(one, two):
    return (one.astype(WIDE) + two.astype(WIDE)).astype(LOW)


def sum_everywhere(value):
    for mask in (1, 2, 4):
        value = value + flip(value, "mp", mask)
    for mask in (1, 2):
        value = value + flip(value, "dp", mask)
    return value


MESH = pl.DeviceIdType.MESH
ANYWHERE = pl.BlockSpec(memory_space=pl.ANY)


def like(value):
    return jax.ShapeDtypeStruct(value.shape, value.dtype)


def partners():
    row, column = lax.axis_index("dp"), lax.axis_index("mp")
    over_x = (row + 1 - 2 * (row % 2), column)
    over_y = ((row + 2) % 4, column)
    over_core = (row, column + 1 - 2 * (column % 2))
    over_low = (row, column + 2 - 4 * ((column // 2) % 2))
    over_high = (row, (column + 4) % 8)
    return over_x, over_y, over_core, over_low, over_high


def greet(others):
    barrier = pltpu.get_barrier_semaphore()
    for other in others:
        pl.semaphore_signal(barrier, inc=1, device_id=other, device_id_type=MESH)
    pl.semaphore_wait(barrier, len(others))


class Sender:
    def __init__(self, sent, got):
        self.sent, self.got, self.count = sent, got, 0

    def __call__(self, source, target, device):
        copy = pltpu.make_async_remote_copy(
            src_ref=source,
            dst_ref=target,
            send_sem=self.sent.at[self.count],
            recv_sem=self.got.at[self.count],
            device_id=device,
            device_id_type=MESH,
        )
        self.count += 1
        copy.start()
        return copy


def open_kernel(text, head, text_got, head_x, head_y, head_far, sent, got):
    over_x, over_y, _, _, over_high = partners()
    greet((over_x, over_y, over_high))
    send = Sender(sent, got)
    half = head.shape[1] // 2
    upper, lower = pl.ds(0, half), pl.ds(half, half)
    copies = [send(text, text_got, over_high)]
    first = send(head.at[:, upper], head_x.at[:, upper], over_x)
    second = send(head.at[:, lower], head_y.at[:, lower], over_y)
    copies.append(send(head.at[:, lower], head_x.at[:, lower], over_x))
    copies.append(send(head.at[:, upper], head_y.at[:, upper], over_y))
    first.wait()
    copies.append(send(head_x.at[:, upper], head_far.at[:, upper], over_y))
    second.wait()
    copies.append(send(head_y.at[:, lower], head_far.at[:, lower], over_x))
    for copy in copies:
        copy.wait()


def open_exchange(text, head):
    return pl.pallas_call(
        open_kernel,
        in_specs=[ANYWHERE] * 2,
        out_specs=[ANYWHERE] * 4,
        out_shape=[like(text), like(head), like(head), like(head)],
        scratch_shapes=[pltpu.SemaphoreType.DMA((7,)), pltpu.SemaphoreType.DMA((7,))],
        compiler_params=pltpu.CompilerParams(collective_id=0, has_side_effects=True),
        cost_estimate=pl.CostEstimate(flops=0, bytes_accessed=100 << 20, transcendentals=0),
    )(text, head)


def normed_kernel(normed, head, outward, near, far, far_near, head_got, pieces, others, sent, got):
    over_x, over_y, over_core, over_low, over_high = partners()
    greet((over_x, over_y, over_core, over_low, over_high))
    send = Sender(sent, got)
    rows = normed.shape[0] // 2
    parts = [pl.ds(b * rows, rows) for b in range(2)]
    crossing = [send(normed.at[part], far.at[part], over_low) for part in parts]
    copies = [send(normed, near, over_core), send(head, head_got, over_high)]
    half = outward.shape[0] // 2
    upper, lower = pl.ds(0, half), pl.ds(half, half)
    first = send(outward.at[upper], pieces.at[0, upper], over_x)
    second = send(outward.at[lower], pieces.at[1, lower], over_y)
    later = [
        (send(outward.at[lower], pieces.at[0, lower], over_x), 0, lower),
        (send(outward.at[upper], pieces.at[1, upper], over_y), 1, upper),
    ]
    first.wait()
    later.append((send(pieces.at[0, upper], pieces.at[2, upper], over_y), 2, upper))
    copies.append(send(pieces.at[0, upper], others.at[0, upper], over_core))
    second.wait()
    later.append((send(pieces.at[1, lower], pieces.at[2, lower], over_x), 2, lower))
    copies.append(send(pieces.at[1, lower], others.at[1, lower], over_core))
    for copy, part in zip(crossing, parts):
        copy.wait()
        copies.append(send(far.at[part], far_near.at[part], over_core))
    for copy, n, part in later:
        copy.wait()
        copies.append(send(pieces.at[n, part], others.at[n, part], over_core))
    for copy in copies:
        copy.wait()


def normed_exchange(normed, head, outward):
    pieces = jax.ShapeDtypeStruct((3,) + outward.shape, LOW)
    return pl.pallas_call(
        normed_kernel,
        in_specs=[ANYWHERE] * 3,
        out_specs=[ANYWHERE] * 6,
        out_shape=[like(normed)] * 3 + [like(head), pieces, pieces],
        scratch_shapes=[pltpu.SemaphoreType.DMA((18,)), pltpu.SemaphoreType.DMA((18,))],
        compiler_params=pltpu.CompilerParams(collective_id=1, has_side_effects=True),
        cost_estimate=pl.CostEstimate(flops=0, bytes_accessed=100 << 20, transcendentals=0),
    )(normed, head, outward)


def rotary_tables(length):
    cosine, sine_part, exponent = xpos_tables(length, HEAD_DIM)
    out = []
    for polarity in (1.0, -1.0):
        factor = jnp.exp(polarity * exponent)
        near = (cosine * factor)[:, 0]
        far = (sine_part * factor)[:, 0]
        out.append(jnp.concatenate([near] * 4, axis=-1))
        out.append(jnp.concatenate([-far, far, -far, far], axis=-1))
    return out


def on_device_paired(
    text_states,
    image_states,
    image_offsets,
    image_counts,
    output_grad,
    head_master,
    head_moment,
    head_square,
    outward_master,
    outward_moment,
    outward_square,
    upward_master,
    upward_moment,
    upward_square,
    downward_master,
    downward_moment,
    downward_square,
    gains_master,
    gains_moment,
    gains_square,
):
    model_rank = lax.axis_index("mp")
    side = model_rank // 4
    rank = model_rank % 4
    place = lax.axis_index("dp")
    ids = jnp.stack([rank, place, side]).astype(jnp.int32)
    _, local_len, model_width = text_states.shape
    length = local_len * 8
    rows = 2 * local_len
    hidden_local = upward_master.shape[1]
    hidden_width = hidden_local * 8

    def pick(value, index):
        return lax.dynamic_index_in_dim(value, index, 0, keepdims=False)

    tables = rotary_tables(length)

    def both(kept, got):
        return jnp.where(side == 0, jnp.stack([kept, got]), jnp.stack([got, kept]))

    core = rank % 2
    half_width = model_width // 2
    text_out = pick(text_states, 1 - side)
    head_own = head_master.astype(LOW)
    upward_own = upward_master.astype(LOW)
    upward_weight = [lax.all_gather(upward_own, "dp", axis=0, tiled=True)]
    text_got, *head_parts = open_exchange(text_out, head_own)
    head_weight = [[head_own] + head_parts]
    downward_own = downward_master.astype(LOW)
    downward_weight = [lax.all_gather(downward_own, "dp", axis=1, tiled=True)]
    text = both(pick(text_states, side), text_got)

    gain_in = gains_master[None, :model_width]
    gain_ctx = gains_master[None, model_width : 2 * model_width]
    gain_mid = gains_master[None, 2 * model_width : 3 * model_width]
    hidden_start = 3 * model_width + model_rank * hidden_local
    other_start = 3 * model_width + (model_rank ^ 4) * hidden_local
    gain_hidden = jnp.concatenate(
        [
            lax.dynamic_slice_in_dim(gains_master, hidden_start, hidden_local),
            lax.dynamic_slice_in_dim(gains_master, other_start, hidden_local),
        ]
    )[None]

    offsets = pick(image_offsets, side)
    image_count = pick(image_counts, side)
    position = (
        jnp.arange(2, dtype=jnp.int32)[:, None] * (4 * local_len)
        + rank * local_len
        + jnp.arange(local_len, dtype=jnp.int32)[None, :]
    ).reshape(rows)
    slot_index = jnp.arange(offsets.shape[0], dtype=jnp.int32)
    inside = (
        (position[:, None] >= offsets[None, :])
        & (position[:, None] < offsets[None, :] + PATCH)
        & (slot_index[None, :] < image_count)
    )
    picked = jnp.sum(
        jnp.where(inside, slot_index[None, :] * PATCH + position[:, None] - offsets[None, :], 0), axis=-1
    )
    covered = jnp.any(inside, axis=-1)
    place_index = jnp.arange(image_states.shape[1], dtype=jnp.int32)
    chosen = (covered[:, None] & (picked[:, None] == place_index[None, :])).astype(LOW)
    images = jnp.dot(chosen, pick(image_states, side), preferred_element_type=WIDE).astype(LOW)
    merged = jnp.where(covered[:, None], images, text.reshape(rows, model_width))

    def turn_heads(pieces):
        return [pieces[0]] + [flip(pieces[j], "mp", j) for j in range(1, 4)]

    normed_own = layer_norm(merged.astype(WIDE), gain_in).astype(LOW)
    outward_low = outward_master.astype(LOW)
    outward_own, outward_other = (
        lax.dynamic_slice_in_dim(outward_low, n * half_width, half_width, 1) for n in (core, 1 - core)
    )
    near, far, far_near, head_got, *pieces = normed_exchange(normed_own, head_own, outward_own)
    outward_weight = [outward_own, pieces[0], outward_other, pieces[1]]
    normed = [normed_own, near, far, far_near]
    head_weight.append(lax.all_gather(head_got, "dp", axis=1, tiled=True))
    upward_weight.append(lax.all_gather(flip(upward_own, "mp", 4), "dp", axis=0, tiled=True))
    cotangent = both(pick(output_grad, side), flip(pick(output_grad, 1 - side), "mp", 4)).reshape(rows, model_width)
    downward_weight.append(lax.all_gather(flip(downward_own, "mp", 4), "dp", axis=1, tiled=True))

    queries, keys, values, contexts, logs, arrived = [], [], [], [], [], []
    for half in range(2):
        projected = [project(ids, chunk, head_weight[half], tables, j) for j, chunk in enumerate(normed)]
        for n, group in enumerate((queries, keys, values)):
            group.append([p[n] for p in projected])
        context, lse = attend(ids, queries[half], keys[half], values[half])
        contexts.append(context)
        logs.append(lse)
        arrived = arrived + turn_heads(context)
    context, mixed, middle, lifted_own = mid_forward(ids, arrived, merged, outward_weight, gain_ctx, gain_mid)
    act, slope, sums, lifted_others, cotangent_others = ffn_up(lifted_own, cotangent, upward_weight)
    squashed_grad, back_sums = ffn_back(cotangent, cotangent_others, downward_weight, act, gain_hidden)
    lifted = [(lifted_own, None)] + [(lifted_others, n) for n in range(3)]
    cotangents = [(cotangent, None)] + [(cotangent_others, n) for n in range(3)]
    sums = sums + back_sums
    others = [flip(sums, "mp", k) for k in range(1, 4)]
    sums = jnp.stack(
        [(sums[j] + others[0][j ^ 1]) + (others[1][j ^ 2] + others[2][j ^ 3]) for j in range(4)]
    )
    squashed, hidden_grad, lifted_kept, lifted_got, hidden_gains = ffn_second(
        act, slope, squashed_grad, sums, gain_hidden, upward_weight, hidden_width
    )

    def split(value):
        return [(value, n) for n in range(4)]

    def whole(values):
        return [(value, None) for value in values]

    down_grad = lax.psum_scatter(
        weight_grad(ids, split(squashed), [cotangents], False), "dp", scatter_dimension=2, tiled=True
    )[0]
    down_got = flip(down_grad[hidden_local:], "mp", 4)
    middle_grad, middle_low, own_grads, other_grads, mid_gains = mid_backward(
        ids, (lifted_kept, lifted_got), middle, cotangent, context, outward_weight, gain_mid, gain_ctx
    )
    context_heads = [turn_heads(own_grads), turn_heads(other_grads)]
    outward_blocks = [
        part[0] for part in weight_grad(ids, whole([mixed]), [whole([middle_low])], True, None, True)
    ]
    up_grad = lax.psum_scatter(
        weight_grad(ids, lifted, [split(hidden_grad)], True), "dp", scatter_dimension=1, tiled=True
    )[0]
    up_got = flip(up_grad[:, hidden_local:], "mp", 4)
    ffn_parts = [ffn_out(ids, squashed, j, downward_weight) for j in range(4)]

    def scatter_tokens(parts):
        passed = add_low(parts[2], flip(parts[3], "mp", 1))
        return add_low(parts[0], flip(parts[1], "mp", 1)), flip(passed, "mp", 2)

    def give_back(pair):
        got = flip(pick(pair, 1 - side).astype(LOW), "mp", 4)
        return both(pick(pair, side), got.astype(pair.dtype))

    ffn_kept, ffn_got = scatter_tokens(ffn_parts)
    output_rows = (middle + (ffn_kept.astype(WIDE) + ffn_got.astype(WIDE))).astype(LOW)
    layer_output = give_back(output_rows.reshape(2, local_len, model_width))

    def scatter_blocks(blocks, one, two):
        passed = add_low(blocks[3 - one], flip(blocks[3], "dp", one))
        return add_low(add_low(blocks[0], flip(blocks[one], "dp", one)), flip(passed, "dp", two))

    head_grads, head_sides = [None, None], [None, None]
    for half in (1, 0):
        head_grads[half] = attend_back(
            ids, queries[half], keys[half], values[half], context_heads[half], contexts[half], logs[half], tables
        )
        blocks = weight_grad(ids, whole(normed), [whole(g) for g in head_grads[half]], True, None, True)
        head_sides[half] = scatter_blocks(blocks, 1, 2)
    head_sum = head_sides[0].astype(WIDE) + flip(head_sides[1], "mp", 4).astype(WIDE)
    normed_parts = [None] * 4
    for j in (3, 2, 1, 0):
        pieces = [group[j] for half in head_grads for group in half]
        normed_parts[j] = unproject(ids, pieces, head_weight)
    normed_kept, normed_got = scatter_tokens(normed_parts)
    normed_grad = normed_kept.astype(WIDE) + normed_got.astype(WIDE)
    _, input_back = jax.vjp(layer_norm, merged.astype(WIDE), gain_in)
    merged_part, in_gain_grad = input_back(normed_grad)
    input_grad = give_back((middle_grad + merged_part).reshape(2, local_len, model_width))

    outward_blocks = [
        add_low(
            lax.dynamic_slice_in_dim(part, core * half_width, half_width, 1),
            flip(lax.dynamic_slice_in_dim(part, (1 - core) * half_width, half_width, 1), "mp", 1),
        )
        for part in outward_blocks
    ]
    outward_grad = scatter_blocks(outward_blocks, 2, 1)
    low_bit = (rank // 2) % 2
    for mask, bit in ((2, low_bit), (4, side)):
        size = outward_grad.shape[0] // 2
        outward_grad = add_low(
            lax.dynamic_slice_in_dim(outward_grad, bit * size, size, 0),
            flip(lax.dynamic_slice_in_dim(outward_grad, (1 - bit) * size, size, 0), "mp", mask),
        )
    for mask, bit, axis in ((4, side, 0), (2, low_bit, 0), (1, core, 1)):
        got = flip(outward_grad, "mp", mask)
        outward_grad = jnp.where(
            bit == 0,
            jnp.concatenate([outward_grad, got], axis=axis),
            jnp.concatenate([got, outward_grad], axis=axis),
        )
    outward_sum = outward_grad.astype(WIDE)

    down_sum = down_grad[:hidden_local].astype(WIDE) + down_got.astype(WIDE)
    up_sum = up_grad[:, :hidden_local].astype(WIDE) + up_got.astype(WIDE)
    moment_head, square_head, head_dir = adapt_step(head_sum, head_master, head_moment, head_square, DECAY_RATE)
    moment_outward, square_outward, outward_dir = adapt_step(
        outward_sum, outward_master, outward_moment, outward_square, DECAY_RATE
    )
    moment_upward, square_upward, upward_dir = adapt_step(
        up_sum, upward_master, upward_moment, upward_square, DECAY_RATE
    )
    moment_downward, square_downward, downward_dir = adapt_step(
        down_sum, downward_master, downward_moment, downward_square, DECAY_RATE
    )
    owner = (model_rank == 0).astype(WIDE)
    norm_early = sum_everywhere(
        jnp.concatenate(
            [
                pair_sums(outward_master, outward_dir) * owner,
                pair_sums(upward_master, upward_dir),
                pair_sums(downward_master, downward_dir),
            ],
            axis=0,
        )
    )
    head_part = jnp.stack(
        [jnp.sum(head_master * head_master, axis=(1, 2)), jnp.sum(head_dir * head_dir, axis=(1, 2))], axis=-1
    )
    hidden_gain = hidden_gains[0]
    gains_part = jnp.concatenate([in_gain_grad[0], mid_gains[1], mid_gains[0], jnp.zeros((hidden_width,), WIDE)])
    gains_part = lax.dynamic_update_slice(gains_part, hidden_gain[:hidden_local], (hidden_start,))
    gains_part = lax.dynamic_update_slice(gains_part, hidden_gain[hidden_local:], (other_start,))
    gains_sum = sum_everywhere(gains_part)
    head_norms = sum_everywhere(head_part)
    norm_sums = jnp.concatenate([head_norms, norm_early], axis=0)
    moment_gains, square_gains, gains_dir = adapt_step(gains_sum, gains_master, gains_moment, gains_square, 0.0)
    gains_sums = jnp.stack(
        [
            gain_segments(gains_master * gains_master, model_width),
            gain_segments(gains_dir * gains_dir, model_width),
        ],
        axis=-1,
    )
    updated_head = trust_move(
        head_master, head_dir, head_norms[:, 0][:, None, None], head_norms[:, 1][:, None, None]
    )
    updated_outward = trust_move(outward_master, outward_dir, norm_early[0, 0], norm_early[0, 1])
    updated_upward = trust_move(upward_master, upward_dir, norm_early[1, 0], norm_early[1, 1])
    updated_downward = trust_move(downward_master, downward_dir, norm_early[2, 0], norm_early[2, 1])
    updated_gains = trust_move(
        gains_master,
        gains_dir,
        gain_spread(gains_sums[:, 0], model_width, hidden_width),
        gain_spread(gains_sums[:, 1], model_width, hidden_width),
    )
    update_norms = jnp.sqrt(jnp.concatenate([norm_sums, gains_sums], axis=0))
    return (
        layer_output,
        input_grad,
        moment_head,
        square_head,
        updated_head,
        updated_head.astype(LOW),
        moment_outward,
        square_outward,
        updated_outward,
        updated_outward.astype(LOW),
        moment_upward,
        square_upward,
        updated_upward,
        updated_upward.astype(LOW),
        moment_downward,
        square_downward,
        updated_downward,
        updated_downward.astype(LOW),
        moment_gains,
        square_gains,
        updated_gains,
        update_norms,
    )


def solution(mesh):
    paired = mesh.shape["dp"] == 4 and mesh.shape["mp"] == 8
    return jax.shard_map(
        on_device_paired if paired else on_device_general,
        mesh=mesh,
        in_specs=(
            P("dp", "mp", None),
            P("dp", None, None),
            P("dp", None),
            P("dp"),
            P("dp", "mp", None),
            P(None, "dp", "mp"),
            P(None, "dp", "mp"),
            P(None, "dp", "mp"),
            P("dp", None),
            P("dp", None),
            P("dp", None),
            P("dp", "mp"),
            P("dp", "mp"),
            P("dp", "mp"),
            P("mp", "dp"),
            P("mp", "dp"),
            P("mp", "dp"),
            P(),
            P(),
            P(),
        ),
        out_specs=(
            P("dp", "mp", None),
            P("dp", "mp", None),
            P(None, "dp", "mp"),
            P(None, "dp", "mp"),
            P(None, "dp", "mp"),
            P(None, "dp", "mp"),
            P("dp", None),
            P("dp", None),
            P("dp", None),
            P("dp", None),
            P("dp", "mp"),
            P("dp", "mp"),
            P("dp", "mp"),
            P("dp", "mp"),
            P("mp", "dp"),
            P("mp", "dp"),
            P("mp", "dp"),
            P("mp", "dp"),
            P(),
            P(),
            P(),
            P(),
        ),
        check_vma=False,
    )
```

```python
from functools import partial

import jax
import jax.numpy as jnp
from jax import lax
from jax.experimental import pallas as pl
from jax.experimental.pallas import tpu as pltpu
from jax.sharding import PartitionSpec as P

HEAD_DIM = 64
FF = 8192
PATCH = 64
STEP = 10


EPS_NORM = 1e-05
BETA_ONE = 0.9
BETA_TWO = 0.999
EPS_ADAM = 1e-06
DECAY_RATE = 0.01
STEP_RATE = 0.5


def layer_norm(inputs, gain_vector):
    centre = jnp.mean(inputs, axis=-1, keepdims=True)
    shifted = inputs - centre
    spread = jnp.mean(shifted * shifted, axis=-1, keepdims=True)
    return shifted * lax.rsqrt(spread + EPS_NORM) * gain_vector


def xpos_tables(length, head_size):
    halfway = head_size // 2
    pair_index = jnp.arange(halfway, dtype=jnp.float32)
    angular = jnp.exp(-(2.0 * pair_index / head_size) * jnp.log(10000.0))
    zeta_base = (2.0 * pair_index + 0.4 * head_size) / (1.4 * head_size)
    position = jnp.arange(length, dtype=jnp.float32)[:, None, None]
    return (
        jnp.cos(position * angular),
        jnp.sin(position * angular),
        position / 512.0 * jnp.log(zeta_base),
    )


def rotate(inputs, tables, polarity):
    cosine, sine_part, exponent = tables
    halfway = inputs.shape[-1] // 2
    factor = jnp.exp(polarity * exponent)
    leading = inputs[..., :halfway]
    behind = inputs[..., halfway:]
    return jnp.concatenate(
        [
            (leading * cosine - behind * sine_part) * factor,
            (behind * cosine + leading * sine_part) * factor,
        ],
        axis=-1,
    )


def merge_images(text_rows, image_rows, offsets, image_count, position):
    slot_index = jnp.arange(offsets.shape[0], dtype=jnp.int32)
    inside = (
        (position[:, None] >= offsets[None, :])
        & (position[:, None] < offsets[None, :] + PATCH)
        & (slot_index[None, :] < image_count)
    )
    picked = jnp.sum(
        jnp.where(inside, slot_index[None, :] * PATCH + position[:, None] - offsets[None, :], 0),
        axis=-1,
    )
    chosen = jnp.take(image_rows, picked, axis=0)
    covered = jnp.any(inside, axis=-1)
    return jnp.where(covered[:, None], chosen, text_rows)


def adapt_step(gradient, master, moment, square, decay_rate):
    moment_new = BETA_ONE * moment + (1.0 - BETA_ONE) * gradient
    square_new = BETA_TWO * square + (1.0 - BETA_TWO) * gradient * gradient
    direction = (
        moment_new
        / (1.0 - BETA_ONE**STEP)
        / (jnp.sqrt(square_new / (1.0 - BETA_TWO**STEP)) + EPS_ADAM)
        + decay_rate * master
    )
    return (moment_new, square_new, direction)


def trust_move(master, direction, weight_sum, update_sum):
    return master - STEP_RATE * jnp.sqrt(weight_sum) / (jnp.sqrt(update_sum) + EPS_ADAM) * direction


def gain_segments(entries, model_width):
    return jnp.stack(
        [
            jnp.sum(entries[:model_width]),
            jnp.sum(entries[model_width : 2 * model_width]),
            jnp.sum(entries[2 * model_width : 3 * model_width]),
            jnp.sum(entries[3 * model_width :]),
        ]
    )


def gain_spread(sums, model_width, hidden_width):
    return jnp.concatenate(
        [
            jnp.broadcast_to(sums[0], (model_width,)),
            jnp.broadcast_to(sums[1], (model_width,)),
            jnp.broadcast_to(sums[2], (model_width,)),
            jnp.broadcast_to(sums[3], (hidden_width,)),
        ]
    )


def pair_sums(master, direction):
    return jnp.stack([jnp.sum(master * master), jnp.sum(direction * direction)])[None]


def on_device_general(
    text_states,
    image_states,
    image_offsets,
    image_counts,
    output_grad,
    head_master,
    head_moment,
    head_square,
    outward_master,
    outward_moment,
    outward_square,
    upward_master,
    upward_moment,
    upward_square,
    downward_master,
    downward_moment,
    downward_square,
    gains_master,
    gains_moment,
    gains_square,
):
    groups = lax.axis_size("mp")
    model_rank = lax.axis_index("mp")
    seq_count, local_len, model_width = text_states.shape
    length = local_len * groups
    hidden_local = upward_master.shape[1]
    heads_local = head_master.shape[2] // HEAD_DIM
    tables = xpos_tables(length, HEAD_DIM)
    position = model_rank * local_len + jnp.arange(local_len, dtype=jnp.int32)
    merged = jax.vmap(
        lambda text_rows, image_rows, offsets, image_count: merge_images(
            text_rows, image_rows, offsets, image_count, position
        )
    )(text_states, image_states, image_offsets, image_counts).astype(jnp.float32)
    gain_in = gains_master[:model_width]
    gain_ctx = gains_master[model_width : 2 * model_width]
    gain_mid = gains_master[2 * model_width : 3 * model_width]
    hidden_start = 3 * model_width + model_rank * hidden_local
    gain_hidden = lax.dynamic_slice_in_dim(gains_master, hidden_start, hidden_local)
    head_weight_whole, outward_weight_whole, upward_weight_whole, down_weight_whole = (
        lax.all_gather(head_master.astype(jnp.bfloat16), "dp", axis=1, tiled=True),
        lax.all_gather(outward_master.astype(jnp.bfloat16), "dp", axis=0, tiled=True),
        lax.all_gather(upward_master.astype(jnp.bfloat16), "dp", axis=0, tiled=True),
        lax.all_gather(downward_master.astype(jnp.bfloat16), "dp", axis=1, tiled=True),
    )
    normed_low = layer_norm(merged, gain_in).astype(jnp.bfloat16)
    normed_rows_full, cotangent_rows_full = (
        lax.all_gather(normed_low, "mp", axis=1, tiled=True),
        lax.all_gather(output_grad, "mp", axis=1, tiled=True),
    )
    projected = jnp.einsum(
        "hvg,bga->bhva", normed_rows_full, head_weight_whole, preferred_element_type=jnp.float32
    )
    shaped = projected.reshape(3, seq_count, length, heads_local, HEAD_DIM)
    queries = rotate(shaped[0], tables, 1.0).astype(jnp.bfloat16)
    key_rows = rotate(shaped[1], tables, -1.0).astype(jnp.bfloat16)
    values = shaped[2].astype(jnp.bfloat16)
    block_len = min(512, length)
    block_count = length // block_len
    starts = jnp.arange(block_count, dtype=jnp.int32) * block_len
    key_place = jnp.arange(length, dtype=jnp.int32)

    def block_scores(query_block, start):
        scores = (
            jnp.einsum("sqhd,skhd->shqk", query_block, key_rows, preferred_element_type=jnp.float32)
            * 0.125
        )
        allowed = key_place[None, :] <= (start + jnp.arange(block_len, dtype=jnp.int32))[:, None]
        return jnp.where(allowed, scores, -1e30)

    def forward_block(start):
        query_block = lax.dynamic_slice_in_dim(queries, start, block_len, 1)
        scores = block_scores(query_block, start)
        highest = jnp.max(scores, axis=-1, keepdims=True)
        exponent = jnp.exp(scores - highest)
        total = jnp.sum(exponent, axis=-1, keepdims=True)
        attention = exponent / total
        context_block = jnp.einsum(
            "shqk,skhd->sqhd",
            attention.astype(jnp.bfloat16),
            values,
            preferred_element_type=jnp.float32,
        )
        return (context_block, highest[..., 0] + jnp.log(total[..., 0]))

    context_blocks, log_sums = lax.map(forward_block, starts)
    context = jnp.transpose(context_blocks, (1, 0, 2, 3, 4)).reshape(
        seq_count, length, heads_local * HEAD_DIM
    )
    context_rows = lax.all_to_all(
        context.astype(jnp.bfloat16), "mp", split_axis=1, concat_axis=2, tiled=True
    )
    context_in = context_rows.astype(jnp.float32)
    mixed_half_precision = layer_norm(context_in, gain_ctx).astype(jnp.bfloat16)
    middle = merged + jnp.einsum(
        "ymq,qc->ymc",
        mixed_half_precision,
        outward_weight_whole,
        preferred_element_type=jnp.float32,
    )
    lifted_low = layer_norm(middle, gain_mid).astype(jnp.bfloat16)
    lifted_rows_full = lax.all_gather(lifted_low, "mp", axis=1, tiled=True)
    hidden_rows = jnp.einsum(
        "orb,bg->org", lifted_rows_full, upward_weight_whole, preferred_element_type=jnp.float32
    )
    activated = jax.nn.gelu(hidden_rows, approximate=False)
    first_sum, second_sum = lax.psum(
        (jnp.sum(activated, axis=-1), jnp.sum(activated * activated, axis=-1)), "mp"
    )
    centre = first_sum / FF
    scale_inv = lax.rsqrt(second_sum / FF - centre * centre + EPS_NORM)[..., None]
    standard = (activated - centre[..., None]) * scale_inv
    squashed_half_precision = (standard * gain_hidden).astype(jnp.bfloat16)
    ffn_part = jnp.einsum(
        "wxp,pk->wxk",
        squashed_half_precision,
        down_weight_whole,
        preferred_element_type=jnp.float32,
    )
    ffn_rows = lax.psum_scatter(
        ffn_part.astype(jnp.bfloat16), "mp", scatter_dimension=1, tiled=True
    ).astype(jnp.float32)
    layer_output = (middle + ffn_rows).astype(jnp.bfloat16)
    down_grad = jnp.einsum(
        "uxy,uxo->yo",
        squashed_half_precision,
        cotangent_rows_full,
        preferred_element_type=jnp.float32,
    )
    squashed_grad = jnp.einsum(
        "yxr,ur->yxu", cotangent_rows_full, down_weight_whole, preferred_element_type=jnp.float32
    )
    hidden_gain_grad = jnp.sum(squashed_grad * standard, axis=(0, 1))
    scaled_grad = squashed_grad * gain_hidden
    mean_one, mean_two = (
        lax.psum(jnp.sum(scaled_grad, axis=-1).astype(jnp.bfloat16), "mp").astype(jnp.float32),
        lax.psum(jnp.sum(scaled_grad * standard, axis=-1).astype(jnp.bfloat16), "mp").astype(
            jnp.float32
        ),
    )
    activated_grad = (
        scaled_grad - mean_one[..., None] / FF - standard * (mean_two[..., None] / FF)
    ) * scale_inv
    gelu_out, gelu_back = jax.vjp(partial(jax.nn.gelu, approximate=False), hidden_rows)
    hidden_rows_grad = gelu_back(activated_grad)[0].astype(jnp.bfloat16)
    upward_gradient = jnp.einsum(
        "gki,gkt->it", lifted_rows_full, hidden_rows_grad, preferred_element_type=jnp.float32
    )
    lifted_part = jnp.einsum(
        "eiw,mw->eim", hidden_rows_grad, upward_weight_whole, preferred_element_type=jnp.float32
    )
    lifted_grad = lax.psum_scatter(lifted_part, "mp", scatter_dimension=1, tiled=True)
    norm_out, middle_back = jax.vjp(layer_norm, middle, gain_mid)
    middle_part, mid_gain_grad = middle_back(lifted_grad)
    middle_grad = output_grad.astype(jnp.float32) + middle_part
    middle_half_precision = middle_grad.astype(jnp.bfloat16)
    outward_part = jnp.einsum(
        "hyk,hyo->ko",
        mixed_half_precision,
        middle_half_precision,
        preferred_element_type=jnp.float32,
    )
    mixed_grad = jnp.einsum(
        "hox,kx->hok",
        middle_half_precision,
        outward_weight_whole,
        preferred_element_type=jnp.float32,
    )
    context_out, context_back = jax.vjp(layer_norm, context_in, gain_ctx)
    context_grad, ctx_gain_grad = context_back(mixed_grad)
    context_heads = lax.all_to_all(
        context_grad.astype(jnp.bfloat16), "mp", split_axis=2, concat_axis=1, tiled=True
    )
    grad_heads = context_heads.reshape(seq_count, length, heads_local, HEAD_DIM)

    def backward_block(totals, inputs):
        key_total, value_total = totals
        start, log_block = inputs
        query_block = lax.dynamic_slice_in_dim(queries, start, block_len, 1)
        grad_block = lax.dynamic_slice_in_dim(grad_heads, start, block_len, 1)
        scores = block_scores(query_block, start)
        attention = jnp.exp(scores - log_block[..., None])
        prob_grad = jnp.einsum(
            "sqhd,skhd->shqk", grad_block, values, preferred_element_type=jnp.float32
        )
        row_dot = jnp.sum(attention * prob_grad, axis=-1, keepdims=True)
        score_low = (attention * (prob_grad - row_dot)).astype(jnp.bfloat16)
        query_turned = (
            jnp.einsum("shqk,skhd->sqhd", score_low, key_rows, preferred_element_type=jnp.float32)
            * 0.125
        )
        key_total = (
            key_total
            + jnp.einsum(
                "shqk,sqhd->skhd", score_low, query_block, preferred_element_type=jnp.float32
            )
            * 0.125
        )
        value_total = value_total + jnp.einsum(
            "shqk,sqhd->skhd",
            attention.astype(jnp.bfloat16),
            grad_block,
            preferred_element_type=jnp.float32,
        )
        return ((key_total, value_total), query_turned)

    zero_heads = jnp.zeros((seq_count, length, heads_local, HEAD_DIM), jnp.float32)
    (key_turned, value_grad), query_blocks = lax.scan(
        backward_block, (zero_heads, zero_heads), (starts, log_sums)
    )
    query_turned = jnp.transpose(query_blocks, (1, 0, 2, 3, 4)).reshape(
        seq_count, length, heads_local, HEAD_DIM
    )
    query_out, query_back = jax.vjp(lambda inputs: rotate(inputs, tables, 1.0), shaped[0])
    key_out, key_back = jax.vjp(lambda inputs: rotate(inputs, tables, -1.0), shaped[1])
    projection_gradient = (
        jnp.stack([query_back(query_turned)[0], key_back(key_turned)[0], value_grad])
        .astype(jnp.bfloat16)
        .reshape(3, seq_count, length, heads_local * HEAD_DIM)
    )
    head_grad = jnp.einsum(
        "fbn,ufbj->unj", normed_rows_full, projection_gradient, preferred_element_type=jnp.float32
    )
    normed_part = jnp.einsum(
        "acqr,aur->cqu", projection_gradient, head_weight_whole, preferred_element_type=jnp.float32
    )
    normed_grad = lax.psum_scatter(
        normed_part.astype(jnp.bfloat16), "mp", scatter_dimension=1, tiled=True
    ).astype(jnp.float32)
    input_out, input_back = jax.vjp(layer_norm, merged, gain_in)
    merged_part, in_gain_grad = input_back(normed_grad)
    input_grad = middle_grad + merged_part
    head_sum, outward_sum, upward_sum, downward_sum = (
        lax.psum_scatter(
            head_grad.astype(jnp.bfloat16), "dp", scatter_dimension=1, tiled=True
        ).astype(jnp.float32),
        lax.psum_scatter(
            outward_part.astype(jnp.bfloat16), "dp", scatter_dimension=0, tiled=True
        ).astype(jnp.float32),
        lax.psum_scatter(
            upward_gradient.astype(jnp.bfloat16), "dp", scatter_dimension=0, tiled=True
        ).astype(jnp.float32),
        lax.psum_scatter(
            down_grad.astype(jnp.bfloat16), "dp", scatter_dimension=1, tiled=True
        ).astype(jnp.float32),
    )
    outward_sum = lax.psum(outward_sum.astype(jnp.bfloat16), "mp").astype(jnp.float32)
    moment_head, square_head, head_dir = adapt_step(
        head_sum, head_master, head_moment, head_square, DECAY_RATE
    )
    moment_outward, square_outward, outward_dir = adapt_step(
        outward_sum, outward_master, outward_moment, outward_square, DECAY_RATE
    )
    moment_upward, square_upward, upward_dir = adapt_step(
        upward_sum, upward_master, upward_moment, upward_square, DECAY_RATE
    )
    moment_downward, square_downward, downward_dir = adapt_step(
        downward_sum, downward_master, downward_moment, downward_square, DECAY_RATE
    )
    owner = (model_rank == 0).astype(jnp.float32)
    head_part = jnp.stack(
        [
            jnp.sum(head_master * head_master, axis=(1, 2)),
            jnp.sum(head_dir * head_dir, axis=(1, 2)),
        ],
        axis=-1,
    )
    norm_part = jnp.concatenate(
        [
            head_part,
            pair_sums(outward_master, outward_dir) * owner,
            pair_sums(upward_master, upward_dir),
            pair_sums(downward_master, downward_dir),
        ],
        axis=0,
    )
    gains_part = jnp.concatenate(
        [in_gain_grad, ctx_gain_grad, mid_gain_grad, jnp.zeros((FF,), jnp.float32)]
    )
    gains_part = lax.dynamic_update_slice(gains_part, hidden_gain_grad, (hidden_start,))
    gains_sum, norm_sums = lax.psum((gains_part, norm_part), ("dp", "mp"))
    moment_gains, square_gains, gains_dir = adapt_step(
        gains_sum, gains_master, gains_moment, gains_square, 0.0
    )
    gains_sums = jnp.stack(
        [
            gain_segments(gains_master * gains_master, model_width),
            gain_segments(gains_dir * gains_dir, model_width),
        ],
        axis=-1,
    )
    updated_head = trust_move(
        head_master, head_dir, norm_sums[0:3, 0][:, None, None], norm_sums[0:3, 1][:, None, None]
    )
    updated_outward = trust_move(outward_master, outward_dir, norm_sums[3, 0], norm_sums[3, 1])
    updated_upward = trust_move(upward_master, upward_dir, norm_sums[4, 0], norm_sums[4, 1])
    updated_downward = trust_move(downward_master, downward_dir, norm_sums[5, 0], norm_sums[5, 1])
    updated_gains = trust_move(
        gains_master,
        gains_dir,
        gain_spread(gains_sums[:, 0], model_width, FF),
        gain_spread(gains_sums[:, 1], model_width, FF),
    )
    update_norms = jnp.sqrt(jnp.concatenate([norm_sums, gains_sums], axis=0))
    return (
        layer_output,
        input_grad,
        moment_head,
        square_head,
        updated_head,
        updated_head.astype(jnp.bfloat16),
        moment_outward,
        square_outward,
        updated_outward,
        updated_outward.astype(jnp.bfloat16),
        moment_upward,
        square_upward,
        updated_upward,
        updated_upward.astype(jnp.bfloat16),
        moment_downward,
        square_downward,
        updated_downward,
        updated_downward.astype(jnp.bfloat16),
        moment_gains,
        square_gains,
        updated_gains,
        update_norms,
    )


SHARE = 0.3
LOG2E = 1.4426950408889634
LANES = 128
NT = (((1,), (1,)), ((), ()))
NN = (((1,), (0,)), ((), ()))
LOW = jnp.bfloat16
WIDE = jnp.float32
ONCE = pl.Buffered(1)
MESH = pl.DeviceIdType.MESH
ANYWHERE = pl.BlockSpec(memory_space=pl.ANY)


def like(value):
    return jax.ShapeDtypeStruct(value.shape, value.dtype)


def dot(left, right, dims):
    return lax.dot_general(left, right, dims, preferred_element_type=WIDE)


def kernel_call(body, grid, in_specs, out_specs, out_shape, scratch, flops, moved, operands, done=(), carry=()):
    count, extra, outs = len(operands), len(done) + len(carry), len(out_specs)

    def whole(*refs):
        inner = refs[count + extra :]
        body(*refs[:count], *inner[:outs], *inner[outs + len(carry) :])

    return pl.pallas_call(
        whole,
        grid_spec=pltpu.PrefetchScalarGridSpec(
            num_scalar_prefetch=1,
            grid=grid,
            in_specs=list(in_specs) + [ANYWHERE] * extra,
            out_specs=list(out_specs) + [ANYWHERE] * len(carry),
            scratch_shapes=scratch,
        ),
        out_shape=list(out_shape) + [like(value) for value in carry],
        input_output_aliases={count + len(done) + n: outs + n for n in range(len(carry))},
        compiler_params=pltpu.CompilerParams(vmem_limit_bytes=56 << 20),
        cost_estimate=pl.CostEstimate(flops=int(flops * SHARE), bytes_accessed=int(moved * SHARE), transcendentals=0),
    )(*operands, *done, *carry)


def mate(rank, j):
    return (rank, rank + 1 - 2 * (rank % 2), (rank + 2) % 4, 3 - rank)[j]


def own_rows(sub, rank, j, b):
    return pl.ds(pl.multiple_of(b * 4 * sub + mate(rank, j) * sub, sub), sub)


def own_block(place, k, width):
    return pl.ds(pl.multiple_of((place ^ k) * width, width), width)


def swap_halves(block):
    low = lax.broadcasted_iota(jnp.int32, (1, LANES), 1) % HEAD_DIM < HEAD_DIM // 2
    return jnp.where(low, pltpu.roll(block, LANES - HEAD_DIM // 2, 1), pltpu.roll(block, HEAD_DIM // 2, 1))


def project_kernel(ids, x, w0, w1, w2, w3, cq, sq, ck, sk, q, k, v):
    depth = w0.shape[1]
    width = w0.shape[2]
    for f, (out, c, s) in enumerate(((q, cq, sq), (k, ck, sk), (v, None, None))):
        total = None
        for n, w in enumerate((w0, w1, w2, w3)):
            part = dot(x[:, own_block(ids[1], n, depth)], w[f], NN)
            total = part if total is None else total + part
        for p in range(width // LANES):
            here = slice(p * LANES, (p + 1) * LANES)
            block = total[:, here]
            if c is not None:
                block = block * c[...] + swap_halves(block) * s[...]
            out[:, here] = block.astype(LOW)


def quarters(weight):
    if isinstance(weight, list):
        spec = pl.BlockSpec(weight[0].shape, lambda b, ids: (0, 0, 0), pipeline_mode=ONCE)
        return weight, [spec] * 4
    kinds, model, width = weight.shape
    return [weight] * 4, [
        pl.BlockSpec((kinds, model // 4, width), partial(lambda n, b, ids: (0, ids[1] ^ n, 0), n), pipeline_mode=ONCE)
        for n in range(4)
    ]


def project(ids, x, weight, tables, j):
    rows, model = x.shape
    sub = rows // 2
    weights, specs = quarters(weight)
    width = weights[0].shape[2]
    table = pl.BlockSpec((sub, LANES), lambda b, ids: (b * 4 + (ids[0] ^ j), 0))
    out = pl.BlockSpec((sub, width), lambda b, ids: (b, 0))
    return kernel_call(
        project_kernel,
        (2,),
        [pl.BlockSpec((sub, model), lambda b, ids: (b, 0))] + specs + [table] * 4,
        [out] * 3,
        [jax.ShapeDtypeStruct((rows, width), LOW)] * 3,
        [],
        6 * rows * model * width,
        6 * model * width + 8 * rows * model,
        (ids, x, *weights, *tables),
    )


def attend_kernel(ids, *refs, bq, bk):
    q_, k_, v_, o_, lse_ref = refs[0:4], refs[4:8], refs[8:12], refs[12:16], refs[16]
    qs, ks, vt, os = refs[17:]
    rank = ids[0]
    length = qs.shape[0]
    sub = q_[0].shape[0] // 2
    for j in range(4):
        for b in range(2):
            rows = own_rows(sub, rank, j, b)
            here = slice(b * sub, (b + 1) * sub)
            qs[rows, :] = q_[j][here, :]
            ks[rows, :] = k_[j][here, :]
            vt[:, rows] = v_[j][here, :].T
    first = lax.broadcasted_iota(jnp.int32, (1, LANES), 1) < HEAD_DIM
    ratio = bq // bk

    def q_block(i, _):
        here = pl.ds(pl.multiple_of(i * bq, bq), bq)
        q = qs[here, :]
        zero = jnp.zeros_like(q)
        parted = (jnp.where(first, q, zero), jnp.where(first, zero, q))

        def step(j, carry, diagonal):
            at = pl.multiple_of(j * bk, bk)
            k = ks[pl.ds(at, bk), :]
            out = []
            for h in range(2):
                highest, total, sums = carry[h]
                scores = dot(k, parted[h], NT) * (0.125 * LOG2E)
                if diagonal is not None:
                    key = diagonal * bk + lax.broadcasted_iota(jnp.int32, (bk, bq), 0)
                    scores = jnp.where(key <= lax.broadcasted_iota(jnp.int32, (bk, bq), 1), scores, -1e30)
                new = jnp.maximum(highest, jnp.max(scores, axis=0, keepdims=True))
                probs = jnp.exp2(scores - new)
                scale = jnp.exp2(highest - new)
                total = total * scale + jnp.sum(probs, axis=0, keepdims=True)
                rows = vt[h * HEAD_DIM : (h + 1) * HEAD_DIM, pl.ds(at, bk)]
                out.append((new, total, sums * scale + dot(rows, probs.astype(LOW), NN)))
            return tuple(out)

        start = tuple(
            (jnp.full((1, bq), -1e30, WIDE), jnp.zeros((1, bq), WIDE), jnp.zeros((HEAD_DIM, bq), WIDE))
            for _ in range(2)
        )
        carry = lax.fori_loop(0, i * ratio, lambda j, c: step(j, c, None), start)
        for d in range(ratio):
            carry = step(i * ratio + d, carry, d)
        turned = jnp.concatenate([carry[h][2] / carry[h][1] for h in range(2)], axis=0)
        os[here, :] = turned.T.astype(LOW)
        for h in range(2):
            lse_ref[0, h : h + 1, here] = carry[h][0] + jnp.log2(carry[h][1])
        return 0

    lax.fori_loop(0, length // bq, q_block, 0)
    for j in range(4):
        for b in range(2):
            o_[j][b * sub : (b + 1) * sub, :] = os[own_rows(sub, rank, j, b), :]


def attend(ids, queries, keys, values, done=(), carry=()):
    rows, width = queries[0].shape
    length, pairs = rows * 4, width // LANES
    chunk = pl.BlockSpec((rows, LANES), lambda p, ids: (0, p))
    low = pltpu.VMEM((length, LANES), LOW)
    result = kernel_call(
        partial(attend_kernel, bq=min(1024, length), bk=min(512, length)),
        (pairs,),
        [chunk] * 12,
        [chunk] * 4 + [pl.BlockSpec((1, 2, length), lambda p, ids: (p, 0, 0))],
        [jax.ShapeDtypeStruct((rows, width), LOW)] * 4 + [jax.ShapeDtypeStruct((pairs, 2, length), WIDE)],
        [low, low, pltpu.VMEM((LANES, length), LOW), low],
        40e9,
        10e6,
        (ids, *queries, *keys, *values),
        done,
        carry,
    )
    return result[:4], result[4], *result[5:]


def attend_back_kernel(*refs, bq, bk):
    q_, k_, v_, d_, o_ = refs[0:4], refs[4:8], refs[8:12], refs[12:16], refs[16:20]
    lse_ref, cq, sq, ck, sk, away = refs[20:26]
    dq_, dk_, dv_, back = refs[-15:-11]
    qs, ks, vs, ds, kt, dqt, dks, dvs, delta, sent, got = refs[-11:]
    over_high = partners()[4]
    crossing = remote(away, back, sent, got, over_high)

    @pl.when(pl.program_id(0) == 0)
    def _():
        greet((over_high,))
        crossing.start()

    rank = lax.axis_index("mp") % 4
    length = qs.shape[0]
    sub = q_[0].shape[0] // 2
    for j in range(4):
        for b in range(2):
            rows = own_rows(sub, rank, j, b)
            here = slice(b * sub, (b + 1) * sub)
            qs[rows, :] = q_[j][here, :]
            ks[rows, :] = k_[j][here, :]
            kt[:, rows] = k_[j][here, :].T
            vs[rows, :] = v_[j][here, :]
            ds[rows, :] = d_[j][here, :]
            product = (d_[j][here, :].astype(WIDE) * o_[j][here, :].astype(WIDE)).T
            delta[0:1, rows] = jnp.sum(product[:HEAD_DIM], axis=0, keepdims=True)
            delta[1:2, rows] = jnp.sum(product[HEAD_DIM:], axis=0, keepdims=True)
    first = lax.broadcasted_iota(jnp.int32, (1, LANES), 1) < HEAD_DIM
    dqt[...] = jnp.zeros_like(dqt)

    def k_block(j, _):
        at = pl.ds(pl.multiple_of(j * bk, bk), bk)
        k = ks[at, :]
        v = vs[at, :]

        def step(i, carry, diagonal):
            dk, dv = carry
            here = pl.ds(pl.multiple_of(i * bq, bq), bq)
            q, do = qs[here, :], ds[here, :]
            zero = jnp.zeros_like(q)
            for h in range(2):
                lanes = slice(h * HEAD_DIM, (h + 1) * HEAD_DIM)
                q_own = jnp.where(first, q, zero) if h == 0 else jnp.where(first, zero, q)
                do_own = jnp.where(first, do, zero) if h == 0 else jnp.where(first, zero, do)
                scores = dot(k, q_own, NT) * (0.125 * LOG2E) - lse_ref[0, h : h + 1, here]
                if diagonal:
                    key = lax.broadcasted_iota(jnp.int32, (bk, bq), 0)
                    scores = jnp.where(key <= lax.broadcasted_iota(jnp.int32, (bk, bq), 1), scores, -1e30)
                probs = jnp.exp2(scores)
                prob_grad = dot(v, do_own, NT)
                grad = (probs * (prob_grad - delta[h : h + 1, here])).astype(LOW)
                dv = dv + dot(probs.astype(LOW), do_own, NN)
                dk = dk + dot(grad, q_own, NN)
                dqt[lanes, here] += dot(kt[lanes, at], grad, NN)
            return dk, dv

        zeros = jnp.zeros((bk, LANES), WIDE)
        carry = step(j, (zeros, zeros), True)
        dk, dv = lax.fori_loop(j + 1, length // bq, lambda i, c: step(i, c, False), carry)
        dks[at, :] = dk * 0.125
        dvs[at, :] = dv.astype(LOW)
        return 0

    lax.fori_loop(0, length // bk, k_block, 0)
    for j in range(4):
        for b in range(2):
            rows = own_rows(sub, rank, j, b)
            here = slice(b * sub, (b + 1) * sub)
            query_grad = dqt[:, rows].T * 0.125
            dq_[j, here, :] = (query_grad * cq[rows, :] - swap_halves(query_grad) * sq[rows, :]).astype(LOW)
            key_grad = dks[rows, :]
            dk_[j, here, :] = (key_grad * ck[rows, :] - swap_halves(key_grad) * sk[rows, :]).astype(LOW)
            dv_[j, here, :] = dvs[rows, :]

    @pl.when(pl.program_id(0) == pl.num_programs(0) - 1)
    def _():
        crossing.wait()


def attend_back(queries, keys, values, cotangents, contexts, lse, tables, away, number, done):
    rows, width = queries[0].shape
    length, pairs = rows * 4, width // LANES
    chunk = pl.BlockSpec((rows, LANES), lambda p: (0, p))
    whole = pl.BlockSpec((length, LANES), lambda p: (0, 0), pipeline_mode=ONCE)
    low = pltpu.VMEM((length, LANES), LOW)
    block = min(512, length)
    return pl.pallas_call(
        partial(attend_back_kernel, bq=block, bk=block),
        grid=(pairs,),
        in_specs=[chunk] * 20 + [pl.BlockSpec((1, 2, length), lambda p: (p, 0, 0))]
        + [whole] * 4
        + [ANYWHERE] * (1 + len(done)),
        out_specs=[pl.BlockSpec((4, rows, LANES), lambda p: (0, 0, p))] * 3 + [ANYWHERE],
        out_shape=[jax.ShapeDtypeStruct((4, rows, width), LOW)] * 3 + [like(away)],
        scratch_shapes=[
            low,
            low,
            low,
            low,
            pltpu.VMEM((LANES, length), LOW),
            pltpu.VMEM((LANES, length), WIDE),
            pltpu.VMEM((length, LANES), WIDE),
            low,
            pltpu.VMEM((2, length), WIDE),
            pltpu.SemaphoreType.DMA,
            pltpu.SemaphoreType.DMA,
        ],
        compiler_params=pltpu.CompilerParams(
            collective_id=number, has_side_effects=True, vmem_limit_bytes=56 << 20
        ),
        cost_estimate=pl.CostEstimate(flops=40 * 10**9, bytes_accessed=20 << 20, transcendentals=0),
    )(*queries, *keys, *values, *cotangents, *contexts, lse, *tables, away, *done)


def centred(block):
    shifted = block - jnp.mean(block, axis=-1, keepdims=True)
    spread = jnp.mean(shifted * shifted, axis=-1, keepdims=True)
    scale = lax.rsqrt(spread + EPS_NORM)
    return shifted * scale, scale


def norm_back(standard, scale, gain, grad):
    scaled = grad * gain
    first = jnp.mean(scaled, axis=-1, keepdims=True)
    second = jnp.mean(scaled * standard, axis=-1, keepdims=True)
    return scale * (scaled - first - standard * second)


def context_lanes(ids, j, side, width):
    half = ids[2] ^ side
    return pl.ds(pl.multiple_of(half * 4 * width + (ids[0] ^ j) * width, width), width)


def mid_kernel(ids, *refs):
    pieces = refs[:8]
    merged, weights, (g_ctx, g_mid, ctx, mixed, middle, lifted) = refs[8], sheets(refs[9:13]), refs[13:]
    width = pieces[0].shape[1]
    for n, c in enumerate(pieces):
        ctx[:, context_lanes(ids, n % 4, n // 4, width)] = c[...]
    standard, _ = centred(ctx[...].astype(WIDE))
    mixed[...] = (standard * g_ctx[...]).astype(LOW)
    depth, half = weights[0].shape
    for n in range(2):
        lanes = core_lanes(ids, n, half)
        total = merged[:, lanes].astype(WIDE)
        for k in range(4):
            total = total + dot(mixed[:, own_block(ids[1], k, depth)], weights[4 * n + k][...], NN)
        middle[:, lanes] = total
    standard, _ = centred(middle[...])
    lifted[...] = (standard * g_mid[...]).astype(LOW)


def sheets(refs):
    own, pieces, other, others = refs
    return [own] + [pieces.at[n] for n in range(3)] + [other] + [others.at[n] for n in range(3)]


def core_lanes(ids, n, half):
    return pl.ds(pl.multiple_of((ids[0] % 2 ^ n) * half, half), half)


def mid_forward(ids, contexts, merged, weights, g_ctx, g_mid, carry):
    rows, model = merged.shape
    specs = [pl.BlockSpec(w.shape, partial(lambda n, b, ids: (0,) * n, w.ndim), pipeline_mode=ONCE) for w in weights]
    block = min(256, rows)
    line = lambda width: pl.BlockSpec((block, width), lambda b, ids: (b, 0))
    gain = pl.BlockSpec((1, model), lambda b, ids: (0, 0))
    shape = lambda kind: jax.ShapeDtypeStruct((rows, model), kind)
    return kernel_call(
        mid_kernel,
        (rows // block,),
        [line(contexts[0].shape[1])] * 8 + [line(model)] + specs + [gain] * 2,
        [line(model)] * 4,
        [shape(LOW), shape(LOW), shape(WIDE), shape(LOW)],
        [],
        2 * rows * model * model,
        2 * model * model + 14 * rows * model,
        (ids, *contexts, merged, *weights, g_ctx, g_mid),
        (),
        carry,
    )


def mid_back_kernel(ids, *refs):
    a, r, middle, og, ctx = refs[:5]
    weights, (g_mid, g_ctx, middle_grad, middle_low) = sheets(refs[5:9]), refs[9:13]
    pieces, gains, mixed_grad = refs[13:21], refs[21], refs[22]
    grad = a[...].astype(WIDE) + r[...].astype(WIDE)
    standard, scale = centred(middle[...])

    @pl.when(pl.program_id(0) == 0)
    def _():
        gains[...] = jnp.zeros_like(gains)

    gains[0:1, :] += jnp.sum(grad * standard, axis=0, keepdims=True)
    total = og[...].astype(WIDE) + norm_back(standard, scale, g_mid[...], grad)
    middle_grad[...] = total
    middle_low[...] = total.astype(LOW)
    depth, half = weights[0].shape
    own, other = middle_low[:, core_lanes(ids, 0, half)], middle_low[:, core_lanes(ids, 1, half)]
    for k in range(4):
        mixed_grad[:, own_block(ids[1], k, depth)] = dot(own, weights[k][...], NT) + dot(other, weights[4 + k][...], NT)
    grad = mixed_grad[...]
    standard, scale = centred(ctx[...].astype(WIDE))
    gains[1:2, :] += jnp.sum(grad * standard, axis=0, keepdims=True)
    mixed_grad[...] = norm_back(standard, scale, g_ctx[...], grad)
    width = pieces[0].shape[1]
    for n, d in enumerate(pieces):
        d[...] = mixed_grad[:, context_lanes(ids, n % 4, n // 4, width)].astype(LOW)


def mid_backward(ids, parts, middle, og, ctx, weights, g_mid, g_ctx):
    rows, model = middle.shape
    specs = [pl.BlockSpec(w.shape, partial(lambda n, b, ids: (0,) * n, w.ndim), pipeline_mode=ONCE) for w in weights]
    block = min(256, rows)
    line = lambda width: pl.BlockSpec((block, width), lambda b, ids: (b, 0))
    gain = pl.BlockSpec((1, model), lambda b, ids: (0, 0))
    shape = lambda width, kind: jax.ShapeDtypeStruct((rows, width), kind)
    result = kernel_call(
        mid_back_kernel,
        (rows // block,),
        [line(model)] * 5 + specs + [gain] * 2,
        [line(model)] * 2 + [line(model // 8)] * 8 + [pl.BlockSpec((8, model), lambda b, ids: (0, 0))],
        [shape(model, WIDE), shape(model, LOW)]
        + [shape(model // 8, LOW)] * 8
        + [jax.ShapeDtypeStruct((8, model), WIDE)],
        [pltpu.VMEM((block, model), WIDE)],
        2 * rows * model * model,
        2 * model * model + 18 * rows * model,
        (ids, *parts, middle, og, ctx, *weights, g_mid, g_ctx),
    )
    return result[0], result[1], result[2:6], result[6:10], result[10]


def gelu_parts(hidden):
    share = 0.5 + 0.5 * lax.erf(hidden * 0.7071067811865476)
    return hidden * share, share


def gelu_slope(hidden, share):
    return share + hidden * (0.3989422804014327 * jnp.exp(-0.5 * hidden * hidden))


def fold(block):
    out = block[:, :LANES]
    for p in range(1, block.shape[1] // LANES):
        out = out + block[:, p * LANES : (p + 1) * LANES]
    return out


def halves(count, rows_first):
    if rows_first:
        return (
            lambda u, ids: (jnp.minimum(u, count - 1), 0),
            lambda u, ids: (jnp.maximum(u - count, 0), 0),
        )
    return (
        lambda u, ids: (0, jnp.minimum(u, count - 1)),
        lambda u, ids: (0, jnp.maximum(u - count, 0)),
    )


def each_half(work, own, got):
    near = pl.program_id(0) < pl.num_programs(0) // 2

    @pl.when(near)
    def _():
        work(own)

    @pl.when(jnp.logical_not(near))
    def _():
        work(got)


def remote(source, target, sent, got, device):
    return pltpu.make_async_remote_copy(
        src_ref=source, dst_ref=target, send_sem=sent, recv_sem=got, device_id=device, device_id_type=MESH
    )


def ffn_up_kernel(
    lifted, up_own, up_got, act, slope, sums, lifted_all, x, acc, sent, got, local
):
    j, u = pl.program_id(0), pl.program_id(1)
    rows = x.shape[0]
    half = rows // 2
    _, _, over_core, over_low, _ = partners()
    parts = [pl.ds(b * half, half) for b in range(2)]

    def moves(source, whole, base):
        near = remote(source, whole.at[0], sent.at[base], got.at[base], over_core)
        far = [
            remote(source.at[part], whole.at[1, part], sent.at[base + 1 + b], got.at[base + 1 + b], over_low)
            for b, part in enumerate(parts)
        ]
        last = [
            remote(whole.at[1, part], whole.at[2, part], sent.at[base + 3 + b], got.at[base + 3 + b], over_core)
            for b, part in enumerate(parts)
        ]
        return near, far, last

    near, far, last = moves(lifted, lifted_all, 0)

    def load(source):
        copy = pltpu.make_async_copy(source, x, local)
        copy.start()
        copy.wait()

    @pl.when(u == 0)
    def _():
        acc[...] = jnp.zeros_like(acc)

    @pl.when((j == 0) & (u == 0))
    def _():
        greet((over_core, over_low))
        for copy in (*far, near):
            copy.start()
        load(lifted)

    @pl.when((j == 1) & (u == 0))
    def _():
        near.wait()
        load(lifted_all.at[0])

    @pl.when((j == 2) & (u == 0))
    def _():
        for copy, onward in zip(far, last):
            copy.wait()
            onward.start()
        load(lifted_all.at[1])

    @pl.when((j == 3) & (u == 0))
    def _():
        for copy in last:
            copy.wait()
        load(lifted_all.at[2])

    def work(up):
        for b in range(2):
            here = slice(b * half, (b + 1) * half)
            h = dot(x[here, :], up[...], NN)
            activated, share = gelu_parts(h)
            low = activated.astype(LOW)
            act[0, here, :] = low
            slope[0, here, :] = gelu_slope(h, share).astype(LOW)
            activated = low.astype(WIDE)
            acc[0, here, :] += fold(activated)
            acc[1, here, :] += fold(activated * activated)

    steps = pl.num_programs(1)
    pl.when(u < steps // 2)(lambda: work(up_own))
    pl.when(u >= steps // 2)(lambda: work(up_got))

    @pl.when(u == steps - 1)
    def _():
        for n in range(2):
            sums[0, n : n + 1, :] = jnp.sum(acc[n].T, axis=0, keepdims=True)
        sums[0, 2:8, :] = jnp.zeros_like(sums[0, 2:8, :])


def in_halves(count, rows_first):
    near, far = (lambda u: jnp.minimum(u, count - 1)), (lambda u: jnp.maximum(u - count, 0))
    if rows_first:
        return [lambda j, u: (near(u), 0), lambda j, u: (far(u), 0)]
    return [lambda j, u: (0, near(u)), lambda j, u: (0, far(u))]


def ffn_up(lifted, upward):
    rows, model = lifted.shape
    units = 2 * upward[0].shape[1]
    block = min(512, units // 2)
    count = units // 2 // block
    out = pl.BlockSpec((1, rows, block), lambda j, u: (j, 0, u))
    kept = jax.ShapeDtypeStruct((4, rows, units), LOW)
    others = jax.ShapeDtypeStruct((3, rows, model), LOW)
    return pl.pallas_call(
        ffn_up_kernel,
        grid=(4, 2 * count),
        in_specs=[ANYWHERE] + [pl.BlockSpec((model, block), at) for at in in_halves(count, False)],
        out_specs=[out] * 2 + [pl.BlockSpec((1, 8, rows), lambda j, u: (j, 0, 0)), ANYWHERE],
        out_shape=[kept] * 2 + [jax.ShapeDtypeStruct((4, 8, rows), WIDE), others],
        scratch_shapes=[
            pltpu.VMEM((rows, model), LOW),
            pltpu.VMEM((2, rows, LANES), WIDE),
            pltpu.SemaphoreType.DMA((5,)),
            pltpu.SemaphoreType.DMA((5,)),
            pltpu.SemaphoreType.DMA,
        ],
        compiler_params=pltpu.CompilerParams(collective_id=2, has_side_effects=True, vmem_limit_bytes=56 << 20),
        cost_estimate=pl.CostEstimate(flops=80 * 10**9, bytes_accessed=100 << 20, transcendentals=0),
    )(lifted, *upward)


def ffn_back_kernel(og, near, far, last, down_own, down_got, act, gain, squashed_grad, sums, x, acc, local):
    j, u = pl.program_id(0), pl.program_id(1)
    rows = x.shape[0]
    half = rows // 2

    @pl.when(u == 0)
    def _():
        acc[...] = jnp.zeros_like(acc)

    def load(source):
        copy = pltpu.make_async_copy(source, x, local)
        copy.start()
        copy.wait()

    for n, source in enumerate((og, near, far, last)):
        pl.when((u == 0) & (j == n))(partial(load, source))

    def work(down):
        for b in range(2):
            here = slice(b * half, (b + 1) * half)
            s = dot(x[here, :], down[...], NT).astype(LOW)
            squashed_grad[0, here, :] = s
            scaled = s.astype(WIDE) * gain[...]
            acc[0, here, :] += fold(scaled)
            acc[1, here, :] += fold(scaled * act[0, here, :].astype(WIDE))

    steps = pl.num_programs(1)
    pl.when(u < steps // 2)(lambda: work(down_own))
    pl.when(u >= steps // 2)(lambda: work(down_got))

    @pl.when(u == steps - 1)
    def _():
        sums[0, 0:2, :] = jnp.zeros_like(sums[0, 0:2, :])
        for n in range(2):
            sums[0, n + 2 : n + 3, :] = jnp.sum(acc[n].T, axis=0, keepdims=True)
        sums[0, 4:8, :] = jnp.zeros_like(sums[0, 4:8, :])


def ffn_back(og, others, downward, act, gain):
    rows, model = og.shape
    units = act.shape[2]
    block = min(512, units // 2)
    count = units // 2 // block
    line = pl.BlockSpec((1, rows, block), lambda j, u: (j, 0, u))
    return pl.pallas_call(
        ffn_back_kernel,
        grid=(4, 2 * count),
        in_specs=[ANYWHERE] * 4
        + [pl.BlockSpec((block, model), at) for at in in_halves(count, True)]
        + [line, pl.BlockSpec((1, block), lambda j, u: (0, u))],
        out_specs=[line, pl.BlockSpec((1, 8, rows), lambda j, u: (j, 0, 0))],
        out_shape=[like(act), jax.ShapeDtypeStruct((4, 8, rows), WIDE)],
        scratch_shapes=[
            pltpu.VMEM((rows, model), LOW),
            pltpu.VMEM((2, rows, LANES), WIDE),
            pltpu.SemaphoreType.DMA,
        ],
        compiler_params=pltpu.CompilerParams(vmem_limit_bytes=56 << 20),
        cost_estimate=pl.CostEstimate(flops=60 * 10**9, bytes_accessed=100 << 20, transcendentals=0),
    )(og, *others, *downward, act, gain)


def ffn_second_kernel(
    act,
    slope,
    squashed_grad,
    sums,
    gain,
    up_own,
    up_got,
    squashed,
    hidden_grad,
    kept,
    arrived,
    gains,
    acc,
    send_core,
    got_core,
    send_low,
    sent,
    got,
    *,
    hidden_width,
):
    n, u = pl.program_id(0), pl.program_id(1)
    steps = pl.num_programs(1)
    rows, block = act.shape[1:]
    half = rows // 2
    _, _, over_core, over_low, _ = partners()
    to_core = [remote(send_core.at[b], got_core.at[b], sent.at[b], got.at[b], over_core) for b in range(2)]
    to_low = remote(send_low, arrived, sent.at[2], got.at[2], over_low)

    @pl.when((n == 0) & (u == 0))
    def _():
        greet((over_core, over_low))
        gains[...] = jnp.zeros_like(gains)

    @pl.when(u == 0)
    def _():
        acc[...] = jnp.zeros_like(acc)

    columns = sums[0].T
    lanes = pl.ds(pl.multiple_of(u * block, block), block)

    def work(up):
        for b in range(2):
            here = slice(b * half, (b + 1) * half)
            centre = columns[here, 0:1] / hidden_width
            scale = lax.rsqrt(columns[here, 1:2] / hidden_width - centre * centre + EPS_NORM)
            mean_one = columns[here, 2:3] / hidden_width
            mean_two = scale * (columns[here, 3:4] - centre * columns[here, 2:3]) / hidden_width
            standard = (act[0, here, :].astype(WIDE) - centre) * scale
            squashed[0, here, :] = (standard * gain[...]).astype(LOW)
            s = squashed_grad[0, here, :].astype(WIDE)
            gains[0:1, lanes] += jnp.sum(s * standard, axis=0, keepdims=True)
            activated_grad = (s * gain[...] - mean_one - standard * mean_two) * scale
            grad = (activated_grad * slope[0, here, :].astype(WIDE)).astype(LOW)
            hidden_grad[0, here, :] = grad
            acc[here, :] += dot(grad, up[...], NT)

    pl.when(u < steps // 2)(lambda: work(up_own))
    pl.when(u >= steps // 2)(lambda: work(up_got))
    ends = u == steps - 1

    @pl.when(ends & (n == 0))
    def _():
        send_core[0] = acc[...].astype(LOW)
        to_core[0].start()

    @pl.when(ends & (n == 1))
    def _():
        to_core[0].wait()
        send_low[...] = (acc[...] + got_core[0].astype(WIDE)).astype(LOW)
        to_low.start()

    @pl.when(ends & (n == 2))
    def _():
        send_core[1] = acc[...].astype(LOW)
        to_core[1].start()

    @pl.when(ends & (n == 3))
    def _():
        to_core[1].wait()
        kept[...] = (acc[...] + got_core[1].astype(WIDE)).astype(LOW)
        to_low.wait()


def ffn_second(act, slope, squashed_grad, sums, gain, upward, hidden_width):
    _, rows, units = act.shape
    model = upward[0].shape[0]
    block = min(512, units // 2)
    count = units // 2 // block
    line = pl.BlockSpec((1, rows, block), lambda n, u: (3 - n, 0, u))
    piece = jax.ShapeDtypeStruct((rows, model), LOW)
    return pl.pallas_call(
        partial(ffn_second_kernel, hidden_width=hidden_width),
        grid=(4, 2 * count),
        in_specs=[line] * 3
        + [pl.BlockSpec((1, 8, rows), lambda n, u: (3 - n, 0, 0)), pl.BlockSpec((1, block), lambda n, u: (0, u))]
        + [pl.BlockSpec((model, block), at) for at in in_halves(count, False)],
        out_specs=[line] * 2
        + [pl.BlockSpec((rows, model), lambda n, u: (0, 0)), ANYWHERE, pl.BlockSpec((8, units), lambda n, u: (0, 0))],
        out_shape=[like(act)] * 2 + [piece] * 2 + [jax.ShapeDtypeStruct((8, units), WIDE)],
        scratch_shapes=[
            pltpu.VMEM((rows, model), WIDE),
            pltpu.VMEM((2, rows, model), LOW),
            pltpu.VMEM((2, rows, model), LOW),
            pltpu.VMEM((rows, model), LOW),
            pltpu.SemaphoreType.DMA((3,)),
            pltpu.SemaphoreType.DMA((3,)),
        ],
        compiler_params=pltpu.CompilerParams(collective_id=3, has_side_effects=True, vmem_limit_bytes=60 << 20),
        cost_estimate=pl.CostEstimate(flops=80 * 10**9, bytes_accessed=100 << 20, transcendentals=0),
    )(act, slope, squashed_grad, sums, gain, *upward)


def spread_kernel(ids, x, own, got, out, acc):
    step = pl.program_id(0)

    @pl.when(step == 0)
    def _():
        acc[...] = jnp.zeros_like(acc)

    def work(weight):
        acc[...] += dot(x[...], weight[...], NN)

    each_half(work, own, got)

    @pl.when(step == pl.num_programs(0) - 1)
    def _():
        out[...] = acc[...].astype(LOW)


def ffn_out(ids, x, j, downward):
    _, rows, units = x.shape
    model = downward[0].shape[1]
    block = min(512, units // 2)
    count = units // 2 // block
    return kernel_call(
        spread_kernel,
        (2 * count,),
        [pl.BlockSpec((pl.Squeezed(), rows, block), lambda u, ids: (j, 0, u))]
        + [pl.BlockSpec((block, model), at) for at in halves(count, True)],
        [pl.BlockSpec((rows, model), lambda u, ids: (0, 0))],
        [jax.ShapeDtypeStruct((rows, model), LOW)],
        [pltpu.VMEM((rows, model), WIDE)],
        2 * rows * model * units,
        2 * model * units + 2 * rows * (units + model),
        (ids, x, *downward),
    )[0]


def unproject_kernel(*refs):
    grads, owns, got_weight, away = refs[0:6], refs[6:10], refs[10], refs[11:13]
    kept, arrived, *back = refs[13:17]
    acc, send_core, got_core, send_low, sent, got = refs[17:]
    n, b = pl.program_id(0), pl.program_id(1)
    rows = acc.shape[0]
    depth = owns[0].shape[1]
    place = lax.axis_index("dp")
    _, _, over_core, over_low, over_high = partners()
    here = pl.ds(pl.multiple_of(b * rows, rows), rows)

    def to_core(slot, half):
        s = 2 * slot + half
        return remote(send_core.at[s], got_core.at[s], sent.at[s], got.at[s], over_core)

    def to_low(half):
        part = pl.ds(half * rows, rows)
        return remote(send_low.at[half], arrived.at[part], sent.at[4 + half], got.at[4 + half], over_low)

    crossing = [remote(away[i], back[i], sent.at[6 + i], got.at[6 + i], over_high) for i in range(2)]

    @pl.when((n == 0) & (b == 0))
    def _():
        greet((over_core, over_low, over_high))
        for copy in crossing:
            copy.start()

    acc[...] = sum(dot(grads[3 + f][0], got_weight[f], NT) for f in range(3))
    for k in range(4):
        lanes = pl.ds(pl.multiple_of(mate(place, k) * depth, depth), depth)
        acc[:, lanes] += sum(dot(grads[f][0], owns[k][f], NT) for f in range(3))

    for half in range(2):

        @pl.when((n == 0) & (b == half))
        def _():
            send_core[half] = acc[...].astype(LOW)
            to_core(0, half).start()

        @pl.when((n == 1) & (b == half))
        def _():
            to_core(0, half).wait()
            send_low[half] = (acc[...] + got_core[half].astype(WIDE)).astype(LOW)
            to_low(half).start()

        @pl.when((n == 2) & (b == half))
        def _():
            send_core[2 + half] = acc[...].astype(LOW)
            to_core(1, half).start()

        @pl.when((n == 3) & (b == half))
        def _():
            to_core(1, half).wait()
            kept[here, :] = (acc[...] + got_core[2 + half].astype(WIDE)).astype(LOW)

    @pl.when((n == 3) & (b == 1))
    def _():
        to_low(0).wait()
        to_low(1).wait()
        for copy in crossing:
            copy.wait()


def unproject(grads, heads, away):
    _, rows, width = grads[0].shape
    own, got = heads
    model = got.shape[1]
    half = rows // 2
    line = pl.BlockSpec((1, half, width), lambda n, b: (3 - n, b, 0))
    still = lambda value: pl.BlockSpec(value.shape, lambda n, b: (0,) * value.ndim, pipeline_mode=ONCE)
    piece = jax.ShapeDtypeStruct((rows, model), LOW)
    buffer = lambda count: pltpu.VMEM((count, half, model), LOW)
    return pl.pallas_call(
        unproject_kernel,
        grid=(4, 2),
        in_specs=[line] * 6 + [still(w) for w in own] + [still(got), ANYWHERE, ANYWHERE],
        out_specs=[pl.BlockSpec((rows, model), lambda n, b: (0, 0)), ANYWHERE, ANYWHERE, ANYWHERE],
        out_shape=[piece, piece] + [like(value) for value in away],
        scratch_shapes=[
            pltpu.VMEM((half, model), WIDE),
            buffer(4),
            buffer(4),
            buffer(2),
            pltpu.SemaphoreType.DMA((8,)),
            pltpu.SemaphoreType.DMA((8,)),
        ],
        compiler_params=pltpu.CompilerParams(collective_id=6, has_side_effects=True, vmem_limit_bytes=56 << 20),
        cost_estimate=pl.CostEstimate(flops=40 * 10**9, bytes_accessed=20 << 20, transcendentals=0),
    )(*grads, *own, got, *away)


def grad_kernel(ids, *refs, chunks, kinds, fixed):
    xs, ys = refs[:chunks], refs[chunks : chunks * (1 + kinds)]
    outs, turned = refs[chunks * (1 + kinds) : -1], refs[-1]
    step = pl.program_id(0)
    rows = xs[0].shape[0]

    def turn():
        for j in range(chunks):
            turned[:, j * rows : (j + 1) * rows] = xs[j][...].T

    if fixed:
        pl.when(step == 0)(turn)
    else:
        turn()
    for f in range(kinds):
        total = None
        for j in range(chunks):
            part = dot(turned[:, j * rows : (j + 1) * rows], ys[f * chunks + j][...], NN)
            total = part if total is None else total + part
        total = total.astype(LOW)
        if len(outs) == 1:
            outs[0][f] = total
        else:
            for k, out in enumerate(outs):

                @pl.when(step == k)
                def _():
                    out[f] = total


def weight_grad(ids, xs, ys, x_blocks, done=(), side=None, apart=False):
    chunks, kinds = len(xs), len(ys)
    rows, x_width = xs[0][0].shape[-2:]
    y_width = ys[0][0][0].shape[-1]

    def spec(piece, width, at, once):
        mode = {"pipeline_mode": ONCE} if once else {}
        if piece[1] is None:
            return pl.BlockSpec((rows, width), at, **mode)
        place = lambda b, ids, n=piece[1]: (n, *at(b, ids))
        return pl.BlockSpec((pl.Squeezed(), rows, width), place, **mode)

    shift = lambda b, ids: (0, ids[1] ^ b if apart else b)
    still = lambda b, ids: (0, side or 0)
    share = 1 if side is None else 2
    if x_blocks:
        x_width, y_width = x_width // 4, y_width // share
        x_at, y_at = (x_width, shift, False), (y_width, still, True)
        whole, out_at = (kinds, 4 * x_width, y_width), lambda b, ids: (0, b, 0)
    else:
        x_width, y_width = x_width // share, y_width // 4
        x_at, y_at = (x_width, still, True), (y_width, shift, False)
        whole, out_at = (kinds, x_width, 4 * y_width), lambda b, ids: (0, 0, b)
    out = (kinds, x_width, y_width)
    if apart:
        out_specs = [pl.BlockSpec(out, lambda b, ids: (0, 0, 0))] * 4
        out_shape = [jax.ShapeDtypeStruct(out, LOW)] * 4
    else:
        out_specs, out_shape = [pl.BlockSpec(out, out_at)], [jax.ShapeDtypeStruct(whole, LOW)]
    result = kernel_call(
        partial(grad_kernel, chunks=chunks, kinds=kinds, fixed=not x_blocks),
        (4,),
        [spec(x, *x_at) for x in xs] + [spec(y, *y_at) for group in ys for y in group],
        out_specs,
        out_shape,
        [pltpu.VMEM((x_width, rows * chunks), LOW)],
        8 * rows * chunks * x_width * y_width * kinds,
        2 * rows * chunks * (4 * x_width + 4 * y_width * kinds),
        (ids, *[x[0] for x in xs], *[y[0] for group in ys for y in group]),
        done,
    )
    return result if apart else result[0]


def flip(value, axis, mask):
    return lax.ppermute(value, axis, [(i, i ^ mask) for i in range(lax.axis_size(axis))])


def add_low(one, two):
    return (one.astype(WIDE) + two.astype(WIDE)).astype(LOW)


def sum_everywhere(value):
    for axis, mask in (("dp", 1), ("dp", 2), ("mp", 1), ("mp", 2), ("mp", 4)):
        value = value + flip(value, axis, mask)
    return value


def partners():
    row, column = lax.axis_index("dp"), lax.axis_index("mp")
    over_x = (row + 1 - 2 * (row % 2), column)
    over_y = ((row + 2) % 4, column)
    over_core = (row, column + 1 - 2 * (column % 2))
    over_low = (row, column + 2 - 4 * ((column // 2) % 2))
    over_high = (row, (column + 4) % 8)
    return over_x, over_y, over_core, over_low, over_high


def greet(others):
    barrier = pltpu.get_barrier_semaphore()
    for other in others:
        pl.semaphore_signal(barrier, inc=1, device_id=other, device_id_type=MESH)
    pl.semaphore_wait(barrier, len(others))


class Sender:
    def __init__(self, sent, got):
        self.sent, self.got, self.count = sent, got, 0

    def __call__(self, source, target, device):
        copy = pltpu.make_async_remote_copy(
            src_ref=source,
            dst_ref=target,
            send_sem=self.sent.at[self.count],
            recv_sem=self.got.at[self.count],
            device_id=device,
            device_id_type=MESH,
        )
        self.count += 1
        copy.start()
        return copy


def open_kernel(text, head, text_got, head_x, head_y, head_far, sent, got):
    over_x, over_y, _, _, over_high = partners()
    greet((over_x, over_y, over_high))
    send = Sender(sent, got)
    half = head.shape[1] // 2
    upper, lower = pl.ds(0, half), pl.ds(half, half)
    copies = [send(text, text_got, over_high)]
    first = send(head.at[:, upper], head_x.at[:, upper], over_x)
    second = send(head.at[:, lower], head_y.at[:, lower], over_y)
    copies.append(send(head.at[:, lower], head_x.at[:, lower], over_x))
    copies.append(send(head.at[:, upper], head_y.at[:, upper], over_y))
    first.wait()
    copies.append(send(head_x.at[:, upper], head_far.at[:, upper], over_y))
    second.wait()
    copies.append(send(head_y.at[:, lower], head_far.at[:, lower], over_x))
    for copy in copies:
        copy.wait()


def open_exchange(text, head):
    return pl.pallas_call(
        open_kernel,
        in_specs=[ANYWHERE] * 2,
        out_specs=[ANYWHERE] * 4,
        out_shape=[like(text), like(head), like(head), like(head)],
        scratch_shapes=[pltpu.SemaphoreType.DMA((7,)), pltpu.SemaphoreType.DMA((7,))],
        compiler_params=pltpu.CompilerParams(collective_id=0, has_side_effects=True),
        cost_estimate=pl.CostEstimate(flops=0, bytes_accessed=100 << 20, transcendentals=0),
    )(text, head)


def normed_kernel(normed, head, outward, upward, near, far, far_near, head_got, pieces, others, up_got, sent, got):
    over_x, over_y, over_core, over_low, over_high = partners()
    greet((over_x, over_y, over_core, over_low, over_high))
    send = Sender(sent, got)
    rows = normed.shape[0] // 2
    parts = [pl.ds(b * rows, rows) for b in range(2)]
    crossing = [send(normed.at[part], far.at[part], over_low) for part in parts]
    copies = [send(normed, near, over_core), send(head, head_got, over_high), send(upward, up_got, over_high)]
    half = outward.shape[0] // 2
    upper, lower = pl.ds(0, half), pl.ds(half, half)
    first = send(outward.at[upper], pieces.at[0, upper], over_x)
    second = send(outward.at[lower], pieces.at[1, lower], over_y)
    later = [
        (send(outward.at[lower], pieces.at[0, lower], over_x), 0, lower),
        (send(outward.at[upper], pieces.at[1, upper], over_y), 1, upper),
    ]
    first.wait()
    later.append((send(pieces.at[0, upper], pieces.at[2, upper], over_y), 2, upper))
    copies.append(send(pieces.at[0, upper], others.at[0, upper], over_core))
    second.wait()
    later.append((send(pieces.at[1, lower], pieces.at[2, lower], over_x), 2, lower))
    copies.append(send(pieces.at[1, lower], others.at[1, lower], over_core))
    for copy, part in zip(crossing, parts):
        copy.wait()
        copies.append(send(far.at[part], far_near.at[part], over_core))
    for copy, n, part in later:
        copy.wait()
        copies.append(send(pieces.at[n, part], others.at[n, part], over_core))
    for copy in copies:
        copy.wait()


def normed_exchange(normed, head, outward, upward):
    pieces = jax.ShapeDtypeStruct((3,) + outward.shape, LOW)
    return pl.pallas_call(
        normed_kernel,
        in_specs=[ANYWHERE] * 4,
        out_specs=[ANYWHERE] * 7,
        out_shape=[like(normed)] * 3 + [like(head), pieces, pieces, like(upward)],
        scratch_shapes=[pltpu.SemaphoreType.DMA((19,)), pltpu.SemaphoreType.DMA((19,))],
        compiler_params=pltpu.CompilerParams(collective_id=1, has_side_effects=True),
        cost_estimate=pl.CostEstimate(flops=0, bytes_accessed=100 << 20, transcendentals=0),
    )(normed, head, outward, upward)


def rotary_tables(length):
    cosine, sine_part, exponent = xpos_tables(length, HEAD_DIM)
    out = []
    for polarity in (1.0, -1.0):
        factor = jnp.exp(polarity * exponent)
        near = (cosine * factor)[:, 0]
        far = (sine_part * factor)[:, 0]
        out.append(jnp.concatenate([near] * 4, axis=-1))
        out.append(jnp.concatenate([-far, far, -far, far], axis=-1))
    return out


def on_device_paired(
    text_states,
    image_states,
    image_offsets,
    image_counts,
    output_grad,
    head_master,
    head_moment,
    head_square,
    outward_master,
    outward_moment,
    outward_square,
    upward_master,
    upward_moment,
    upward_square,
    downward_master,
    downward_moment,
    downward_square,
    gains_master,
    gains_moment,
    gains_square,
):
    model_rank = lax.axis_index("mp")
    side = model_rank // 4
    rank = model_rank % 4
    place = lax.axis_index("dp")
    ids = jnp.stack([rank, place, side]).astype(jnp.int32)
    _, local_len, model_width = text_states.shape
    length = local_len * 8
    rows = 2 * local_len
    hidden_local = upward_master.shape[1]
    hidden_width = hidden_local * 8

    def pick(value, index):
        return lax.dynamic_index_in_dim(value, index, 0, keepdims=False)

    tables = rotary_tables(length)

    def both(kept, got):
        return jnp.where(side == 0, jnp.stack([kept, got]), jnp.stack([got, kept]))

    core = rank % 2
    half_width = model_width // 2
    text_out = pick(text_states, 1 - side)
    head_own = head_master.astype(LOW)
    upward_own = upward_master.astype(LOW)
    upward_weight = [lax.all_gather(upward_own, "dp", axis=0, tiled=True)]
    text_got, *head_parts = open_exchange(text_out, head_own)
    head_weight = [[head_own] + head_parts]
    downward_own = downward_master.astype(LOW)
    downward_weight = [lax.all_gather(downward_own, "dp", axis=1, tiled=True)]
    text = both(pick(text_states, side), text_got)

    gain_in = gains_master[None, :model_width]
    gain_ctx = gains_master[None, model_width : 2 * model_width]
    gain_mid = gains_master[None, 2 * model_width : 3 * model_width]
    hidden_start = 3 * model_width + model_rank * hidden_local
    other_start = 3 * model_width + (model_rank ^ 4) * hidden_local
    gain_hidden = jnp.concatenate(
        [
            lax.dynamic_slice_in_dim(gains_master, hidden_start, hidden_local),
            lax.dynamic_slice_in_dim(gains_master, other_start, hidden_local),
        ]
    )[None]

    offsets = pick(image_offsets, side)
    image_count = pick(image_counts, side)
    position = (
        jnp.arange(2, dtype=jnp.int32)[:, None] * (4 * local_len)
        + rank * local_len
        + jnp.arange(local_len, dtype=jnp.int32)[None, :]
    ).reshape(rows)
    slot_index = jnp.arange(offsets.shape[0], dtype=jnp.int32)
    inside = (
        (position[:, None] >= offsets[None, :])
        & (position[:, None] < offsets[None, :] + PATCH)
        & (slot_index[None, :] < image_count)
    )
    picked = jnp.sum(
        jnp.where(inside, slot_index[None, :] * PATCH + position[:, None] - offsets[None, :], 0), axis=-1
    )
    covered = jnp.any(inside, axis=-1)
    place_index = jnp.arange(image_states.shape[1], dtype=jnp.int32)
    chosen = (covered[:, None] & (picked[:, None] == place_index[None, :])).astype(LOW)
    images = jnp.dot(chosen, pick(image_states, side), preferred_element_type=WIDE).astype(LOW)
    merged = jnp.where(covered[:, None], images, text.reshape(rows, model_width))

    def turn_heads(pieces):
        return [pieces[0]] + [flip(pieces[j], "mp", j) for j in range(1, 4)]

    normed_own = layer_norm(merged.astype(WIDE), gain_in).astype(LOW)
    outward_low = outward_master.astype(LOW)
    outward_own, outward_other = (
        lax.dynamic_slice_in_dim(outward_low, n * half_width, half_width, 1) for n in (core, 1 - core)
    )
    near, far, far_near, head_got, *pieces, upward_got = normed_exchange(
        normed_own, head_own, outward_own, upward_own
    )
    outward_weight = [outward_own, pieces[0], outward_other, pieces[1]]
    normed = [normed_own, near, far, far_near]
    head_weight.append(lax.all_gather(head_got, "dp", axis=1, tiled=True))
    upward_weight.append(lax.all_gather(upward_got, "dp", axis=0, tiled=True))
    cotangent = both(pick(output_grad, side), flip(pick(output_grad, 1 - side), "mp", 4)).reshape(rows, model_width)
    cotangent_far = flip(cotangent, "mp", 2)
    cotangent_others = [flip(cotangent, "mp", 1), cotangent_far, flip(cotangent_far, "mp", 1)]

    queries, keys, values, contexts, logs, arrived = [], [], [], [], [], []
    for half in range(2):
        projected = [project(ids, chunk, head_weight[half], tables, j) for j, chunk in enumerate(normed)]
        for n, group in enumerate((queries, keys, values)):
            group.append([p[n] for p in projected])
        if half == 0:
            context, lse, leaving = attend(
                ids, queries[half], keys[half], values[half], [], [downward_own]
            )
            downward_got = flip(leaving, "mp", 4)
        else:
            context, lse = attend(ids, queries[half], keys[half], values[half])
        contexts.append(context)
        logs.append(lse)
        arrived = arrived + turn_heads(context)
    context, mixed, middle, lifted_own, downward_got = mid_forward(
        ids, arrived, merged, outward_weight, gain_ctx, gain_mid, [downward_got]
    )
    downward_weight.append(lax.all_gather(downward_got, "dp", axis=1, tiled=True))
    act, slope, sums, lifted_others = ffn_up(lifted_own, upward_weight)
    squashed_grad, back_sums = ffn_back(cotangent, cotangent_others, downward_weight, act, gain_hidden)
    lifted = [(lifted_own, None)] + [(lifted_others, n) for n in range(3)]
    cotangents = [(value, None) for value in [cotangent] + cotangent_others]
    sums = sums + back_sums
    others = [flip(sums, "mp", k) for k in range(1, 4)]
    sums = jnp.stack(
        [(sums[j] + others[0][j ^ 1]) + (others[1][j ^ 2] + others[2][j ^ 3]) for j in range(4)]
    )
    squashed, hidden_grad, lifted_kept, lifted_got, hidden_gains = ffn_second(
        act, slope, squashed_grad, sums, gain_hidden, upward_weight, hidden_width
    )

    def split(value):
        return [(value, n) for n in range(4)]

    def whole(values):
        return [(value, None) for value in values]

    down_grad = lax.psum_scatter(
        weight_grad(ids, split(squashed), [cotangents], False), "dp", scatter_dimension=2, tiled=True
    )[0]
    middle_grad, middle_low, own_grads, other_grads, mid_gains = mid_backward(
        ids, (lifted_kept, lifted_got), middle, cotangent, context, outward_weight, gain_mid, gain_ctx
    )
    context_heads = [turn_heads(own_grads), turn_heads(other_grads)]
    up_grad = lax.psum_scatter(
        weight_grad(ids, lifted, [split(hidden_grad)], True), "dp", scatter_dimension=1, tiled=True
    )[0]
    ffn_parts = [ffn_out(ids, squashed, j, downward_weight) for j in range(4)]

    def scatter_tokens(parts):
        passed = add_low(parts[2], flip(parts[3], "mp", 1))
        return add_low(parts[0], flip(parts[1], "mp", 1)), flip(passed, "mp", 2)

    def give_back(pair):
        got = flip(pick(pair, 1 - side).astype(LOW), "mp", 4)
        return both(pick(pair, side), got.astype(pair.dtype))

    ffn_kept, ffn_got = scatter_tokens(ffn_parts)
    output_rows = (middle + (ffn_kept.astype(WIDE) + ffn_got.astype(WIDE))).astype(LOW)
    output_rows = output_rows.reshape(2, local_len, model_width)

    head_grads, head_sides, backs = [None, None], [None, None], [None, None]
    leaving = (pick(output_rows, 1 - side), down_grad[hidden_local:])
    for half in (1, 0):
        *head_grads[half], backs[half] = attend_back(
            queries[half],
            keys[half],
            values[half],
            context_heads[half],
            contexts[half],
            logs[half],
            tables,
            leaving[half],
            4 + half,
            [ffn_kept] if half else [],
        )
        head_part = weight_grad(ids, whole(normed), [split(g) for g in head_grads[half]], True)
        head_sides[half] = lax.psum_scatter(head_part, "dp", scatter_dimension=1, tiled=True)
        if half == 1:
            outward_part = weight_grad(ids, whole([mixed]), [whole([middle_low])], True, [head_part])[0]
            outward_sent = lax.dynamic_slice_in_dim(outward_part, (1 - core) * half_width, half_width, 1)
            outward_half = add_low(
                lax.dynamic_slice_in_dim(outward_part, core * half_width, half_width, 1), flip(outward_sent, "mp", 1)
            )
    output_got, down_got = backs
    layer_output = both(pick(output_rows, side), output_got)
    normed_kept, normed_got, up_got, head_got_grad = unproject(
        head_grads[0] + head_grads[1], head_weight, [up_grad[:, hidden_local:], head_sides[1]]
    )
    head_sum = head_sides[0].astype(WIDE) + head_got_grad.astype(WIDE)
    normed_grad = normed_kept.astype(WIDE) + normed_got.astype(WIDE)
    _, input_back = jax.vjp(layer_norm, merged.astype(WIDE), gain_in)
    merged_part, in_gain_grad = input_back(normed_grad)
    input_grad = give_back((middle_grad + merged_part).reshape(2, local_len, model_width))

    outward_grad = lax.psum_scatter(outward_half, "dp", scatter_dimension=0, tiled=True)
    outward_grad = lax.psum(outward_grad, "mp", axis_index_groups=[[0, 2, 4, 6], [1, 3, 5, 7]])
    outward_got = flip(outward_grad, "mp", 1)
    outward_grad = jnp.where(
        core == 0,
        jnp.concatenate([outward_grad, outward_got], axis=1),
        jnp.concatenate([outward_got, outward_grad], axis=1),
    )
    outward_sum = outward_grad.astype(WIDE)

    down_sum = down_grad[:hidden_local].astype(WIDE) + down_got.astype(WIDE)
    up_sum = up_grad[:, :hidden_local].astype(WIDE) + up_got.astype(WIDE)
    moment_head, square_head, head_dir = adapt_step(head_sum, head_master, head_moment, head_square, DECAY_RATE)
    moment_outward, square_outward, outward_dir = adapt_step(
        outward_sum, outward_master, outward_moment, outward_square, DECAY_RATE
    )
    moment_upward, square_upward, upward_dir = adapt_step(
        up_sum, upward_master, upward_moment, upward_square, DECAY_RATE
    )
    moment_downward, square_downward, downward_dir = adapt_step(
        down_sum, downward_master, downward_moment, downward_square, DECAY_RATE
    )
    owner = (model_rank == 0).astype(WIDE)
    norm_part = jnp.concatenate(
        [
            jnp.stack([jnp.sum(head_master * head_master, axis=(1, 2)), jnp.sum(head_dir * head_dir, axis=(1, 2))], axis=-1),
            pair_sums(outward_master, outward_dir) * owner,
            pair_sums(upward_master, upward_dir),
            pair_sums(downward_master, downward_dir),
        ],
        axis=0,
    )
    hidden_gain = hidden_gains[0]
    gains_part = jnp.concatenate([in_gain_grad[0], mid_gains[1], mid_gains[0], jnp.zeros((hidden_width,), WIDE)])
    gains_part = lax.dynamic_update_slice(gains_part, hidden_gain[:hidden_local], (hidden_start,))
    gains_part = lax.dynamic_update_slice(gains_part, hidden_gain[hidden_local:], (other_start,))
    every = sum_everywhere(jnp.concatenate([gains_part, norm_part.reshape(-1)]))
    gains_sum, norm_sums = every[: gains_part.shape[0]], every[gains_part.shape[0] :].reshape(6, 2)
    moment_gains, square_gains, gains_dir = adapt_step(gains_sum, gains_master, gains_moment, gains_square, 0.0)
    gains_sums = jnp.stack(
        [
            gain_segments(gains_master * gains_master, model_width),
            gain_segments(gains_dir * gains_dir, model_width),
        ],
        axis=-1,
    )
    updated_head = trust_move(
        head_master, head_dir, norm_sums[:3, 0][:, None, None], norm_sums[:3, 1][:, None, None]
    )
    updated_outward = trust_move(outward_master, outward_dir, norm_sums[3, 0], norm_sums[3, 1])
    updated_upward = trust_move(upward_master, upward_dir, norm_sums[4, 0], norm_sums[4, 1])
    updated_downward = trust_move(downward_master, downward_dir, norm_sums[5, 0], norm_sums[5, 1])
    updated_gains = trust_move(
        gains_master,
        gains_dir,
        gain_spread(gains_sums[:, 0], model_width, hidden_width),
        gain_spread(gains_sums[:, 1], model_width, hidden_width),
    )
    update_norms = jnp.sqrt(jnp.concatenate([norm_sums, gains_sums], axis=0))
    return (
        layer_output,
        input_grad,
        moment_head,
        square_head,
        updated_head,
        updated_head.astype(LOW),
        moment_outward,
        square_outward,
        updated_outward,
        updated_outward.astype(LOW),
        moment_upward,
        square_upward,
        updated_upward,
        updated_upward.astype(LOW),
        moment_downward,
        square_downward,
        updated_downward,
        updated_downward.astype(LOW),
        moment_gains,
        square_gains,
        updated_gains,
        update_norms,
    )


def solution(mesh):
    paired = mesh.shape["dp"] == 4 and mesh.shape["mp"] == 8
    return jax.shard_map(
        on_device_paired if paired else on_device_general,
        mesh=mesh,
        in_specs=(
            P("dp", "mp", None),
            P("dp", None, None),
            P("dp", None),
            P("dp"),
            P("dp", "mp", None),
            P(None, "dp", "mp"),
            P(None, "dp", "mp"),
            P(None, "dp", "mp"),
            P("dp", None),
            P("dp", None),
            P("dp", None),
            P("dp", "mp"),
            P("dp", "mp"),
            P("dp", "mp"),
            P("mp", "dp"),
            P("mp", "dp"),
            P("mp", "dp"),
            P(),
            P(),
            P(),
        ),
        out_specs=(
            P("dp", "mp", None),
            P("dp", "mp", None),
            P(None, "dp", "mp"),
            P(None, "dp", "mp"),
            P(None, "dp", "mp"),
            P(None, "dp", "mp"),
            P("dp", None),
            P("dp", None),
            P("dp", None),
            P("dp", None),
            P("dp", "mp"),
            P("dp", "mp"),
            P("dp", "mp"),
            P("dp", "mp"),
            P("mp", "dp"),
            P("mp", "dp"),
            P("mp", "dp"),
            P("mp", "dp"),
            P(),
            P(),
            P(),
            P(),
        ),
        check_vma=False,
    )
```

```python
from functools import partial

import jax
import jax.numpy as jnp
from jax import lax
from jax.experimental import pallas as pl
from jax.experimental.pallas import tpu as pltpu
from jax.sharding import PartitionSpec as P

HEAD_DIM = 64
FF = 8192
PATCH = 64
STEP = 10


EPS_NORM = 1e-05
BETA_ONE = 0.9
BETA_TWO = 0.999
EPS_ADAM = 1e-06
DECAY_RATE = 0.01
STEP_RATE = 0.5


def layer_norm(inputs, gain_vector):
    centre = jnp.mean(inputs, axis=-1, keepdims=True)
    shifted = inputs - centre
    spread = jnp.mean(shifted * shifted, axis=-1, keepdims=True)
    return shifted * lax.rsqrt(spread + EPS_NORM) * gain_vector


def xpos_tables(length, head_size):
    halfway = head_size // 2
    pair_index = jnp.arange(halfway, dtype=jnp.float32)
    angular = jnp.exp(-(2.0 * pair_index / head_size) * jnp.log(10000.0))
    zeta_base = (2.0 * pair_index + 0.4 * head_size) / (1.4 * head_size)
    position = jnp.arange(length, dtype=jnp.float32)[:, None, None]
    return (
        jnp.cos(position * angular),
        jnp.sin(position * angular),
        position / 512.0 * jnp.log(zeta_base),
    )


def rotate(inputs, tables, polarity):
    cosine, sine_part, exponent = tables
    halfway = inputs.shape[-1] // 2
    factor = jnp.exp(polarity * exponent)
    leading = inputs[..., :halfway]
    behind = inputs[..., halfway:]
    return jnp.concatenate(
        [
            (leading * cosine - behind * sine_part) * factor,
            (behind * cosine + leading * sine_part) * factor,
        ],
        axis=-1,
    )


def merge_images(text_rows, image_rows, offsets, image_count, position):
    slot_index = jnp.arange(offsets.shape[0], dtype=jnp.int32)
    inside = (
        (position[:, None] >= offsets[None, :])
        & (position[:, None] < offsets[None, :] + PATCH)
        & (slot_index[None, :] < image_count)
    )
    picked = jnp.sum(
        jnp.where(inside, slot_index[None, :] * PATCH + position[:, None] - offsets[None, :], 0),
        axis=-1,
    )
    chosen = jnp.take(image_rows, picked, axis=0)
    covered = jnp.any(inside, axis=-1)
    return jnp.where(covered[:, None], chosen, text_rows)


def adapt_step(gradient, master, moment, square, decay_rate):
    moment_new = BETA_ONE * moment + (1.0 - BETA_ONE) * gradient
    square_new = BETA_TWO * square + (1.0 - BETA_TWO) * gradient * gradient
    direction = (
        moment_new
        / (1.0 - BETA_ONE**STEP)
        / (jnp.sqrt(square_new / (1.0 - BETA_TWO**STEP)) + EPS_ADAM)
        + decay_rate * master
    )
    return (moment_new, square_new, direction)


def trust_move(master, direction, weight_sum, update_sum):
    return master - STEP_RATE * jnp.sqrt(weight_sum) / (jnp.sqrt(update_sum) + EPS_ADAM) * direction


def gain_segments(entries, model_width):
    return jnp.stack(
        [
            jnp.sum(entries[:model_width]),
            jnp.sum(entries[model_width : 2 * model_width]),
            jnp.sum(entries[2 * model_width : 3 * model_width]),
            jnp.sum(entries[3 * model_width :]),
        ]
    )


def gain_spread(sums, model_width, hidden_width):
    return jnp.concatenate(
        [
            jnp.broadcast_to(sums[0], (model_width,)),
            jnp.broadcast_to(sums[1], (model_width,)),
            jnp.broadcast_to(sums[2], (model_width,)),
            jnp.broadcast_to(sums[3], (hidden_width,)),
        ]
    )


def pair_sums(master, direction):
    return jnp.stack([jnp.sum(master * master), jnp.sum(direction * direction)])[None]


def on_device_general(
    text_states,
    image_states,
    image_offsets,
    image_counts,
    output_grad,
    head_master,
    head_moment,
    head_square,
    outward_master,
    outward_moment,
    outward_square,
    upward_master,
    upward_moment,
    upward_square,
    downward_master,
    downward_moment,
    downward_square,
    gains_master,
    gains_moment,
    gains_square,
):
    groups = lax.axis_size("mp")
    model_rank = lax.axis_index("mp")
    seq_count, local_len, model_width = text_states.shape
    length = local_len * groups
    hidden_local = upward_master.shape[1]
    heads_local = head_master.shape[2] // HEAD_DIM
    tables = xpos_tables(length, HEAD_DIM)
    position = model_rank * local_len + jnp.arange(local_len, dtype=jnp.int32)
    merged = jax.vmap(
        lambda text_rows, image_rows, offsets, image_count: merge_images(
            text_rows, image_rows, offsets, image_count, position
        )
    )(text_states, image_states, image_offsets, image_counts).astype(jnp.float32)
    gain_in = gains_master[:model_width]
    gain_ctx = gains_master[model_width : 2 * model_width]
    gain_mid = gains_master[2 * model_width : 3 * model_width]
    hidden_start = 3 * model_width + model_rank * hidden_local
    gain_hidden = lax.dynamic_slice_in_dim(gains_master, hidden_start, hidden_local)
    head_weight_whole, outward_weight_whole, upward_weight_whole, down_weight_whole = (
        lax.all_gather(head_master.astype(jnp.bfloat16), "dp", axis=1, tiled=True),
        lax.all_gather(outward_master.astype(jnp.bfloat16), "dp", axis=0, tiled=True),
        lax.all_gather(upward_master.astype(jnp.bfloat16), "dp", axis=0, tiled=True),
        lax.all_gather(downward_master.astype(jnp.bfloat16), "dp", axis=1, tiled=True),
    )
    normed_low = layer_norm(merged, gain_in).astype(jnp.bfloat16)
    normed_rows_full, cotangent_rows_full = (
        lax.all_gather(normed_low, "mp", axis=1, tiled=True),
        lax.all_gather(output_grad, "mp", axis=1, tiled=True),
    )
    projected = jnp.einsum(
        "hvg,bga->bhva", normed_rows_full, head_weight_whole, preferred_element_type=jnp.float32
    )
    shaped = projected.reshape(3, seq_count, length, heads_local, HEAD_DIM)
    queries = rotate(shaped[0], tables, 1.0).astype(jnp.bfloat16)
    key_rows = rotate(shaped[1], tables, -1.0).astype(jnp.bfloat16)
    values = shaped[2].astype(jnp.bfloat16)
    block_len = min(512, length)
    block_count = length // block_len
    starts = jnp.arange(block_count, dtype=jnp.int32) * block_len
    key_place = jnp.arange(length, dtype=jnp.int32)

    def block_scores(query_block, start):
        scores = (
            jnp.einsum("sqhd,skhd->shqk", query_block, key_rows, preferred_element_type=jnp.float32)
            * 0.125
        )
        allowed = key_place[None, :] <= (start + jnp.arange(block_len, dtype=jnp.int32))[:, None]
        return jnp.where(allowed, scores, -1e30)

    def forward_block(start):
        query_block = lax.dynamic_slice_in_dim(queries, start, block_len, 1)
        scores = block_scores(query_block, start)
        highest = jnp.max(scores, axis=-1, keepdims=True)
        exponent = jnp.exp(scores - highest)
        total = jnp.sum(exponent, axis=-1, keepdims=True)
        attention = exponent / total
        context_block = jnp.einsum(
            "shqk,skhd->sqhd",
            attention.astype(jnp.bfloat16),
            values,
            preferred_element_type=jnp.float32,
        )
        return (context_block, highest[..., 0] + jnp.log(total[..., 0]))

    context_blocks, log_sums = lax.map(forward_block, starts)
    context = jnp.transpose(context_blocks, (1, 0, 2, 3, 4)).reshape(
        seq_count, length, heads_local * HEAD_DIM
    )
    context_rows = lax.all_to_all(
        context.astype(jnp.bfloat16), "mp", split_axis=1, concat_axis=2, tiled=True
    )
    context_in = context_rows.astype(jnp.float32)
    mixed_half_precision = layer_norm(context_in, gain_ctx).astype(jnp.bfloat16)
    middle = merged + jnp.einsum(
        "ymq,qc->ymc",
        mixed_half_precision,
        outward_weight_whole,
        preferred_element_type=jnp.float32,
    )
    lifted_low = layer_norm(middle, gain_mid).astype(jnp.bfloat16)
    lifted_rows_full = lax.all_gather(lifted_low, "mp", axis=1, tiled=True)
    hidden_rows = jnp.einsum(
        "orb,bg->org", lifted_rows_full, upward_weight_whole, preferred_element_type=jnp.float32
    )
    activated = jax.nn.gelu(hidden_rows, approximate=False)
    first_sum, second_sum = lax.psum(
        (jnp.sum(activated, axis=-1), jnp.sum(activated * activated, axis=-1)), "mp"
    )
    centre = first_sum / FF
    scale_inv = lax.rsqrt(second_sum / FF - centre * centre + EPS_NORM)[..., None]
    standard = (activated - centre[..., None]) * scale_inv
    squashed_half_precision = (standard * gain_hidden).astype(jnp.bfloat16)
    ffn_part = jnp.einsum(
        "wxp,pk->wxk",
        squashed_half_precision,
        down_weight_whole,
        preferred_element_type=jnp.float32,
    )
    ffn_rows = lax.psum_scatter(
        ffn_part.astype(jnp.bfloat16), "mp", scatter_dimension=1, tiled=True
    ).astype(jnp.float32)
    layer_output = (middle + ffn_rows).astype(jnp.bfloat16)
    down_grad = jnp.einsum(
        "uxy,uxo->yo",
        squashed_half_precision,
        cotangent_rows_full,
        preferred_element_type=jnp.float32,
    )
    squashed_grad = jnp.einsum(
        "yxr,ur->yxu", cotangent_rows_full, down_weight_whole, preferred_element_type=jnp.float32
    )
    hidden_gain_grad = jnp.sum(squashed_grad * standard, axis=(0, 1))
    scaled_grad = squashed_grad * gain_hidden
    mean_one, mean_two = (
        lax.psum(jnp.sum(scaled_grad, axis=-1).astype(jnp.bfloat16), "mp").astype(jnp.float32),
        lax.psum(jnp.sum(scaled_grad * standard, axis=-1).astype(jnp.bfloat16), "mp").astype(
            jnp.float32
        ),
    )
    activated_grad = (
        scaled_grad - mean_one[..., None] / FF - standard * (mean_two[..., None] / FF)
    ) * scale_inv
    gelu_out, gelu_back = jax.vjp(partial(jax.nn.gelu, approximate=False), hidden_rows)
    hidden_rows_grad = gelu_back(activated_grad)[0].astype(jnp.bfloat16)
    upward_gradient = jnp.einsum(
        "gki,gkt->it", lifted_rows_full, hidden_rows_grad, preferred_element_type=jnp.float32
    )
    lifted_part = jnp.einsum(
        "eiw,mw->eim", hidden_rows_grad, upward_weight_whole, preferred_element_type=jnp.float32
    )
    lifted_grad = lax.psum_scatter(lifted_part, "mp", scatter_dimension=1, tiled=True)
    norm_out, middle_back = jax.vjp(layer_norm, middle, gain_mid)
    middle_part, mid_gain_grad = middle_back(lifted_grad)
    middle_grad = output_grad.astype(jnp.float32) + middle_part
    middle_half_precision = middle_grad.astype(jnp.bfloat16)
    outward_part = jnp.einsum(
        "hyk,hyo->ko",
        mixed_half_precision,
        middle_half_precision,
        preferred_element_type=jnp.float32,
    )
    mixed_grad = jnp.einsum(
        "hox,kx->hok",
        middle_half_precision,
        outward_weight_whole,
        preferred_element_type=jnp.float32,
    )
    context_out, context_back = jax.vjp(layer_norm, context_in, gain_ctx)
    context_grad, ctx_gain_grad = context_back(mixed_grad)
    context_heads = lax.all_to_all(
        context_grad.astype(jnp.bfloat16), "mp", split_axis=2, concat_axis=1, tiled=True
    )
    grad_heads = context_heads.reshape(seq_count, length, heads_local, HEAD_DIM)

    def backward_block(totals, inputs):
        key_total, value_total = totals
        start, log_block = inputs
        query_block = lax.dynamic_slice_in_dim(queries, start, block_len, 1)
        grad_block = lax.dynamic_slice_in_dim(grad_heads, start, block_len, 1)
        scores = block_scores(query_block, start)
        attention = jnp.exp(scores - log_block[..., None])
        prob_grad = jnp.einsum(
            "sqhd,skhd->shqk", grad_block, values, preferred_element_type=jnp.float32
        )
        row_dot = jnp.sum(attention * prob_grad, axis=-1, keepdims=True)
        score_low = (attention * (prob_grad - row_dot)).astype(jnp.bfloat16)
        query_turned = (
            jnp.einsum("shqk,skhd->sqhd", score_low, key_rows, preferred_element_type=jnp.float32)
            * 0.125
        )
        key_total = (
            key_total
            + jnp.einsum(
                "shqk,sqhd->skhd", score_low, query_block, preferred_element_type=jnp.float32
            )
            * 0.125
        )
        value_total = value_total + jnp.einsum(
            "shqk,sqhd->skhd",
            attention.astype(jnp.bfloat16),
            grad_block,
            preferred_element_type=jnp.float32,
        )
        return ((key_total, value_total), query_turned)

    zero_heads = jnp.zeros((seq_count, length, heads_local, HEAD_DIM), jnp.float32)
    (key_turned, value_grad), query_blocks = lax.scan(
        backward_block, (zero_heads, zero_heads), (starts, log_sums)
    )
    query_turned = jnp.transpose(query_blocks, (1, 0, 2, 3, 4)).reshape(
        seq_count, length, heads_local, HEAD_DIM
    )
    query_out, query_back = jax.vjp(lambda inputs: rotate(inputs, tables, 1.0), shaped[0])
    key_out, key_back = jax.vjp(lambda inputs: rotate(inputs, tables, -1.0), shaped[1])
    projection_gradient = (
        jnp.stack([query_back(query_turned)[0], key_back(key_turned)[0], value_grad])
        .astype(jnp.bfloat16)
        .reshape(3, seq_count, length, heads_local * HEAD_DIM)
    )
    head_grad = jnp.einsum(
        "fbn,ufbj->unj", normed_rows_full, projection_gradient, preferred_element_type=jnp.float32
    )
    normed_part = jnp.einsum(
        "acqr,aur->cqu", projection_gradient, head_weight_whole, preferred_element_type=jnp.float32
    )
    normed_grad = lax.psum_scatter(
        normed_part.astype(jnp.bfloat16), "mp", scatter_dimension=1, tiled=True
    ).astype(jnp.float32)
    input_out, input_back = jax.vjp(layer_norm, merged, gain_in)
    merged_part, in_gain_grad = input_back(normed_grad)
    input_grad = middle_grad + merged_part
    head_sum, outward_sum, upward_sum, downward_sum = (
        lax.psum_scatter(
            head_grad.astype(jnp.bfloat16), "dp", scatter_dimension=1, tiled=True
        ).astype(jnp.float32),
        lax.psum_scatter(
            outward_part.astype(jnp.bfloat16), "dp", scatter_dimension=0, tiled=True
        ).astype(jnp.float32),
        lax.psum_scatter(
            upward_gradient.astype(jnp.bfloat16), "dp", scatter_dimension=0, tiled=True
        ).astype(jnp.float32),
        lax.psum_scatter(
            down_grad.astype(jnp.bfloat16), "dp", scatter_dimension=1, tiled=True
        ).astype(jnp.float32),
    )
    outward_sum = lax.psum(outward_sum.astype(jnp.bfloat16), "mp").astype(jnp.float32)
    moment_head, square_head, head_dir = adapt_step(
        head_sum, head_master, head_moment, head_square, DECAY_RATE
    )
    moment_outward, square_outward, outward_dir = adapt_step(
        outward_sum, outward_master, outward_moment, outward_square, DECAY_RATE
    )
    moment_upward, square_upward, upward_dir = adapt_step(
        upward_sum, upward_master, upward_moment, upward_square, DECAY_RATE
    )
    moment_downward, square_downward, downward_dir = adapt_step(
        downward_sum, downward_master, downward_moment, downward_square, DECAY_RATE
    )
    owner = (model_rank == 0).astype(jnp.float32)
    head_part = jnp.stack(
        [
            jnp.sum(head_master * head_master, axis=(1, 2)),
            jnp.sum(head_dir * head_dir, axis=(1, 2)),
        ],
        axis=-1,
    )
    norm_part = jnp.concatenate(
        [
            head_part,
            pair_sums(outward_master, outward_dir) * owner,
            pair_sums(upward_master, upward_dir),
            pair_sums(downward_master, downward_dir),
        ],
        axis=0,
    )
    gains_part = jnp.concatenate(
        [in_gain_grad, ctx_gain_grad, mid_gain_grad, jnp.zeros((FF,), jnp.float32)]
    )
    gains_part = lax.dynamic_update_slice(gains_part, hidden_gain_grad, (hidden_start,))
    gains_sum, norm_sums = lax.psum((gains_part, norm_part), ("dp", "mp"))
    moment_gains, square_gains, gains_dir = adapt_step(
        gains_sum, gains_master, gains_moment, gains_square, 0.0
    )
    gains_sums = jnp.stack(
        [
            gain_segments(gains_master * gains_master, model_width),
            gain_segments(gains_dir * gains_dir, model_width),
        ],
        axis=-1,
    )
    updated_head = trust_move(
        head_master, head_dir, norm_sums[0:3, 0][:, None, None], norm_sums[0:3, 1][:, None, None]
    )
    updated_outward = trust_move(outward_master, outward_dir, norm_sums[3, 0], norm_sums[3, 1])
    updated_upward = trust_move(upward_master, upward_dir, norm_sums[4, 0], norm_sums[4, 1])
    updated_downward = trust_move(downward_master, downward_dir, norm_sums[5, 0], norm_sums[5, 1])
    updated_gains = trust_move(
        gains_master,
        gains_dir,
        gain_spread(gains_sums[:, 0], model_width, FF),
        gain_spread(gains_sums[:, 1], model_width, FF),
    )
    update_norms = jnp.sqrt(jnp.concatenate([norm_sums, gains_sums], axis=0))
    return (
        layer_output,
        input_grad,
        moment_head,
        square_head,
        updated_head,
        updated_head.astype(jnp.bfloat16),
        moment_outward,
        square_outward,
        updated_outward,
        updated_outward.astype(jnp.bfloat16),
        moment_upward,
        square_upward,
        updated_upward,
        updated_upward.astype(jnp.bfloat16),
        moment_downward,
        square_downward,
        updated_downward,
        updated_downward.astype(jnp.bfloat16),
        moment_gains,
        square_gains,
        updated_gains,
        update_norms,
    )


SHARE = 0.3
LOG2E = 1.4426950408889634
LANES = 128
NT = (((1,), (1,)), ((), ()))
NN = (((1,), (0,)), ((), ()))
LOW = jnp.bfloat16
WIDE = jnp.float32
ONCE = pl.Buffered(1)
MESH = pl.DeviceIdType.MESH
ANYWHERE = pl.BlockSpec(memory_space=pl.ANY)


def like(value):
    return jax.ShapeDtypeStruct(value.shape, value.dtype)


def dot(left, right, dims):
    return lax.dot_general(left, right, dims, preferred_element_type=WIDE)


def kernel_call(body, grid, in_specs, out_specs, out_shape, scratch, flops, moved, operands, done=(), carry=()):
    count, extra, outs = len(operands), len(done) + len(carry), len(out_specs)

    def whole(*refs):
        inner = refs[count + extra :]
        body(*refs[:count], *inner[:outs], *inner[outs + len(carry) :])

    return pl.pallas_call(
        whole,
        grid_spec=pltpu.PrefetchScalarGridSpec(
            num_scalar_prefetch=1,
            grid=grid,
            in_specs=list(in_specs) + [ANYWHERE] * extra,
            out_specs=list(out_specs) + [ANYWHERE] * len(carry),
            scratch_shapes=scratch,
        ),
        out_shape=list(out_shape) + [like(value) for value in carry],
        input_output_aliases={count + len(done) + n: outs + n for n in range(len(carry))},
        compiler_params=pltpu.CompilerParams(vmem_limit_bytes=56 << 20),
        cost_estimate=pl.CostEstimate(flops=int(flops * SHARE), bytes_accessed=int(moved * SHARE), transcendentals=0),
    )(*operands, *done, *carry)


def mate(rank, j):
    return (rank, rank + 1 - 2 * (rank % 2), (rank + 2) % 4, 3 - rank)[j]


def hand_on(value, done):
    return pl.pallas_call(
        lambda *refs: None,
        in_specs=[ANYWHERE] * (1 + len(done)),
        out_specs=ANYWHERE,
        out_shape=like(value),
        input_output_aliases={0: 0},
    )(value, *done)


def own_rows(sub, rank, j, b):
    return pl.ds(pl.multiple_of(b * 4 * sub + mate(rank, j) * sub, sub), sub)


def own_block(place, k, width):
    return pl.ds(pl.multiple_of((place ^ k) * width, width), width)


def swap_halves(block):
    low = lax.broadcasted_iota(jnp.int32, (1, LANES), 1) % HEAD_DIM < HEAD_DIM // 2
    return jnp.where(low, pltpu.roll(block, LANES - HEAD_DIM // 2, 1), pltpu.roll(block, HEAD_DIM // 2, 1))


def project_kernel(ids, x, w0, w1, w2, w3, cq, sq, ck, sk, q, k, v):
    depth = w0.shape[1]
    width = w0.shape[2]
    for f, (out, c, s) in enumerate(((q, cq, sq), (k, ck, sk), (v, None, None))):
        total = None
        for n, w in enumerate((w0, w1, w2, w3)):
            part = dot(x[:, own_block(ids[1], n, depth)], w[f], NN)
            total = part if total is None else total + part
        for p in range(width // LANES):
            here = slice(p * LANES, (p + 1) * LANES)
            block = total[:, here]
            if c is not None:
                block = block * c[...] + swap_halves(block) * s[...]
            out[:, here] = block.astype(LOW)


def quarters(weight):
    if isinstance(weight, list):
        spec = pl.BlockSpec(weight[0].shape, lambda b, ids: (0, 0, 0), pipeline_mode=ONCE)
        return weight, [spec] * 4
    kinds, model, width = weight.shape
    return [weight] * 4, [
        pl.BlockSpec((kinds, model // 4, width), partial(lambda n, b, ids: (0, ids[1] ^ n, 0), n), pipeline_mode=ONCE)
        for n in range(4)
    ]


def project(ids, x, weight, tables, j, done=(), carry=()):
    rows, model = x.shape
    sub = rows // 2
    weights, specs = quarters(weight)
    width = weights[0].shape[2]
    table = pl.BlockSpec((sub, LANES), lambda b, ids: (b * 4 + (ids[0] ^ j), 0))
    out = pl.BlockSpec((sub, width), lambda b, ids: (b, 0))
    return kernel_call(
        project_kernel,
        (2,),
        [pl.BlockSpec((sub, model), lambda b, ids: (b, 0))] + specs + [table] * 4,
        [out] * 3,
        [jax.ShapeDtypeStruct((rows, width), LOW)] * 3,
        [],
        6 * rows * model * width,
        6 * model * width + 8 * rows * model,
        (ids, x, *weights, *tables),
        done,
        carry,
    )


def attend_kernel(ids, *refs, bq, bk):
    q_, k_, v_, o_, lse_ref = refs[0:4], refs[4:8], refs[8:12], refs[12:16], refs[16]
    qs, ks, vt, os = refs[17:]
    rank = ids[0]
    length = qs.shape[0]
    sub = q_[0].shape[0] // 2
    for j in range(4):
        for b in range(2):
            rows = own_rows(sub, rank, j, b)
            here = slice(b * sub, (b + 1) * sub)
            qs[rows, :] = q_[j][here, :]
            ks[rows, :] = k_[j][here, :]
            vt[:, rows] = v_[j][here, :].T
    first = lax.broadcasted_iota(jnp.int32, (1, LANES), 1) < HEAD_DIM
    ratio = bq // bk

    def q_block(i, _):
        here = pl.ds(pl.multiple_of(i * bq, bq), bq)
        q = qs[here, :]
        zero = jnp.zeros_like(q)
        parted = (jnp.where(first, q, zero), jnp.where(first, zero, q))

        def step(j, carry, diagonal):
            at = pl.multiple_of(j * bk, bk)
            k = ks[pl.ds(at, bk), :]
            out = []
            for h in range(2):
                highest, total, sums = carry[h]
                scores = dot(k, parted[h], NT) * (0.125 * LOG2E)
                if diagonal is not None:
                    key = diagonal * bk + lax.broadcasted_iota(jnp.int32, (bk, bq), 0)
                    scores = jnp.where(key <= lax.broadcasted_iota(jnp.int32, (bk, bq), 1), scores, -1e30)
                new = jnp.maximum(highest, jnp.max(scores, axis=0, keepdims=True))
                probs = jnp.exp2(scores - new)
                scale = jnp.exp2(highest - new)
                total = total * scale + jnp.sum(probs, axis=0, keepdims=True)
                rows = vt[h * HEAD_DIM : (h + 1) * HEAD_DIM, pl.ds(at, bk)]
                out.append((new, total, sums * scale + dot(rows, probs.astype(LOW), NN)))
            return tuple(out)

        start = tuple(
            (jnp.full((1, bq), -1e30, WIDE), jnp.zeros((1, bq), WIDE), jnp.zeros((HEAD_DIM, bq), WIDE))
            for _ in range(2)
        )
        carry = lax.fori_loop(0, i * ratio, lambda j, c: step(j, c, None), start)
        for d in range(ratio):
            carry = step(i * ratio + d, carry, d)
        turned = jnp.concatenate([carry[h][2] / carry[h][1] for h in range(2)], axis=0)
        os[here, :] = turned.T.astype(LOW)
        for h in range(2):
            lse_ref[0, h : h + 1, here] = carry[h][0] + jnp.log2(carry[h][1])
        return 0

    lax.fori_loop(0, length // bq, q_block, 0)
    for j in range(4):
        for b in range(2):
            o_[j][b * sub : (b + 1) * sub, :] = os[own_rows(sub, rank, j, b), :]


def attend(ids, queries, keys, values, done=(), carry=()):
    rows, width = queries[0].shape
    length, pairs = rows * 4, width // LANES
    chunk = pl.BlockSpec((rows, LANES), lambda p, ids: (0, p))
    low = pltpu.VMEM((length, LANES), LOW)
    result = kernel_call(
        partial(attend_kernel, bq=min(1024, length), bk=min(512, length)),
        (pairs,),
        [chunk] * 12,
        [chunk] * 4 + [pl.BlockSpec((1, 2, length), lambda p, ids: (p, 0, 0))],
        [jax.ShapeDtypeStruct((rows, width), LOW)] * 4 + [jax.ShapeDtypeStruct((pairs, 2, length), WIDE)],
        [low, low, pltpu.VMEM((LANES, length), LOW), low],
        40e9,
        10e6,
        (ids, *queries, *keys, *values),
        done,
        carry,
    )
    return result[:4], result[4], *result[5:]


def attend_back_kernel(*refs, bq, bk):
    q_, k_, v_, d_, o_ = refs[0:4], refs[4:8], refs[8:12], refs[12:16], refs[16:20]
    lse_ref, cq, sq, ck, sk, away = refs[20:26]
    dq_, dk_, dv_, back = refs[-15:-11]
    qs, ks, vs, ds, kt, dqt, dks, dvs, delta, sent, got = refs[-11:]
    over_high = partners()[4]
    crossing = remote(away, back, sent, got, over_high)

    @pl.when(pl.program_id(0) == 0)
    def _():
        greet((over_high,))
        crossing.start()

    rank = lax.axis_index("mp") % 4
    length = qs.shape[0]
    sub = q_[0].shape[0] // 2
    for j in range(4):
        for b in range(2):
            rows = own_rows(sub, rank, j, b)
            here = slice(b * sub, (b + 1) * sub)
            qs[rows, :] = q_[j][here, :]
            ks[rows, :] = k_[j][here, :]
            kt[:, rows] = k_[j][here, :].T
            vs[rows, :] = v_[j][here, :]
            ds[rows, :] = d_[j][here, :]
            product = (d_[j][here, :].astype(WIDE) * o_[j][here, :].astype(WIDE)).T
            delta[0:1, rows] = jnp.sum(product[:HEAD_DIM], axis=0, keepdims=True)
            delta[1:2, rows] = jnp.sum(product[HEAD_DIM:], axis=0, keepdims=True)
    first = lax.broadcasted_iota(jnp.int32, (1, LANES), 1) < HEAD_DIM
    dqt[...] = jnp.zeros_like(dqt)

    def k_block(j, _):
        at = pl.ds(pl.multiple_of(j * bk, bk), bk)
        k = ks[at, :]
        v = vs[at, :]

        def step(i, carry, diagonal):
            dk, dv = carry
            here = pl.ds(pl.multiple_of(i * bq, bq), bq)
            q, do = qs[here, :], ds[here, :]
            zero = jnp.zeros_like(q)
            for h in range(2):
                lanes = slice(h * HEAD_DIM, (h + 1) * HEAD_DIM)
                q_own = jnp.where(first, q, zero) if h == 0 else jnp.where(first, zero, q)
                do_own = jnp.where(first, do, zero) if h == 0 else jnp.where(first, zero, do)
                scores = dot(k, q_own, NT) * (0.125 * LOG2E) - lse_ref[0, h : h + 1, here]
                if diagonal:
                    key = lax.broadcasted_iota(jnp.int32, (bk, bq), 0)
                    scores = jnp.where(key <= lax.broadcasted_iota(jnp.int32, (bk, bq), 1), scores, -1e30)
                probs = jnp.exp2(scores)
                prob_grad = dot(v, do_own, NT)
                grad = (probs * (prob_grad - delta[h : h + 1, here])).astype(LOW)
                dv = dv + dot(probs.astype(LOW), do_own, NN)
                dk = dk + dot(grad, q_own, NN)
                dqt[lanes, here] += dot(kt[lanes, at], grad, NN)
            return dk, dv

        zeros = jnp.zeros((bk, LANES), WIDE)
        carry = step(j, (zeros, zeros), True)
        dk, dv = lax.fori_loop(j + 1, length // bq, lambda i, c: step(i, c, False), carry)
        dks[at, :] = dk * 0.125
        dvs[at, :] = dv.astype(LOW)
        return 0

    lax.fori_loop(0, length // bk, k_block, 0)
    for j in range(4):
        for b in range(2):
            rows = own_rows(sub, rank, j, b)
            here = slice(b * sub, (b + 1) * sub)
            query_grad = dqt[:, rows].T * 0.125
            dq_[j, here, :] = (query_grad * cq[rows, :] - swap_halves(query_grad) * sq[rows, :]).astype(LOW)
            key_grad = dks[rows, :]
            dk_[j, here, :] = (key_grad * ck[rows, :] - swap_halves(key_grad) * sk[rows, :]).astype(LOW)
            dv_[j, here, :] = dvs[rows, :]

    @pl.when(pl.program_id(0) == pl.num_programs(0) - 1)
    def _():
        crossing.wait()


def attend_back(queries, keys, values, cotangents, contexts, lse, tables, away, number, done):
    rows, width = queries[0].shape
    length, pairs = rows * 4, width // LANES
    chunk = pl.BlockSpec((rows, LANES), lambda p: (0, p))
    whole = pl.BlockSpec((length, LANES), lambda p: (0, 0), pipeline_mode=ONCE)
    low = pltpu.VMEM((length, LANES), LOW)
    block = min(512, length)
    return pl.pallas_call(
        partial(attend_back_kernel, bq=block, bk=block),
        grid=(pairs,),
        in_specs=[chunk] * 20 + [pl.BlockSpec((1, 2, length), lambda p: (p, 0, 0))]
        + [whole] * 4
        + [ANYWHERE] * (1 + len(done)),
        out_specs=[pl.BlockSpec((4, rows, LANES), lambda p: (0, 0, p))] * 3 + [ANYWHERE],
        out_shape=[jax.ShapeDtypeStruct((4, rows, width), LOW)] * 3 + [like(away)],
        scratch_shapes=[
            low,
            low,
            low,
            low,
            pltpu.VMEM((LANES, length), LOW),
            pltpu.VMEM((LANES, length), WIDE),
            pltpu.VMEM((length, LANES), WIDE),
            low,
            pltpu.VMEM((2, length), WIDE),
            pltpu.SemaphoreType.DMA,
            pltpu.SemaphoreType.DMA,
        ],
        compiler_params=pltpu.CompilerParams(
            collective_id=number, has_side_effects=True, vmem_limit_bytes=56 << 20
        ),
        cost_estimate=pl.CostEstimate(flops=40 * 10**9, bytes_accessed=20 << 20, transcendentals=0),
    )(*queries, *keys, *values, *cotangents, *contexts, lse, *tables, away, *done)


def centred(block):
    shifted = block - jnp.mean(block, axis=-1, keepdims=True)
    spread = jnp.mean(shifted * shifted, axis=-1, keepdims=True)
    scale = lax.rsqrt(spread + EPS_NORM)
    return shifted * scale, scale


def norm_back(standard, scale, gain, grad):
    scaled = grad * gain
    first = jnp.mean(scaled, axis=-1, keepdims=True)
    second = jnp.mean(scaled * standard, axis=-1, keepdims=True)
    return scale * (scaled - first - standard * second)


def context_lanes(ids, j, side, width):
    half = ids[2] ^ side
    return pl.ds(pl.multiple_of(half * 4 * width + (ids[0] ^ j) * width, width), width)


def mid_kernel(ids, *refs):
    pieces = refs[:8]
    merged, weights, (g_ctx, g_mid, ctx, mixed, middle, lifted) = refs[8], sheets(refs[9:13]), refs[13:]
    width = pieces[0].shape[1]
    for n, c in enumerate(pieces):
        ctx[:, context_lanes(ids, n % 4, n // 4, width)] = c[...]
    standard, _ = centred(ctx[...].astype(WIDE))
    mixed[...] = (standard * g_ctx[...]).astype(LOW)
    depth, half = weights[0].shape
    for n in range(2):
        lanes = core_lanes(ids, n, half)
        total = merged[:, lanes].astype(WIDE)
        for k in range(4):
            total = total + dot(mixed[:, own_block(ids[1], k, depth)], weights[4 * n + k][...], NN)
        middle[:, lanes] = total
    standard, _ = centred(middle[...])
    lifted[...] = (standard * g_mid[...]).astype(LOW)


def sheets(refs):
    own, pieces, other, others = refs
    return [own] + [pieces.at[n] for n in range(3)] + [other] + [others.at[n] for n in range(3)]


def core_lanes(ids, n, half):
    return pl.ds(pl.multiple_of((ids[0] % 2 ^ n) * half, half), half)


def mid_forward(ids, contexts, merged, weights, g_ctx, g_mid, carry):
    rows, model = merged.shape
    specs = [pl.BlockSpec(w.shape, partial(lambda n, b, ids: (0,) * n, w.ndim), pipeline_mode=ONCE) for w in weights]
    block = min(256, rows)
    line = lambda width: pl.BlockSpec((block, width), lambda b, ids: (b, 0))
    gain = pl.BlockSpec((1, model), lambda b, ids: (0, 0))
    shape = lambda kind: jax.ShapeDtypeStruct((rows, model), kind)
    return kernel_call(
        mid_kernel,
        (rows // block,),
        [line(contexts[0].shape[1])] * 8 + [line(model)] + specs + [gain] * 2,
        [line(model)] * 4,
        [shape(LOW), shape(LOW), shape(WIDE), shape(LOW)],
        [],
        2 * rows * model * model,
        2 * model * model + 14 * rows * model,
        (ids, *contexts, merged, *weights, g_ctx, g_mid),
        (),
        carry,
    )


def mid_back_kernel(ids, *refs):
    a, r, middle, og, ctx = refs[:5]
    weights, (g_mid, g_ctx, middle_grad, middle_low) = sheets(refs[5:9]), refs[9:13]
    pieces, gains, mixed_grad = refs[13:21], refs[21], refs[22]
    grad = a[...].astype(WIDE) + r[...].astype(WIDE)
    standard, scale = centred(middle[...])

    @pl.when(pl.program_id(0) == 0)
    def _():
        gains[...] = jnp.zeros_like(gains)

    gains[0:1, :] += jnp.sum(grad * standard, axis=0, keepdims=True)
    total = og[...].astype(WIDE) + norm_back(standard, scale, g_mid[...], grad)
    middle_grad[...] = total
    middle_low[...] = total.astype(LOW)
    depth, half = weights[0].shape
    own, other = middle_low[:, core_lanes(ids, 0, half)], middle_low[:, core_lanes(ids, 1, half)]
    for k in range(4):
        mixed_grad[:, own_block(ids[1], k, depth)] = dot(own, weights[k][...], NT) + dot(other, weights[4 + k][...], NT)
    grad = mixed_grad[...]
    standard, scale = centred(ctx[...].astype(WIDE))
    gains[1:2, :] += jnp.sum(grad * standard, axis=0, keepdims=True)
    mixed_grad[...] = norm_back(standard, scale, g_ctx[...], grad)
    width = pieces[0].shape[1]
    for n, d in enumerate(pieces):
        d[...] = mixed_grad[:, context_lanes(ids, n % 4, n // 4, width)].astype(LOW)


def mid_backward(ids, parts, middle, og, ctx, weights, g_mid, g_ctx):
    rows, model = middle.shape
    specs = [pl.BlockSpec(w.shape, partial(lambda n, b, ids: (0,) * n, w.ndim), pipeline_mode=ONCE) for w in weights]
    block = min(256, rows)
    line = lambda width: pl.BlockSpec((block, width), lambda b, ids: (b, 0))
    gain = pl.BlockSpec((1, model), lambda b, ids: (0, 0))
    shape = lambda width, kind: jax.ShapeDtypeStruct((rows, width), kind)
    result = kernel_call(
        mid_back_kernel,
        (rows // block,),
        [line(model)] * 5 + specs + [gain] * 2,
        [line(model)] * 2 + [line(model // 8)] * 8 + [pl.BlockSpec((8, model), lambda b, ids: (0, 0))],
        [shape(model, WIDE), shape(model, LOW)]
        + [shape(model // 8, LOW)] * 8
        + [jax.ShapeDtypeStruct((8, model), WIDE)],
        [pltpu.VMEM((block, model), WIDE)],
        2 * rows * model * model,
        2 * model * model + 18 * rows * model,
        (ids, *parts, middle, og, ctx, *weights, g_mid, g_ctx),
    )
    return result[0], result[1], result[2:6], result[6:10], result[10]


def gelu_parts(hidden):
    share = 0.5 + 0.5 * lax.erf(hidden * 0.7071067811865476)
    return hidden * share, share


def gelu_slope(hidden, share):
    return share + hidden * (0.3989422804014327 * jnp.exp(-0.5 * hidden * hidden))


def fold(block):
    out = block[..., :LANES]
    for p in range(1, block.shape[-1] // LANES):
        out = out + block[..., p * LANES : (p + 1) * LANES]
    return out


def halves(count, rows_first):
    if rows_first:
        return (
            lambda u, ids: (jnp.minimum(u, count - 1), 0),
            lambda u, ids: (jnp.maximum(u - count, 0), 0),
        )
    return (
        lambda u, ids: (0, jnp.minimum(u, count - 1)),
        lambda u, ids: (0, jnp.maximum(u - count, 0)),
    )


def each_half(work, own, got):
    near = pl.program_id(0) < pl.num_programs(0) // 2

    @pl.when(near)
    def _():
        work(own)

    @pl.when(jnp.logical_not(near))
    def _():
        work(got)


def remote(source, target, sent, got, device):
    return pltpu.make_async_remote_copy(
        src_ref=source, dst_ref=target, send_sem=sent, recv_sem=got, device_id=device, device_id_type=MESH
    )


def ffn_up_kernel(
    lifted, up_own, up_got, act, slope, sums, lifted_all, x, acc, sent, got, local
):
    j, u = pl.program_id(0), pl.program_id(1)
    rows = x.shape[0]
    half = rows // 2
    _, _, over_core, over_low, _ = partners()
    parts = [pl.ds(b * half, half) for b in range(2)]

    def moves(source, whole, base):
        near = remote(source, whole.at[0], sent.at[base], got.at[base], over_core)
        far = [
            remote(source.at[part], whole.at[1, part], sent.at[base + 1 + b], got.at[base + 1 + b], over_low)
            for b, part in enumerate(parts)
        ]
        last = [
            remote(whole.at[1, part], whole.at[2, part], sent.at[base + 3 + b], got.at[base + 3 + b], over_core)
            for b, part in enumerate(parts)
        ]
        return near, far, last

    near, far, last = moves(lifted, lifted_all, 0)

    def load(source):
        copy = pltpu.make_async_copy(source, x, local)
        copy.start()
        copy.wait()

    @pl.when(u == 0)
    def _():
        acc[...] = jnp.zeros_like(acc)

    @pl.when((j == 0) & (u == 0))
    def _():
        greet((over_core, over_low))
        for copy in (*far, near):
            copy.start()
        load(lifted)

    @pl.when((j == 1) & (u == 0))
    def _():
        near.wait()
        load(lifted_all.at[0])

    @pl.when((j == 2) & (u == 0))
    def _():
        for copy, onward in zip(far, last):
            copy.wait()
            onward.start()
        load(lifted_all.at[1])

    @pl.when((j == 3) & (u == 0))
    def _():
        for copy in last:
            copy.wait()
        load(lifted_all.at[2])

    def work(up):
        for b in range(2):
            here = slice(b * half, (b + 1) * half)
            h = dot(x[here, :], up[...], NN)
            activated, share = gelu_parts(h)
            low = activated.astype(LOW)
            act[0, here, :] = low
            slope[0, here, :] = gelu_slope(h, share).astype(LOW)
            activated = low.astype(WIDE)
            acc[0, here, :] += fold(activated)
            acc[1, here, :] += fold(activated * activated)

    steps = pl.num_programs(1)
    pl.when(u < steps // 2)(lambda: work(up_own))
    pl.when(u >= steps // 2)(lambda: work(up_got))

    @pl.when(u == steps - 1)
    def _():
        for n in range(2):
            sums[0, n : n + 1, :] = jnp.sum(acc[n].T, axis=0, keepdims=True)
        sums[0, 2:8, :] = jnp.zeros_like(sums[0, 2:8, :])


def in_halves(count, rows_first):
    near, far = (lambda u: jnp.minimum(u, count - 1)), (lambda u: jnp.maximum(u - count, 0))
    if rows_first:
        return [lambda j, u: (near(u), 0), lambda j, u: (far(u), 0)]
    return [lambda j, u: (0, near(u)), lambda j, u: (0, far(u))]


def ffn_up(lifted, upward):
    rows, model = lifted.shape
    units = 2 * upward[0].shape[1]
    block = min(512, units // 2)
    count = units // 2 // block
    out = pl.BlockSpec((1, rows, block), lambda j, u: (j, 0, u))
    kept = jax.ShapeDtypeStruct((4, rows, units), LOW)
    others = jax.ShapeDtypeStruct((3, rows, model), LOW)
    return pl.pallas_call(
        ffn_up_kernel,
        grid=(4, 2 * count),
        in_specs=[ANYWHERE] + [pl.BlockSpec((model, block), at) for at in in_halves(count, False)],
        out_specs=[out] * 2 + [pl.BlockSpec((1, 8, rows), lambda j, u: (j, 0, 0)), ANYWHERE],
        out_shape=[kept] * 2 + [jax.ShapeDtypeStruct((4, 8, rows), WIDE), others],
        scratch_shapes=[
            pltpu.VMEM((rows, model), LOW),
            pltpu.VMEM((2, rows, LANES), WIDE),
            pltpu.SemaphoreType.DMA((5,)),
            pltpu.SemaphoreType.DMA((5,)),
            pltpu.SemaphoreType.DMA,
        ],
        compiler_params=pltpu.CompilerParams(collective_id=2, has_side_effects=True, vmem_limit_bytes=56 << 20),
        cost_estimate=pl.CostEstimate(flops=80 * 10**9, bytes_accessed=100 << 20, transcendentals=0),
    )(lifted, *upward)


def ffn_back_kernel(og, near, far, last, down_own, down_got, act, gain, squashed_grad, sums, x, acc, local):
    j, u = pl.program_id(0), pl.program_id(1)
    rows = x.shape[0]
    half = rows // 2

    @pl.when(u == 0)
    def _():
        acc[...] = jnp.zeros_like(acc)

    def load(source):
        copy = pltpu.make_async_copy(source, x, local)
        copy.start()
        copy.wait()

    for n, source in enumerate((og, near, far, last)):
        pl.when((u == 0) & (j == n))(partial(load, source))

    def work(down):
        for b in range(2):
            here = slice(b * half, (b + 1) * half)
            s = dot(x[here, :], down[...], NT).astype(LOW)
            squashed_grad[0, here, :] = s
            scaled = s.astype(WIDE) * gain[...]
            acc[0, here, :] += fold(scaled)
            acc[1, here, :] += fold(scaled * act[0, here, :].astype(WIDE))

    steps = pl.num_programs(1)
    pl.when(u < steps // 2)(lambda: work(down_own))
    pl.when(u >= steps // 2)(lambda: work(down_got))

    @pl.when(u == steps - 1)
    def _():
        sums[0, 0:2, :] = jnp.zeros_like(sums[0, 0:2, :])
        for n in range(2):
            sums[0, n + 2 : n + 3, :] = jnp.sum(acc[n].T, axis=0, keepdims=True)
        sums[0, 4:8, :] = jnp.zeros_like(sums[0, 4:8, :])


def ffn_back(og, others, downward, act, gain):
    rows, model = og.shape
    units = act.shape[2]
    block = min(512, units // 2)
    count = units // 2 // block
    line = pl.BlockSpec((1, rows, block), lambda j, u: (j, 0, u))
    return pl.pallas_call(
        ffn_back_kernel,
        grid=(4, 2 * count),
        in_specs=[ANYWHERE] * 4
        + [pl.BlockSpec((block, model), at) for at in in_halves(count, True)]
        + [line, pl.BlockSpec((1, block), lambda j, u: (0, u))],
        out_specs=[line, pl.BlockSpec((1, 8, rows), lambda j, u: (j, 0, 0))],
        out_shape=[like(act), jax.ShapeDtypeStruct((4, 8, rows), WIDE)],
        scratch_shapes=[
            pltpu.VMEM((rows, model), LOW),
            pltpu.VMEM((2, rows, LANES), WIDE),
            pltpu.SemaphoreType.DMA,
        ],
        compiler_params=pltpu.CompilerParams(vmem_limit_bytes=56 << 20),
        cost_estimate=pl.CostEstimate(flops=60 * 10**9, bytes_accessed=100 << 20, transcendentals=0),
    )(og, *others, *downward, act, gain)


def ffn_second_kernel(
    act,
    slope,
    squashed_grad,
    sums,
    gain,
    up_own,
    up_got,
    squashed,
    hidden_grad,
    kept,
    arrived,
    gains,
    acc,
    send_core,
    got_core,
    send_low,
    sent,
    got,
    *,
    hidden_width,
):
    n, u = pl.program_id(0), pl.program_id(1)
    steps = pl.num_programs(1)
    rows, block = act.shape[1:]
    half = rows // 2
    _, _, over_core, over_low, _ = partners()
    to_core = [remote(send_core.at[b], got_core.at[b], sent.at[b], got.at[b], over_core) for b in range(2)]
    to_low = remote(send_low, arrived, sent.at[2], got.at[2], over_low)

    @pl.when((n == 0) & (u == 0))
    def _():
        greet((over_core, over_low))
        gains[...] = jnp.zeros_like(gains)

    @pl.when(u == 0)
    def _():
        acc[...] = jnp.zeros_like(acc)

    columns = sums[0].T
    lanes = pl.ds(pl.multiple_of(u * block, block), block)

    def work(up):
        for b in range(2):
            here = slice(b * half, (b + 1) * half)
            centre = columns[here, 0:1] / hidden_width
            scale = lax.rsqrt(columns[here, 1:2] / hidden_width - centre * centre + EPS_NORM)
            mean_one = columns[here, 2:3] / hidden_width
            mean_two = scale * (columns[here, 3:4] - centre * columns[here, 2:3]) / hidden_width
            standard = (act[0, here, :].astype(WIDE) - centre) * scale
            squashed[0, here, :] = (standard * gain[...]).astype(LOW)
            s = squashed_grad[0, here, :].astype(WIDE)
            gains[0:1, lanes] += jnp.sum(s * standard, axis=0, keepdims=True)
            activated_grad = (s * gain[...] - mean_one - standard * mean_two) * scale
            grad = (activated_grad * slope[0, here, :].astype(WIDE)).astype(LOW)
            hidden_grad[0, here, :] = grad
            acc[here, :] += dot(grad, up[...], NT)

    pl.when(u < steps // 2)(lambda: work(up_own))
    pl.when(u >= steps // 2)(lambda: work(up_got))
    ends = u == steps - 1

    @pl.when(ends & (n == 0))
    def _():
        send_core[0] = acc[...].astype(LOW)
        to_core[0].start()

    @pl.when(ends & (n == 1))
    def _():
        to_core[0].wait()
        send_low[...] = (acc[...] + got_core[0].astype(WIDE)).astype(LOW)
        to_low.start()

    @pl.when(ends & (n == 2))
    def _():
        send_core[1] = acc[...].astype(LOW)
        to_core[1].start()

    @pl.when(ends & (n == 3))
    def _():
        to_core[1].wait()
        kept[...] = (acc[...] + got_core[1].astype(WIDE)).astype(LOW)
        to_low.wait()


def ffn_second(act, slope, squashed_grad, sums, gain, upward, hidden_width):
    _, rows, units = act.shape
    model = upward[0].shape[0]
    block = min(512, units // 2)
    count = units // 2 // block
    line = pl.BlockSpec((1, rows, block), lambda n, u: (3 - n, 0, u))
    piece = jax.ShapeDtypeStruct((rows, model), LOW)
    return pl.pallas_call(
        partial(ffn_second_kernel, hidden_width=hidden_width),
        grid=(4, 2 * count),
        in_specs=[line] * 3
        + [pl.BlockSpec((1, 8, rows), lambda n, u: (3 - n, 0, 0)), pl.BlockSpec((1, block), lambda n, u: (0, u))]
        + [pl.BlockSpec((model, block), at) for at in in_halves(count, False)],
        out_specs=[line] * 2
        + [pl.BlockSpec((rows, model), lambda n, u: (0, 0)), ANYWHERE, pl.BlockSpec((8, units), lambda n, u: (0, 0))],
        out_shape=[like(act)] * 2 + [piece] * 2 + [jax.ShapeDtypeStruct((8, units), WIDE)],
        scratch_shapes=[
            pltpu.VMEM((rows, model), WIDE),
            pltpu.VMEM((2, rows, model), LOW),
            pltpu.VMEM((2, rows, model), LOW),
            pltpu.VMEM((rows, model), LOW),
            pltpu.SemaphoreType.DMA((3,)),
            pltpu.SemaphoreType.DMA((3,)),
        ],
        compiler_params=pltpu.CompilerParams(collective_id=3, has_side_effects=True, vmem_limit_bytes=60 << 20),
        cost_estimate=pl.CostEstimate(flops=80 * 10**9, bytes_accessed=100 << 20, transcendentals=0),
    )(act, slope, squashed_grad, sums, gain, *upward)


def spread_kernel(ids, x, own, got, out, acc):
    step = pl.program_id(0)

    @pl.when(step == 0)
    def _():
        acc[...] = jnp.zeros_like(acc)

    def work(weight):
        acc[...] += dot(x[...], weight[...], NN)

    each_half(work, own, got)

    @pl.when(step == pl.num_programs(0) - 1)
    def _():
        out[...] = acc[...].astype(LOW)


def ffn_out(ids, x, j, downward):
    _, rows, units = x.shape
    model = downward[0].shape[1]
    block = min(512, units // 2)
    count = units // 2 // block
    return kernel_call(
        spread_kernel,
        (2 * count,),
        [pl.BlockSpec((pl.Squeezed(), rows, block), lambda u, ids: (j, 0, u))]
        + [pl.BlockSpec((block, model), at) for at in halves(count, True)],
        [pl.BlockSpec((rows, model), lambda u, ids: (0, 0))],
        [jax.ShapeDtypeStruct((rows, model), LOW)],
        [pltpu.VMEM((rows, model), WIDE)],
        2 * rows * model * units,
        2 * model * units + 2 * rows * (units + model),
        (ids, x, *downward),
    )[0]


def unproject_kernel(*refs):
    grads, owns, got_weight, away = refs[0:6], refs[6:10], refs[10], refs[11:13]
    kept, arrived, *back = refs[-10:-6]
    acc, send_core, got_core, send_low, sent, got = refs[-6:]
    n, b = pl.program_id(0), pl.program_id(1)
    rows = acc.shape[0]
    depth = owns[0].shape[1]
    place = lax.axis_index("dp")
    _, _, over_core, over_low, over_high = partners()
    here = pl.ds(pl.multiple_of(b * rows, rows), rows)

    def to_core(slot, half):
        s = 2 * slot + half
        return remote(send_core.at[s], got_core.at[s], sent.at[s], got.at[s], over_core)

    def to_low(half):
        part = pl.ds(half * rows, rows)
        return remote(send_low.at[half], arrived.at[part], sent.at[4 + half], got.at[4 + half], over_low)

    crossing = [remote(away[i], back[i], sent.at[6 + i], got.at[6 + i], over_high) for i in range(2)]

    @pl.when((n == 0) & (b == 0))
    def _():
        greet((over_core, over_low, over_high))
        for copy in crossing:
            copy.start()

    acc[...] = sum(dot(grads[3 + f][0], got_weight[f], NT) for f in range(3))
    for k in range(4):
        lanes = pl.ds(pl.multiple_of(mate(place, k) * depth, depth), depth)
        acc[:, lanes] += sum(dot(grads[f][0], owns[k][f], NT) for f in range(3))

    for half in range(2):

        @pl.when((n == 0) & (b == half))
        def _():
            send_core[half] = acc[...].astype(LOW)
            to_core(0, half).start()

        @pl.when((n == 1) & (b == half))
        def _():
            to_core(0, half).wait()
            send_low[half] = (acc[...] + got_core[half].astype(WIDE)).astype(LOW)
            to_low(half).start()

        @pl.when((n == 2) & (b == half))
        def _():
            send_core[2 + half] = acc[...].astype(LOW)
            to_core(1, half).start()

        @pl.when((n == 3) & (b == half))
        def _():
            to_core(1, half).wait()
            kept[here, :] = (acc[...] + got_core[2 + half].astype(WIDE)).astype(LOW)

    @pl.when((n == 3) & (b == 1))
    def _():
        to_low(0).wait()
        to_low(1).wait()
        for copy in crossing:
            copy.wait()


def unproject(grads, heads, away, done):
    _, rows, width = grads[0].shape
    own, got = heads
    model = got.shape[1]
    half = rows // 2
    line = pl.BlockSpec((1, half, width), lambda n, b: (3 - n, b, 0))
    still = lambda value: pl.BlockSpec(value.shape, lambda n, b: (0,) * value.ndim, pipeline_mode=ONCE)
    piece = jax.ShapeDtypeStruct((rows, model), LOW)
    buffer = lambda count: pltpu.VMEM((count, half, model), LOW)
    return pl.pallas_call(
        unproject_kernel,
        grid=(4, 2),
        in_specs=[line] * 6 + [still(w) for w in own] + [still(got)] + [ANYWHERE] * (2 + len(done)),
        out_specs=[pl.BlockSpec((rows, model), lambda n, b: (0, 0)), ANYWHERE, ANYWHERE, ANYWHERE],
        out_shape=[piece, piece] + [like(value) for value in away],
        scratch_shapes=[
            pltpu.VMEM((half, model), WIDE),
            buffer(4),
            buffer(4),
            buffer(2),
            pltpu.SemaphoreType.DMA((8,)),
            pltpu.SemaphoreType.DMA((8,)),
        ],
        compiler_params=pltpu.CompilerParams(collective_id=6, has_side_effects=True, vmem_limit_bytes=56 << 20),
        cost_estimate=pl.CostEstimate(flops=40 * 10**9, bytes_accessed=20 << 20, transcendentals=0),
    )(*grads, *own, got, *away, *done)


def grad_kernel(ids, *refs, chunks, kinds, fixed):
    xs, ys = refs[:chunks], refs[chunks : chunks * (1 + kinds)]
    outs, turned = refs[chunks * (1 + kinds) : -1], refs[-1]
    step = pl.program_id(0)
    rows = xs[0].shape[0]

    def turn():
        for j in range(chunks):
            turned[:, j * rows : (j + 1) * rows] = xs[j][...].T

    if fixed:
        pl.when(step == 0)(turn)
    else:
        turn()
    for f in range(kinds):
        total = None
        for j in range(chunks):
            part = dot(turned[:, j * rows : (j + 1) * rows], ys[f * chunks + j][...], NN)
            total = part if total is None else total + part
        total = total.astype(LOW)
        if len(outs) == 1:
            outs[0][f] = total
        else:
            for k, out in enumerate(outs):

                @pl.when(step == k)
                def _():
                    out[f] = total


def weight_grad(ids, xs, ys, x_blocks, done=(), side=None, apart=False):
    chunks, kinds = len(xs), len(ys)
    rows, x_width = xs[0][0].shape[-2:]
    y_width = ys[0][0][0].shape[-1]

    def spec(piece, width, at, once):
        mode = {"pipeline_mode": ONCE} if once else {}
        if piece[1] is None:
            return pl.BlockSpec((rows, width), at, **mode)
        place = lambda b, ids, n=piece[1]: (n, *at(b, ids))
        return pl.BlockSpec((pl.Squeezed(), rows, width), place, **mode)

    shift = lambda b, ids: (0, ids[1] ^ b if apart else b)
    still = lambda b, ids: (0, side or 0)
    share = 1 if side is None else 2
    if x_blocks:
        x_width, y_width = x_width // 4, y_width // share
        x_at, y_at = (x_width, shift, False), (y_width, still, True)
        whole, out_at = (kinds, 4 * x_width, y_width), lambda b, ids: (0, b, 0)
    else:
        x_width, y_width = x_width // share, y_width // 4
        x_at, y_at = (x_width, still, True), (y_width, shift, False)
        whole, out_at = (kinds, x_width, 4 * y_width), lambda b, ids: (0, 0, b)
    out = (kinds, x_width, y_width)
    if apart:
        out_specs = [pl.BlockSpec(out, lambda b, ids: (0, 0, 0))] * 4
        out_shape = [jax.ShapeDtypeStruct(out, LOW)] * 4
    else:
        out_specs, out_shape = [pl.BlockSpec(out, out_at)], [jax.ShapeDtypeStruct(whole, LOW)]
    result = kernel_call(
        partial(grad_kernel, chunks=chunks, kinds=kinds, fixed=not x_blocks),
        (4,),
        [spec(x, *x_at) for x in xs] + [spec(y, *y_at) for group in ys for y in group],
        out_specs,
        out_shape,
        [pltpu.VMEM((x_width, rows * chunks), LOW)],
        8 * rows * chunks * x_width * y_width * kinds,
        2 * rows * chunks * (4 * x_width + 4 * y_width * kinds),
        (ids, *[x[0] for x in xs], *[y[0] for group in ys for y in group]),
        done,
    )
    return result if apart else result[0]


def flip(value, axis, mask):
    return lax.ppermute(value, axis, [(i, i ^ mask) for i in range(lax.axis_size(axis))])


def add_low(one, two):
    return (one.astype(WIDE) + two.astype(WIDE)).astype(LOW)


def sum_everywhere(value):
    for axis, mask in (("dp", 1), ("dp", 2), ("mp", 1), ("mp", 2), ("mp", 4)):
        value = value + flip(value, axis, mask)
    return value


def partners():
    row, column = lax.axis_index("dp"), lax.axis_index("mp")
    over_x = (row + 1 - 2 * (row % 2), column)
    over_y = ((row + 2) % 4, column)
    over_core = (row, column + 1 - 2 * (column % 2))
    over_low = (row, column + 2 - 4 * ((column // 2) % 2))
    over_high = (row, (column + 4) % 8)
    return over_x, over_y, over_core, over_low, over_high


def greet(others):
    barrier = pltpu.get_barrier_semaphore()
    for other in others:
        pl.semaphore_signal(barrier, inc=1, device_id=other, device_id_type=MESH)
    pl.semaphore_wait(barrier, len(others))


class Sender:
    def __init__(self, sent, got):
        self.sent, self.got, self.count = sent, got, 0

    def __call__(self, source, target, device):
        copy = pltpu.make_async_remote_copy(
            src_ref=source,
            dst_ref=target,
            send_sem=self.sent.at[self.count],
            recv_sem=self.got.at[self.count],
            device_id=device,
            device_id_type=MESH,
        )
        self.count += 1
        copy.start()
        return copy


def open_kernel(text, head, text_got, head_x, head_y, head_far, sent, got):
    over_x, over_y, _, _, over_high = partners()
    greet((over_x, over_y, over_high))
    send = Sender(sent, got)
    half = head.shape[1] // 2
    upper, lower = pl.ds(0, half), pl.ds(half, half)
    copies = [send(text, text_got, over_high)]
    first = send(head.at[:, upper], head_x.at[:, upper], over_x)
    second = send(head.at[:, lower], head_y.at[:, lower], over_y)
    copies.append(send(head.at[:, lower], head_x.at[:, lower], over_x))
    copies.append(send(head.at[:, upper], head_y.at[:, upper], over_y))
    first.wait()
    copies.append(send(head_x.at[:, upper], head_far.at[:, upper], over_y))
    second.wait()
    copies.append(send(head_y.at[:, lower], head_far.at[:, lower], over_x))
    for copy in copies:
        copy.wait()


def open_exchange(text, head):
    return pl.pallas_call(
        open_kernel,
        in_specs=[ANYWHERE] * 2,
        out_specs=[ANYWHERE] * 4,
        out_shape=[like(text), like(head), like(head), like(head)],
        scratch_shapes=[pltpu.SemaphoreType.DMA((7,)), pltpu.SemaphoreType.DMA((7,))],
        compiler_params=pltpu.CompilerParams(collective_id=0, has_side_effects=True),
        cost_estimate=pl.CostEstimate(flops=0, bytes_accessed=100 << 20, transcendentals=0),
    )(text, head)


def normed_kernel(normed, head, outward, upward, _, near, far, far_near, head_got, pieces, others, up_got, sent, got):
    over_x, over_y, over_core, over_low, over_high = partners()
    greet((over_x, over_y, over_core, over_low, over_high))
    send = Sender(sent, got)
    rows = normed.shape[0] // 2
    parts = [pl.ds(b * rows, rows) for b in range(2)]
    crossing = [send(normed.at[part], far.at[part], over_low) for part in parts]
    copies = [send(normed, near, over_core), send(head, head_got, over_high), send(upward, up_got, over_high)]
    half = outward.shape[0] // 2
    upper, lower = pl.ds(0, half), pl.ds(half, half)
    first = send(outward.at[upper], pieces.at[0, upper], over_x)
    second = send(outward.at[lower], pieces.at[1, lower], over_y)
    later = [
        (send(outward.at[lower], pieces.at[0, lower], over_x), 0, lower),
        (send(outward.at[upper], pieces.at[1, upper], over_y), 1, upper),
    ]
    first.wait()
    later.append((send(pieces.at[0, upper], pieces.at[2, upper], over_y), 2, upper))
    copies.append(send(pieces.at[0, upper], others.at[0, upper], over_core))
    second.wait()
    later.append((send(pieces.at[1, lower], pieces.at[2, lower], over_x), 2, lower))
    copies.append(send(pieces.at[1, lower], others.at[1, lower], over_core))
    for copy, part in zip(crossing, parts):
        copy.wait()
        copies.append(send(far.at[part], far_near.at[part], over_core))
    for copy, n, part in later:
        copy.wait()
        copies.append(send(pieces.at[n, part], others.at[n, part], over_core))
    for copy in copies:
        copy.wait()


def normed_exchange(normed, head, outward, upward, done):
    pieces = jax.ShapeDtypeStruct((3,) + outward.shape, LOW)
    return pl.pallas_call(
        normed_kernel,
        in_specs=[ANYWHERE] * 5,
        out_specs=[ANYWHERE] * 7,
        out_shape=[like(normed)] * 3 + [like(head), pieces, pieces, like(upward)],
        scratch_shapes=[pltpu.SemaphoreType.DMA((19,)), pltpu.SemaphoreType.DMA((19,))],
        compiler_params=pltpu.CompilerParams(collective_id=1, has_side_effects=True),
        cost_estimate=pl.CostEstimate(flops=0, bytes_accessed=100 << 20, transcendentals=0),
    )(normed, head, outward, upward, done)


def adapt(kept, got, master, moment, square):
    gradient = kept if got is None else kept + got
    moment_new = BETA_ONE * moment + (1.0 - BETA_ONE) * gradient
    square_new = BETA_TWO * square + (1.0 - BETA_TWO) * gradient * gradient
    return moment_new, square_new, direction_of(master, moment_new, square_new)


def direction_of(master, moment_new, square_new):
    root = jnp.sqrt(square_new / (1.0 - BETA_TWO**STEP)) + EPS_ADAM
    return moment_new / (1.0 - BETA_ONE**STEP) / root + DECAY_RATE * master


def close_kernel(*refs, groups, first_steps):
    kept, got, merged, middle, gain = refs[:5]
    count = 5 + sum(groups) + 3 * len(groups)
    weights, outs = refs[5:count], refs[count:]
    moments, (rows, gains, norms, arrived) = outs[: 2 * len(groups)], outs[2 * len(groups) : 2 * len(groups) + 4]
    sending, sent, got_sem = outs[2 * len(groups) + 4 :]
    step = pl.program_id(0)
    over_high = partners()[4]
    side = lax.axis_index("mp") // 4
    crossing = remote(sending, arrived, sent, got_sem, over_high)

    @pl.when(step == 0)
    def _():
        greet((over_high,))
        gains[...] = jnp.zeros_like(gains)
        norms[...] = jnp.zeros_like(norms)

    @pl.when(step < first_steps)
    def _():
        grad = kept[...].astype(WIDE) + got[...].astype(WIDE)
        standard, scale = centred(merged[...].astype(WIDE))
        gains[0:1, :] += jnp.sum(grad * standard, axis=0, keepdims=True)
        total = middle[...] + norm_back(standard, scale, gain[...], grad)
        rows[...] = total
        half = first_steps // 2
        here = pl.ds(pl.multiple_of((step % half) * total.shape[0], total.shape[0]), total.shape[0])

        @pl.when(step // half != side)
        def _():
            sending[here, :] = total.astype(LOW)

    @pl.when(step == first_steps - 1)
    def _():
        crossing.start()

    at = 0
    for n, size in enumerate(groups):
        grads, (master, moment, square) = weights[at : at + size], weights[at + size : at + size + 3]
        at += size + 3
        wide = [g[...].astype(WIDE) for g in grads] + [None]
        moment_new, square_new, direction = adapt(wide[0], wide[1], master[...], moment[...], square[...])
        moments[2 * n][...] = moment_new
        moments[2 * n + 1][...] = square_new
        for k, value in enumerate((master[...], direction)):
            norms[k, n : n + 1, :] += jnp.sum(fold(value * value), axis=0, keepdims=True)

    @pl.when(step == pl.num_programs(0) - 1)
    def _():
        crossing.wait()


def close(kept, got, merged, middle, gain, weights):
    rows, model = kept.shape
    steps, first_steps = 16, 4
    line = pl.BlockSpec((rows // first_steps, model), lambda i: (jnp.minimum(i, first_steps - 1), 0))
    in_specs, out_specs, out_shape, operands = [line] * 4 + [pl.BlockSpec((1, model), lambda i: (0, 0))], [], [], []
    for group in weights:
        shape = group[-1].shape
        block = shape[:-2] + (shape[-2] // steps, shape[-1])
        spec = pl.BlockSpec(block, lambda i, lead=len(shape) - 2: (0,) * lead + (i, 0))
        in_specs += [spec] * len(group)
        out_specs += [spec] * 2
        out_shape += [jax.ShapeDtypeStruct(shape, WIDE)] * 2
        operands += group
    out_specs += [
        line,
        pl.BlockSpec((8, model), lambda i: (0, 0)),
        pl.BlockSpec((2, 8, LANES), lambda i: (0, 0, 0)),
        ANYWHERE,
    ]
    out_shape += [
        jax.ShapeDtypeStruct((rows, model), WIDE),
        jax.ShapeDtypeStruct((8, model), WIDE),
        jax.ShapeDtypeStruct((2, 8, LANES), WIDE),
        jax.ShapeDtypeStruct((rows // 2, model), LOW),
    ]
    return pl.pallas_call(
        partial(close_kernel, groups=[len(group) - 3 for group in weights], first_steps=first_steps),
        grid=(steps,),
        in_specs=in_specs,
        out_specs=out_specs,
        out_shape=out_shape,
        scratch_shapes=[
            pltpu.VMEM((rows // 2, model), LOW),
            pltpu.SemaphoreType.DMA,
            pltpu.SemaphoreType.DMA,
        ],
        compiler_params=pltpu.CompilerParams(collective_id=7, has_side_effects=True, vmem_limit_bytes=56 << 20),
        cost_estimate=pl.CostEstimate(flops=10**9, bytes_accessed=100 << 20, transcendentals=0),
    )(kept, got, merged, middle, gain, *operands)


def rotary_tables(length):
    lane = jnp.arange(LANES, dtype=jnp.int32)
    pair_index = (lane % (HEAD_DIM // 2)).astype(WIDE)[None]
    sign = jnp.where(lane % HEAD_DIM < HEAD_DIM // 2, -1.0, 1.0)[None]
    angular = jnp.exp(-(2.0 * pair_index / HEAD_DIM) * jnp.log(10000.0))
    zeta_base = (2.0 * pair_index + 0.4 * HEAD_DIM) / (1.4 * HEAD_DIM)
    position = jnp.arange(length, dtype=WIDE)[:, None]
    cosine, sine_part = jnp.cos(position * angular), jnp.sin(position * angular) * sign
    exponent = position / 512.0 * jnp.log(zeta_base)
    up, down = jnp.exp(exponent), jnp.exp(-exponent)
    return [cosine * up, sine_part * up, cosine * down, sine_part * down]


def on_device_paired(
    text_states,
    image_states,
    image_offsets,
    image_counts,
    output_grad,
    head_master,
    head_moment,
    head_square,
    outward_master,
    outward_moment,
    outward_square,
    upward_master,
    upward_moment,
    upward_square,
    downward_master,
    downward_moment,
    downward_square,
    gains_master,
    gains_moment,
    gains_square,
):
    model_rank = lax.axis_index("mp")
    side = model_rank // 4
    rank = model_rank % 4
    place = lax.axis_index("dp")
    ids = jnp.stack([rank, place, side]).astype(jnp.int32)
    _, local_len, model_width = text_states.shape
    length = local_len * 8
    rows = 2 * local_len
    hidden_local = upward_master.shape[1]
    hidden_width = hidden_local * 8

    def pick(value, index):
        return lax.dynamic_index_in_dim(value, index, 0, keepdims=False)

    tables = rotary_tables(length)

    def both(kept, got):
        return jnp.where(side == 0, jnp.stack([kept, got]), jnp.stack([got, kept]))

    core = rank % 2
    half_width = model_width // 2
    text_out = pick(text_states, 1 - side)
    head_own = head_master.astype(LOW)
    upward_own = upward_master.astype(LOW)
    upward_weight = [lax.all_gather(upward_own, "dp", axis=0, tiled=True)]
    text_got, *head_parts = open_exchange(text_out, head_own)
    head_weight = [[head_own] + head_parts]
    downward_own = downward_master.astype(LOW)
    downward_weight = [lax.all_gather(downward_own, "dp", axis=1, tiled=True)]
    text = both(pick(text_states, side), text_got)

    gain_in = gains_master[None, :model_width]
    gain_ctx = gains_master[None, model_width : 2 * model_width]
    gain_mid = gains_master[None, 2 * model_width : 3 * model_width]
    hidden_start = 3 * model_width + model_rank * hidden_local
    other_start = 3 * model_width + (model_rank ^ 4) * hidden_local
    gain_hidden = jnp.concatenate(
        [
            lax.dynamic_slice_in_dim(gains_master, hidden_start, hidden_local),
            lax.dynamic_slice_in_dim(gains_master, other_start, hidden_local),
        ]
    )[None]

    offsets = pick(image_offsets, side)
    image_count = pick(image_counts, side)
    position = (
        jnp.arange(2, dtype=jnp.int32)[:, None] * (4 * local_len)
        + rank * local_len
        + jnp.arange(local_len, dtype=jnp.int32)[None, :]
    ).reshape(rows)
    slot_index = jnp.arange(offsets.shape[0], dtype=jnp.int32)
    inside = (
        (position[:, None] >= offsets[None, :])
        & (position[:, None] < offsets[None, :] + PATCH)
        & (slot_index[None, :] < image_count)
    )
    picked = jnp.sum(
        jnp.where(inside, slot_index[None, :] * PATCH + position[:, None] - offsets[None, :], 0), axis=-1
    )
    covered = jnp.any(inside, axis=-1)
    place_index = jnp.arange(image_states.shape[1], dtype=jnp.int32)
    chosen = (covered[:, None] & (picked[:, None] == place_index[None, :])).astype(LOW)
    images = jnp.dot(chosen, pick(image_states, side), preferred_element_type=WIDE).astype(LOW)
    merged = jnp.where(covered[:, None], images, text.reshape(rows, model_width))

    def turn_heads(pieces):
        return [pieces[0]] + [flip(pieces[j], "mp", j) for j in range(1, 4)]

    normed_own = layer_norm(merged.astype(WIDE), gain_in).astype(LOW)
    outward_low = outward_master.astype(LOW)
    outward_own, outward_other = (
        lax.dynamic_slice_in_dim(outward_low, n * half_width, half_width, 1) for n in (core, 1 - core)
    )
    near, far, far_near, head_got, *pieces, upward_got = normed_exchange(
        normed_own, head_own, outward_own, upward_own, upward_weight[0]
    )
    outward_weight = [outward_own, pieces[0], outward_other, pieces[1]]
    normed = [normed_own, near, far, far_near]
    head_weight.append(lax.all_gather(head_got, "dp", axis=1, tiled=True))
    upward_weight.append(lax.all_gather(upward_got, "dp", axis=0, tiled=True))
    got_cotangent = flip(pick(output_grad, 1 - side), "mp", 4)

    queries, keys, values, contexts, logs, arrived = [], [], [], [], [], []
    for half in range(2):
        projected = []
        for j, chunk in enumerate(normed):
            carry = [downward_own, got_cotangent] if half == 1 and j == 0 else []
            done = [projected[0][0]] if j > 0 else []
            outs = project(ids, chunk, head_weight[half], tables, j, done, carry)
            projected.append(outs[:3])
            if carry:
                downward_got = flip(outs[3], "mp", 4)
                cotangent = both(pick(output_grad, side), outs[4]).reshape(rows, model_width)
                cotangent_far = flip(cotangent, "mp", 2)
                cotangent_others = [flip(cotangent, "mp", 1), cotangent_far, flip(cotangent_far, "mp", 1)]
        for n, group in enumerate((queries, keys, values)):
            group.append([p[n] for p in projected])
        context, lse = attend(ids, queries[half], keys[half], values[half])
        contexts.append(context)
        logs.append(lse)
        arrived = arrived + turn_heads(context)
    context, mixed, middle, lifted_own, downward_got = mid_forward(
        ids, arrived, merged, outward_weight, gain_ctx, gain_mid, [downward_got]
    )
    downward_weight.append(lax.all_gather(downward_got, "dp", axis=1, tiled=True))
    act, slope, sums, lifted_others = ffn_up(lifted_own, upward_weight)
    squashed_grad, back_sums = ffn_back(cotangent, cotangent_others, downward_weight, act, gain_hidden)
    lifted = [(lifted_own, None)] + [(lifted_others, n) for n in range(3)]
    cotangents = [(value, None) for value in [cotangent] + cotangent_others]
    sums = sums + back_sums
    others = [flip(sums, "mp", k) for k in range(1, 4)]
    sums = jnp.stack(
        [(sums[j] + others[0][j ^ 1]) + (others[1][j ^ 2] + others[2][j ^ 3]) for j in range(4)]
    )
    squashed, hidden_grad, lifted_kept, lifted_got, hidden_gains = ffn_second(
        act, slope, squashed_grad, sums, gain_hidden, upward_weight, hidden_width
    )

    def split(value):
        return [(value, n) for n in range(4)]

    def whole(values):
        return [(value, None) for value in values]

    down_grad = lax.psum_scatter(
        weight_grad(ids, split(squashed), [cotangents], False), "dp", scatter_dimension=2, tiled=True
    )[0]
    middle_grad, middle_low, own_grads, other_grads, mid_gains = mid_backward(
        ids, (lifted_kept, lifted_got), middle, cotangent, context, outward_weight, gain_mid, gain_ctx
    )
    context_heads = [turn_heads(own_grads), turn_heads(other_grads)]
    up_part = weight_grad(ids, lifted, [split(hidden_grad)], True)
    up_grad = lax.psum_scatter(up_part, "dp", scatter_dimension=1, tiled=True)[0]
    ffn_parts = [ffn_out(ids, squashed, j, downward_weight) for j in range(4)]

    def scatter_tokens(parts):
        passed = add_low(parts[2], flip(parts[3], "mp", 1))
        return add_low(parts[0], flip(parts[1], "mp", 1)), flip(passed, "mp", 2)

    def give_back(pair):
        got = flip(pick(pair, 1 - side).astype(LOW), "mp", 4)
        return both(pick(pair, side), got.astype(pair.dtype))

    ffn_kept, ffn_got = scatter_tokens(ffn_parts)
    output_rows = (middle + (ffn_kept.astype(WIDE) + ffn_got.astype(WIDE))).astype(LOW)
    output_rows = output_rows.reshape(2, local_len, model_width)

    head_grads, head_sides, backs = [None, None], [None, None], [None, None]
    leaving = (pick(output_rows, 1 - side), down_grad[hidden_local:])
    for half in (1, 0):
        *head_grads[half], backs[half] = attend_back(
            queries[half],
            keys[half],
            values[half],
            context_heads[half],
            contexts[half],
            logs[half],
            tables,
            leaving[half],
            4 + half,
            [ffn_kept] if half else [],
        )
        head_part = weight_grad(ids, whole(normed), [split(g) for g in head_grads[half]], True)
        head_sides[half] = lax.psum_scatter(head_part, "dp", scatter_dimension=1, tiled=True)
        if half == 1:
            outward_part = weight_grad(ids, whole([mixed]), [whole([middle_low])], True, [head_part])[0]
            outward_sent = lax.dynamic_slice_in_dim(outward_part, (1 - core) * half_width, half_width, 1)
            outward_half = add_low(
                lax.dynamic_slice_in_dim(outward_part, core * half_width, half_width, 1), flip(outward_sent, "mp", 1)
            )
            outward_grad = lax.psum_scatter(outward_half, "dp", scatter_dimension=0, tiled=True)
    output_got, down_got = backs
    layer_output = both(pick(output_rows, side), output_got)
    normed_kept, normed_got, up_got, head_got_grad = unproject(
        head_grads[0] + head_grads[1], head_weight, [up_grad[:, hidden_local:], head_sides[1]], [head_part, outward_grad]
    )
    result = close(
        normed_kept,
        normed_got,
        merged,
        middle_grad,
        gain_in,
        [
            [up_grad[:, :hidden_local], up_got, upward_master, upward_moment, upward_square],
            [down_grad[:hidden_local], down_got, downward_master, downward_moment, downward_square],
        ],
    )
    moment_upward, square_upward, moment_downward, square_downward = result[:4]
    input_rows, in_gain_grad, norm_lanes, input_got = result[4:]
    moment_head, square_head, head_dir = adapt_step(
        head_sides[0].astype(WIDE) + head_got_grad.astype(WIDE), head_master, head_moment, head_square, DECAY_RATE
    )
    outward_grad = lax.psum(outward_grad, "mp", axis_index_groups=[[0, 2, 4, 6], [1, 3, 5, 7]])
    outward_grad = hand_on(outward_grad, [input_got])
    outward_got = flip(outward_grad, "mp", 1)
    outward_grad = jnp.where(
        core == 0,
        jnp.concatenate([outward_grad, outward_got], axis=1),
        jnp.concatenate([outward_got, outward_grad], axis=1),
    )
    moment_outward, square_outward, outward_dir = adapt_step(
        outward_grad.astype(WIDE), outward_master, outward_moment, outward_square, DECAY_RATE
    )
    upward_dir = direction_of(upward_master, moment_upward, square_upward)
    downward_dir = direction_of(downward_master, moment_downward, square_downward)
    input_grad = both(pick(input_rows.reshape(2, local_len, model_width), side), input_got.astype(WIDE))
    owner = (model_rank == 0).astype(WIDE)
    norm_part = jnp.concatenate(
        [
            jnp.stack([jnp.sum(head_master * head_master, axis=(1, 2)), jnp.sum(head_dir * head_dir, axis=(1, 2))], axis=-1),
            pair_sums(outward_master, outward_dir) * owner,
            jnp.sum(norm_lanes, axis=-1)[:, :2].T,
        ],
        axis=0,
    )
    hidden_gain = hidden_gains[0]
    gains_part = jnp.concatenate([in_gain_grad[0], mid_gains[1], mid_gains[0], jnp.zeros((hidden_width,), WIDE)])
    gains_part = lax.dynamic_update_slice(gains_part, hidden_gain[:hidden_local], (hidden_start,))
    gains_part = lax.dynamic_update_slice(gains_part, hidden_gain[hidden_local:], (other_start,))
    every = sum_everywhere(jnp.concatenate([gains_part, norm_part.reshape(-1)]))
    gains_sum, norm_sums = every[: gains_part.shape[0]], every[gains_part.shape[0] :].reshape(6, 2)
    moment_gains, square_gains, gains_dir = adapt_step(gains_sum, gains_master, gains_moment, gains_square, 0.0)
    gains_sums = jnp.stack(
        [
            gain_segments(gains_master * gains_master, model_width),
            gain_segments(gains_dir * gains_dir, model_width),
        ],
        axis=-1,
    )
    updated_head = trust_move(
        head_master, head_dir, norm_sums[:3, 0][:, None, None], norm_sums[:3, 1][:, None, None]
    )
    updated_outward = trust_move(outward_master, outward_dir, norm_sums[3, 0], norm_sums[3, 1])
    updated_upward = trust_move(upward_master, upward_dir, norm_sums[4, 0], norm_sums[4, 1])
    updated_downward = trust_move(downward_master, downward_dir, norm_sums[5, 0], norm_sums[5, 1])
    updated_gains = trust_move(
        gains_master,
        gains_dir,
        gain_spread(gains_sums[:, 0], model_width, hidden_width),
        gain_spread(gains_sums[:, 1], model_width, hidden_width),
    )
    update_norms = jnp.sqrt(jnp.concatenate([norm_sums, gains_sums], axis=0))
    return (
        layer_output,
        input_grad,
        moment_head,
        square_head,
        updated_head,
        updated_head.astype(LOW),
        moment_outward,
        square_outward,
        updated_outward,
        updated_outward.astype(LOW),
        moment_upward,
        square_upward,
        updated_upward,
        updated_upward.astype(LOW),
        moment_downward,
        square_downward,
        updated_downward,
        updated_downward.astype(LOW),
        moment_gains,
        square_gains,
        updated_gains,
        update_norms,
    )


def solution(mesh):
    paired = mesh.shape["dp"] == 4 and mesh.shape["mp"] == 8
    return jax.shard_map(
        on_device_paired if paired else on_device_general,
        mesh=mesh,
        in_specs=(
            P("dp", "mp", None),
            P("dp", None, None),
            P("dp", None),
            P("dp"),
            P("dp", "mp", None),
            P(None, "dp", "mp"),
            P(None, "dp", "mp"),
            P(None, "dp", "mp"),
            P("dp", None),
            P("dp", None),
            P("dp", None),
            P("dp", "mp"),
            P("dp", "mp"),
            P("dp", "mp"),
            P("mp", "dp"),
            P("mp", "dp"),
            P("mp", "dp"),
            P(),
            P(),
            P(),
        ),
        out_specs=(
            P("dp", "mp", None),
            P("dp", "mp", None),
            P(None, "dp", "mp"),
            P(None, "dp", "mp"),
            P(None, "dp", "mp"),
            P(None, "dp", "mp"),
            P("dp", None),
            P("dp", None),
            P("dp", None),
            P("dp", None),
            P("dp", "mp"),
            P("dp", "mp"),
            P("dp", "mp"),
            P("dp", "mp"),
            P("mp", "dp"),
            P("mp", "dp"),
            P("mp", "dp"),
            P("mp", "dp"),
            P(),
            P(),
            P(),
            P(),
        ),
        check_vma=False,
    )
```

```python
from functools import partial

import jax
import jax.numpy as jnp
from jax import lax
from jax.experimental import pallas as pl
from jax.experimental.pallas import tpu as pltpu
from jax.sharding import PartitionSpec as P

HEAD_DIM = 64
FF = 8192
PATCH = 64
STEP = 10


EPS_NORM = 1e-05
BETA_ONE = 0.9
BETA_TWO = 0.999
EPS_ADAM = 1e-06
DECAY_RATE = 0.01
STEP_RATE = 0.5


def layer_norm(inputs, gain_vector):
    centre = jnp.mean(inputs, axis=-1, keepdims=True)
    shifted = inputs - centre
    spread = jnp.mean(shifted * shifted, axis=-1, keepdims=True)
    return shifted * lax.rsqrt(spread + EPS_NORM) * gain_vector


def xpos_tables(length, head_size):
    halfway = head_size // 2
    pair_index = jnp.arange(halfway, dtype=jnp.float32)
    angular = jnp.exp(-(2.0 * pair_index / head_size) * jnp.log(10000.0))
    zeta_base = (2.0 * pair_index + 0.4 * head_size) / (1.4 * head_size)
    position = jnp.arange(length, dtype=jnp.float32)[:, None, None]
    return (
        jnp.cos(position * angular),
        jnp.sin(position * angular),
        position / 512.0 * jnp.log(zeta_base),
    )


def rotate(inputs, tables, polarity):
    cosine, sine_part, exponent = tables
    halfway = inputs.shape[-1] // 2
    factor = jnp.exp(polarity * exponent)
    leading = inputs[..., :halfway]
    behind = inputs[..., halfway:]
    return jnp.concatenate(
        [
            (leading * cosine - behind * sine_part) * factor,
            (behind * cosine + leading * sine_part) * factor,
        ],
        axis=-1,
    )


def merge_images(text_rows, image_rows, offsets, image_count, position):
    slot_index = jnp.arange(offsets.shape[0], dtype=jnp.int32)
    inside = (
        (position[:, None] >= offsets[None, :])
        & (position[:, None] < offsets[None, :] + PATCH)
        & (slot_index[None, :] < image_count)
    )
    picked = jnp.sum(
        jnp.where(inside, slot_index[None, :] * PATCH + position[:, None] - offsets[None, :], 0),
        axis=-1,
    )
    chosen = jnp.take(image_rows, picked, axis=0)
    covered = jnp.any(inside, axis=-1)
    return jnp.where(covered[:, None], chosen, text_rows)


def adapt_step(gradient, master, moment, square, decay_rate):
    moment_new = BETA_ONE * moment + (1.0 - BETA_ONE) * gradient
    square_new = BETA_TWO * square + (1.0 - BETA_TWO) * gradient * gradient
    direction = (
        moment_new
        / (1.0 - BETA_ONE**STEP)
        / (jnp.sqrt(square_new / (1.0 - BETA_TWO**STEP)) + EPS_ADAM)
        + decay_rate * master
    )
    return (moment_new, square_new, direction)


def trust_move(master, direction, weight_sum, update_sum):
    return master - STEP_RATE * jnp.sqrt(weight_sum) / (jnp.sqrt(update_sum) + EPS_ADAM) * direction


def gain_segments(entries, model_width):
    return jnp.stack(
        [
            jnp.sum(entries[:model_width]),
            jnp.sum(entries[model_width : 2 * model_width]),
            jnp.sum(entries[2 * model_width : 3 * model_width]),
            jnp.sum(entries[3 * model_width :]),
        ]
    )


def gain_spread(sums, model_width, hidden_width):
    return jnp.concatenate(
        [
            jnp.broadcast_to(sums[0], (model_width,)),
            jnp.broadcast_to(sums[1], (model_width,)),
            jnp.broadcast_to(sums[2], (model_width,)),
            jnp.broadcast_to(sums[3], (hidden_width,)),
        ]
    )


def pair_sums(master, direction):
    return jnp.stack([jnp.sum(master * master), jnp.sum(direction * direction)])[None]


def on_device_general(
    text_states,
    image_states,
    image_offsets,
    image_counts,
    output_grad,
    head_master,
    head_moment,
    head_square,
    outward_master,
    outward_moment,
    outward_square,
    upward_master,
    upward_moment,
    upward_square,
    downward_master,
    downward_moment,
    downward_square,
    gains_master,
    gains_moment,
    gains_square,
):
    groups = lax.axis_size("mp")
    model_rank = lax.axis_index("mp")
    seq_count, local_len, model_width = text_states.shape
    length = local_len * groups
    hidden_local = upward_master.shape[1]
    heads_local = head_master.shape[2] // HEAD_DIM
    tables = xpos_tables(length, HEAD_DIM)
    position = model_rank * local_len + jnp.arange(local_len, dtype=jnp.int32)
    merged = jax.vmap(
        lambda text_rows, image_rows, offsets, image_count: merge_images(
            text_rows, image_rows, offsets, image_count, position
        )
    )(text_states, image_states, image_offsets, image_counts).astype(jnp.float32)
    gain_in = gains_master[:model_width]
    gain_ctx = gains_master[model_width : 2 * model_width]
    gain_mid = gains_master[2 * model_width : 3 * model_width]
    hidden_start = 3 * model_width + model_rank * hidden_local
    gain_hidden = lax.dynamic_slice_in_dim(gains_master, hidden_start, hidden_local)
    head_weight_whole, outward_weight_whole, upward_weight_whole, down_weight_whole = (
        lax.all_gather(head_master.astype(jnp.bfloat16), "dp", axis=1, tiled=True),
        lax.all_gather(outward_master.astype(jnp.bfloat16), "dp", axis=0, tiled=True),
        lax.all_gather(upward_master.astype(jnp.bfloat16), "dp", axis=0, tiled=True),
        lax.all_gather(downward_master.astype(jnp.bfloat16), "dp", axis=1, tiled=True),
    )
    normed_low = layer_norm(merged, gain_in).astype(jnp.bfloat16)
    normed_rows_full, cotangent_rows_full = (
        lax.all_gather(normed_low, "mp", axis=1, tiled=True),
        lax.all_gather(output_grad, "mp", axis=1, tiled=True),
    )
    projected = jnp.einsum(
        "hvg,bga->bhva", normed_rows_full, head_weight_whole, preferred_element_type=jnp.float32
    )
    shaped = projected.reshape(3, seq_count, length, heads_local, HEAD_DIM)
    queries = rotate(shaped[0], tables, 1.0).astype(jnp.bfloat16)
    key_rows = rotate(shaped[1], tables, -1.0).astype(jnp.bfloat16)
    values = shaped[2].astype(jnp.bfloat16)
    block_len = min(512, length)
    block_count = length // block_len
    starts = jnp.arange(block_count, dtype=jnp.int32) * block_len
    key_place = jnp.arange(length, dtype=jnp.int32)

    def block_scores(query_block, start):
        scores = (
            jnp.einsum("sqhd,skhd->shqk", query_block, key_rows, preferred_element_type=jnp.float32)
            * 0.125
        )
        allowed = key_place[None, :] <= (start + jnp.arange(block_len, dtype=jnp.int32))[:, None]
        return jnp.where(allowed, scores, -1e30)

    def forward_block(start):
        query_block = lax.dynamic_slice_in_dim(queries, start, block_len, 1)
        scores = block_scores(query_block, start)
        highest = jnp.max(scores, axis=-1, keepdims=True)
        exponent = jnp.exp(scores - highest)
        total = jnp.sum(exponent, axis=-1, keepdims=True)
        attention = exponent / total
        context_block = jnp.einsum(
            "shqk,skhd->sqhd",
            attention.astype(jnp.bfloat16),
            values,
            preferred_element_type=jnp.float32,
        )
        return (context_block, highest[..., 0] + jnp.log(total[..., 0]))

    context_blocks, log_sums = lax.map(forward_block, starts)
    context = jnp.transpose(context_blocks, (1, 0, 2, 3, 4)).reshape(
        seq_count, length, heads_local * HEAD_DIM
    )
    context_rows = lax.all_to_all(
        context.astype(jnp.bfloat16), "mp", split_axis=1, concat_axis=2, tiled=True
    )
    context_in = context_rows.astype(jnp.float32)
    mixed_half_precision = layer_norm(context_in, gain_ctx).astype(jnp.bfloat16)
    middle = merged + jnp.einsum(
        "ymq,qc->ymc",
        mixed_half_precision,
        outward_weight_whole,
        preferred_element_type=jnp.float32,
    )
    lifted_low = layer_norm(middle, gain_mid).astype(jnp.bfloat16)
    lifted_rows_full = lax.all_gather(lifted_low, "mp", axis=1, tiled=True)
    hidden_rows = jnp.einsum(
        "orb,bg->org", lifted_rows_full, upward_weight_whole, preferred_element_type=jnp.float32
    )
    activated = jax.nn.gelu(hidden_rows, approximate=False)
    first_sum, second_sum = lax.psum(
        (jnp.sum(activated, axis=-1), jnp.sum(activated * activated, axis=-1)), "mp"
    )
    centre = first_sum / FF
    scale_inv = lax.rsqrt(second_sum / FF - centre * centre + EPS_NORM)[..., None]
    standard = (activated - centre[..., None]) * scale_inv
    squashed_half_precision = (standard * gain_hidden).astype(jnp.bfloat16)
    ffn_part = jnp.einsum(
        "wxp,pk->wxk",
        squashed_half_precision,
        down_weight_whole,
        preferred_element_type=jnp.float32,
    )
    ffn_rows = lax.psum_scatter(
        ffn_part.astype(jnp.bfloat16), "mp", scatter_dimension=1, tiled=True
    ).astype(jnp.float32)
    layer_output = (middle + ffn_rows).astype(jnp.bfloat16)
    down_grad = jnp.einsum(
        "uxy,uxo->yo",
        squashed_half_precision,
        cotangent_rows_full,
        preferred_element_type=jnp.float32,
    )
    squashed_grad = jnp.einsum(
        "yxr,ur->yxu", cotangent_rows_full, down_weight_whole, preferred_element_type=jnp.float32
    )
    hidden_gain_grad = jnp.sum(squashed_grad * standard, axis=(0, 1))
    scaled_grad = squashed_grad * gain_hidden
    mean_one, mean_two = (
        lax.psum(jnp.sum(scaled_grad, axis=-1).astype(jnp.bfloat16), "mp").astype(jnp.float32),
        lax.psum(jnp.sum(scaled_grad * standard, axis=-1).astype(jnp.bfloat16), "mp").astype(
            jnp.float32
        ),
    )
    activated_grad = (
        scaled_grad - mean_one[..., None] / FF - standard * (mean_two[..., None] / FF)
    ) * scale_inv
    gelu_out, gelu_back = jax.vjp(partial(jax.nn.gelu, approximate=False), hidden_rows)
    hidden_rows_grad = gelu_back(activated_grad)[0].astype(jnp.bfloat16)
    upward_gradient = jnp.einsum(
        "gki,gkt->it", lifted_rows_full, hidden_rows_grad, preferred_element_type=jnp.float32
    )
    lifted_part = jnp.einsum(
        "eiw,mw->eim", hidden_rows_grad, upward_weight_whole, preferred_element_type=jnp.float32
    )
    lifted_grad = lax.psum_scatter(lifted_part, "mp", scatter_dimension=1, tiled=True)
    norm_out, middle_back = jax.vjp(layer_norm, middle, gain_mid)
    middle_part, mid_gain_grad = middle_back(lifted_grad)
    middle_grad = output_grad.astype(jnp.float32) + middle_part
    middle_half_precision = middle_grad.astype(jnp.bfloat16)
    outward_part = jnp.einsum(
        "hyk,hyo->ko",
        mixed_half_precision,
        middle_half_precision,
        preferred_element_type=jnp.float32,
    )
    mixed_grad = jnp.einsum(
        "hox,kx->hok",
        middle_half_precision,
        outward_weight_whole,
        preferred_element_type=jnp.float32,
    )
    context_out, context_back = jax.vjp(layer_norm, context_in, gain_ctx)
    context_grad, ctx_gain_grad = context_back(mixed_grad)
    context_heads = lax.all_to_all(
        context_grad.astype(jnp.bfloat16), "mp", split_axis=2, concat_axis=1, tiled=True
    )
    grad_heads = context_heads.reshape(seq_count, length, heads_local, HEAD_DIM)

    def backward_block(totals, inputs):
        key_total, value_total = totals
        start, log_block = inputs
        query_block = lax.dynamic_slice_in_dim(queries, start, block_len, 1)
        grad_block = lax.dynamic_slice_in_dim(grad_heads, start, block_len, 1)
        scores = block_scores(query_block, start)
        attention = jnp.exp(scores - log_block[..., None])
        prob_grad = jnp.einsum(
            "sqhd,skhd->shqk", grad_block, values, preferred_element_type=jnp.float32
        )
        row_dot = jnp.sum(attention * prob_grad, axis=-1, keepdims=True)
        score_low = (attention * (prob_grad - row_dot)).astype(jnp.bfloat16)
        query_turned = (
            jnp.einsum("shqk,skhd->sqhd", score_low, key_rows, preferred_element_type=jnp.float32)
            * 0.125
        )
        key_total = (
            key_total
            + jnp.einsum(
                "shqk,sqhd->skhd", score_low, query_block, preferred_element_type=jnp.float32
            )
            * 0.125
        )
        value_total = value_total + jnp.einsum(
            "shqk,sqhd->skhd",
            attention.astype(jnp.bfloat16),
            grad_block,
            preferred_element_type=jnp.float32,
        )
        return ((key_total, value_total), query_turned)

    zero_heads = jnp.zeros((seq_count, length, heads_local, HEAD_DIM), jnp.float32)
    (key_turned, value_grad), query_blocks = lax.scan(
        backward_block, (zero_heads, zero_heads), (starts, log_sums)
    )
    query_turned = jnp.transpose(query_blocks, (1, 0, 2, 3, 4)).reshape(
        seq_count, length, heads_local, HEAD_DIM
    )
    query_out, query_back = jax.vjp(lambda inputs: rotate(inputs, tables, 1.0), shaped[0])
    key_out, key_back = jax.vjp(lambda inputs: rotate(inputs, tables, -1.0), shaped[1])
    projection_gradient = (
        jnp.stack([query_back(query_turned)[0], key_back(key_turned)[0], value_grad])
        .astype(jnp.bfloat16)
        .reshape(3, seq_count, length, heads_local * HEAD_DIM)
    )
    head_grad = jnp.einsum(
        "fbn,ufbj->unj", normed_rows_full, projection_gradient, preferred_element_type=jnp.float32
    )
    normed_part = jnp.einsum(
        "acqr,aur->cqu", projection_gradient, head_weight_whole, preferred_element_type=jnp.float32
    )
    normed_grad = lax.psum_scatter(
        normed_part.astype(jnp.bfloat16), "mp", scatter_dimension=1, tiled=True
    ).astype(jnp.float32)
    input_out, input_back = jax.vjp(layer_norm, merged, gain_in)
    merged_part, in_gain_grad = input_back(normed_grad)
    input_grad = middle_grad + merged_part
    head_sum, outward_sum, upward_sum, downward_sum = (
        lax.psum_scatter(
            head_grad.astype(jnp.bfloat16), "dp", scatter_dimension=1, tiled=True
        ).astype(jnp.float32),
        lax.psum_scatter(
            outward_part.astype(jnp.bfloat16), "dp", scatter_dimension=0, tiled=True
        ).astype(jnp.float32),
        lax.psum_scatter(
            upward_gradient.astype(jnp.bfloat16), "dp", scatter_dimension=0, tiled=True
        ).astype(jnp.float32),
        lax.psum_scatter(
            down_grad.astype(jnp.bfloat16), "dp", scatter_dimension=1, tiled=True
        ).astype(jnp.float32),
    )
    outward_sum = lax.psum(outward_sum.astype(jnp.bfloat16), "mp").astype(jnp.float32)
    moment_head, square_head, head_dir = adapt_step(
        head_sum, head_master, head_moment, head_square, DECAY_RATE
    )
    moment_outward, square_outward, outward_dir = adapt_step(
        outward_sum, outward_master, outward_moment, outward_square, DECAY_RATE
    )
    moment_upward, square_upward, upward_dir = adapt_step(
        upward_sum, upward_master, upward_moment, upward_square, DECAY_RATE
    )
    moment_downward, square_downward, downward_dir = adapt_step(
        downward_sum, downward_master, downward_moment, downward_square, DECAY_RATE
    )
    owner = (model_rank == 0).astype(jnp.float32)
    head_part = jnp.stack(
        [
            jnp.sum(head_master * head_master, axis=(1, 2)),
            jnp.sum(head_dir * head_dir, axis=(1, 2)),
        ],
        axis=-1,
    )
    norm_part = jnp.concatenate(
        [
            head_part,
            pair_sums(outward_master, outward_dir) * owner,
            pair_sums(upward_master, upward_dir),
            pair_sums(downward_master, downward_dir),
        ],
        axis=0,
    )
    gains_part = jnp.concatenate(
        [in_gain_grad, ctx_gain_grad, mid_gain_grad, jnp.zeros((FF,), jnp.float32)]
    )
    gains_part = lax.dynamic_update_slice(gains_part, hidden_gain_grad, (hidden_start,))
    gains_sum, norm_sums = lax.psum((gains_part, norm_part), ("dp", "mp"))
    moment_gains, square_gains, gains_dir = adapt_step(
        gains_sum, gains_master, gains_moment, gains_square, 0.0
    )
    gains_sums = jnp.stack(
        [
            gain_segments(gains_master * gains_master, model_width),
            gain_segments(gains_dir * gains_dir, model_width),
        ],
        axis=-1,
    )
    updated_head = trust_move(
        head_master, head_dir, norm_sums[0:3, 0][:, None, None], norm_sums[0:3, 1][:, None, None]
    )
    updated_outward = trust_move(outward_master, outward_dir, norm_sums[3, 0], norm_sums[3, 1])
    updated_upward = trust_move(upward_master, upward_dir, norm_sums[4, 0], norm_sums[4, 1])
    updated_downward = trust_move(downward_master, downward_dir, norm_sums[5, 0], norm_sums[5, 1])
    updated_gains = trust_move(
        gains_master,
        gains_dir,
        gain_spread(gains_sums[:, 0], model_width, FF),
        gain_spread(gains_sums[:, 1], model_width, FF),
    )
    update_norms = jnp.sqrt(jnp.concatenate([norm_sums, gains_sums], axis=0))
    return (
        layer_output,
        input_grad,
        moment_head,
        square_head,
        updated_head,
        updated_head.astype(jnp.bfloat16),
        moment_outward,
        square_outward,
        updated_outward,
        updated_outward.astype(jnp.bfloat16),
        moment_upward,
        square_upward,
        updated_upward,
        updated_upward.astype(jnp.bfloat16),
        moment_downward,
        square_downward,
        updated_downward,
        updated_downward.astype(jnp.bfloat16),
        moment_gains,
        square_gains,
        updated_gains,
        update_norms,
    )


SHARE = 0.3
LOG2E = 1.4426950408889634
LANES = 128
NT = (((1,), (1,)), ((), ()))
NN = (((1,), (0,)), ((), ()))
LOW = jnp.bfloat16
WIDE = jnp.float32
ONCE = pl.Buffered(1)
MESH = pl.DeviceIdType.MESH
ANYWHERE = pl.BlockSpec(memory_space=pl.ANY)


def like(value):
    return jax.ShapeDtypeStruct(value.shape, value.dtype)


def dot(left, right, dims):
    return lax.dot_general(left, right, dims, preferred_element_type=WIDE)


def kernel_call(body, grid, in_specs, out_specs, out_shape, scratch, flops, moved, operands, done=(), carry=()):
    count, extra, outs = len(operands), len(done) + len(carry), len(out_specs)

    def whole(*refs):
        inner = refs[count + extra :]
        body(*refs[:count], *inner[:outs], *inner[outs + len(carry) :])

    return pl.pallas_call(
        whole,
        grid_spec=pltpu.PrefetchScalarGridSpec(
            num_scalar_prefetch=1,
            grid=grid,
            in_specs=list(in_specs) + [ANYWHERE] * extra,
            out_specs=list(out_specs) + [ANYWHERE] * len(carry),
            scratch_shapes=scratch,
        ),
        out_shape=list(out_shape) + [like(value) for value in carry],
        input_output_aliases={count + len(done) + n: outs + n for n in range(len(carry))},
        compiler_params=pltpu.CompilerParams(vmem_limit_bytes=56 << 20),
        cost_estimate=pl.CostEstimate(flops=int(flops * SHARE), bytes_accessed=int(moved * SHARE), transcendentals=0),
    )(*operands, *done, *carry)


def mate(rank, j):
    return (rank, rank + 1 - 2 * (rank % 2), (rank + 2) % 4, 3 - rank)[j]


def hand_on(value, done):
    return pl.pallas_call(
        lambda *refs: None,
        in_specs=[ANYWHERE] * (1 + len(done)),
        out_specs=ANYWHERE,
        out_shape=like(value),
        input_output_aliases={0: 0},
    )(value, *done)


def own_rows(sub, rank, j, b):
    return pl.ds(pl.multiple_of(b * 4 * sub + mate(rank, j) * sub, sub), sub)


def own_block(place, k, width):
    return pl.ds(pl.multiple_of((place ^ k) * width, width), width)


def swap_halves(block):
    low = lax.broadcasted_iota(jnp.int32, (1, LANES), 1) % HEAD_DIM < HEAD_DIM // 2
    return jnp.where(low, pltpu.roll(block, LANES - HEAD_DIM // 2, 1), pltpu.roll(block, HEAD_DIM // 2, 1))


def project_kernel(ids, x, w0, w1, w2, w3, cq, sq, ck, sk, q, k, v):
    depth = w0.shape[1]
    width = w0.shape[2]
    for f, (out, c, s) in enumerate(((q, cq, sq), (k, ck, sk), (v, None, None))):
        total = None
        for n, w in enumerate((w0, w1, w2, w3)):
            part = dot(x[:, own_block(ids[1], n, depth)], w[f], NN)
            total = part if total is None else total + part
        for p in range(width // LANES):
            here = slice(p * LANES, (p + 1) * LANES)
            block = total[:, here]
            if c is not None:
                block = block * c[...] + swap_halves(block) * s[...]
            out[:, here] = block.astype(LOW)


def quarters(weight):
    if isinstance(weight, list):
        spec = pl.BlockSpec(weight[0].shape, lambda b, ids: (0, 0, 0), pipeline_mode=ONCE)
        return weight, [spec] * 4
    kinds, model, width = weight.shape
    return [weight] * 4, [
        pl.BlockSpec((kinds, model // 4, width), partial(lambda n, b, ids: (0, ids[1] ^ n, 0), n), pipeline_mode=ONCE)
        for n in range(4)
    ]


def project(ids, x, weight, tables, j, done=(), carry=()):
    rows, model = x.shape
    sub = rows // 2
    weights, specs = quarters(weight)
    width = weights[0].shape[2]
    table = pl.BlockSpec((sub, LANES), lambda b, ids: (b * 4 + (ids[0] ^ j), 0))
    out = pl.BlockSpec((sub, width), lambda b, ids: (b, 0))
    return kernel_call(
        project_kernel,
        (2,),
        [pl.BlockSpec((sub, model), lambda b, ids: (b, 0))] + specs + [table] * 4,
        [out] * 3,
        [jax.ShapeDtypeStruct((rows, width), LOW)] * 3,
        [],
        6 * rows * model * width,
        6 * model * width + 8 * rows * model,
        (ids, x, *weights, *tables),
        done,
        carry,
    )


def attend_kernel(ids, *refs, bq, bk):
    q_, k_, v_, o_, lse_ref = refs[0:4], refs[4:8], refs[8:12], refs[12:16], refs[16]
    qs, ks, vt, os = refs[17:]
    rank = ids[0]
    length = qs.shape[0]
    sub = q_[0].shape[0] // 2
    for j in range(4):
        for b in range(2):
            rows = own_rows(sub, rank, j, b)
            here = slice(b * sub, (b + 1) * sub)
            qs[rows, :] = q_[j][here, :]
            ks[rows, :] = k_[j][here, :]
            vt[:, rows] = v_[j][here, :].T
    first = lax.broadcasted_iota(jnp.int32, (1, LANES), 1) < HEAD_DIM
    ratio = bq // bk

    def q_block(i, _):
        here = pl.ds(pl.multiple_of(i * bq, bq), bq)
        q = qs[here, :]
        zero = jnp.zeros_like(q)
        parted = (jnp.where(first, q, zero), jnp.where(first, zero, q))

        def step(j, carry, diagonal):
            at = pl.multiple_of(j * bk, bk)
            k = ks[pl.ds(at, bk), :]
            out = []
            for h in range(2):
                highest, total, sums = carry[h]
                scores = dot(k, parted[h], NT) * (0.125 * LOG2E)
                if diagonal is not None:
                    key = diagonal * bk + lax.broadcasted_iota(jnp.int32, (bk, bq), 0)
                    scores = jnp.where(key <= lax.broadcasted_iota(jnp.int32, (bk, bq), 1), scores, -1e30)
                new = jnp.maximum(highest, jnp.max(scores, axis=0, keepdims=True))
                probs = jnp.exp2(scores - new)
                scale = jnp.exp2(highest - new)
                total = total * scale + jnp.sum(probs, axis=0, keepdims=True)
                rows = vt[h * HEAD_DIM : (h + 1) * HEAD_DIM, pl.ds(at, bk)]
                out.append((new, total, sums * scale + dot(rows, probs.astype(LOW), NN)))
            return tuple(out)

        start = tuple(
            (jnp.full((1, bq), -1e30, WIDE), jnp.zeros((1, bq), WIDE), jnp.zeros((HEAD_DIM, bq), WIDE))
            for _ in range(2)
        )
        carry = lax.fori_loop(0, i * ratio, lambda j, c: step(j, c, None), start)
        for d in range(ratio):
            carry = step(i * ratio + d, carry, d)
        turned = jnp.concatenate([carry[h][2] / carry[h][1] for h in range(2)], axis=0)
        os[here, :] = turned.T.astype(LOW)
        for h in range(2):
            lse_ref[0, h : h + 1, here] = carry[h][0] + jnp.log2(carry[h][1])
        return 0

    lax.fori_loop(0, length // bq, q_block, 0)
    for j in range(4):
        for b in range(2):
            o_[j][b * sub : (b + 1) * sub, :] = os[own_rows(sub, rank, j, b), :]


def attend(ids, queries, keys, values, done=(), carry=()):
    rows, width = queries[0].shape
    length, pairs = rows * 4, width // LANES
    chunk = pl.BlockSpec((rows, LANES), lambda p, ids: (0, p))
    low = pltpu.VMEM((length, LANES), LOW)
    result = kernel_call(
        partial(attend_kernel, bq=min(1024, length), bk=min(512, length)),
        (pairs,),
        [chunk] * 12,
        [chunk] * 4 + [pl.BlockSpec((1, 2, length), lambda p, ids: (p, 0, 0))],
        [jax.ShapeDtypeStruct((rows, width), LOW)] * 4 + [jax.ShapeDtypeStruct((pairs, 2, length), WIDE)],
        [low, low, pltpu.VMEM((LANES, length), LOW), low],
        40e9,
        10e6,
        (ids, *queries, *keys, *values),
        done,
        carry,
    )
    return result[:4], result[4], *result[5:]


def attend_back_kernel(*refs, bq, bk):
    q_, k_, v_, d_, o_ = refs[0:4], refs[4:8], refs[8:12], refs[12:16], refs[16:20]
    lse_ref, cq, sq, ck, sk, away = refs[20:26]
    dq_, dk_, dv_, back = refs[-15:-11]
    qs, ks, vs, ds, kt, dqt, dks, dvs, delta, sent, got = refs[-11:]
    over_high = partners()[4]
    crossing = remote(away, back, sent, got, over_high)

    @pl.when(pl.program_id(0) == 0)
    def _():
        greet((over_high,))
        crossing.start()

    rank = lax.axis_index("mp") % 4
    length = qs.shape[0]
    sub = q_[0].shape[0] // 2
    for j in range(4):
        for b in range(2):
            rows = own_rows(sub, rank, j, b)
            here = slice(b * sub, (b + 1) * sub)
            qs[rows, :] = q_[j][here, :]
            ks[rows, :] = k_[j][here, :]
            kt[:, rows] = k_[j][here, :].T
            vs[rows, :] = v_[j][here, :]
            ds[rows, :] = d_[j][here, :]
            product = (d_[j][here, :].astype(WIDE) * o_[j][here, :].astype(WIDE)).T
            delta[0:1, rows] = jnp.sum(product[:HEAD_DIM], axis=0, keepdims=True)
            delta[1:2, rows] = jnp.sum(product[HEAD_DIM:], axis=0, keepdims=True)
    first = lax.broadcasted_iota(jnp.int32, (1, LANES), 1) < HEAD_DIM
    dqt[...] = jnp.zeros_like(dqt)

    def k_block(j, _):
        at = pl.ds(pl.multiple_of(j * bk, bk), bk)
        k = ks[at, :]
        v = vs[at, :]

        def step(i, carry, diagonal):
            dk, dv = carry
            here = pl.ds(pl.multiple_of(i * bq, bq), bq)
            q, do = qs[here, :], ds[here, :]
            zero = jnp.zeros_like(q)
            for h in range(2):
                lanes = slice(h * HEAD_DIM, (h + 1) * HEAD_DIM)
                q_own = jnp.where(first, q, zero) if h == 0 else jnp.where(first, zero, q)
                do_own = jnp.where(first, do, zero) if h == 0 else jnp.where(first, zero, do)
                scores = dot(k, q_own, NT) * (0.125 * LOG2E) - lse_ref[0, h : h + 1, here]
                if diagonal:
                    key = lax.broadcasted_iota(jnp.int32, (bk, bq), 0)
                    scores = jnp.where(key <= lax.broadcasted_iota(jnp.int32, (bk, bq), 1), scores, -1e30)
                probs = jnp.exp2(scores)
                prob_grad = dot(v, do_own, NT)
                grad = (probs * (prob_grad - delta[h : h + 1, here])).astype(LOW)
                dv = dv + dot(probs.astype(LOW), do_own, NN)
                dk = dk + dot(grad, q_own, NN)
                dqt[lanes, here] += dot(kt[lanes, at], grad, NN)
            return dk, dv

        zeros = jnp.zeros((bk, LANES), WIDE)
        carry = step(j, (zeros, zeros), True)
        dk, dv = lax.fori_loop(j + 1, length // bq, lambda i, c: step(i, c, False), carry)
        dks[at, :] = dk * 0.125
        dvs[at, :] = dv.astype(LOW)
        return 0

    lax.fori_loop(0, length // bk, k_block, 0)
    for j in range(4):
        for b in range(2):
            rows = own_rows(sub, rank, j, b)
            here = slice(b * sub, (b + 1) * sub)
            query_grad = dqt[:, rows].T * 0.125
            dq_[j, here, :] = (query_grad * cq[rows, :] - swap_halves(query_grad) * sq[rows, :]).astype(LOW)
            key_grad = dks[rows, :]
            dk_[j, here, :] = (key_grad * ck[rows, :] - swap_halves(key_grad) * sk[rows, :]).astype(LOW)
            dv_[j, here, :] = dvs[rows, :]

    @pl.when(pl.program_id(0) == pl.num_programs(0) - 1)
    def _():
        crossing.wait()


def attend_back(queries, keys, values, cotangents, contexts, lse, tables, away, number, done):
    rows, width = queries[0].shape
    length, pairs = rows * 4, width // LANES
    chunk = pl.BlockSpec((rows, LANES), lambda p: (0, p))
    whole = pl.BlockSpec((length, LANES), lambda p: (0, 0), pipeline_mode=ONCE)
    low = pltpu.VMEM((length, LANES), LOW)
    block = min(512, length)
    return pl.pallas_call(
        partial(attend_back_kernel, bq=block, bk=block),
        grid=(pairs,),
        in_specs=[chunk] * 20 + [pl.BlockSpec((1, 2, length), lambda p: (p, 0, 0))]
        + [whole] * 4
        + [ANYWHERE] * (1 + len(done)),
        out_specs=[pl.BlockSpec((4, rows, LANES), lambda p: (0, 0, p))] * 3 + [ANYWHERE],
        out_shape=[jax.ShapeDtypeStruct((4, rows, width), LOW)] * 3 + [like(away)],
        scratch_shapes=[
            low,
            low,
            low,
            low,
            pltpu.VMEM((LANES, length), LOW),
            pltpu.VMEM((LANES, length), WIDE),
            pltpu.VMEM((length, LANES), WIDE),
            low,
            pltpu.VMEM((2, length), WIDE),
            pltpu.SemaphoreType.DMA,
            pltpu.SemaphoreType.DMA,
        ],
        compiler_params=pltpu.CompilerParams(
            collective_id=number, has_side_effects=True, vmem_limit_bytes=56 << 20
        ),
        cost_estimate=pl.CostEstimate(flops=40 * 10**9, bytes_accessed=20 << 20, transcendentals=0),
    )(*queries, *keys, *values, *cotangents, *contexts, lse, *tables, away, *done)


def centred(block):
    shifted = block - jnp.mean(block, axis=-1, keepdims=True)
    spread = jnp.mean(shifted * shifted, axis=-1, keepdims=True)
    scale = lax.rsqrt(spread + EPS_NORM)
    return shifted * scale, scale


def norm_back(standard, scale, gain, grad):
    scaled = grad * gain
    first = jnp.mean(scaled, axis=-1, keepdims=True)
    second = jnp.mean(scaled * standard, axis=-1, keepdims=True)
    return scale * (scaled - first - standard * second)


def context_lanes(ids, j, side, width):
    half = ids[2] ^ side
    return pl.ds(pl.multiple_of(half * 4 * width + (ids[0] ^ j) * width, width), width)


def mid_kernel(ids, *refs):
    pieces = refs[:8]
    merged, weights, (g_ctx, g_mid, ctx, mixed, middle, lifted) = refs[8], sheets(refs[9:13]), refs[13:]
    width = pieces[0].shape[1]
    for n, c in enumerate(pieces):
        ctx[:, context_lanes(ids, n % 4, n // 4, width)] = c[...]
    standard, _ = centred(ctx[...].astype(WIDE))
    mixed[...] = (standard * g_ctx[...]).astype(LOW)
    depth, half = weights[0].shape
    for n in range(2):
        lanes = core_lanes(ids, n, half)
        total = merged[:, lanes].astype(WIDE)
        for k in range(4):
            total = total + dot(mixed[:, own_block(ids[1], k, depth)], weights[4 * n + k][...], NN)
        middle[:, lanes] = total
    standard, _ = centred(middle[...])
    lifted[...] = (standard * g_mid[...]).astype(LOW)


def sheets(refs):
    own, pieces, other, others = refs
    return [own] + [pieces.at[n] for n in range(3)] + [other] + [others.at[n] for n in range(3)]


def core_lanes(ids, n, half):
    return pl.ds(pl.multiple_of((ids[0] % 2 ^ n) * half, half), half)


def mid_forward(ids, contexts, merged, weights, g_ctx, g_mid, carry):
    rows, model = merged.shape
    specs = [pl.BlockSpec(w.shape, partial(lambda n, b, ids: (0,) * n, w.ndim), pipeline_mode=ONCE) for w in weights]
    block = min(256, rows)
    line = lambda width: pl.BlockSpec((block, width), lambda b, ids: (b, 0))
    gain = pl.BlockSpec((1, model), lambda b, ids: (0, 0))
    shape = lambda kind: jax.ShapeDtypeStruct((rows, model), kind)
    return kernel_call(
        mid_kernel,
        (rows // block,),
        [line(contexts[0].shape[1])] * 8 + [line(model)] + specs + [gain] * 2,
        [line(model)] * 4,
        [shape(LOW), shape(LOW), shape(WIDE), shape(LOW)],
        [],
        2 * rows * model * model,
        2 * model * model + 14 * rows * model,
        (ids, *contexts, merged, *weights, g_ctx, g_mid),
        (),
        carry,
    )


def mid_back_kernel(ids, *refs):
    a, r, middle, og, ctx = refs[:5]
    weights, (g_mid, g_ctx, middle_grad, middle_low) = sheets(refs[5:9]), refs[9:13]
    pieces, gains, mixed_grad = refs[13:21], refs[21], refs[22]
    grad = a[...].astype(WIDE) + r[...].astype(WIDE)
    standard, scale = centred(middle[...])

    @pl.when(pl.program_id(0) == 0)
    def _():
        gains[...] = jnp.zeros_like(gains)

    gains[0:1, :] += jnp.sum(grad * standard, axis=0, keepdims=True)
    total = og[...].astype(WIDE) + norm_back(standard, scale, g_mid[...], grad)
    middle_grad[...] = total
    middle_low[...] = total.astype(LOW)
    depth, half = weights[0].shape
    own, other = middle_low[:, core_lanes(ids, 0, half)], middle_low[:, core_lanes(ids, 1, half)]
    for k in range(4):
        mixed_grad[:, own_block(ids[1], k, depth)] = dot(own, weights[k][...], NT) + dot(other, weights[4 + k][...], NT)
    grad = mixed_grad[...]
    standard, scale = centred(ctx[...].astype(WIDE))
    gains[1:2, :] += jnp.sum(grad * standard, axis=0, keepdims=True)
    mixed_grad[...] = norm_back(standard, scale, g_ctx[...], grad)
    width = pieces[0].shape[1]
    for n, d in enumerate(pieces):
        d[...] = mixed_grad[:, context_lanes(ids, n % 4, n // 4, width)].astype(LOW)


def mid_backward(ids, parts, middle, og, ctx, weights, g_mid, g_ctx):
    rows, model = middle.shape
    specs = [pl.BlockSpec(w.shape, partial(lambda n, b, ids: (0,) * n, w.ndim), pipeline_mode=ONCE) for w in weights]
    block = min(256, rows)
    line = lambda width: pl.BlockSpec((block, width), lambda b, ids: (b, 0))
    gain = pl.BlockSpec((1, model), lambda b, ids: (0, 0))
    shape = lambda width, kind: jax.ShapeDtypeStruct((rows, width), kind)
    result = kernel_call(
        mid_back_kernel,
        (rows // block,),
        [line(model)] * 5 + specs + [gain] * 2,
        [line(model)] * 2 + [line(model // 8)] * 8 + [pl.BlockSpec((8, model), lambda b, ids: (0, 0))],
        [shape(model, WIDE), shape(model, LOW)]
        + [shape(model // 8, LOW)] * 8
        + [jax.ShapeDtypeStruct((8, model), WIDE)],
        [pltpu.VMEM((block, model), WIDE)],
        2 * rows * model * model,
        2 * model * model + 18 * rows * model,
        (ids, *parts, middle, og, ctx, *weights, g_mid, g_ctx),
    )
    return result[0], result[1], result[2:6], result[6:10], result[10]


def gelu_parts(hidden):
    share = 0.5 + 0.5 * lax.erf(hidden * 0.7071067811865476)
    return hidden * share, share


def gelu_slope(hidden, share):
    return share + hidden * (0.3989422804014327 * jnp.exp(-0.5 * hidden * hidden))


def fold(block):
    out = block[..., :LANES]
    for p in range(1, block.shape[-1] // LANES):
        out = out + block[..., p * LANES : (p + 1) * LANES]
    return out


def halves(count, rows_first):
    if rows_first:
        return (
            lambda u, ids: (jnp.minimum(u, count - 1), 0),
            lambda u, ids: (jnp.maximum(u - count, 0), 0),
        )
    return (
        lambda u, ids: (0, jnp.minimum(u, count - 1)),
        lambda u, ids: (0, jnp.maximum(u - count, 0)),
    )


def each_half(work, own, got):
    near = pl.program_id(0) < pl.num_programs(0) // 2

    @pl.when(near)
    def _():
        work(own)

    @pl.when(jnp.logical_not(near))
    def _():
        work(got)


def remote(source, target, sent, got, device):
    return pltpu.make_async_remote_copy(
        src_ref=source, dst_ref=target, send_sem=sent, recv_sem=got, device_id=device, device_id_type=MESH
    )


def ffn_up_kernel(
    lifted, up_own, up_got, act, slope, sums, lifted_all, x, acc, sent, got, local
):
    j, u = pl.program_id(0), pl.program_id(1)
    rows = x.shape[0]
    half = rows // 2
    _, _, over_core, over_low, _ = partners()
    parts = [pl.ds(b * half, half) for b in range(2)]

    def moves(source, whole, base):
        near = remote(source, whole.at[0], sent.at[base], got.at[base], over_core)
        far = [
            remote(source.at[part], whole.at[1, part], sent.at[base + 1 + b], got.at[base + 1 + b], over_low)
            for b, part in enumerate(parts)
        ]
        last = [
            remote(whole.at[1, part], whole.at[2, part], sent.at[base + 3 + b], got.at[base + 3 + b], over_core)
            for b, part in enumerate(parts)
        ]
        return near, far, last

    near, far, last = moves(lifted, lifted_all, 0)

    def load(source):
        copy = pltpu.make_async_copy(source, x, local)
        copy.start()
        copy.wait()

    @pl.when(u == 0)
    def _():
        acc[...] = jnp.zeros_like(acc)

    @pl.when((j == 0) & (u == 0))
    def _():
        greet((over_core, over_low))
        for copy in (*far, near):
            copy.start()
        load(lifted)

    @pl.when((j == 1) & (u == 0))
    def _():
        near.wait()
        load(lifted_all.at[0])

    @pl.when((j == 2) & (u == 0))
    def _():
        for copy, onward in zip(far, last):
            copy.wait()
            onward.start()
        load(lifted_all.at[1])

    @pl.when((j == 3) & (u == 0))
    def _():
        for copy in last:
            copy.wait()
        load(lifted_all.at[2])

    def work(up):
        for b in range(2):
            here = slice(b * half, (b + 1) * half)
            h = dot(x[here, :], up[...], NN)
            activated, share = gelu_parts(h)
            low = activated.astype(LOW)
            act[0, here, :] = low
            slope[0, here, :] = gelu_slope(h, share).astype(LOW)
            activated = low.astype(WIDE)
            acc[0, here, :] += fold(activated)
            acc[1, here, :] += fold(activated * activated)

    steps = pl.num_programs(1)
    pl.when(u < steps // 2)(lambda: work(up_own))
    pl.when(u >= steps // 2)(lambda: work(up_got))

    @pl.when(u == steps - 1)
    def _():
        for n in range(2):
            sums[0, n : n + 1, :] = jnp.sum(acc[n].T, axis=0, keepdims=True)
        sums[0, 2:8, :] = jnp.zeros_like(sums[0, 2:8, :])


def in_halves(count, rows_first):
    near, far = (lambda u: jnp.minimum(u, count - 1)), (lambda u: jnp.maximum(u - count, 0))
    if rows_first:
        return [lambda j, u: (near(u), 0), lambda j, u: (far(u), 0)]
    return [lambda j, u: (0, near(u)), lambda j, u: (0, far(u))]


def ffn_up(lifted, upward):
    rows, model = lifted.shape
    units = 2 * upward[0].shape[1]
    block = min(512, units // 2)
    count = units // 2 // block
    out = pl.BlockSpec((1, rows, block), lambda j, u: (j, 0, u))
    kept = jax.ShapeDtypeStruct((4, rows, units), LOW)
    others = jax.ShapeDtypeStruct((3, rows, model), LOW)
    return pl.pallas_call(
        ffn_up_kernel,
        grid=(4, 2 * count),
        in_specs=[ANYWHERE] + [pl.BlockSpec((model, block), at) for at in in_halves(count, False)],
        out_specs=[out] * 2 + [pl.BlockSpec((1, 8, rows), lambda j, u: (j, 0, 0)), ANYWHERE],
        out_shape=[kept] * 2 + [jax.ShapeDtypeStruct((4, 8, rows), WIDE), others],
        scratch_shapes=[
            pltpu.VMEM((rows, model), LOW),
            pltpu.VMEM((2, rows, LANES), WIDE),
            pltpu.SemaphoreType.DMA((5,)),
            pltpu.SemaphoreType.DMA((5,)),
            pltpu.SemaphoreType.DMA,
        ],
        compiler_params=pltpu.CompilerParams(collective_id=2, has_side_effects=True, vmem_limit_bytes=56 << 20),
        cost_estimate=pl.CostEstimate(flops=80 * 10**9, bytes_accessed=100 << 20, transcendentals=0),
    )(lifted, *upward)


def ffn_back_kernel(og, near, far, last, down_own, down_got, act, gain, squashed_grad, sums, x, acc, local):
    j, u = pl.program_id(0), pl.program_id(1)
    rows = x.shape[0]
    half = rows // 2

    @pl.when(u == 0)
    def _():
        acc[...] = jnp.zeros_like(acc)

    def load(source):
        copy = pltpu.make_async_copy(source, x, local)
        copy.start()
        copy.wait()

    for n, source in enumerate((og, near, far, last)):
        pl.when((u == 0) & (j == n))(partial(load, source))

    def work(down):
        for b in range(2):
            here = slice(b * half, (b + 1) * half)
            s = dot(x[here, :], down[...], NT).astype(LOW)
            squashed_grad[0, here, :] = s
            scaled = s.astype(WIDE) * gain[...]
            acc[0, here, :] += fold(scaled)
            acc[1, here, :] += fold(scaled * act[0, here, :].astype(WIDE))

    steps = pl.num_programs(1)
    pl.when(u < steps // 2)(lambda: work(down_own))
    pl.when(u >= steps // 2)(lambda: work(down_got))

    @pl.when(u == steps - 1)
    def _():
        sums[0, 0:2, :] = jnp.zeros_like(sums[0, 0:2, :])
        for n in range(2):
            sums[0, n + 2 : n + 3, :] = jnp.sum(acc[n].T, axis=0, keepdims=True)
        sums[0, 4:8, :] = jnp.zeros_like(sums[0, 4:8, :])


def ffn_back(og, others, downward, act, gain):
    rows, model = og.shape
    units = act.shape[2]
    block = min(512, units // 2)
    count = units // 2 // block
    line = pl.BlockSpec((1, rows, block), lambda j, u: (j, 0, u))
    return pl.pallas_call(
        ffn_back_kernel,
        grid=(4, 2 * count),
        in_specs=[ANYWHERE] * 4
        + [pl.BlockSpec((block, model), at) for at in in_halves(count, True)]
        + [line, pl.BlockSpec((1, block), lambda j, u: (0, u))],
        out_specs=[line, pl.BlockSpec((1, 8, rows), lambda j, u: (j, 0, 0))],
        out_shape=[like(act), jax.ShapeDtypeStruct((4, 8, rows), WIDE)],
        scratch_shapes=[
            pltpu.VMEM((rows, model), LOW),
            pltpu.VMEM((2, rows, LANES), WIDE),
            pltpu.SemaphoreType.DMA,
        ],
        compiler_params=pltpu.CompilerParams(vmem_limit_bytes=56 << 20),
        cost_estimate=pl.CostEstimate(flops=60 * 10**9, bytes_accessed=100 << 20, transcendentals=0),
    )(og, *others, *downward, act, gain)


def ffn_second_kernel(
    act,
    slope,
    squashed_grad,
    sums,
    gain,
    up_own,
    up_got,
    squashed,
    hidden_grad,
    kept,
    arrived,
    gains,
    acc,
    send_core,
    got_core,
    send_low,
    sent,
    got,
    *,
    hidden_width,
):
    n, u = pl.program_id(0), pl.program_id(1)
    steps = pl.num_programs(1)
    rows, block = act.shape[1:]
    half = rows // 2
    _, _, over_core, over_low, _ = partners()
    to_core = [remote(send_core.at[b], got_core.at[b], sent.at[b], got.at[b], over_core) for b in range(2)]
    to_low = remote(send_low, arrived, sent.at[2], got.at[2], over_low)

    @pl.when((n == 0) & (u == 0))
    def _():
        greet((over_core, over_low))
        gains[...] = jnp.zeros_like(gains)

    @pl.when(u == 0)
    def _():
        acc[...] = jnp.zeros_like(acc)

    columns = sums[0].T
    lanes = pl.ds(pl.multiple_of(u * block, block), block)

    def work(up):
        for b in range(2):
            here = slice(b * half, (b + 1) * half)
            centre = columns[here, 0:1] / hidden_width
            scale = lax.rsqrt(columns[here, 1:2] / hidden_width - centre * centre + EPS_NORM)
            mean_one = columns[here, 2:3] / hidden_width
            mean_two = scale * (columns[here, 3:4] - centre * columns[here, 2:3]) / hidden_width
            standard = (act[0, here, :].astype(WIDE) - centre) * scale
            squashed[0, here, :] = (standard * gain[...]).astype(LOW)
            s = squashed_grad[0, here, :].astype(WIDE)
            gains[0:1, lanes] += jnp.sum(s * standard, axis=0, keepdims=True)
            activated_grad = (s * gain[...] - mean_one - standard * mean_two) * scale
            grad = (activated_grad * slope[0, here, :].astype(WIDE)).astype(LOW)
            hidden_grad[0, here, :] = grad
            acc[here, :] += dot(grad, up[...], NT)

    pl.when(u < steps // 2)(lambda: work(up_own))
    pl.when(u >= steps // 2)(lambda: work(up_got))
    ends = u == steps - 1

    @pl.when(ends & (n == 0))
    def _():
        send_core[0] = acc[...].astype(LOW)
        to_core[0].start()

    @pl.when(ends & (n == 1))
    def _():
        to_core[0].wait()
        send_low[...] = (acc[...] + got_core[0].astype(WIDE)).astype(LOW)
        to_low.start()

    @pl.when(ends & (n == 2))
    def _():
        send_core[1] = acc[...].astype(LOW)
        to_core[1].start()

    @pl.when(ends & (n == 3))
    def _():
        to_core[1].wait()
        kept[...] = (acc[...] + got_core[1].astype(WIDE)).astype(LOW)
        to_low.wait()


def ffn_second(act, slope, squashed_grad, sums, gain, upward, hidden_width):
    _, rows, units = act.shape
    model = upward[0].shape[0]
    block = min(512, units // 2)
    count = units // 2 // block
    line = pl.BlockSpec((1, rows, block), lambda n, u: (3 - n, 0, u))
    piece = jax.ShapeDtypeStruct((rows, model), LOW)
    return pl.pallas_call(
        partial(ffn_second_kernel, hidden_width=hidden_width),
        grid=(4, 2 * count),
        in_specs=[line] * 3
        + [pl.BlockSpec((1, 8, rows), lambda n, u: (3 - n, 0, 0)), pl.BlockSpec((1, block), lambda n, u: (0, u))]
        + [pl.BlockSpec((model, block), at) for at in in_halves(count, False)],
        out_specs=[line] * 2
        + [pl.BlockSpec((rows, model), lambda n, u: (0, 0)), ANYWHERE, pl.BlockSpec((8, units), lambda n, u: (0, 0))],
        out_shape=[like(act)] * 2 + [piece] * 2 + [jax.ShapeDtypeStruct((8, units), WIDE)],
        scratch_shapes=[
            pltpu.VMEM((rows, model), WIDE),
            pltpu.VMEM((2, rows, model), LOW),
            pltpu.VMEM((2, rows, model), LOW),
            pltpu.VMEM((rows, model), LOW),
            pltpu.SemaphoreType.DMA((3,)),
            pltpu.SemaphoreType.DMA((3,)),
        ],
        compiler_params=pltpu.CompilerParams(collective_id=3, has_side_effects=True, vmem_limit_bytes=60 << 20),
        cost_estimate=pl.CostEstimate(flops=80 * 10**9, bytes_accessed=100 << 20, transcendentals=0),
    )(act, slope, squashed_grad, sums, gain, *upward)


def spread_kernel(ids, x, own, got, out, acc):
    step = pl.program_id(0)

    @pl.when(step == 0)
    def _():
        acc[...] = jnp.zeros_like(acc)

    def work(weight):
        acc[...] += dot(x[...], weight[...], NN)

    each_half(work, own, got)

    @pl.when(step == pl.num_programs(0) - 1)
    def _():
        out[...] = acc[...].astype(LOW)


def ffn_out(ids, x, j, downward):
    _, rows, units = x.shape
    model = downward[0].shape[1]
    block = min(512, units // 2)
    count = units // 2 // block
    return kernel_call(
        spread_kernel,
        (2 * count,),
        [pl.BlockSpec((pl.Squeezed(), rows, block), lambda u, ids: (j, 0, u))]
        + [pl.BlockSpec((block, model), at) for at in halves(count, True)],
        [pl.BlockSpec((rows, model), lambda u, ids: (0, 0))],
        [jax.ShapeDtypeStruct((rows, model), LOW)],
        [pltpu.VMEM((rows, model), WIDE)],
        2 * rows * model * units,
        2 * model * units + 2 * rows * (units + model),
        (ids, x, *downward),
    )[0]


def unproject_kernel(*refs):
    grads, owns, got_weight, away = refs[0:6], refs[6:10], refs[10], refs[11:13]
    kept, arrived, *back = refs[-10:-6]
    acc, send_core, got_core, send_low, sent, got = refs[-6:]
    n, b = pl.program_id(0), pl.program_id(1)
    rows = acc.shape[0]
    depth = owns[0].shape[1]
    place = lax.axis_index("dp")
    _, _, over_core, over_low, over_high = partners()
    here = pl.ds(pl.multiple_of(b * rows, rows), rows)

    def to_core(slot, half):
        s = 2 * slot + half
        return remote(send_core.at[s], got_core.at[s], sent.at[s], got.at[s], over_core)

    def to_low(half):
        part = pl.ds(half * rows, rows)
        return remote(send_low.at[half], arrived.at[part], sent.at[4 + half], got.at[4 + half], over_low)

    crossing = [remote(away[i], back[i], sent.at[6 + i], got.at[6 + i], over_high) for i in range(2)]

    @pl.when((n == 0) & (b == 0))
    def _():
        greet((over_core, over_low, over_high))
        for copy in crossing:
            copy.start()

    acc[...] = sum(dot(grads[3 + f][0], got_weight[f], NT) for f in range(3))
    for k in range(4):
        lanes = pl.ds(pl.multiple_of(mate(place, k) * depth, depth), depth)
        acc[:, lanes] += sum(dot(grads[f][0], owns[k][f], NT) for f in range(3))

    for half in range(2):

        @pl.when((n == 0) & (b == half))
        def _():
            send_core[half] = acc[...].astype(LOW)
            to_core(0, half).start()

        @pl.when((n == 1) & (b == half))
        def _():
            to_core(0, half).wait()
            send_low[half] = (acc[...] + got_core[half].astype(WIDE)).astype(LOW)
            to_low(half).start()

        @pl.when((n == 2) & (b == half))
        def _():
            send_core[2 + half] = acc[...].astype(LOW)
            to_core(1, half).start()

        @pl.when((n == 3) & (b == half))
        def _():
            to_core(1, half).wait()
            kept[here, :] = (acc[...] + got_core[2 + half].astype(WIDE)).astype(LOW)

    @pl.when((n == 3) & (b == 1))
    def _():
        to_low(0).wait()
        to_low(1).wait()
        for copy in crossing:
            copy.wait()


def unproject(grads, heads, away, done):
    _, rows, width = grads[0].shape
    own, got = heads
    model = got.shape[1]
    half = rows // 2
    line = pl.BlockSpec((1, half, width), lambda n, b: (3 - n, b, 0))
    still = lambda value: pl.BlockSpec(value.shape, lambda n, b: (0,) * value.ndim, pipeline_mode=ONCE)
    piece = jax.ShapeDtypeStruct((rows, model), LOW)
    buffer = lambda count: pltpu.VMEM((count, half, model), LOW)
    return pl.pallas_call(
        unproject_kernel,
        grid=(4, 2),
        in_specs=[line] * 6 + [still(w) for w in own] + [still(got)] + [ANYWHERE] * (2 + len(done)),
        out_specs=[pl.BlockSpec((rows, model), lambda n, b: (0, 0)), ANYWHERE, ANYWHERE, ANYWHERE],
        out_shape=[piece, piece] + [like(value) for value in away],
        scratch_shapes=[
            pltpu.VMEM((half, model), WIDE),
            buffer(4),
            buffer(4),
            buffer(2),
            pltpu.SemaphoreType.DMA((8,)),
            pltpu.SemaphoreType.DMA((8,)),
        ],
        compiler_params=pltpu.CompilerParams(collective_id=6, has_side_effects=True, vmem_limit_bytes=56 << 20),
        cost_estimate=pl.CostEstimate(flops=40 * 10**9, bytes_accessed=20 << 20, transcendentals=0),
    )(*grads, *own, got, *away, *done)


def grad_kernel(ids, *refs, chunks, kinds, fixed):
    xs, ys = refs[:chunks], refs[chunks : chunks * (1 + kinds)]
    outs, turned = refs[chunks * (1 + kinds) : -1], refs[-1]
    step = pl.program_id(0)
    rows = xs[0].shape[0]

    def turn():
        for j in range(chunks):
            turned[:, j * rows : (j + 1) * rows] = xs[j][...].T

    if fixed:
        pl.when(step == 0)(turn)
    else:
        turn()
    for f in range(kinds):
        total = None
        for j in range(chunks):
            part = dot(turned[:, j * rows : (j + 1) * rows], ys[f * chunks + j][...], NN)
            total = part if total is None else total + part
        total = total.astype(LOW)
        if len(outs) == 1:
            outs[0][f] = total
        else:
            for k, out in enumerate(outs):

                @pl.when(step == k)
                def _():
                    out[f] = total


def weight_grad(ids, xs, ys, x_blocks, done=(), side=None, apart=False):
    chunks, kinds = len(xs), len(ys)
    rows, x_width = xs[0][0].shape[-2:]
    y_width = ys[0][0][0].shape[-1]

    def spec(piece, width, at, once):
        mode = {"pipeline_mode": ONCE} if once else {}
        if piece[1] is None:
            return pl.BlockSpec((rows, width), at, **mode)
        place = lambda b, ids, n=piece[1]: (n, *at(b, ids))
        return pl.BlockSpec((pl.Squeezed(), rows, width), place, **mode)

    shift = lambda b, ids: (0, ids[1] ^ b if apart else b)
    still = lambda b, ids: (0, side or 0)
    share = 1 if side is None else 2
    if x_blocks:
        x_width, y_width = x_width // 4, y_width // share
        x_at, y_at = (x_width, shift, False), (y_width, still, True)
        whole, out_at = (kinds, 4 * x_width, y_width), lambda b, ids: (0, b, 0)
    else:
        x_width, y_width = x_width // share, y_width // 4
        x_at, y_at = (x_width, still, True), (y_width, shift, False)
        whole, out_at = (kinds, x_width, 4 * y_width), lambda b, ids: (0, 0, b)
    out = (kinds, x_width, y_width)
    if apart:
        out_specs = [pl.BlockSpec(out, lambda b, ids: (0, 0, 0))] * 4
        out_shape = [jax.ShapeDtypeStruct(out, LOW)] * 4
    else:
        out_specs, out_shape = [pl.BlockSpec(out, out_at)], [jax.ShapeDtypeStruct(whole, LOW)]
    result = kernel_call(
        partial(grad_kernel, chunks=chunks, kinds=kinds, fixed=not x_blocks),
        (4,),
        [spec(x, *x_at) for x in xs] + [spec(y, *y_at) for group in ys for y in group],
        out_specs,
        out_shape,
        [pltpu.VMEM((x_width, rows * chunks), LOW)],
        8 * rows * chunks * x_width * y_width * kinds,
        2 * rows * chunks * (4 * x_width + 4 * y_width * kinds),
        (ids, *[x[0] for x in xs], *[y[0] for group in ys for y in group]),
        done,
    )
    return result if apart else result[0]


def flip(value, axis, mask):
    return lax.ppermute(value, axis, [(i, i ^ mask) for i in range(lax.axis_size(axis))])


def add_low(one, two):
    return (one.astype(WIDE) + two.astype(WIDE)).astype(LOW)


def sum_everywhere(value):
    for axis, mask in (("dp", 1), ("dp", 2), ("mp", 1), ("mp", 2), ("mp", 4)):
        value = value + flip(value, axis, mask)
    return value


def partners():
    row, column = lax.axis_index("dp"), lax.axis_index("mp")
    over_x = (row + 1 - 2 * (row % 2), column)
    over_y = ((row + 2) % 4, column)
    over_core = (row, column + 1 - 2 * (column % 2))
    over_low = (row, column + 2 - 4 * ((column // 2) % 2))
    over_high = (row, (column + 4) % 8)
    return over_x, over_y, over_core, over_low, over_high


def greet(others):
    barrier = pltpu.get_barrier_semaphore()
    for other in others:
        pl.semaphore_signal(barrier, inc=1, device_id=other, device_id_type=MESH)
    pl.semaphore_wait(barrier, len(others))


class Sender:
    def __init__(self, sent, got):
        self.sent, self.got, self.count = sent, got, 0

    def __call__(self, source, target, device):
        copy = pltpu.make_async_remote_copy(
            src_ref=source,
            dst_ref=target,
            send_sem=self.sent.at[self.count],
            recv_sem=self.got.at[self.count],
            device_id=device,
            device_id_type=MESH,
        )
        self.count += 1
        copy.start()
        return copy


def open_kernel(text, head, text_got, head_x, head_y, head_far, sent, got):
    over_x, over_y, _, _, over_high = partners()
    greet((over_x, over_y, over_high))
    send = Sender(sent, got)
    half = head.shape[1] // 2
    upper, lower = pl.ds(0, half), pl.ds(half, half)
    copies = [send(text, text_got, over_high)]
    first = send(head.at[:, upper], head_x.at[:, upper], over_x)
    second = send(head.at[:, lower], head_y.at[:, lower], over_y)
    copies.append(send(head.at[:, lower], head_x.at[:, lower], over_x))
    copies.append(send(head.at[:, upper], head_y.at[:, upper], over_y))
    first.wait()
    copies.append(send(head_x.at[:, upper], head_far.at[:, upper], over_y))
    second.wait()
    copies.append(send(head_y.at[:, lower], head_far.at[:, lower], over_x))
    for copy in copies:
        copy.wait()


def open_exchange(text, head):
    return pl.pallas_call(
        open_kernel,
        in_specs=[ANYWHERE] * 2,
        out_specs=[ANYWHERE] * 4,
        out_shape=[like(text), like(head), like(head), like(head)],
        scratch_shapes=[pltpu.SemaphoreType.DMA((7,)), pltpu.SemaphoreType.DMA((7,))],
        compiler_params=pltpu.CompilerParams(collective_id=0, has_side_effects=True),
        cost_estimate=pl.CostEstimate(flops=0, bytes_accessed=100 << 20, transcendentals=0),
    )(text, head)


def normed_kernel(normed, head, outward, upward, _, near, far, far_near, head_got, pieces, others, up_got, sent, got):
    over_x, over_y, over_core, over_low, over_high = partners()
    greet((over_x, over_y, over_core, over_low, over_high))
    send = Sender(sent, got)
    rows = normed.shape[0] // 2
    parts = [pl.ds(b * rows, rows) for b in range(2)]
    crossing = [send(normed.at[part], far.at[part], over_low) for part in parts]
    copies = [send(normed, near, over_core), send(head, head_got, over_high), send(upward, up_got, over_high)]
    half = outward.shape[0] // 2
    upper, lower = pl.ds(0, half), pl.ds(half, half)
    first = send(outward.at[upper], pieces.at[0, upper], over_x)
    second = send(outward.at[lower], pieces.at[1, lower], over_y)
    later = [
        (send(outward.at[lower], pieces.at[0, lower], over_x), 0, lower),
        (send(outward.at[upper], pieces.at[1, upper], over_y), 1, upper),
    ]
    first.wait()
    later.append((send(pieces.at[0, upper], pieces.at[2, upper], over_y), 2, upper))
    copies.append(send(pieces.at[0, upper], others.at[0, upper], over_core))
    second.wait()
    later.append((send(pieces.at[1, lower], pieces.at[2, lower], over_x), 2, lower))
    copies.append(send(pieces.at[1, lower], others.at[1, lower], over_core))
    for copy, part in zip(crossing, parts):
        copy.wait()
        copies.append(send(far.at[part], far_near.at[part], over_core))
    for copy, n, part in later:
        copy.wait()
        copies.append(send(pieces.at[n, part], others.at[n, part], over_core))
    for copy in copies:
        copy.wait()


def normed_exchange(normed, head, outward, upward, done):
    pieces = jax.ShapeDtypeStruct((3,) + outward.shape, LOW)
    return pl.pallas_call(
        normed_kernel,
        in_specs=[ANYWHERE] * 5,
        out_specs=[ANYWHERE] * 7,
        out_shape=[like(normed)] * 3 + [like(head), pieces, pieces, like(upward)],
        scratch_shapes=[pltpu.SemaphoreType.DMA((19,)), pltpu.SemaphoreType.DMA((19,))],
        compiler_params=pltpu.CompilerParams(collective_id=1, has_side_effects=True),
        cost_estimate=pl.CostEstimate(flops=0, bytes_accessed=100 << 20, transcendentals=0),
    )(normed, head, outward, upward, done)


def adapt(kept, got, master, moment, square):
    gradient = kept if got is None else kept + got
    moment_new = BETA_ONE * moment + (1.0 - BETA_ONE) * gradient
    square_new = BETA_TWO * square + (1.0 - BETA_TWO) * gradient * gradient
    return moment_new, square_new, direction_of(master, moment_new, square_new)


def direction_of(master, moment_new, square_new):
    root = jnp.sqrt(square_new / (1.0 - BETA_TWO**STEP)) + EPS_ADAM
    return moment_new / (1.0 - BETA_ONE**STEP) / root + DECAY_RATE * master


def close_kernel(*refs, groups, first_steps):
    kept, got, merged, middle, gain = refs[:5]
    count = 5 + sum(groups) + 3 * len(groups)
    weights, outs = refs[5:count], refs[count:]
    moments, (rows, gains, norms, arrived) = outs[: 2 * len(groups)], outs[2 * len(groups) : 2 * len(groups) + 4]
    sending, sent, got_sem = outs[2 * len(groups) + 4 :]
    step = pl.program_id(0)
    over_high = partners()[4]
    side = lax.axis_index("mp") // 4
    crossing = remote(sending, arrived, sent, got_sem, over_high)

    @pl.when(step == 0)
    def _():
        greet((over_high,))
        gains[...] = jnp.zeros_like(gains)
        norms[...] = jnp.zeros_like(norms)

    @pl.when(step < first_steps)
    def _():
        grad = kept[...].astype(WIDE) + got[...].astype(WIDE)
        standard, scale = centred(merged[...].astype(WIDE))
        gains[0:1, :] += jnp.sum(grad * standard, axis=0, keepdims=True)
        total = middle[...] + norm_back(standard, scale, gain[...], grad)
        rows[...] = total
        half = first_steps // 2
        here = pl.ds(pl.multiple_of((step % half) * total.shape[0], total.shape[0]), total.shape[0])

        @pl.when(step // half != side)
        def _():
            sending[here, :] = total.astype(LOW)

    @pl.when(step == first_steps - 1)
    def _():
        crossing.start()

    at = 0
    for n, size in enumerate(groups):
        grads, (master, moment, square) = weights[at : at + size], weights[at + size : at + size + 3]
        at += size + 3
        wide = [g[...].astype(WIDE) for g in grads] + [None]
        moment_new, square_new, direction = adapt(wide[0], wide[1], master[...], moment[...], square[...])
        moments[2 * n][...] = moment_new
        moments[2 * n + 1][...] = square_new
        for k, value in enumerate((master[...], direction)):
            norms[k, n : n + 1, :] += jnp.sum(fold(value * value), axis=0, keepdims=True)

    @pl.when(step == pl.num_programs(0) - 1)
    def _():
        crossing.wait()


def close(kept, got, merged, middle, gain, weights):
    rows, model = kept.shape
    steps, first_steps = 16, 4
    line = pl.BlockSpec((rows // first_steps, model), lambda i: (jnp.minimum(i, first_steps - 1), 0))
    in_specs, out_specs, out_shape, operands = [line] * 4 + [pl.BlockSpec((1, model), lambda i: (0, 0))], [], [], []
    for group in weights:
        shape = group[-1].shape
        block = shape[:-2] + (shape[-2] // steps, shape[-1])
        spec = pl.BlockSpec(block, lambda i, lead=len(shape) - 2: (0,) * lead + (i, 0))
        in_specs += [spec] * len(group)
        out_specs += [spec] * 2
        out_shape += [jax.ShapeDtypeStruct(shape, WIDE)] * 2
        operands += group
    out_specs += [
        line,
        pl.BlockSpec((8, model), lambda i: (0, 0)),
        pl.BlockSpec((2, 8, LANES), lambda i: (0, 0, 0)),
        ANYWHERE,
    ]
    out_shape += [
        jax.ShapeDtypeStruct((rows, model), WIDE),
        jax.ShapeDtypeStruct((8, model), WIDE),
        jax.ShapeDtypeStruct((2, 8, LANES), WIDE),
        jax.ShapeDtypeStruct((rows // 2, model), LOW),
    ]
    return pl.pallas_call(
        partial(close_kernel, groups=[len(group) - 3 for group in weights], first_steps=first_steps),
        grid=(steps,),
        in_specs=in_specs,
        out_specs=out_specs,
        out_shape=out_shape,
        scratch_shapes=[
            pltpu.VMEM((rows // 2, model), LOW),
            pltpu.SemaphoreType.DMA,
            pltpu.SemaphoreType.DMA,
        ],
        compiler_params=pltpu.CompilerParams(collective_id=7, has_side_effects=True, vmem_limit_bytes=56 << 20),
        cost_estimate=pl.CostEstimate(flops=10**9, bytes_accessed=100 << 20, transcendentals=0),
    )(kept, got, merged, middle, gain, *operands)


def rotary_tables(length):
    lane = jnp.arange(LANES, dtype=jnp.int32)
    pair_index = (lane % (HEAD_DIM // 2)).astype(WIDE)[None]
    sign = jnp.where(lane % HEAD_DIM < HEAD_DIM // 2, -1.0, 1.0)[None]
    angular = jnp.exp(-(2.0 * pair_index / HEAD_DIM) * jnp.log(10000.0))
    zeta_base = (2.0 * pair_index + 0.4 * HEAD_DIM) / (1.4 * HEAD_DIM)
    position = jnp.arange(length, dtype=WIDE)[:, None]
    cosine, sine_part = jnp.cos(position * angular), jnp.sin(position * angular) * sign
    exponent = position / 512.0 * jnp.log(zeta_base)
    up, down = jnp.exp(exponent), jnp.exp(-exponent)
    return [cosine * up, sine_part * up, cosine * down, sine_part * down]


def on_device_paired(
    text_states,
    image_states,
    image_offsets,
    image_counts,
    output_grad,
    head_master,
    head_moment,
    head_square,
    outward_master,
    outward_moment,
    outward_square,
    upward_master,
    upward_moment,
    upward_square,
    downward_master,
    downward_moment,
    downward_square,
    gains_master,
    gains_moment,
    gains_square,
):
    model_rank = lax.axis_index("mp")
    side = model_rank // 4
    rank = model_rank % 4
    place = lax.axis_index("dp")
    ids = jnp.stack([rank, place, side]).astype(jnp.int32)
    _, local_len, model_width = text_states.shape
    length = local_len * 8
    rows = 2 * local_len
    hidden_local = upward_master.shape[1]
    hidden_width = hidden_local * 8

    def pick(value, index):
        return lax.dynamic_index_in_dim(value, index, 0, keepdims=False)

    tables = rotary_tables(length)

    def both(kept, got):
        return jnp.where(side == 0, jnp.stack([kept, got]), jnp.stack([got, kept]))

    core = rank % 2
    half_width = model_width // 2
    text_out = pick(text_states, 1 - side)
    head_own = head_master.astype(LOW)
    upward_own = upward_master.astype(LOW)
    upward_weight = [lax.all_gather(upward_own, "dp", axis=0, tiled=True)]
    text_got, *head_parts = open_exchange(text_out, head_own)
    head_weight = [[head_own] + head_parts]
    downward_own = downward_master.astype(LOW)
    downward_weight = [lax.all_gather(downward_own, "dp", axis=1, tiled=True)]
    text = both(pick(text_states, side), text_got)

    gain_in = gains_master[None, :model_width]
    gain_ctx = gains_master[None, model_width : 2 * model_width]
    gain_mid = gains_master[None, 2 * model_width : 3 * model_width]
    hidden_start = 3 * model_width + model_rank * hidden_local
    other_start = 3 * model_width + (model_rank ^ 4) * hidden_local
    gain_hidden = jnp.concatenate(
        [
            lax.dynamic_slice_in_dim(gains_master, hidden_start, hidden_local),
            lax.dynamic_slice_in_dim(gains_master, other_start, hidden_local),
        ]
    )[None]

    offsets = pick(image_offsets, side)
    image_count = pick(image_counts, side)
    position = (
        jnp.arange(2, dtype=jnp.int32)[:, None] * (4 * local_len)
        + rank * local_len
        + jnp.arange(local_len, dtype=jnp.int32)[None, :]
    ).reshape(rows)
    slot_index = jnp.arange(offsets.shape[0], dtype=jnp.int32)
    inside = (
        (position[:, None] >= offsets[None, :])
        & (position[:, None] < offsets[None, :] + PATCH)
        & (slot_index[None, :] < image_count)
    )
    picked = jnp.sum(
        jnp.where(inside, slot_index[None, :] * PATCH + position[:, None] - offsets[None, :], 0), axis=-1
    )
    covered = jnp.any(inside, axis=-1)
    place_index = jnp.arange(image_states.shape[1], dtype=jnp.int32)
    chosen = (covered[:, None] & (picked[:, None] == place_index[None, :])).astype(LOW)
    images = jnp.dot(chosen, pick(image_states, side), preferred_element_type=WIDE).astype(LOW)
    merged = jnp.where(covered[:, None], images, text.reshape(rows, model_width))

    def turn_heads(pieces):
        return [pieces[0]] + [flip(pieces[j], "mp", j) for j in range(1, 4)]

    normed_own = layer_norm(merged.astype(WIDE), gain_in).astype(LOW)
    outward_low = outward_master.astype(LOW)
    outward_own, outward_other = (
        lax.dynamic_slice_in_dim(outward_low, n * half_width, half_width, 1) for n in (core, 1 - core)
    )
    near, far, far_near, head_got, *pieces, upward_got = normed_exchange(
        normed_own, head_own, outward_own, upward_own, upward_weight[0]
    )
    outward_weight = [outward_own, pieces[0], outward_other, pieces[1]]
    normed = [normed_own, near, far, far_near]
    head_weight.append(lax.all_gather(head_got, "dp", axis=1, tiled=True))
    upward_weight.append(lax.all_gather(upward_got, "dp", axis=0, tiled=True))
    got_cotangent = flip(pick(output_grad, 1 - side), "mp", 4)

    queries, keys, values, contexts, logs, arrived = [], [], [], [], [], []
    for half in range(2):
        projected = []
        for j, chunk in enumerate(normed):
            carry = [downward_own, got_cotangent] if half == 1 and j == 0 else []
            done = [projected[0][0]] if j > 0 else []
            outs = project(ids, chunk, head_weight[half], tables, j, done, carry)
            projected.append(outs[:3])
            if carry:
                downward_got = flip(outs[3], "mp", 4)
                cotangent = both(pick(output_grad, side), outs[4]).reshape(rows, model_width)
                cotangent_far = flip(cotangent, "mp", 2)
                cotangent_others = [flip(cotangent, "mp", 1), cotangent_far, flip(cotangent_far, "mp", 1)]
        for n, group in enumerate((queries, keys, values)):
            group.append([p[n] for p in projected])
        context, lse = attend(ids, queries[half], keys[half], values[half])
        contexts.append(context)
        logs.append(lse)
        arrived = arrived + turn_heads(context)
    context, mixed, middle, lifted_own, downward_got = mid_forward(
        ids, arrived, merged, outward_weight, gain_ctx, gain_mid, [downward_got]
    )
    downward_weight.append(lax.all_gather(downward_got, "dp", axis=1, tiled=True))
    act, slope, sums, lifted_others = ffn_up(lifted_own, upward_weight)
    squashed_grad, back_sums = ffn_back(cotangent, cotangent_others, downward_weight, act, gain_hidden)
    lifted = [(lifted_own, None)] + [(lifted_others, n) for n in range(3)]
    cotangents = [(value, None) for value in [cotangent] + cotangent_others]
    sums = sums + back_sums
    others = [flip(sums, "mp", k) for k in range(1, 4)]
    sums = jnp.stack(
        [(sums[j] + others[0][j ^ 1]) + (others[1][j ^ 2] + others[2][j ^ 3]) for j in range(4)]
    )
    squashed, hidden_grad, lifted_kept, lifted_got, hidden_gains = ffn_second(
        act, slope, squashed_grad, sums, gain_hidden, upward_weight, hidden_width
    )

    def split(value):
        return [(value, n) for n in range(4)]

    def whole(values):
        return [(value, None) for value in values]

    down_grad = lax.psum_scatter(
        weight_grad(ids, split(squashed), [cotangents], False), "dp", scatter_dimension=2, tiled=True
    )[0]
    middle_grad, middle_low, own_grads, other_grads, mid_gains = mid_backward(
        ids, (lifted_kept, lifted_got), middle, cotangent, context, outward_weight, gain_mid, gain_ctx
    )
    context_heads = [turn_heads(own_grads), turn_heads(other_grads)]
    up_part = weight_grad(ids, lifted, [split(hidden_grad)], True)
    up_grad = lax.psum_scatter(up_part, "dp", scatter_dimension=1, tiled=True)[0]
    ffn_parts = [ffn_out(ids, squashed, j, downward_weight) for j in range(4)]

    def scatter_tokens(parts):
        passed = add_low(parts[2], flip(parts[3], "mp", 1))
        return add_low(parts[0], flip(parts[1], "mp", 1)), flip(passed, "mp", 2)

    def give_back(pair):
        got = flip(pick(pair, 1 - side).astype(LOW), "mp", 4)
        return both(pick(pair, side), got.astype(pair.dtype))

    ffn_kept, ffn_got = scatter_tokens(ffn_parts)
    output_rows = (middle + (ffn_kept.astype(WIDE) + ffn_got.astype(WIDE))).astype(LOW)
    output_rows = output_rows.reshape(2, local_len, model_width)

    head_grads, head_sides, backs = [None, None], [None, None], [None, None]
    leaving = (pick(output_rows, 1 - side), down_grad[hidden_local:])
    for half in (1, 0):
        *head_grads[half], backs[half] = attend_back(
            queries[half],
            keys[half],
            values[half],
            context_heads[half],
            contexts[half],
            logs[half],
            tables,
            leaving[half],
            4 + half,
            [ffn_kept] if half else [],
        )
        head_part = weight_grad(ids, whole(normed), [split(g) for g in head_grads[half]], True)
        head_sides[half] = lax.psum_scatter(head_part, "dp", scatter_dimension=1, tiled=True)
        if half == 1:
            outward_part = weight_grad(ids, whole([mixed]), [whole([middle_low])], True, [head_part])[0]
            outward_sent = lax.dynamic_slice_in_dim(outward_part, (1 - core) * half_width, half_width, 1)
            outward_half = add_low(
                lax.dynamic_slice_in_dim(outward_part, core * half_width, half_width, 1), flip(outward_sent, "mp", 1)
            )
            outward_grad = lax.psum_scatter(outward_half, "dp", scatter_dimension=0, tiled=True)
    output_got, down_got = backs
    layer_output = both(pick(output_rows, side), output_got)
    outward_grad = lax.psum(outward_grad, "mp", axis_index_groups=[[0, 2, 4, 6], [1, 3, 5, 7]])
    normed_kept, normed_got, up_got, head_got_grad = unproject(
        head_grads[0] + head_grads[1], head_weight, [up_grad[:, hidden_local:], head_sides[1]], [head_part, outward_grad]
    )
    result = close(
        normed_kept,
        normed_got,
        merged,
        middle_grad,
        gain_in,
        [
            [up_grad[:, :hidden_local], up_got, upward_master, upward_moment, upward_square],
            [down_grad[:hidden_local], down_got, downward_master, downward_moment, downward_square],
        ],
    )
    moment_upward, square_upward, moment_downward, square_downward = result[:4]
    input_rows, in_gain_grad, norm_lanes, input_got = result[4:]
    moment_head, square_head, head_dir = adapt_step(
        head_sides[0].astype(WIDE) + head_got_grad.astype(WIDE), head_master, head_moment, head_square, DECAY_RATE
    )
    outward_grad = hand_on(outward_grad, [input_got])
    outward_got = flip(outward_grad, "mp", 1)
    outward_grad = jnp.where(
        core == 0,
        jnp.concatenate([outward_grad, outward_got], axis=1),
        jnp.concatenate([outward_got, outward_grad], axis=1),
    )
    moment_outward, square_outward, outward_dir = adapt_step(
        outward_grad.astype(WIDE), outward_master, outward_moment, outward_square, DECAY_RATE
    )
    upward_dir = direction_of(upward_master, moment_upward, square_upward)
    downward_dir = direction_of(downward_master, moment_downward, square_downward)
    input_grad = both(pick(input_rows.reshape(2, local_len, model_width), side), input_got.astype(WIDE))
    owner = (model_rank == 0).astype(WIDE)
    norm_part = jnp.concatenate(
        [
            jnp.stack([jnp.sum(head_master * head_master, axis=(1, 2)), jnp.sum(head_dir * head_dir, axis=(1, 2))], axis=-1),
            pair_sums(outward_master, outward_dir) * owner,
            jnp.sum(norm_lanes, axis=-1)[:, :2].T,
        ],
        axis=0,
    )
    hidden_gain = hidden_gains[0]
    gains_part = jnp.concatenate([in_gain_grad[0], mid_gains[1], mid_gains[0], jnp.zeros((hidden_width,), WIDE)])
    gains_part = lax.dynamic_update_slice(gains_part, hidden_gain[:hidden_local], (hidden_start,))
    gains_part = lax.dynamic_update_slice(gains_part, hidden_gain[hidden_local:], (other_start,))
    every = sum_everywhere(jnp.concatenate([gains_part, norm_part.reshape(-1)]))
    gains_sum, norm_sums = every[: gains_part.shape[0]], every[gains_part.shape[0] :].reshape(6, 2)
    moment_gains, square_gains, gains_dir = adapt_step(gains_sum, gains_master, gains_moment, gains_square, 0.0)
    gains_sums = jnp.stack(
        [
            gain_segments(gains_master * gains_master, model_width),
            gain_segments(gains_dir * gains_dir, model_width),
        ],
        axis=-1,
    )
    updated_head = trust_move(
        head_master, head_dir, norm_sums[:3, 0][:, None, None], norm_sums[:3, 1][:, None, None]
    )
    updated_outward = trust_move(outward_master, outward_dir, norm_sums[3, 0], norm_sums[3, 1])
    updated_upward = trust_move(upward_master, upward_dir, norm_sums[4, 0], norm_sums[4, 1])
    updated_downward = trust_move(downward_master, downward_dir, norm_sums[5, 0], norm_sums[5, 1])
    updated_gains = trust_move(
        gains_master,
        gains_dir,
        gain_spread(gains_sums[:, 0], model_width, hidden_width),
        gain_spread(gains_sums[:, 1], model_width, hidden_width),
    )
    update_norms = jnp.sqrt(jnp.concatenate([norm_sums, gains_sums], axis=0))
    return (
        layer_output,
        input_grad,
        moment_head,
        square_head,
        updated_head,
        updated_head.astype(LOW),
        moment_outward,
        square_outward,
        updated_outward,
        updated_outward.astype(LOW),
        moment_upward,
        square_upward,
        updated_upward,
        updated_upward.astype(LOW),
        moment_downward,
        square_downward,
        updated_downward,
        updated_downward.astype(LOW),
        moment_gains,
        square_gains,
        updated_gains,
        update_norms,
    )


def solution(mesh):
    paired = mesh.shape["dp"] == 4 and mesh.shape["mp"] == 8
    return jax.shard_map(
        on_device_paired if paired else on_device_general,
        mesh=mesh,
        in_specs=(
            P("dp", "mp", None),
            P("dp", None, None),
            P("dp", None),
            P("dp"),
            P("dp", "mp", None),
            P(None, "dp", "mp"),
            P(None, "dp", "mp"),
            P(None, "dp", "mp"),
            P("dp", None),
            P("dp", None),
            P("dp", None),
            P("dp", "mp"),
            P("dp", "mp"),
            P("dp", "mp"),
            P("mp", "dp"),
            P("mp", "dp"),
            P("mp", "dp"),
            P(),
            P(),
            P(),
        ),
        out_specs=(
            P("dp", "mp", None),
            P("dp", "mp", None),
            P(None, "dp", "mp"),
            P(None, "dp", "mp"),
            P(None, "dp", "mp"),
            P(None, "dp", "mp"),
            P("dp", None),
            P("dp", None),
            P("dp", None),
            P("dp", None),
            P("dp", "mp"),
            P("dp", "mp"),
            P("dp", "mp"),
            P("dp", "mp"),
            P("mp", "dp"),
            P("mp", "dp"),
            P("mp", "dp"),
            P("mp", "dp"),
            P(),
            P(),
            P(),
            P(),
        ),
        check_vma=False,
    )
```
